32 devices in a mesh: dp: 4 (over x, core), ctx: 8 (over z, y).
Axes of the slice: x: 2, y: 2, z: 4, core: 2. Of those that a mesh axis runs over, the one named last changes fastest.
Arguments:
- tokens: bfloat16 [4, 8, 2, 64, 2048], P('dp', 'ctx'), may hold values from -6 to 6
- cotangent: bfloat16 [4, 8, 2, 64, 2048], P('dp', 'ctx'), may hold values from -6 to 6
- w_qkv: bfloat16 [2048, 6144], P('dp'), may hold values from -0.125 to 0.125
- b_qkv: bfloat16 [6144], P('dp'), may hold values from -0.119628906 to 0.119628906
- w_out: bfloat16 [2048, 2048], P('dp'), may hold values from -3 to 3
- w_gate: bfloat16 [2048, 5632], P('dp'), may hold values from -0.125 to 0.125
- w_up: bfloat16 [2048, 5632], P('dp'), may hold values from -0.125 to 0.125
- w_down: bfloat16 [5632, 2048], P('dp'), may hold values from -0.078125 to 0.078125
- norms: bfloat16 [4, 2048], P(None, 'dp'), may hold values from -1 to 2, as said below
Outputs:
- output: bfloat16 [4, 8, 2, 64, 2048], P('dp', 'ctx')
- tokens_grad: float32 [4, 8, 2, 64, 2048], P('dp', 'ctx')
- w_qkv_grad: float32 [2048, 6144], P(('dp', 'ctx'))
- b_qkv_grad: float32 [6144], P(('dp', 'ctx'))
- w_out_grad: float32 [2048, 2048], P(('dp', 'ctx'))
- w_gate_grad: float32 [2048, 5632], P(('dp', 'ctx'))
- w_up_grad: float32 [2048, 5632], P(('dp', 'ctx'))
- w_down_grad: float32 [5632, 2048], P(('dp', 'ctx'))
- norms_grad: float32 [4, 2048], P(None, ('dp', 'ctx'))
The draws below stay inside these ranges and needn't reach their ends.
Inputs may be any that keep to these rules, and one draw needn't show every extreme that they name: `norms`: rows 0 and 2 lie near one, rows 1 and 3 near zero.
All inputs are finite; a program needn't handle non-finite values.
Results may differ from the reference program's by a relative error of at most 0.014.
Values may be sent and summed in bfloat16 or wider, within the bound.
A program may use at most 448 MiB of HBM per device.

```python
import math
import jax
import jax.numpy as jnp
from jax import lax

D = 2048
HEADS = 32
HDIM = 64
FF = 5632
ROT = 16
HALF = 64
SEQS = 4
N_CTX = 8


def draw_norms(key, part):
    key = jax.random.fold_in(key, 7)
    noise = jnp.clip(jax.random.normal(key, (4, D), jnp.float32), -4.0, 4.0)
    base = jnp.array([1.0, 0.0, 1.0, 0.0], jnp.float32)[:, None]
    spread = jnp.array([0.15, 0.1, 0.15, 0.1], jnp.float32)[:, None]
    return (base + spread * noise).astype(jnp.bfloat16)


def levels(stream_key, shape, cuts, least, top_value):
    level = 1.0
    for position, blocks in cuts:
        heights = jax.random.uniform(jax.random.fold_in(jax.random.fold_in(stream_key, 6), position), (blocks,), jnp.float32, least / len(cuts), top_value / len(cuts))
        level = level * jnp.repeat(jnp.exp(heights), shape[position] // blocks).reshape((-1,) + (1,) * (len(shape) - 1 - position))
    return level


def bell_draw(own_key, dims, width, most, split=(), kind=jnp.bfloat16):
    level = levels(own_key, dims, split, -0.22, 0.18) if split else 1.0
    drawn = jax.random.normal(own_key, dims, jnp.float32) * width * level
    return jnp.minimum(jnp.maximum(drawn, -most), most).astype(kind)


def setup_inputs(seed: int = 0) -> dict:
    seeds = jax.random.split(jax.random.key(seed), 10)
    return {
        "tokens": bell_draw(seeds[0], (SEQS, N_CTX, 2, HALF, D), 1.0, 6.0, ((0, 4), (1, 8))),
        "cotangent": bell_draw(seeds[1], (SEQS, N_CTX, 2, HALF, D), 1.0, 6.0, ((0, 4), (1, 8))),
        "w_qkv": bell_draw(seeds[2], (D, 3 * D), D ** -0.5, 0.125, ((0, 4),)),
        "b_qkv": bell_draw(seeds[3], (3 * D,), 0.02, 0.119628906, ((0, 4),)),
        "w_out": bell_draw(seeds[4], (D, D), 4 ** -0.5, 3.0, ((0, 4),)),
        "w_gate": bell_draw(seeds[5], (D, FF), D ** -0.5, 0.125, ((0, 4),)),
        "w_up": bell_draw(seeds[6], (D, FF), D ** -0.5, 0.125, ((0, 4),)),
        "w_down": bell_draw(seeds[7], (FF, D), FF ** -0.5, 0.078125, ((0, 4),)),
        "norms": draw_norms(jax.random.fold_in(seeds[9], 71), 0),
    }


@jax.custom_vjp
def low(v):
    return lax.optimization_barrier(v.astype(jnp.bfloat16)).astype(jnp.float32)

@jax.custom_vjp
def low_back(v):
    return v

def low_keep(v):
    return (low(v), None)

def low_pass(kept, incoming_gradient):
    return (incoming_gradient,)

def back_keep(v):
    return (v, None)

def back_low(kept, incoming_gradient):
    return (low(incoming_gradient),)
low.defvjp(low_keep, low_pass)
low_back.defvjp(back_keep, back_low)
HIGH = lax.Precision.HIGHEST

def matmul(left, right):
    return jnp.dot(left, right, precision=HIGH)

def layer_norm(field, norm_gain, shift):
    centre = field - lax.optimization_barrier(jnp.mean(field, axis=-1, keepdims=True))
    spread = lax.optimization_barrier(jnp.mean(centre * centre, axis=-1, keepdims=True))
    return centre * lax.rsqrt(spread + 1e-05) * norm_gain + shift

def rotary_table(positions):
    pairs = ROT // 2
    inverse = jnp.power(10000.0, -jnp.arange(pairs, dtype=jnp.float32) / pairs)
    angle = positions.astype(jnp.float32)[:, None] * inverse[None, :]
    return (jnp.cos(angle), jnp.sin(angle))

def rotate(field, cosine, sine):
    pairs = ROT // 2
    first = field[..., :pairs]
    second = field[..., pairs:ROT]
    cosine = cosine[:, None, :]
    sine = sine[:, None, :]
    return jnp.concatenate([first * cosine - second * sine, second * cosine + first * sine, field[..., ROT:]], axis=-1)

def layer(x, w_qkv, b_qkv, w_out, w_gate, w_up, w_down, norms):
    length = x.shape[0]
    h1 = low(layer_norm(x, norms[0], norms[1]))
    qkv = low_back(matmul(h1, w_qkv) + b_qkv)
    positions = jnp.arange(length, dtype=jnp.int32)
    cosine, sine = rotary_table(positions)
    query = low(rotate(qkv[:, :D].reshape(length, HEADS, HDIM), cosine, sine))
    key = low(rotate(qkv[:, D:2 * D].reshape(length, HEADS, HDIM), cosine, sine))
    value = low(qkv[:, 2 * D:].reshape(length, HEADS, HDIM))
    block = math.gcd(length, 512)

    def attend(index):
        start = index * block
        rows = lax.dynamic_slice_in_dim(query, start, block, 0)
        scores = low_back(0.125 * jnp.einsum('qhd,khd->hqk', rows, key, precision=HIGH))
        row_pos = start + jnp.arange(block, dtype=jnp.int32)
        allowed = positions[None, :] <= row_pos[:, None]
        scores = jnp.where(allowed[None], scores, -1e+30)
        top = lax.optimization_barrier(jnp.max(scores, axis=-1, keepdims=True))
        expo = jnp.exp(scores - top)
        probs = low(expo / lax.optimization_barrier(jnp.sum(expo, axis=-1, keepdims=True)))
        return jnp.einsum('hqk,khd->qhd', probs, value, precision=HIGH)
    mixed = lax.map(jax.checkpoint(attend), jnp.arange(length // block, dtype=jnp.int32))
    mixed = low(low_back(mixed.reshape(length, D)))
    first_residual = x + low_back(matmul(mixed, w_out))
    h2 = low(layer_norm(first_residual, norms[2], norms[3]))
    gate = low_back(matmul(h2, w_gate))
    up = low_back(matmul(h2, w_up))
    hidden = low(gate * jax.nn.sigmoid(gate) * up)
    return first_residual + low_back(matmul(hidden, w_down))

def natural(blocks):
    return jnp.concatenate([blocks[:, 0].reshape(-1, D), blocks[::-1, 1].reshape(-1, D)], axis=0)

def dealt(whole):
    first = whole[:N_CTX * HALF].reshape(N_CTX, HALF, D)
    second = whole[N_CTX * HALF:].reshape(N_CTX, HALF, D)[::-1]
    return jnp.stack([first, second], axis=1)

def reference(tokens, cotangent, w_qkv, b_qkv, w_out, w_gate, w_up, w_down, norms):
    weights = (w_qkv.astype(jnp.float32), b_qkv.astype(jnp.float32), w_out.astype(jnp.float32), w_gate.astype(jnp.float32), w_up.astype(jnp.float32), w_down.astype(jnp.float32), norms.astype(jnp.float32))

    def one(totals, pair):
        seq_in, seq_cot = pair
        xs = natural(seq_in.astype(jnp.float32))
        cot = natural(seq_cot.astype(jnp.float32))
        result, pull = jax.vjp(layer, xs, *weights)
        grads = pull(cot)
        summed = tuple((a + b for a, b in zip(totals, grads[1:])))
        return (summed, (dealt(result).astype(jnp.bfloat16), dealt(grads[0])))
    start = tuple((jnp.zeros_like(w) for w in weights))
    totals, (output, tokens_grad) = lax.scan(one, start, (tokens, cotangent))
    return (output, tokens_grad, totals[0], totals[1], totals[2], totals[3], totals[4], totals[5], totals[6])
```

```python
import jax
import jax.numpy as jnp
from jax import lax
from jax.experimental import pallas as pl
from jax.experimental.pallas import tpu as pltpu
from jax.sharding import PartitionSpec as P

HEADS = 32
HDIM = 64
ROT = 16
MESH = pl.DeviceIdType.MESH
F32 = jnp.float32
BF16 = jnp.bfloat16
VMEM_BYTES = 56 * 1024 * 1024


def normalize_rows(field):
    centre = field - jnp.mean(field, axis=-1, keepdims=True)
    inverse = lax.rsqrt(jnp.mean(centre * centre, axis=-1, keepdims=True) + 1e-05)
    return (centre * inverse, inverse)


def norm_reverse(incoming, gain, scaled, inverse):
    inner = incoming * gain
    return inverse * (
        inner
        - jnp.mean(inner, axis=-1, keepdims=True)
        - scaled * jnp.mean(inner * scaled, axis=-1, keepdims=True)
    )


def rotary_factors(positions):
    pairs = ROT // 2
    inverse = jnp.power(10000.0, -jnp.arange(pairs, dtype=F32) / pairs)
    angle = positions.astype(F32)[:, None] * inverse[None, :]
    cosine, sine = jnp.cos(angle), jnp.sin(angle)
    rows = positions.shape[0]
    none = jnp.zeros((rows, HDIM - ROT), F32)
    blank = jnp.zeros((rows, pairs), F32)
    keep = jnp.concatenate([cosine, cosine, none + 1.0], axis=1)
    left = jnp.concatenate([-sine, blank, none], axis=1)
    right = jnp.concatenate([blank, sine, none], axis=1)
    return keep, left, right


def turn(field, factors, sign):
    keep, left, right = factors
    heads = field.shape[-1] // HDIM
    pairs = ROT // 2
    keep, left, right = (jnp.tile(t, (1, heads)) for t in (keep, left, right))
    return (
        field * keep
        + jnp.roll(field, -pairs, axis=-1) * (left * sign)
        + jnp.roll(field, pairs, axis=-1) * (right * sign)
    )


def exchange(axis, size, cid, items):
    counts = [len(plan(0, 0)) for _, _, plan in items]
    total = sum(counts)

    def body(*refs):
        ins = refs[: len(items)]
        outs = refs[len(items) : 2 * len(items)]
        send, recv, local = refs[2 * len(items) :]
        me = lax.axis_index(axis)
        barrier = pltpu.get_barrier_semaphore()
        for k in range(1, size):
            pl.semaphore_signal(
                barrier, inc=1, device_id={axis: lax.rem(me + k, size)}, device_id_type=MESH
            )
        pl.semaphore_wait(barrier, size - 1)
        copies = []
        for k in range(1, size):
            peer = lax.rem(me + k, size)
            at = 0
            for (_, _, plan), src, dst in zip(items, ins, outs):
                for a, b in plan(me, peer):
                    copy = pltpu.make_async_remote_copy(
                        src_ref=src.at[a],
                        dst_ref=dst.at[b],
                        send_sem=send.at[k - 1, at],
                        recv_sem=recv.at[k - 1, at],
                        device_id={axis: peer},
                        device_id_type=MESH,
                    )
                    copy.start()
                    copies.append(copy)
                    at += 1
        at = 0
        for (_, _, plan), src, dst in zip(items, ins, outs):
            for a, b in plan(me, me):
                copy = pltpu.make_async_copy(src.at[a], dst.at[b], local.at[at])
                copy.start()
                copies.append(copy)
                at += 1
        for copy in copies:
            copy.wait()

    anywhere = pl.BlockSpec(memory_space=pl.ANY)
    return pl.pallas_call(
        body,
        out_shape=[jax.ShapeDtypeStruct(shape, x.dtype) for x, shape, _ in items],
        in_specs=[anywhere] * len(items),
        out_specs=[anywhere] * len(items),
        scratch_shapes=[
            pltpu.SemaphoreType.DMA((size - 1, total)),
            pltpu.SemaphoreType.DMA((size - 1, total)),
            pltpu.SemaphoreType.DMA((total,)),
        ],
        compiler_params=pltpu.CompilerParams(collective_id=cid, has_side_effects=True),
    )(*[x for x, _, _ in items])


def gather(axis, size, cid, *arrays):
    return exchange(
        axis,
        size,
        cid,
        [(x, (size,) + x.shape, lambda me, peer: [(slice(None), me)]) for x in arrays],
    )


def swap_blocks(axis, size, cid, x):
    return exchange(axis, size, cid, [(x, x.shape, lambda me, peer: [(peer, me)])])[0]


def to_sequence(size, cid, x):
    half = x.shape[1] // 2

    def plan(me, peer):
        return [
            ((peer, pl.ds(0, half)), me),
            ((peer, pl.ds(half, half)), 2 * size - 1 - me),
        ]

    return exchange("ctx", size, cid, [(x, (2 * size, half, x.shape[2]), plan)])[0]


def from_sequence(size, cid, x):
    half = x.shape[1]

    def plan(me, peer):
        return [
            (peer, (me, pl.ds(0, half))),
            (2 * size - 1 - peer, (me, pl.ds(half, half))),
        ]

    return exchange("ctx", size, cid, [(x, (size, 2 * half, x.shape[2]), plan)])[0]


def last_dims(a, b):
    return lax.dot_general(a, b, (((1,), (1,)), ((), ())), preferred_element_type=F32)


def first_dims(a, b):
    return lax.dot_general(a, b, (((0,), (0,)), ((), ())), preferred_element_type=F32)


def plain(a, b):
    return lax.dot_general(a, b, (((1,), (0,)), ((), ())), preferred_element_type=F32)


def attention_shapes(length):
    block = min(256, length)
    segments = min(4, length // block)
    return block, segments, length // block // segments


def head_columns(heads, what, head):
    at = (what * heads + head) * HDIM
    return slice(at, at + HDIM)


def causal(scores, first_query):
    keys = lax.broadcasted_iota(jnp.int32, scores.shape, 0)
    queries = lax.broadcasted_iota(jnp.int32, scores.shape, 1) + first_query
    return jnp.where(keys <= queries, scores, -1e30)


def attention_forward(qkv, heads):
    length = qkv.shape[0]
    block, segments, inner = attention_shapes(length)

    def body(x_ref, o_ref, lse_ref):
        for head in range(heads):
            q_at, k_at, v_at = (head_columns(heads, i, head) for i in range(3))
            for segment in range(segments):
                count = (segment + 1) * inner * block
                keys = x_ref[:count, k_at]
                values = x_ref[:count, v_at]

                def step(i, _):
                    start = pl.multiple_of((segment * inner + i) * block, block)
                    query = x_ref[pl.ds(start, block), q_at] * 0.125
                    scores = causal(last_dims(keys, query), start)
                    top = jnp.max(scores, axis=0, keepdims=True)
                    expo = jnp.exp(scores - top)
                    total = jnp.sum(expo, axis=0, keepdims=True)
                    mixed = first_dims(values, expo.astype(BF16)) / total
                    o_ref[pl.ds(start, block), head * HDIM : (head + 1) * HDIM] = mixed.T.astype(
                        BF16
                    )
                    lse_ref[head : head + 1, pl.ds(start, block)] = top + jnp.log(total)
                    return 0

                if inner == 1:
                    step(0, 0)
                else:
                    lax.fori_loop(0, inner, step, 0)

    return pl.pallas_call(
        body,
        out_shape=[
            jax.ShapeDtypeStruct((length, heads * HDIM), BF16),
            jax.ShapeDtypeStruct((heads, length), F32),
        ],
        compiler_params=pltpu.CompilerParams(vmem_limit_bytes=VMEM_BYTES),
    )(qkv)


def attention_backward(qkv, lse, d_mixed, heads):
    length = qkv.shape[0]
    block, segments, inner = attention_shapes(length)

    def body(x_ref, lse_ref, do_ref, d_ref):
        d_ref[...] = jnp.zeros_like(d_ref)
        for head in range(heads):
            q_at, k_at, v_at = (head_columns(heads, i, head) for i in range(3))
            o_at = slice(head * HDIM, (head + 1) * HDIM)
            for segment in range(segments):
                count = (segment + 1) * inner * block
                keys = x_ref[:count, k_at]
                values = x_ref[:count, v_at]

                def step(i, _):
                    start = pl.multiple_of((segment * inner + i) * block, block)
                    query = x_ref[pl.ds(start, block), q_at] * 0.125
                    dout = do_ref[pl.ds(start, block), o_at]
                    scores = causal(last_dims(keys, query), start)
                    probs = jnp.exp(scores - lse_ref[head : head + 1, pl.ds(start, block)])
                    d_probs = last_dims(values, dout)
                    centre = jnp.sum(probs * d_probs, axis=0, keepdims=True)
                    d_scores = (probs * (d_probs - centre)).astype(BF16)
                    d_ref[:count, v_at] += plain(probs.astype(BF16), dout)
                    d_ref[:count, k_at] += plain(d_scores, query)
                    d_ref[pl.ds(start, block), q_at] = first_dims(keys, d_scores).T * 0.125
                    return 0

                if inner == 1:
                    step(0, 0)
                else:
                    lax.fori_loop(0, inner, step, 0)

    return pl.pallas_call(
        body,
        out_shape=jax.ShapeDtypeStruct(qkv.shape, F32),
        compiler_params=pltpu.CompilerParams(vmem_limit_bytes=VMEM_BYTES),
    )(qkv, lse, d_mixed)


def take(x, index):
    return lax.dynamic_index_in_dim(x, index, 0, keepdims=False)


def shards(tokens, cotangent, w_qkv, b_qkv, w_out, w_gate, w_up, w_down, norms):
    width = tokens.shape[-1]
    half = tokens.shape[3]
    rows = 2 * half
    nd, nc = lax.axis_size("dp"), lax.axis_size("ctx")
    dp, ctx = lax.axis_index("dp"), lax.axis_index("ctx")
    heads_here = HEADS // nd
    groups = nc // nd
    heads_mine = heads_here // groups
    span = heads_mine * HDIM
    many = nd * rows

    def flip(x, axis, bits):
        size = nd if axis == "dp" else nc
        return lax.ppermute(x, axis, [(i, i ^ bits) for i in range(size)])

    def columns_of(w):
        depth, cols = w.shape[1:]
        odd = ctx % 2
        other = jnp.stack([take(w, dp ^ 2), take(w, dp ^ 3)])
        there = other.reshape(2, 2, depth // 2, cols)
        mine = lax.dynamic_index_in_dim(there, odd, 1, keepdims=False)
        near = flip(mine, "dp", 2)
        far = flip(near, "ctx", 1)
        buffer = jnp.zeros((nd, 2, depth // 2, cols), w.dtype)
        place = lambda buf, block, a, b: lax.dynamic_update_slice(
            buf, block.reshape(1, -1, depth // 2, cols), (a, b, 0, 0)
        )
        buffer = place(buffer, take(w, dp), dp, 0)
        buffer = place(buffer, flip(take(w, dp ^ 1), "dp", 1), dp ^ 1, 0)
        buffer = place(buffer, near[0], dp ^ 2, odd)
        buffer = place(buffer, far[0], dp ^ 2, 1 - odd)
        swapped = flip(jnp.stack([near[1], far[1]]), "dp", 1)
        buffer = place(buffer, swapped[0], dp ^ 3, odd)
        buffer = place(buffer, swapped[1], dp ^ 3, 1 - odd)
        return buffer.reshape(nd * depth, cols)

    def sum_over_dp(partial):
        blocks = partial.astype(BF16).reshape(nd, rows, width)
        total = take(blocks, dp).astype(F32)
        for k in range(1, nd):
            total = total + flip(take(blocks, dp ^ k), "dp", k).astype(F32)
        return total

    def sum_over_ctx(left, right, outer):
        part = left.shape[1] // (outer * nc)
        split = left.reshape(many, outer, nc // 2, 2, part).transpose(3, 0, 2, 1, 4)
        odd, place = ctx % 2, ctx // 2
        size = (nc // 2, outer * part, right.shape[1])
        sent = first_dims(take(split, 1 - odd).reshape(many, -1), right).astype(BF16)
        got = flip(sent, "ctx", 1)
        kept = first_dims(take(split, odd).reshape(many, -1), right) + got.astype(F32)
        kept = kept.astype(BF16).reshape(size)
        total = take(kept, place).astype(F32)
        for k in range(1, nc // 2):
            block = take(kept, lax.rem(place + k, nc // 2))
            total = total + lax.ppermute(
                block, "ctx", [(i, (i + 2 * k) % nc) for i in range(nc)]
            ).astype(F32)
        return total

    def to_rows(total, outer):
        blocks = total.astype(BF16).reshape(nd, -1, total.shape[1])
        part, cols = blocks.shape[1:]
        out = jnp.zeros((part, nd, cols), BF16)
        for k in range(nd):
            block = take(blocks, dp ^ k)
            if k:
                block = flip(block, "dp", k)
            out = lax.dynamic_update_slice(out, block[:, None], (0, dp ^ k, 0))
        return out.astype(F32)

    wq = columns_of(w_qkv.reshape(-1, 3, nd, width // nd).transpose(2, 0, 1, 3).reshape(nd, -1, 3 * width // nd))
    hidden = w_gate.shape[1] // nd
    both = jnp.stack([w_gate.reshape(-1, nd, hidden), w_up.reshape(-1, nd, hidden)], axis=2)
    wgu = columns_of(both.transpose(1, 0, 2, 3).reshape(nd, -1, 2 * hidden))

    small = jnp.concatenate([norms.reshape(-1), b_qkv]).reshape(-1, 128)
    all_tokens, all_cotangents, all_small = gather(
        "dp", nd, 0, tokens.reshape(rows, width), cotangent.reshape(rows, width), small
    )
    all_small = all_small.reshape(nd, -1)
    gains = all_small[:, : 4 * (width // nd)].reshape(nd, 4, -1).transpose(1, 0, 2)
    gains = gains.reshape(4, width).astype(F32)
    bias = all_small[:, 4 * (width // nd) :].reshape(3, nd, width // nd)
    bias = lax.dynamic_index_in_dim(bias, dp, 1, keepdims=False).reshape(-1).astype(F32)

    x_all = all_tokens.reshape(many, width).astype(F32)
    dyb = all_cotangents.reshape(many, width)
    hat1_all, _ = normalize_rows(x_all)
    h1 = (hat1_all * gains[0] + gains[1]).astype(BF16)
    qkv = plain(h1, wq) + bias

    offsets = jnp.arange(rows, dtype=jnp.int32)
    positions = jnp.where(
        offsets < half, ctx * half + offsets, (2 * nc - 1 - ctx) * half + offsets - half
    )
    turned = turn(
        qkv[:, : 2 * heads_here * HDIM].reshape(nd, rows, -1), rotary_factors(positions), 1.0
    )
    qkv = jnp.concatenate(
        [turned.astype(BF16).reshape(many, -1), qkv[:, 2 * heads_here * HDIM :].astype(BF16)], axis=1
    )
    packed = qkv.reshape(nd, rows, 3, groups, span).transpose(0, 3, 1, 2, 4)
    seq = to_sequence(nc, 1, packed.reshape(nc, rows, 3 * span)).reshape(-1, 3 * span)
    mixed_seq, lse = attention_forward(seq, heads_mine)
    mixed = from_sequence(nc, 2, mixed_seq.reshape(2 * nc, half, span))
    mixed = mixed.reshape(nd, groups, rows, span).transpose(0, 2, 1, 3).reshape(many, -1)

    x = tokens.reshape(rows, width).astype(F32)
    partial = plain(mixed, w_out).astype(BF16).reshape(nd, rows, width)
    r1 = x + jnp.sum(swap_blocks("dp", nd, 3, partial).astype(F32), axis=0)
    hat2, inverse2 = normalize_rows(r1)
    h2_own = (hat2 * gains[2] + gains[3]).astype(BF16)
    h2 = gather("dp", nd, 4, h2_own)[0].reshape(many, width)
    gu = plain(h2, wgu)
    gate, up = gu[:, :hidden], gu[:, hidden:]
    sig = jax.nn.sigmoid(gate)
    m = (gate * sig * up).astype(BF16)
    result = r1 + sum_over_dp(plain(m, w_down))

    dm = last_dims(dyb, w_down)
    d_gate = (dm * up * sig * (1.0 + gate * (1.0 - sig))).astype(BF16)
    d_up = (dm * gate * sig).astype(BF16)
    d_gu = jnp.concatenate([d_gate, d_up], axis=1)
    grad_down = sum_over_ctx(m, dyb, 1)
    partial = last_dims(d_gu, wgu).astype(BF16).reshape(nd, rows, width)
    dh2 = jnp.sum(swap_blocks("dp", nd, 5, partial).astype(F32), axis=0)
    grad_gu = to_rows(sum_over_ctx(h2, d_gu, nd), nd)
    dy = cotangent.reshape(rows, width).astype(F32)
    dr1 = dy + norm_reverse(dh2, gains[2], hat2, inverse2)
    da = gather("dp", nd, 6, dr1.astype(BF16))[0].reshape(many, width)
    grad_out = sum_over_ctx(mixed, da, 1)
    d_mixed = last_dims(da, w_out).astype(BF16)
    packed = d_mixed.reshape(nd, rows, groups, span).transpose(0, 2, 1, 3).reshape(nc, rows, span)
    d_seq = to_sequence(nc, 7, packed).reshape(-1, span)
    d_qkv_seq = attention_backward(seq, lse, d_seq, heads_mine)
    everywhere = rotary_factors(jnp.arange(2 * nc * half, dtype=jnp.int32))
    d_qkv_seq = jnp.concatenate(
        [
            turn(d_qkv_seq[:, : 2 * span], everywhere, -1.0).astype(BF16),
            d_qkv_seq[:, 2 * span :].astype(BF16),
        ],
        axis=1,
    )
    d_qkv = from_sequence(nc, 8, d_qkv_seq.reshape(2 * nc, half, 3 * span))
    d_qkv = d_qkv.reshape(nd, groups, rows, 3, span).transpose(0, 2, 3, 1, 4).reshape(many, -1)
    partial = last_dims(d_qkv, wq).astype(BF16).reshape(nd, rows, width)
    grad_qkv = to_rows(sum_over_ctx(h1, d_qkv, nd), nd)
    grad_qkv = grad_qkv.reshape(-1, nd, 3, width // nd).transpose(0, 2, 1, 3).reshape(-1, 3 * width)
    dh1 = jnp.sum(swap_blocks("dp", nd, 9, partial).astype(F32), axis=0)
    hat1, inverse1 = normalize_rows(x)
    tokens_grad = dr1 + norm_reverse(dh1, gains[0], hat1, inverse1)

    norm_sums = jnp.stack(
        [
            jnp.sum(dh1 * hat1, axis=0),
            jnp.sum(dh1, axis=0),
            jnp.sum(dh2 * hat2, axis=0),
            jnp.sum(dh2, axis=0),
        ]
    )
    bias_sums = jnp.sum(d_qkv.astype(F32), axis=0)
    sums = jnp.concatenate([norm_sums.reshape(-1), bias_sums]).reshape(-1, 128)
    sums = jnp.sum(gather("ctx", nc, 10, sums)[0], axis=0).reshape(-1)
    norm_part = sums[: 4 * width].reshape(4, nd, nc, -1)
    norm_part = lax.dynamic_index_in_dim(norm_part, ctx, 2, keepdims=False)
    small = jnp.concatenate([norm_part.reshape(-1), sums[4 * width :]])
    pad = -small.shape[0] % 1024
    sums = gather("dp", nd, 11, jnp.pad(small, (0, pad)).reshape(-1, 128))[0].reshape(nd, -1)
    norm_sums = jnp.sum(sums[:, : norm_part.size], axis=0).reshape(norm_part.shape)
    norms_grad = lax.dynamic_index_in_dim(norm_sums, dp, 1, keepdims=False)
    bias_sums = sums[:, norm_part.size : small.shape[0]].reshape(nd, 3, -1).transpose(1, 0, 2)
    bias_grad = take(bias_sums.reshape(nd * nc, -1), dp * nc + ctx)

    return (
        result.astype(BF16).reshape(tokens.shape),
        tokens_grad.reshape(tokens.shape),
        grad_qkv,
        bias_grad,
        grad_out,
        grad_gu.reshape(-1, nd, 2, hidden)[:, :, 0].reshape(-1, nd * hidden),
        grad_gu.reshape(-1, nd, 2, hidden)[:, :, 1].reshape(-1, nd * hidden),
        grad_down,
        norms_grad,
    )


def solution(mesh):
    blocks = P("dp", "ctx", None, None, None)
    owned = P(("dp", "ctx"), None)
    return jax.shard_map(
        shards,
        mesh=mesh,
        in_specs=(
            blocks,
            blocks,
            P("dp", None),
            P("dp"),
            P("dp", None),
            P("dp", None),
            P("dp", None),
            P("dp", None),
            P(None, "dp"),
        ),
        out_specs=(
            blocks,
            blocks,
            owned,
            P(("dp", "ctx")),
            owned,
            owned,
            owned,
            owned,
            P(None, ("dp", "ctx")),
        ),
        check_vma=False,
    )
```

```python
import jax
import jax.numpy as jnp
import numpy as np
from jax import lax
from jax.experimental import pallas as pl
from jax.experimental.pallas import tpu as pltpu
from jax.sharding import PartitionSpec as P

HEADS = 32
HDIM = 64
ROT = 16
MESH = pl.DeviceIdType.MESH
F32 = jnp.float32
BF16 = jnp.bfloat16
VMEM_BYTES = 60 * 1024 * 1024


def normalize_rows(field):
    centre = field - jnp.mean(field, axis=-1, keepdims=True)
    inverse = lax.rsqrt(jnp.mean(centre * centre, axis=-1, keepdims=True) + 1e-05)
    return (centre * inverse, inverse)


def norm_reverse(incoming, gain, scaled, inverse):
    inner = incoming * gain
    return inverse * (
        inner
        - jnp.mean(inner, axis=-1, keepdims=True)
        - scaled * jnp.mean(inner * scaled, axis=-1, keepdims=True)
    )


def rotary_factors(positions):
    pairs = ROT // 2
    inverse = jnp.power(10000.0, -jnp.arange(pairs, dtype=F32) / pairs)
    angle = positions.astype(F32)[:, None] * inverse[None, :]
    cosine, sine = jnp.cos(angle), jnp.sin(angle)
    rows = positions.shape[0]
    none = jnp.zeros((rows, HDIM - ROT), F32)
    blank = jnp.zeros((rows, pairs), F32)
    keep = jnp.concatenate([cosine, cosine, none + 1.0], axis=1)
    left = jnp.concatenate([-sine, blank, none], axis=1)
    right = jnp.concatenate([blank, sine, none], axis=1)
    return keep, left, right


def turn(field, factors, sign):
    keep, left, right = factors
    heads = field.shape[-1] // HDIM
    pairs = ROT // 2
    keep, left, right = (jnp.tile(t, (1, heads)) for t in (keep, left, right))
    return (
        field * keep
        + jnp.roll(field, -pairs, axis=-1) * (left * sign)
        + jnp.roll(field, pairs, axis=-1) * (right * sign)
    )


def exchange(axis, size, cid, items):
    counts = [len(plan(0, 0)) for _, _, plan in items]
    total = sum(counts)

    def body(*refs):
        ins = refs[: len(items)]
        outs = refs[len(items) : 2 * len(items)]
        send, recv, local = refs[2 * len(items) :]
        me = lax.axis_index(axis)
        barrier = pltpu.get_barrier_semaphore()
        for k in range(1, size):
            pl.semaphore_signal(
                barrier, inc=1, device_id={axis: lax.rem(me + k, size)}, device_id_type=MESH
            )
        pl.semaphore_wait(barrier, size - 1)
        copies = []
        for k in range(1, size):
            peer = lax.rem(me + k, size)
            at = 0
            for (_, _, plan), src, dst in zip(items, ins, outs):
                for a, b in plan(me, peer):
                    copy = pltpu.make_async_remote_copy(
                        src_ref=src.at[a],
                        dst_ref=dst.at[b],
                        send_sem=send.at[k - 1, at],
                        recv_sem=recv.at[k - 1, at],
                        device_id={axis: peer},
                        device_id_type=MESH,
                    )
                    copy.start()
                    copies.append(copy)
                    at += 1
        at = 0
        for (_, _, plan), src, dst in zip(items, ins, outs):
            for a, b in plan(me, me):
                copy = pltpu.make_async_copy(src.at[a], dst.at[b], local.at[at])
                copy.start()
                copies.append(copy)
                at += 1
        for copy in copies:
            copy.wait()

    anywhere = pl.BlockSpec(memory_space=pl.ANY)
    return pl.pallas_call(
        body,
        out_shape=[jax.ShapeDtypeStruct(shape, x.dtype) for x, shape, _ in items],
        in_specs=[anywhere] * len(items),
        out_specs=[anywhere] * len(items),
        scratch_shapes=[
            pltpu.SemaphoreType.DMA((size - 1, total)),
            pltpu.SemaphoreType.DMA((size - 1, total)),
            pltpu.SemaphoreType.DMA((total,)),
        ],
        compiler_params=pltpu.CompilerParams(collective_id=cid, has_side_effects=True),
    )(*[x for x, _, _ in items])


def gather(axis, size, cid, *arrays):
    return exchange(
        axis,
        size,
        cid,
        [(x, (size,) + x.shape, lambda me, peer: [(slice(None), me)]) for x in arrays],
    )


def swap_blocks(axis, size, cid, x):
    return exchange(axis, size, cid, [(x, x.shape, lambda me, peer: [(peer, me)])])[0]


def to_sequence(size, cid, x):
    half = x.shape[1] // 2

    def plan(me, peer):
        return [
            ((peer, pl.ds(0, half)), me),
            ((peer, pl.ds(half, half)), 2 * size - 1 - me),
        ]

    return exchange("ctx", size, cid, [(x, (2 * size, half, x.shape[2]), plan)])[0]


def from_sequence(size, cid, x):
    half = x.shape[1]

    def plan(me, peer):
        return [
            (peer, (me, pl.ds(0, half))),
            (2 * size - 1 - peer, (me, pl.ds(half, half))),
        ]

    return exchange("ctx", size, cid, [(x, (size, 2 * half, x.shape[2]), plan)])[0]


def last_dims(a, b):
    return lax.dot_general(a, b, (((1,), (1,)), ((), ())), preferred_element_type=F32)


def first_dims(a, b):
    return lax.dot_general(a, b, (((0,), (0,)), ((), ())), preferred_element_type=F32)


def plain(a, b):
    return lax.dot_general(a, b, (((1,), (0,)), ((), ())), preferred_element_type=F32)


def attention_shapes(length):
    block = min(256, length)
    segments = min(4, length // block)
    return block, segments, length // block // segments


def head_columns(heads, what, head):
    at = (what * heads + head) * HDIM
    return slice(at, at + HDIM)


def causal(scores, first_query):
    keys = lax.broadcasted_iota(jnp.int32, scores.shape, 0)
    queries = lax.broadcasted_iota(jnp.int32, scores.shape, 1) + first_query
    return jnp.where(keys <= queries, scores, -1e30)


def flip_one(i):
    return i + 1 - 2 * (i % 2)


def halves(start, size):
    return pl.ds(pl.multiple_of(start, 64), size)


def lanes(start, size):
    return pl.ds(pl.multiple_of(start, 128), size)


class Copies:
    def __init__(self, send, recv, local):
        self.send, self.recv, self.local = send, recv, local
        self.remotes, self.locals = [], []

    def to(self, device, src, dst):
        at = len(self.remotes)
        copy = pltpu.make_async_remote_copy(
            src_ref=src,
            dst_ref=dst,
            send_sem=self.send.at[at],
            recv_sem=self.recv.at[at],
            device_id=device,
            device_id_type=MESH,
        )
        copy.start()
        self.remotes.append(copy)
        return copy

    def here(self, src, dst):
        copy = pltpu.make_async_copy(src, dst, self.local.at[len(self.locals)])
        copy.start()
        self.locals.append(copy)
        return copy


def meet(axis_sizes):
    barrier = pltpu.get_barrier_semaphore()
    met = 0
    for axis, size in axis_sizes:
        me = lax.axis_index(axis)
        for k in range(1, size):
            pl.semaphore_signal(
                barrier, inc=1, device_id={axis: lax.rem(me + k, size)}, device_id_type=MESH
            )
            met += 1
    pl.semaphore_wait(barrier, met)


def attend(x_ref, o_ref, lse_ref, heads, head):
    length = x_ref.shape[0]
    block, segments, inner = attention_shapes(length)
    q_at, k_at, v_at = (head_columns(heads, i, head) for i in range(3))
    for segment in range(segments):
        count = (segment + 1) * inner * block
        keys = x_ref[:count, k_at]
        values = x_ref[:count, v_at]

        def step(i, _):
            start = pl.multiple_of((segment * inner + i) * block, block)
            query = x_ref[pl.ds(start, block), q_at] * 0.125
            scores = causal(last_dims(keys, query), start)
            top = jnp.max(scores, axis=0, keepdims=True)
            expo = jnp.exp(scores - top)
            total = jnp.sum(expo, axis=0, keepdims=True)
            mixed = first_dims(values, expo.astype(BF16)) / total
            o_ref[pl.ds(start, block), head * HDIM : (head + 1) * HDIM] = mixed.T.astype(BF16)
            lse_ref[head : head + 1, pl.ds(start, block)] = top + jnp.log(total)
            return 0

        if inner == 1:
            step(0, 0)
        else:
            lax.fori_loop(0, inner, step, 0)


def rotate_pair(u, keep, sine):
    lane = lax.broadcasted_iota(jnp.int32, u.shape, 1) % HDIM
    other = jnp.where(lane < ROT // 2, pltpu.roll(u, 128 - ROT // 2, 1), pltpu.roll(u, ROT // 2, 1))
    return u * keep + other * sine


def rotary_pair_tables(length):
    pairs = ROT // 2
    inverse = np.power(np.float32(10000.0), -np.arange(pairs, dtype=np.float32) / np.float32(pairs))
    angle = np.arange(length, dtype=np.float32)[:, None] * inverse.astype(np.float32)[None, :]
    cosine, sine = np.cos(angle), np.sin(angle)
    keep = np.concatenate([cosine, cosine, np.ones((length, HDIM - ROT), np.float32)], axis=1)
    signed = np.concatenate([-sine, sine, np.zeros((length, HDIM - ROT), np.float32)], axis=1)
    return np.tile(keep, (1, 2)).astype(np.float32), np.tile(signed, (1, 2)).astype(np.float32)


def tiles(total, size):
    return [(at, min(size, total - at)) for at in range(0, total, size)]


def over_tiles(total, size, step):
    whole = total // size
    if whole:

        def run(i, _):
            step(pl.multiple_of(i * size, size), size)
            return 0

        lax.fori_loop(0, whole, run, 0)
    if total % size:
        step(whole * size, total % size)


def forward(nd, nc, tokens, cotangent, small, w_qkv, w_gate, w_up, w_out, w_down):
    rows, width = tokens.shape
    half = rows // 2
    many = nd * rows
    length = 2 * nc * half
    depth = w_qkv.shape[0]
    part_depth = depth // 2
    heads_here = HEADS // nd
    groups = nc // nd
    heads = heads_here // groups
    span = heads * HDIM
    cols = heads_here * HDIM
    hidden = w_gate.shape[1] // nd
    down = w_down.shape[0]
    keep, sine = rotary_pair_tables(length)

    def body(
        tok_i, cot_i, small_i, wq_i, wg_i, wu_i, wo_i, wd_i, keep_i, sine_i,
        h1_o, dy_o, wq_o, seq_o, lse_o, mixed_o, r1_o, h2_o, m_o, dgu_o, pout_o, pdh2_o, small_o,
        tok, dy, sm, wq, h1, qkv, seq, lse, o, mixed, wo, part, ra, rb, r1, h2, wg, wu, wd, m, dgu,
        turns, send, recv, local,
    ):
        dp, ctx = lax.axis_index("dp"), lax.axis_index("ctx")
        odd = ctx % 2
        near, across, far = flip_one(dp), (dp + 2) % nd, nd - 1 - dp
        beside = flip_one(ctx)
        links = Copies(send, recv, local)
        blocks = lambda ref, b: ref.at[halves(b * rows, rows)]

        get_tok = links.here(tok_i, blocks(tok, dp))
        get_turns = [
            links.here(table.at[halves(block * half, half)], turns.at[t, pl.ds(i * half, half)])
            for t, table in enumerate((keep_i, sine_i))
            for i, block in enumerate((ctx, 2 * nc - 1 - ctx))
        ]
        get_small = links.here(small_i, sm.at[dp])
        get_wq = [
            links.here(
                wq_i.at[:, lanes(j * width + dp * cols, cols)],
                wq.at[halves(dp * depth, depth), pl.ds(j * cols, cols)],
            )
            for j in range(3)
        ]
        meet((("dp", nd), ("ctx", nc)))

        send_tok = [links.to({"dp": e}, tok_i, blocks(tok, dp)) for e in (near, across)]
        send_small = [links.to({"dp": e}, small_i, sm.at[dp]) for e in (near, across, far)]

        def columns(w_i, w, e, at, n, to, full):
            start = dp * depth + (0 if full else odd * part_depth)
            size = depth if full else part_depth
            first = 0 if full else odd * part_depth
            return links.to(
                {"dp": e},
                w_i.at[halves(first, size), lanes(at, n)],
                w.at[halves(start, size), pl.ds(to, n)],
            )

        def relay(w, source):
            block = w.at[halves(source * depth + odd * part_depth, part_depth)]
            return links.to({"ctx": beside}, block, block)

        wq_x = [
            [columns(wq_i, wq, e, j * width + e * cols, cols, j * cols, False) for j in range(3)]
            for e in (across, far)
        ]
        wq_near = [
            columns(wq_i, wq, near, j * width + near * cols, cols, j * cols, True) for j in range(3)
        ]
        get_wo = links.here(wo_i, wo)
        get_wd = links.here(wd_i, wd)
        get_dy = links.here(cot_i, blocks(dy, dp))
        get_wgu = [
            links.here(w_i.at[:, lanes(dp * hidden, hidden)], w.at[halves(dp * depth, depth)])
            for w_i, w in ((wg_i, wg), (wu_i, wu))
        ]

        send_tok[1].wait_recv()
        forward_tok = links.to({"dp": near}, blocks(tok, across), blocks(tok, across))
        get_small.wait()
        for copy in send_small:
            copy.wait_recv()

        def gain(row):
            lines = [
                sm[b, row * 4 + q : row * 4 + q + 1, :]
                for b in range(nd)
                for q in range(width // nd // 128)
            ]
            return jnp.concatenate(lines, axis=1)

        def first_norm(b):
            at = halves(b * rows, rows)
            hat, _ = normalize_rows(tok[at, :].astype(F32))
            h1[at, :] = (hat * gain(0) + gain(1)).astype(BF16)

        get_tok.wait()
        first_norm(dp)
        send_tok[0].wait_recv()
        first_norm(near)
        first_norm(across)
        forward_tok.wait_recv()
        first_norm(far)
        put_h1 = links.here(h1, h1_o)
        put_small = links.here(sm, small_o)

        wq_y = []
        for source, copies in ((across, wq_x[0]), (far, wq_x[1])):
            for copy in copies:
                copy.wait_recv()
            wq_y.append(relay(wq, source))
        wgu_x = [
            [columns(w_i, w, e, e * hidden, hidden, 0, False) for e in (across, far)]
            for w_i, w in ((wg_i, wg), (wu_i, wu))
        ]
        wgu_near = [
            columns(w_i, w, near, near * hidden, hidden, 0, True)
            for w_i, w in ((wg_i, wg), (wu_i, wu))
        ]
        for copy in get_wq + get_turns:
            copy.wait()
        for copy in wq_near + wq_y:
            copy.wait_recv()
        put_wq = links.here(wq, wq_o)

        for at, n in tiles(3 * cols, 256):
            j = at // cols
            acc = plain(h1[...], wq[:, at : at + n])
            for q in range(n // 128):
                first = at % cols + q * 128
                line = (j * width + dp * cols + first) // 128
                per = 3 * width // nd // 128
                bias = sm[line // per, pl.ds(4 * (width // nd) // 128 + line % per, 1), :]
                for s in range(nd):
                    u = acc[s * rows : (s + 1) * rows, q * 128 : (q + 1) * 128] + bias
                    if j < 2:
                        u = rotate_pair(u, turns[0], turns[1])
                    u = u.astype(BF16)
                    if heads > 1:
                        g, off = first // span, first % span
                        qkv[g, s * rows : (s + 1) * rows, j * span + off : j * span + off + 128] = u
                    else:
                        for i in range(2):
                            qkv[
                                first // HDIM + i, s * rows : (s + 1) * rows, j * HDIM : (j + 1) * HDIM
                            ] = u[:, i * HDIM : (i + 1) * HDIM]

        mirror = 2 * nc - 1 - ctx
        go = []
        for k in range(1, nc):
            peer = lax.rem(ctx + k, nc)
            s, g = peer // groups, peer % groups
            for i, block in enumerate((ctx, mirror)):
                go.append(
                    links.to(
                        {"ctx": peer},
                        qkv.at[g, halves(s * rows + i * half, half)],
                        seq.at[halves(block * half, half)],
                    )
                )
        s, g = ctx // groups, ctx % groups
        stay = [
            links.here(
                qkv.at[g, halves(s * rows + i * half, half)], seq.at[halves(block * half, half)]
            )
            for i, block in enumerate((ctx, mirror))
        ]
        send_dy = [links.to({"dp": e}, cot_i, blocks(dy, dp)) for e in (near, across)]
        wgu_y = []

        def pass_on(w, source, copy):
            copy.wait_recv()
            wgu_y.append(relay(w, source))

        pass_on(wg, across, wgu_x[0][0])
        pass_on(wg, far, wgu_x[0][1])
        for copy in stay:
            copy.wait()
        for copy in go:
            copy.wait_recv()
        put_seq = links.here(seq, seq_o)
        pass_on(wu, across, wgu_x[1][0])

        for head in range(heads):
            attend(seq, o, lse, heads, head)

        back = []
        for k in range(1, nc):
            peer = lax.rem(ctx + k, nc)
            for i, block in enumerate((peer, 2 * nc - 1 - peer)):
                back.append(
                    links.to(
                        {"ctx": peer},
                        o.at[halves(block * half, half)],
                        mixed.at[g, halves(s * rows + i * half, half)],
                    )
                )
        stay = [
            links.here(
                o.at[halves(block * half, half)], mixed.at[g, halves(s * rows + i * half, half)]
            )
            for i, block in enumerate((ctx, mirror))
        ]
        put_lse = links.here(lse, lse_o)
        pass_on(wu, far, wgu_x[1][1])
        send_dy[1].wait_recv()
        forward_dy = links.to({"dp": near}, blocks(dy, across), blocks(dy, across))
        get_wo.wait()
        for copy in stay:
            copy.wait()
        for copy in back:
            copy.wait_recv()
        put_mixed = links.here(mixed, mixed_o)

        def out_tile(at, n):
            acc = plain(mixed[0], wo[0:span, pl.ds(at, n)])
            for i in range(1, groups):
                acc += plain(mixed[i], wo[i * span : (i + 1) * span, pl.ds(at, n)])
            part[:, pl.ds(at, n)] = acc.astype(BF16)

        over_tiles(width, 512, out_tile)

        to_near = [
            links.to({"dp": near}, blocks(part, far), blocks(ra, 0)),
            links.to({"dp": near}, blocks(part, near), blocks(ra, 1)),
        ]
        to_near[0].wait_recv()
        across_at = halves(across * rows, rows)
        part[across_at, :] = (part[across_at, :].astype(F32) + ra[:rows, :].astype(F32)).astype(BF16)
        to_across = links.to({"dp": across}, blocks(part, across), rb)
        to_near[1].wait_recv()
        own_at = halves(dp * rows, rows)
        r1[...] = tok[own_at, :].astype(F32) + (
            part[own_at, :].astype(F32) + ra[rows:, :].astype(F32)
        )
        to_across.wait_recv()
        r1[...] += rb[...].astype(F32)
        put_r1 = links.here(r1, r1_o)
        hat, _ = normalize_rows(r1[...])
        h2[own_at, :] = (hat * gain(2) + gain(3)).astype(BF16)
        send_h2 = [links.to({"dp": e}, blocks(h2, dp), blocks(h2, dp)) for e in (near, across)]
        send_h2[1].wait_recv()
        forward_h2 = links.to({"dp": near}, blocks(h2, across), blocks(h2, across))
        get_wd.wait()
        get_dy.wait()
        for copy in get_wgu:
            copy.wait()
        for copy in wgu_near + wgu_y + [send_dy[0], forward_dy, send_h2[0], forward_h2]:
            copy.wait_recv()
        put_h2 = links.here(h2, h2_o)
        put_dy = links.here(dy, dy_o)
        put_h1.wait()

        def hidden_tile(at, n):
            here = pl.ds(at, n)
            gate = plain(h2[...], wg[:, here])
            up = plain(h2[...], wu[:, here])
            dm = last_dims(dy[...], wd[here, :])
            sig = jax.nn.sigmoid(gate)
            m[:, here] = (gate * sig * up).astype(BF16)
            dgu[:, here] = (dm * up * sig * (1.0 + gate * (1.0 - sig))).astype(BF16)
            dgu[:, pl.ds(hidden + at, n)] = (dm * gate * sig).astype(BF16)

        over_tiles(hidden, 256, hidden_tile)
        put_m = links.here(m, m_o)
        put_dgu = links.here(dgu, dgu_o)

        def dh2_tile(at, n):
            here = pl.ds(at, n)
            acc = last_dims(dgu[:, :hidden], wg[here, :]) + last_dims(dgu[:, hidden:], wu[here, :])
            h1[:, here] = acc.astype(BF16)

        over_tiles(width, 256, dh2_tile)
        put_pdh2 = links.here(h1, pdh2_o)
        for copy in send_tok + [forward_tok]:
            copy.wait_send()

        def result_tile(at, n):
            here = pl.ds(at, n)
            tok[:, here] = plain(m[...], wd[:, here]).astype(BF16)

        over_tiles(width, 256, result_tile)
        put_pout = links.here(tok, pout_o)

        done = send_tok + [forward_tok]
        for copy in links.remotes:
            if not any(copy is other for other in done):
                copy.wait_send()
        for copy in (
            put_small, put_wq, put_seq, put_lse, put_mixed, put_r1, put_h2, put_dy, put_m, put_dgu,
            put_pdh2, put_pout,
        ):
            copy.wait()

    anywhere = pl.BlockSpec(memory_space=pl.ANY)
    shape = jax.ShapeDtypeStruct
    remotes = 2 + 3 + 6 + 3 + 1 + 2 + 4 + 2 + 2 * (nc - 1) * 2 + 2 + 4 + 1 + 3 + 2 + 1
    outs = dict(
        h1=((many, width), BF16),
        dy=((many, width), BF16),
        wq=((width, 3 * cols), BF16),
        seq=((length, 3 * span), BF16),
        lse=((heads, length), F32),
        mixed=((groups, many, span), BF16),
        r1=((rows, width), F32),
        h2=((many, width), BF16),
        m=((many, hidden), BF16),
        dgu=((many, 2 * hidden), BF16),
        pout=((many, width), BF16),
        pdh2=((many, width), BF16),
        small=((nd,) + small.shape, F32),
    )
    scratch = [
        ((many, width), BF16),
        ((many, width), BF16),
        ((nd,) + small.shape, F32),
        ((width, 3 * cols), BF16),
        ((many, width), BF16),
        ((groups, many, 3 * span), BF16),
        ((length, 3 * span), BF16),
        ((heads, length), F32),
        ((length, span), BF16),
        ((groups, many, span), BF16),
        ((cols, width), BF16),
        ((many, width), BF16),
        ((2 * rows, width), BF16),
        ((rows, width), BF16),
        ((rows, width), F32),
        ((many, width), BF16),
        ((width, hidden), BF16),
        ((width, hidden), BF16),
        ((down, width), BF16),
        ((many, hidden), BF16),
        ((many, 2 * hidden), BF16),
        ((2, rows, 128), F32),
    ]
    results = pl.pallas_call(
        body,
        out_shape=[shape(*o) for o in outs.values()],
        in_specs=[anywhere] * 10,
        out_specs=[anywhere] * len(outs),
        scratch_shapes=[pltpu.VMEM(*s) for s in scratch]
        + [
            pltpu.SemaphoreType.DMA((remotes,)),
            pltpu.SemaphoreType.DMA((remotes,)),
            pltpu.SemaphoreType.DMA((40,)),
        ],
        compiler_params=pltpu.CompilerParams(
            collective_id=0, has_side_effects=True, vmem_limit_bytes=VMEM_BYTES
        ),
    )(tokens, cotangent, small, w_qkv, w_gate, w_up, w_out, w_down, keep, sine)
    return dict(zip(outs, results))


def attention_backward(qkv, lse, d_mixed, heads):
    length = qkv.shape[0]
    block, segments, inner = attention_shapes(length)

    def body(x_ref, lse_ref, do_ref, d_ref):
        d_ref[...] = jnp.zeros_like(d_ref)
        for head in range(heads):
            q_at, k_at, v_at = (head_columns(heads, i, head) for i in range(3))
            o_at = slice(head * HDIM, (head + 1) * HDIM)
            for segment in range(segments):
                count = (segment + 1) * inner * block
                keys = x_ref[:count, k_at]
                values = x_ref[:count, v_at]

                def step(i, _):
                    start = pl.multiple_of((segment * inner + i) * block, block)
                    query = x_ref[pl.ds(start, block), q_at] * 0.125
                    dout = do_ref[pl.ds(start, block), o_at]
                    scores = causal(last_dims(keys, query), start)
                    probs = jnp.exp(scores - lse_ref[head : head + 1, pl.ds(start, block)])
                    d_probs = last_dims(values, dout)
                    centre = jnp.sum(probs * d_probs, axis=0, keepdims=True)
                    d_scores = (probs * (d_probs - centre)).astype(BF16)
                    d_ref[:count, v_at] += plain(probs.astype(BF16), dout)
                    d_ref[:count, k_at] += plain(d_scores, query)
                    d_ref[pl.ds(start, block), q_at] = first_dims(keys, d_scores).T * 0.125
                    return 0

                if inner == 1:
                    step(0, 0)
                else:
                    lax.fori_loop(0, inner, step, 0)

    return pl.pallas_call(
        body,
        out_shape=jax.ShapeDtypeStruct(qkv.shape, F32),
        compiler_params=pltpu.CompilerParams(vmem_limit_bytes=VMEM_BYTES),
    )(qkv, lse, d_mixed)


def take(x, index):
    return lax.dynamic_index_in_dim(x, index, 0, keepdims=False)


def shards(tokens, cotangent, w_qkv, b_qkv, w_out, w_gate, w_up, w_down, norms):
    width = tokens.shape[-1]
    half = tokens.shape[3]
    rows = 2 * half
    nd, nc = lax.axis_size("dp"), lax.axis_size("ctx")
    dp, ctx = lax.axis_index("dp"), lax.axis_index("ctx")
    heads_here = HEADS // nd
    groups = nc // nd
    heads_mine = heads_here // groups
    span = heads_mine * HDIM
    many = nd * rows

    def flip(x, axis, bits):
        size = nd if axis == "dp" else nc
        return lax.ppermute(x, axis, [(i, i ^ bits) for i in range(size)])

    def sum_over_dp(partial):
        blocks = partial.astype(BF16).reshape(nd, rows, width)
        total = take(blocks, dp).astype(F32)
        for k in range(1, nd):
            total = total + flip(take(blocks, dp ^ k), "dp", k).astype(F32)
        return total

    def sum_over_ctx(left, right, outer):
        part = left.shape[1] // (outer * nc)
        split = left.reshape(many, outer, nc // 2, 2, part).transpose(3, 0, 2, 1, 4)
        odd, place = ctx % 2, ctx // 2
        size = (nc // 2, outer * part, right.shape[1])
        sent = first_dims(take(split, 1 - odd).reshape(many, -1), right).astype(BF16)
        got = flip(sent, "ctx", 1)
        kept = first_dims(take(split, odd).reshape(many, -1), right) + got.astype(F32)
        kept = kept.astype(BF16).reshape(size)
        total = take(kept, place).astype(F32)
        for k in range(1, nc // 2):
            block = take(kept, lax.rem(place + k, nc // 2))
            total = total + lax.ppermute(
                block, "ctx", [(i, (i + 2 * k) % nc) for i in range(nc)]
            ).astype(F32)
        return total

    def to_rows(total, outer):
        blocks = total.astype(BF16).reshape(nd, -1, total.shape[1])
        part, cols = blocks.shape[1:]
        out = jnp.zeros((part, nd, cols), BF16)
        for k in range(nd):
            block = take(blocks, dp ^ k)
            if k:
                block = flip(block, "dp", k)
            out = lax.dynamic_update_slice(out, block[:, None], (0, dp ^ k, 0))
        return out.astype(F32)

    hidden = w_gate.shape[1] // nd
    small = jnp.concatenate([norms.reshape(-1), b_qkv]).astype(F32)
    small = jnp.pad(small, (0, -small.shape[0] % 1024)).reshape(-1, 128)
    f = forward(
        nd, nc, tokens.reshape(rows, width), cotangent.reshape(rows, width), small,
        w_qkv, w_gate, w_up, w_out, w_down,
    )
    h1, dyb, wq, seq, lse, r1, h2 = (f[k] for k in ("h1", "dy", "wq", "seq", "lse", "r1", "h2"))
    m, d_gu = f["m"], f["dgu"]
    gains = f["small"].reshape(nd, -1)[:, : 4 * (width // nd)].reshape(nd, 4, -1)
    gains = gains.transpose(1, 0, 2).reshape(4, width)
    mixed = f["mixed"].transpose(1, 0, 2).reshape(many, -1)
    x = tokens.reshape(rows, width).astype(F32)
    hat2, inverse2 = normalize_rows(r1)
    result = r1 + sum_over_dp(f["pout"])

    grad_down = sum_over_ctx(m, dyb, 1)
    partial = f["pdh2"].reshape(nd, rows, width)
    dh2 = jnp.sum(swap_blocks("dp", nd, 5, partial).astype(F32), axis=0)
    grad_gu = to_rows(sum_over_ctx(h2, d_gu, nd), nd)
    dy = cotangent.reshape(rows, width).astype(F32)
    dr1 = dy + norm_reverse(dh2, gains[2], hat2, inverse2)
    da = gather("dp", nd, 6, dr1.astype(BF16))[0].reshape(many, width)
    grad_out = sum_over_ctx(mixed, da, 1)
    d_mixed = last_dims(da, w_out).astype(BF16)
    packed = d_mixed.reshape(nd, rows, groups, span).transpose(0, 2, 1, 3).reshape(nc, rows, span)
    d_seq = to_sequence(nc, 7, packed).reshape(-1, span)
    d_qkv_seq = attention_backward(seq, lse, d_seq, heads_mine)
    everywhere = rotary_factors(jnp.arange(2 * nc * half, dtype=jnp.int32))
    d_qkv_seq = jnp.concatenate(
        [
            turn(d_qkv_seq[:, : 2 * span], everywhere, -1.0).astype(BF16),
            d_qkv_seq[:, 2 * span :].astype(BF16),
        ],
        axis=1,
    )
    d_qkv = from_sequence(nc, 8, d_qkv_seq.reshape(2 * nc, half, 3 * span))
    d_qkv = d_qkv.reshape(nd, groups, rows, 3, span).transpose(0, 2, 3, 1, 4).reshape(many, -1)
    partial = last_dims(d_qkv, wq).astype(BF16).reshape(nd, rows, width)
    grad_qkv = to_rows(sum_over_ctx(h1, d_qkv, nd), nd)
    grad_qkv = grad_qkv.reshape(-1, nd, 3, width // nd).transpose(0, 2, 1, 3).reshape(-1, 3 * width)
    dh1 = jnp.sum(swap_blocks("dp", nd, 9, partial).astype(F32), axis=0)
    hat1, inverse1 = normalize_rows(x)
    tokens_grad = dr1 + norm_reverse(dh1, gains[0], hat1, inverse1)

    norm_sums = jnp.stack(
        [
            jnp.sum(dh1 * hat1, axis=0),
            jnp.sum(dh1, axis=0),
            jnp.sum(dh2 * hat2, axis=0),
            jnp.sum(dh2, axis=0),
        ]
    )
    bias_sums = jnp.sum(d_qkv.astype(F32), axis=0)
    sums = jnp.concatenate([norm_sums.reshape(-1), bias_sums]).reshape(-1, 128)
    sums = jnp.sum(gather("ctx", nc, 10, sums)[0], axis=0).reshape(-1)
    norm_part = sums[: 4 * width].reshape(4, nd, nc, -1)
    norm_part = lax.dynamic_index_in_dim(norm_part, ctx, 2, keepdims=False)
    small = jnp.concatenate([norm_part.reshape(-1), sums[4 * width :]])
    pad = -small.shape[0] % 1024
    sums = gather("dp", nd, 11, jnp.pad(small, (0, pad)).reshape(-1, 128))[0].reshape(nd, -1)
    norm_sums = jnp.sum(sums[:, : norm_part.size], axis=0).reshape(norm_part.shape)
    norms_grad = lax.dynamic_index_in_dim(norm_sums, dp, 1, keepdims=False)
    bias_sums = sums[:, norm_part.size : small.shape[0]].reshape(nd, 3, -1).transpose(1, 0, 2)
    bias_grad = take(bias_sums.reshape(nd * nc, -1), dp * nc + ctx)

    return (
        result.astype(BF16).reshape(tokens.shape),
        tokens_grad.reshape(tokens.shape),
        grad_qkv,
        bias_grad,
        grad_out,
        grad_gu.reshape(-1, nd, 2, hidden)[:, :, 0].reshape(-1, nd * hidden),
        grad_gu.reshape(-1, nd, 2, hidden)[:, :, 1].reshape(-1, nd * hidden),
        grad_down,
        norms_grad,
    )


def solution(mesh):
    blocks = P("dp", "ctx", None, None, None)
    owned = P(("dp", "ctx"), None)
    return jax.shard_map(
        shards,
        mesh=mesh,
        in_specs=(
            blocks,
            blocks,
            P("dp", None),
            P("dp"),
            P("dp", None),
            P("dp", None),
            P("dp", None),
            P("dp", None),
            P(None, "dp"),
        ),
        out_specs=(
            blocks,
            blocks,
            owned,
            P(("dp", "ctx")),
            owned,
            owned,
            owned,
            owned,
            P(None, ("dp", "ctx")),
        ),
        check_vma=False,
    )
```

```python
import jax
import jax.numpy as jnp
import numpy as np
from jax import lax
from jax.experimental import pallas as pl
from jax.experimental.pallas import tpu as pltpu
from jax.sharding import PartitionSpec as P

HEADS = 32
HDIM = 64
ROT = 16
MESH = pl.DeviceIdType.MESH
F32 = jnp.float32
BF16 = jnp.bfloat16
VMEM_BYTES = 62 * 1024 * 1024


def normalize_rows(field):
    centre = field - jnp.mean(field, axis=-1, keepdims=True)
    inverse = lax.rsqrt(jnp.mean(centre * centre, axis=-1, keepdims=True) + 1e-05)
    return (centre * inverse, inverse)


def norm_reverse(incoming, gain, scaled, inverse):
    inner = incoming * gain
    return inverse * (
        inner
        - jnp.mean(inner, axis=-1, keepdims=True)
        - scaled * jnp.mean(inner * scaled, axis=-1, keepdims=True)
    )


def last_dims(a, b):
    return lax.dot_general(a, b, (((1,), (1,)), ((), ())), preferred_element_type=F32)


def first_dims(a, b):
    return lax.dot_general(a, b, (((0,), (0,)), ((), ())), preferred_element_type=F32)


def plain(a, b):
    return lax.dot_general(a, b, (((1,), (0,)), ((), ())), preferred_element_type=F32)


def attention_shapes(length):
    block = min(256 if length <= 1024 else 128, length)
    segments = min(4, length // block)
    return block, segments, length // block // segments


def head_columns(heads, what, head):
    at = (what * heads + head) * HDIM
    return slice(at, at + HDIM)


def causal(scores, first_query):
    keys = lax.broadcasted_iota(jnp.int32, scores.shape, 0)
    queries = lax.broadcasted_iota(jnp.int32, scores.shape, 1) + first_query
    return jnp.where(keys <= queries, scores, -1e30)


def flip_one(i):
    return i + 1 - 2 * (i % 2)


def halves(start, size):
    return pl.ds(pl.multiple_of(start, 64), size)


def lanes(start, size):
    return pl.ds(pl.multiple_of(start, 128), size)


class Copies:
    def __init__(self, send, recv, local):
        self.send, self.recv, self.local = send, recv, local
        self.remotes, self.locals, self.left = [], [], []

    def to(self, device, src, dst):
        at = len(self.remotes)
        copy = pltpu.make_async_remote_copy(
            src_ref=src,
            dst_ref=dst,
            send_sem=self.send.at[at],
            recv_sem=self.recv.at[at],
            device_id=device,
            device_id_type=MESH,
        )
        copy.start()
        self.remotes.append(copy)
        self.left.append(copy)
        return copy

    def gone(self, *copies):
        for copy in copies:
            copy.wait_send()
            self.left = [other for other in self.left if other is not copy]

    def here(self, src, dst):
        copy = pltpu.make_async_copy(src, dst, self.local.at[len(self.locals)])
        copy.start()
        self.locals.append(copy)
        return copy


def meet(axis_sizes):
    barrier = pltpu.get_barrier_semaphore()
    met = 0
    for axis, size in axis_sizes:
        me = lax.axis_index(axis)
        for k in range(1, size):
            pl.semaphore_signal(
                barrier, inc=1, device_id={axis: lax.rem(me + k, size)}, device_id_type=MESH
            )
            met += 1
    pl.semaphore_wait(barrier, met)


def attend(x_ref, o_ref, lse_ref, heads, head):
    length = x_ref.shape[0]
    block, segments, inner = attention_shapes(length)
    q_at, k_at, v_at = (head_columns(heads, i, head) for i in range(3))
    for segment in range(segments):
        count = (segment + 1) * inner * block
        keys = x_ref[:count, k_at]
        values = x_ref[:count, v_at]

        def step(i, _):
            start = pl.multiple_of((segment * inner + i) * block, block)
            query = x_ref[pl.ds(start, block), q_at] * 0.125
            scores = causal(last_dims(keys, query), start)
            top = jnp.max(scores, axis=0, keepdims=True)
            expo = jnp.exp(scores - top)
            total = jnp.sum(expo, axis=0, keepdims=True)
            mixed = first_dims(values, expo.astype(BF16)) / total
            o_ref[pl.ds(start, block), head * HDIM : (head + 1) * HDIM] = mixed.T.astype(BF16)
            lse_ref[head : head + 1, pl.ds(start, block)] = top + jnp.log(total)
            return 0

        if inner == 1:
            step(0, 0)
        else:
            lax.fori_loop(0, inner, step, 0)


def rotate_pair(u, keep, sine):
    lane = lax.broadcasted_iota(jnp.int32, u.shape, 1) % HDIM
    other = jnp.where(lane < ROT // 2, pltpu.roll(u, 128 - ROT // 2, 1), pltpu.roll(u, ROT // 2, 1))
    return u * keep + other * sine


def rotary_pair_tables(length):
    pairs = ROT // 2
    inverse = np.power(np.float32(10000.0), -np.arange(pairs, dtype=np.float32) / np.float32(pairs))
    angle = np.arange(length, dtype=np.float32)[:, None] * inverse.astype(np.float32)[None, :]
    cosine, sine = np.cos(angle), np.sin(angle)
    keep = np.concatenate([cosine, cosine, np.ones((length, HDIM - ROT), np.float32)], axis=1)
    signed = np.concatenate([-sine, sine, np.zeros((length, HDIM - ROT), np.float32)], axis=1)
    return np.tile(keep, (1, 2)).astype(np.float32), np.tile(signed, (1, 2)).astype(np.float32)


def tiles(total, size):
    return [(at, min(size, total - at)) for at in range(0, total, size)]


def over_tiles(total, size, step):
    whole = total // size
    if whole:

        def run(i, _):
            step(pl.multiple_of(i * size, size), size)
            return 0

        lax.fori_loop(0, whole, run, 0)
    if total % size:
        step(whole * size, total % size)


def forward(nd, nc, tokens, cotangent, small, w_qkv, w_gate, w_up, w_out, w_down):
    rows, width = tokens.shape
    half = rows // 2
    many = nd * rows
    length = 2 * nc * half
    depth = w_qkv.shape[0]
    part_depth = depth // 2
    heads_here = HEADS // nd
    groups = nc // nd
    heads = heads_here // groups
    span = heads * HDIM
    cols = heads_here * HDIM
    hidden = w_gate.shape[1] // nd
    down = w_down.shape[0]
    keep, sine = rotary_pair_tables(length)

    def body(
        tok_i, cot_i, small_i, wq_i, wg_i, wu_i, wo_i, wd_i, keep_i, sine_i,
        h1_o, dy_o, wq_o, seq_o, lse_o, mixed_o, r1_o, h2_o, m_o, dgu_o, pout_o, pdh2_o, small_o,
        tok, dy, sm, wq, h1, qkv, seq, lse, o, mixed, wo, part, ra, rb, r1, h2, wg, wu, wd, m, dgu,
        turns, send, recv, local,
    ):
        dp, ctx = lax.axis_index("dp"), lax.axis_index("ctx")
        odd = ctx % 2
        near, across, far = flip_one(dp), (dp + 2) % nd, nd - 1 - dp
        beside = flip_one(ctx)
        links = Copies(send, recv, local)
        blocks = lambda ref, b: ref.at[halves(b * rows, rows)]

        get_tok = links.here(tok_i, blocks(tok, dp))
        get_turns = [
            links.here(table.at[halves(block * half, half)], turns.at[t, pl.ds(i * half, half)])
            for t, table in enumerate((keep_i, sine_i))
            for i, block in enumerate((ctx, 2 * nc - 1 - ctx))
        ]
        get_small = links.here(small_i, sm.at[dp])
        get_wq = [
            links.here(
                wq_i.at[:, lanes(j * width + dp * cols, cols)],
                wq.at[halves(dp * depth, depth), pl.ds(j * cols, cols)],
            )
            for j in range(3)
        ]
        meet((("dp", nd), ("ctx", nc)))

        send_tok = [links.to({"dp": e}, tok_i, blocks(tok, dp)) for e in (near, across)]
        send_small = [links.to({"dp": e}, small_i, sm.at[dp]) for e in (near, across, far)]

        def columns(w_i, w, e, at, n, to, full):
            start = dp * depth + (0 if full else odd * part_depth)
            size = depth if full else part_depth
            first = 0 if full else odd * part_depth
            return links.to(
                {"dp": e},
                w_i.at[halves(first, size), lanes(at, n)],
                w.at[halves(start, size), pl.ds(to, n)],
            )

        def relay(w, source):
            block = w.at[halves(source * depth + odd * part_depth, part_depth)]
            return links.to({"ctx": beside}, block, block)

        wq_x = [
            [columns(wq_i, wq, e, j * width + e * cols, cols, j * cols, False) for j in range(3)]
            for e in (across, far)
        ]
        wq_near = [
            columns(wq_i, wq, near, j * width + near * cols, cols, j * cols, True) for j in range(3)
        ]
        get_wo = links.here(wo_i, wo)
        get_wd = links.here(wd_i, wd)
        get_dy = links.here(cot_i, blocks(dy, dp))
        get_wgu = [
            links.here(w_i.at[:, lanes(dp * hidden, hidden)], w.at[halves(dp * depth, depth)])
            for w_i, w in ((wg_i, wg), (wu_i, wu))
        ]

        send_tok[1].wait_recv()
        forward_tok = links.to({"dp": near}, blocks(tok, across), blocks(tok, across))
        get_small.wait()
        for copy in send_small:
            copy.wait_recv()

        def gain(row):
            lines = [
                sm[b, row * 4 + q : row * 4 + q + 1, :]
                for b in range(nd)
                for q in range(width // nd // 128)
            ]
            return jnp.concatenate(lines, axis=1)

        def first_norm(b):
            at = halves(b * rows, rows)
            hat, _ = normalize_rows(tok[at, :].astype(F32))
            h1[at, :] = (hat * gain(0) + gain(1)).astype(BF16)

        get_tok.wait()
        first_norm(dp)
        send_tok[0].wait_recv()
        first_norm(near)
        first_norm(across)
        forward_tok.wait_recv()
        first_norm(far)
        put_h1 = links.here(h1, h1_o)
        put_small = links.here(sm, small_o)

        wq_y = []
        for source, copies in ((across, wq_x[0]), (far, wq_x[1])):
            for copy in copies:
                copy.wait_recv()
            wq_y.append(relay(wq, source))
        wgu_x = [
            [columns(w_i, w, e, e * hidden, hidden, 0, False) for e in (across, far)]
            for w_i, w in ((wg_i, wg), (wu_i, wu))
        ]
        wgu_near = [
            columns(w_i, w, near, near * hidden, hidden, 0, True)
            for w_i, w in ((wg_i, wg), (wu_i, wu))
        ]
        for copy in get_wq + get_turns:
            copy.wait()
        for copy in wq_near + wq_y:
            copy.wait_recv()
        put_wq = links.here(wq, wq_o)

        for at, n in tiles(3 * cols, 256):
            j = at // cols
            acc = plain(h1[...], wq[:, at : at + n])
            for q in range(n // 128):
                first = at % cols + q * 128
                line = (j * width + dp * cols + first) // 128
                per = 3 * width // nd // 128
                bias = sm[line // per, pl.ds(4 * (width // nd) // 128 + line % per, 1), :]
                for s in range(nd):
                    u = acc[s * rows : (s + 1) * rows, q * 128 : (q + 1) * 128] + bias
                    if j < 2:
                        u = rotate_pair(u, turns[0], turns[1])
                    u = u.astype(BF16)
                    if heads > 1:
                        g, off = first // span, first % span
                        qkv[g, s * rows : (s + 1) * rows, j * span + off : j * span + off + 128] = u
                    else:
                        for i in range(2):
                            qkv[
                                first // HDIM + i, s * rows : (s + 1) * rows, j * HDIM : (j + 1) * HDIM
                            ] = u[:, i * HDIM : (i + 1) * HDIM]

        mirror = 2 * nc - 1 - ctx
        go = []
        for k in range(1, nc):
            peer = lax.rem(ctx + k, nc)
            s, g = peer // groups, peer % groups
            for i, block in enumerate((ctx, mirror)):
                go.append(
                    links.to(
                        {"ctx": peer},
                        qkv.at[g, halves(s * rows + i * half, half)],
                        seq.at[halves(block * half, half)],
                    )
                )
        s, g = ctx // groups, ctx % groups
        stay = [
            links.here(
                qkv.at[g, halves(s * rows + i * half, half)], seq.at[halves(block * half, half)]
            )
            for i, block in enumerate((ctx, mirror))
        ]
        send_dy = [links.to({"dp": e}, cot_i, blocks(dy, dp)) for e in (near, across)]
        wgu_y = []

        def pass_on(w, source, copy):
            copy.wait_recv()
            wgu_y.append(relay(w, source))

        pass_on(wg, across, wgu_x[0][0])
        pass_on(wg, far, wgu_x[0][1])
        for copy in stay:
            copy.wait()
        for copy in go:
            copy.wait_recv()
        put_seq = links.here(seq, seq_o)
        pass_on(wu, across, wgu_x[1][0])

        for head in range(heads):
            attend(seq, o, lse, heads, head)

        back = []
        for k in range(1, nc):
            peer = lax.rem(ctx + k, nc)
            for i, block in enumerate((peer, 2 * nc - 1 - peer)):
                back.append(
                    links.to(
                        {"ctx": peer},
                        o.at[halves(block * half, half)],
                        mixed.at[g, halves(s * rows + i * half, half)],
                    )
                )
        stay = [
            links.here(
                o.at[halves(block * half, half)], mixed.at[g, halves(s * rows + i * half, half)]
            )
            for i, block in enumerate((ctx, mirror))
        ]
        put_lse = links.here(lse, lse_o)
        pass_on(wu, far, wgu_x[1][1])
        send_dy[1].wait_recv()
        forward_dy = links.to({"dp": near}, blocks(dy, across), blocks(dy, across))
        get_wo.wait()
        for copy in stay:
            copy.wait()
        for copy in back:
            copy.wait_recv()
        put_mixed = links.here(mixed, mixed_o)

        def out_tile(at, n):
            acc = plain(mixed[0], wo[0:span, pl.ds(at, n)])
            for i in range(1, groups):
                acc += plain(mixed[i], wo[i * span : (i + 1) * span, pl.ds(at, n)])
            part[:, pl.ds(at, n)] = acc.astype(BF16)

        over_tiles(width, 512, out_tile)

        to_near = [
            links.to({"dp": near}, blocks(part, far), blocks(ra, 0)),
            links.to({"dp": near}, blocks(part, near), blocks(ra, 1)),
        ]
        to_near[0].wait_recv()
        across_at = halves(across * rows, rows)
        part[across_at, :] = (part[across_at, :].astype(F32) + ra[:rows, :].astype(F32)).astype(BF16)
        to_across = links.to({"dp": across}, blocks(part, across), rb)
        to_near[1].wait_recv()
        own_at = halves(dp * rows, rows)
        r1[...] = tok[own_at, :].astype(F32) + (
            part[own_at, :].astype(F32) + ra[rows:, :].astype(F32)
        )
        to_across.wait_recv()
        r1[...] += rb[...].astype(F32)
        put_r1 = links.here(r1, r1_o)
        hat, _ = normalize_rows(r1[...])
        h2[own_at, :] = (hat * gain(2) + gain(3)).astype(BF16)
        send_h2 = [links.to({"dp": e}, blocks(h2, dp), blocks(h2, dp)) for e in (near, across)]
        send_h2[1].wait_recv()
        forward_h2 = links.to({"dp": near}, blocks(h2, across), blocks(h2, across))
        get_wd.wait()
        get_dy.wait()
        for copy in get_wgu:
            copy.wait()
        for copy in wgu_near + wgu_y + [send_dy[0], forward_dy, send_h2[0], forward_h2]:
            copy.wait_recv()
        put_h2 = links.here(h2, h2_o)
        put_dy = links.here(dy, dy_o)
        put_h1.wait()

        def hidden_tile(at, n):
            here = pl.ds(at, n)
            gate = plain(h2[...], wg[:, here])
            up = plain(h2[...], wu[:, here])
            dm = last_dims(dy[...], wd[here, :])
            sig = jax.nn.sigmoid(gate)
            m[:, here] = (gate * sig * up).astype(BF16)
            dgu[:, here] = (dm * up * sig * (1.0 + gate * (1.0 - sig))).astype(BF16)
            dgu[:, pl.ds(hidden + at, n)] = (dm * gate * sig).astype(BF16)

        over_tiles(hidden, 256, hidden_tile)
        put_m = links.here(m, m_o)
        put_dgu = links.here(dgu, dgu_o)

        def dh2_tile(at, n):
            here = pl.ds(at, n)
            acc = last_dims(dgu[:, :hidden], wg[here, :]) + last_dims(dgu[:, hidden:], wu[here, :])
            h1[:, here] = acc.astype(BF16)

        over_tiles(width, 256, dh2_tile)
        put_pdh2 = links.here(h1, pdh2_o)
        links.gone(*send_tok, forward_tok)

        def result_tile(at, n):
            here = pl.ds(at, n)
            tok[:, here] = plain(m[...], wd[:, here]).astype(BF16)

        over_tiles(width, 256, result_tile)
        put_pout = links.here(tok, pout_o)

        links.gone(*links.left)
        for copy in (
            put_small, put_wq, put_seq, put_lse, put_mixed, put_r1, put_h2, put_dy, put_m, put_dgu,
            put_pdh2, put_pout,
        ):
            copy.wait()

    anywhere = pl.BlockSpec(memory_space=pl.ANY)
    shape = jax.ShapeDtypeStruct
    remotes = 2 + 3 + 6 + 3 + 1 + 2 + 4 + 2 + 2 * (nc - 1) * 2 + 2 + 4 + 1 + 3 + 2 + 1
    outs = dict(
        h1=((many, width), BF16),
        dy=((many, width), BF16),
        wq=((width, 3 * cols), BF16),
        seq=((length, 3 * span), BF16),
        lse=((heads, length), F32),
        mixed=((groups, many, span), BF16),
        r1=((rows, width), F32),
        h2=((many, width), BF16),
        m=((many, hidden), BF16),
        dgu=((many, 2 * hidden), BF16),
        pout=((many, width), BF16),
        pdh2=((many, width), BF16),
        small=((nd,) + small.shape, F32),
    )
    scratch = [
        ((many, width), BF16),
        ((many, width), BF16),
        ((nd,) + small.shape, F32),
        ((width, 3 * cols), BF16),
        ((many, width), BF16),
        ((groups, many, 3 * span), BF16),
        ((length, 3 * span), BF16),
        ((heads, length), F32),
        ((length, span), BF16),
        ((groups, many, span), BF16),
        ((cols, width), BF16),
        ((many, width), BF16),
        ((2 * rows, width), BF16),
        ((rows, width), BF16),
        ((rows, width), F32),
        ((many, width), BF16),
        ((width, hidden), BF16),
        ((width, hidden), BF16),
        ((down, width), BF16),
        ((many, hidden), BF16),
        ((many, 2 * hidden), BF16),
        ((2, rows, 128), F32),
    ]
    results = pl.pallas_call(
        body,
        out_shape=[shape(*o) for o in outs.values()],
        in_specs=[anywhere] * 10,
        out_specs=[anywhere] * len(outs),
        scratch_shapes=[pltpu.VMEM(*s) for s in scratch]
        + [
            pltpu.SemaphoreType.DMA((remotes,)),
            pltpu.SemaphoreType.DMA((remotes,)),
            pltpu.SemaphoreType.DMA((40,)),
        ],
        compiler_params=pltpu.CompilerParams(
            collective_id=0, has_side_effects=True, vmem_limit_bytes=VMEM_BYTES
        ),
    )(tokens, cotangent, small, w_qkv, w_gate, w_up, w_out, w_down, keep, sine)
    return dict(zip(outs, results))


def flip_bit(i, bit):
    return i + (1 << bit) - (2 << bit) * ((i // (1 << bit)) % 2)


def attend_back(x_ref, lse_ref, do_ref, d_ref, heads, head):
    length = x_ref.shape[0]
    block, segments, inner = attention_shapes(length)
    q_at, k_at, v_at = (head_columns(heads, i, head) for i in range(3))
    o_at = slice(head * HDIM, (head + 1) * HDIM)
    for segment in range(segments):
        count = (segment + 1) * inner * block
        keys = x_ref[:count, k_at]
        values = x_ref[:count, v_at]

        def step(i, _):
            start = pl.multiple_of((segment * inner + i) * block, block)
            query = x_ref[pl.ds(start, block), q_at] * 0.125
            dout = do_ref[pl.ds(start, block), o_at]
            scores = causal(last_dims(keys, query), start)
            probs = jnp.exp(scores - lse_ref[head : head + 1, pl.ds(start, block)])
            d_probs = last_dims(values, dout)
            centre = jnp.sum(probs * d_probs, axis=0, keepdims=True)
            d_scores = (probs * (d_probs - centre)).astype(BF16)
            d_ref[:count, v_at] += plain(probs.astype(BF16), dout)
            d_ref[:count, k_at] += plain(d_scores, query)
            d_ref[pl.ds(start, block), q_at] = first_dims(keys, d_scores).T * 0.125
            return 0

        if inner == 1:
            step(0, 0)
        else:
            lax.fori_loop(0, inner, step, 0)


class GroupSum:
    def __init__(self, links, dp, nd, rows, part, ra, rb):
        self.links, self.rows = links, rows
        self.part, self.ra, self.rb = part, ra, rb
        self.near, self.across, self.far = flip_one(dp), (dp + 2) % nd, nd - 1 - dp
        self.dp = dp
        block = lambda ref, b: ref.at[halves(b * rows, rows)]
        self.a = [
            links.to({"dp": self.near}, block(part, self.far), block(ra, 0)),
            links.to({"dp": self.near}, block(part, self.near), block(ra, 1)),
        ]

    def middle(self):
        rows, at = self.rows, halves(self.across * self.rows, self.rows)
        self.a[0].wait_recv()
        self.part[at, :] = (
            self.part[at, :].astype(F32) + self.ra[:rows, :].astype(F32)
        ).astype(BF16)
        self.b = self.links.to({"dp": self.across}, self.part.at[at], self.rb)

    def total(self):
        rows, at = self.rows, halves(self.dp * self.rows, self.rows)
        self.a[1].wait_recv()
        self.b.wait_recv()
        return (
            self.part[at, :].astype(F32)
            + self.ra[rows:, :].astype(F32)
            + self.rb[...].astype(F32)
        )


class Gradient:
    def __init__(self, links, ctx, nc, left, right, slots, landing, stage):
        self.links, self.ctx, self.nc = links, ctx, nc
        self.left, self.right, self.slots = left, right, slots
        self.landing = landing
        self.stage = stage.at[pl.ds(0, slots.shape[1]), pl.ds(0, slots.shape[2])]
        self.sent = {}

    def _landing(self, bit, j):
        base = sum(self.nc >> (b + 1) for b in range(bit))
        return self.landing.at[base + (j >> bit)]

    def _owner(self, e):
        owner = self.ctx
        bit = 0
        while e >> bit:
            if (e >> bit) & 1:
                owner = flip_bit(owner, bit)
            bit += 1
        return owner

    def give(self, j):
        left = self.left[self._owner(2 * j + 1)]

        def step(at, n):
            here = pl.ds(at, n)
            self.slots[j, :, here] = plain(left, self.right[:, here]).astype(BF16)

        over_tiles(self.right.shape[1], 512, step)
        self.sent[0, j] = self.links.to(
            {"ctx": flip_bit(self.ctx, 0)}, self.slots.at[j], self._landing(0, j)
        )

    def _load(self, bit, j):
        self.sent[bit, j if bit == 0 else j + (1 << (bit - 1))].wait_recv()
        copy = self.links.here(self._landing(bit, j), self.stage)
        copy.wait()

    def keep(self, j):
        left = self.left[self._owner(2 * j)]
        self._load(0, j)
        self.links.gone(self.sent[0, j])

        def step(at, n):
            here = pl.ds(at, n)
            acc = plain(left, self.right[:, here]) + self.stage[:, here].astype(F32)
            self.slots[j, :, here] = acc.astype(BF16)

        over_tiles(self.right.shape[1], 512, step)
        self._pass(1, j)

    def _pass(self, bit, j):
        low = j & -j
        if j and low == 1 << (bit - 1):
            self.sent[bit, j] = self.links.to(
                {"ctx": flip_bit(self.ctx, bit)}, self.slots.at[j], self._landing(bit, j - low)
            )

    def add(self, bit, j):
        self._load(bit, j)

        def step(at, n):
            here = pl.ds(at, n)
            acc = self.slots[j, :, here].astype(F32) + self.stage[:, here].astype(F32)
            self.slots[j, :, here] = acc.astype(BF16)

        over_tiles(self.right.shape[1], 512, step)
        self._pass(bit + 1, j)

    def order(self):
        return sorted(range(self.nc // 2), key=lambda j: (j & -j) or self.nc)

    def finish(self, after=1):
        bit = after
        while 1 << bit < self.nc:
            step = 1 << bit
            for j in sorted(range(0, self.nc // 2, step), key=lambda j: (j & -j) or self.nc):
                self.add(bit, j)
            bit += 1


def backward(nd, nc, f, small, tokens, w_out, lefts):
    rows, width = tokens.shape
    half = rows // 2
    many = nd * rows
    length, wide = f["seq"].shape
    heads = f["lse"].shape[0]
    span = heads * HDIM
    groups = nc // nd
    cols = groups * span
    cot_rows = f["dy"]
    keep_t, sine_t = rotary_pair_tables(length)
    chunk = min(length, 1024)
    names = ("gu", "down", "out", "qkv")
    right_cols = {"gu": f["dgu"].shape[1], "down": width, "out": width, "qkv": 3 * cols}
    left_rows = {k: lefts[k].shape[1] for k in names}
    slots = nc // 2

    def body(
        h2_l, m_l, mixed_l, h1_l, dy_i, dgu_i, wq_i, seq_i, lse_i, r1_i, pdh2_i, pout_i,
        small_i, tok_i, wo_i, keep_i, sine_i,
        out_o, tg_o, gu_o, down_o, out_g_o, qkv_o, sums_o, land_gu, land_down, land_out, land_qkv,
        l_gu, l_down, l_out, l_qkv, dgu, dy, da, dq, s_gu, s_down, s_out, s_qkv,
        stage,
        part, ra, rb, ra2, rb2, r1, dr1, x, sm, wq, wo, seq, lse,
        dmix, dseq, dx, keep, sine, dback, sums, sums_in,
        send, recv, local,
    ):
        dp, ctx = lax.axis_index("dp"), lax.axis_index("ctx")
        near, across, far = flip_one(dp), (dp + 2) % nd, nd - 1 - dp
        links = Copies(send, recv, local)
        blocks = lambda ref, b: ref.at[halves(b * rows, rows)]
        own_at = halves(dp * rows, rows)

        get_part = links.here(pdh2_i, part)
        get_gu = [links.here(h2_l, l_gu), links.here(dgu_i, dgu)]
        get_first = [links.here(a, b) for a, b in ((r1_i, r1), (small_i, sm), (dy_i, dy))]
        get_wo = links.here(wo_i, wo)
        get_down = links.here(m_l, l_down)
        get_attn = [
            links.here(a, b)
            for a, b in ((seq_i, seq), (lse_i, lse))
        ]

        def tables(c):
            at = pl.ds(c * chunk, chunk)
            return [links.here(a.at[at], b) for a, b in ((keep_i, keep), (sine_i, sine))]

        get_tables = tables(0)
        get_out = links.here(mixed_l, l_out)
        get_qkv = [links.here(a, b) for a, b in ((wq_i, wq), (h1_l, l_qkv), (tok_i, x))]

        gu = Gradient(links, ctx, nc, l_gu, dgu, s_gu, land_gu, stage)
        down = Gradient(links, ctx, nc, l_down, dy, s_down, land_down, stage)
        out = Gradient(links, ctx, nc, l_out, da, s_out, land_out, stage)
        qkv = Gradient(links, ctx, nc, l_qkv, dq, s_qkv, land_qkv, stage)
        order = gu.order()
        quarter = max(1, len(order) // 4)
        turns = [order[i : i + quarter] for i in range(0, len(order), quarter)]

        def gain(row):
            lines = [
                sm[b, row * 4 + q : row * 4 + q + 1, :]
                for b in range(nd)
                for q in range(width // nd // 128)
            ]
            return jnp.concatenate(lines, axis=1)

        meet((("dp", nd), ("ctx", nc)))
        get_part.wait()
        sum2 = GroupSum(links, dp, nd, rows, part, ra, rb)
        for copy in get_gu:
            copy.wait()
        for j in turns[0]:
            gu.give(j)
        sum2.middle()
        for copy in get_first:
            copy.wait()
        for j in turns[1]:
            gu.give(j)

        dh2 = sum2.total()
        hat, inverse = normalize_rows(r1[...])
        dr1[...] = dy[own_at, :].astype(F32) + norm_reverse(dh2, gain(2), hat, inverse)
        da[own_at, :] = dr1[...].astype(BF16)
        send_da = [links.to({"dp": e}, blocks(da, dp), blocks(da, dp)) for e in (near, across)]
        sums[2:3, :] = jnp.sum(dh2 * hat, axis=0, keepdims=True)
        sums[3:4, :] = jnp.sum(dh2, axis=0, keepdims=True)
        get_down.wait()
        send_da[1].wait_recv()
        forward_da = links.to({"dp": near}, blocks(da, across), blocks(da, across))
        get_wo.wait()
        send_da[0].wait_recv()
        forward_da.wait_recv()

        for g in range(groups):
            dmix[g] = last_dims(da[...], wo[g * span : (g + 1) * span, :]).astype(BF16)
        mirror = 2 * nc - 1 - ctx
        go = []
        for k in range(1, nc):
            peer = lax.rem(ctx + k, nc)
            s, g = peer // groups, peer % groups
            for i, block in enumerate((ctx, mirror)):
                go.append(
                    links.to(
                        {"ctx": peer},
                        dmix.at[g, halves(s * rows + i * half, half)],
                        dseq.at[halves(block * half, half)],
                    )
                )
        s, g = ctx // groups, ctx % groups
        stay = [
            links.here(
                dmix.at[g, halves(s * rows + i * half, half)], dseq.at[halves(block * half, half)]
            )
            for i, block in enumerate((ctx, mirror))
        ]
        dx[...] = jnp.zeros_like(dx)
        for j in turns[0]:
            gu.keep(j)
        for copy in get_attn + stay:
            copy.wait()
        for copy in go:
            copy.wait_recv()
        for j in turns[2]:
            gu.give(j)
        for head in range(heads):
            attend_back(seq, lse, dseq, dx, heads, head)
        for c in range(length // chunk):
            for copy in get_tables if c == 0 else tables(c):
                copy.wait()
            here = slice(c * chunk, (c + 1) * chunk)
            for at in range(0, wide, 128):
                n = min(128, wide - at)
                u = dx[here, at : at + n]
                if at < 2 * span:
                    u = rotate_pair(u, keep[...], -sine[...])
                seq[here, at : at + n] = u.astype(BF16)

        back = []
        for k in range(1, nc):
            peer = lax.rem(ctx + k, nc)
            for i, block in enumerate((peer, 2 * nc - 1 - peer)):
                back.append(
                    links.to(
                        {"ctx": peer},
                        seq.at[halves(block * half, half)],
                        dback.at[g, halves(s * rows + i * half, half)],
                    )
                )
        stay = [
            links.here(
                seq.at[halves(block * half, half)], dback.at[g, halves(s * rows + i * half, half)]
            )
            for i, block in enumerate((ctx, mirror))
        ]
        for j in turns[3]:
            gu.give(j)
        for j in turns[1]:
            gu.keep(j)
        for j in turns[0]:
            down.give(j)
        for copy in get_qkv + stay:
            copy.wait()
        for copy in back:
            copy.wait_recv()
        for g_ in range(groups):
            for j in range(3):
                at = j * cols + g_ * span
                dq[:, at : at + span] = dback[g_, :, j * span : (j + 1) * span]

        def dh1_tile(at, n):
            here = pl.ds(at, n)
            part[:, here] = last_dims(dq[...], wq[here, :]).astype(BF16)

        links.gone(*sum2.a, sum2.b)
        over_tiles(width, 256, dh1_tile)
        sum1 = GroupSum(links, dp, nd, rows, part, ra2, rb2)
        for j in turns[1]:
            down.give(j)
        sums[4:, :] = jnp.zeros((nd, width), F32)
        sums[pl.ds(4 + dp, 1), : 3 * cols] = jnp.sum(dq[...].astype(F32), axis=0, keepdims=True)
        sum1.middle()
        for j in turns[2] + turns[3]:
            down.give(j)
        dh1 = sum1.total()
        hat1, inverse1 = normalize_rows(x[...].astype(F32))
        sums[0:1, :] = jnp.sum(dh1 * hat1, axis=0, keepdims=True)
        sums[1:2, :] = jnp.sum(dh1, axis=0, keepdims=True)
        partners = [("ctx", flip_bit(ctx, b)) for b in range(nc.bit_length() - 1)]
        partners += [("dp", flip_bit(dp, b)) for b in range(nd.bit_length() - 1)]

        def exchange_sums(i):
            copy = links.to({partners[i][0]: partners[i][1]}, sums, sums_in.at[i])
            copy.wait_recv()
            links.gone(copy)
            sums[...] += sums_in[i]

        dr1[...] += norm_reverse(dh1, gain(0), hat1, inverse1)
        put_tg = links.here(dr1, tg_o)
        links.gone(*sum1.a, sum1.b)
        get_pout = links.here(pout_i, part)
        get_pout.wait()
        sum0 = GroupSum(links, dp, nd, rows, part, ra, rb)
        for j in turns[2]:
            gu.keep(j)
        for j in order:
            qkv.give(j)
        get_out.wait()
        sum0.middle()
        for j in order:
            out.give(j)
        for j in turns[3]:
            gu.keep(j)
        x[...] = (r1[...] + sum0.total()).astype(BF16)
        put_out = links.here(x, out_o)
        for i in range(len(partners)):
            exchange_sums(i)
        for piece, before in ((down, gu), (qkv, down), (out, qkv)):
            for j in order:
                piece.keep(j)
            before.finish()
        out.finish()
        put = [
            links.here(s_gu.at[0], gu_o),
            links.here(s_down.at[0], down_o),
            links.here(s_out.at[0], out_g_o),
            links.here(s_qkv.at[0], qkv_o),
        ]
        put_sums = [links.here(sums, sums_o), put_tg, put_out]
        links.gone(*links.left)
        for copy in put + put_sums:
            copy.wait()

    anywhere = pl.BlockSpec(memory_space=pl.ANY)
    shape = jax.ShapeDtypeStruct
    landings = nc - 1
    outs = [
        ((rows, width), BF16),
        ((rows, width), F32),
        *[((left_rows[k], right_cols[k]), BF16) for k in names],
        ((4 + nd, width), F32),
        *[((landings, left_rows[k], right_cols[k]), BF16) for k in names],
    ]
    scratch = [
        *[((nc, left_rows[k], many), BF16) for k in names],
        ((many, right_cols["gu"]), BF16),
        ((many, width), BF16),
        ((many, width), BF16),
        ((many, 3 * cols), BF16),
        *[((slots, left_rows[k], right_cols[k]), BF16) for k in names],
        ((max(left_rows.values()), max(right_cols.values())), BF16),
        ((many, width), BF16),
        *[((2 * rows, width), BF16), ((rows, width), BF16)] * 2,
        ((rows, width), F32),
        ((rows, width), F32),
        ((rows, width), BF16),
        (small.shape, F32),
        ((width, 3 * cols), BF16),
        ((cols, width), BF16),
        ((length, wide), BF16),
        ((heads, length), F32),
        ((groups, many, span), BF16),
        ((length, span), BF16),
        ((length, wide), F32),
        ((chunk, 128), F32),
        ((chunk, 128), F32),
        ((groups, many, wide), BF16),
        ((4 + nd, width), F32),
        ((nc.bit_length() + nd.bit_length() - 2, 4 + nd, width), F32),
    ]
    remotes = 9 + 3 + 4 * (nc - 1) + 4 * (nc - 1) + (nc - 1) + 3 + 8
    return pl.pallas_call(
        body,
        out_shape=[shape(*o) for o in outs],
        in_specs=[anywhere] * 17,
        out_specs=[anywhere] * len(outs),
        scratch_shapes=[pltpu.VMEM(*s) for s in scratch]
        + [
            pltpu.SemaphoreType.DMA((remotes,)),
            pltpu.SemaphoreType.DMA((remotes,)),
            pltpu.SemaphoreType.DMA((40 + 4 * nc,)),
        ],
        compiler_params=pltpu.CompilerParams(
            collective_id=1, has_side_effects=True, vmem_limit_bytes=VMEM_BYTES
        ),
    )(
        lefts["gu"], lefts["down"], lefts["out"], lefts["qkv"],
        f["dy"], f["dgu"], f["wq"], f["seq"], f["lse"], f["r1"], f["pdh2"], f["pout"],
        small, tokens, w_out, keep_t, sine_t,
    )


def take(x, index):
    return lax.dynamic_index_in_dim(x, index, 0, keepdims=False)


def shards(tokens, cotangent, w_qkv, b_qkv, w_out, w_gate, w_up, w_down, norms):
    width = tokens.shape[-1]
    rows = 2 * tokens.shape[3]
    nd, nc = lax.axis_size("dp"), lax.axis_size("ctx")
    dp, ctx = lax.axis_index("dp"), lax.axis_index("ctx")
    many = nd * rows
    hidden = w_gate.shape[1] // nd
    x = tokens.reshape(rows, width)

    small = jnp.concatenate([norms.reshape(-1), b_qkv]).astype(F32)
    small = jnp.pad(small, (0, -small.shape[0] % 1024)).reshape(-1, 128)
    f = forward(
        nd, nc, x, cotangent.reshape(rows, width), small, w_qkv, w_gate, w_up, w_out, w_down
    )

    def by_owner(left, outer):
        part = left.shape[1] // (outer * nc)
        left = left.T.reshape(outer, nc, part, many).transpose(1, 0, 2, 3)
        left = left.reshape(nc, outer * part, many)
        return jnp.pad(left, ((0, 0), (0, -left.shape[1] % 16), (0, 0)))

    lefts = {
        "gu": by_owner(f["h2"], nd),
        "down": by_owner(f["m"], 1),
        "out": by_owner(f["mixed"].transpose(1, 0, 2).reshape(many, -1), 1),
        "qkv": by_owner(f["h1"], nd),
    }
    result, tokens_grad, g_gu, g_down, g_out, g_qkv, sums = backward(
        nd, nc, f, f["small"], x, w_out, lefts
    )[:7]

    def to_rows(total):
        blocks = total.reshape(nd, -1, total.shape[1])
        part, cols = blocks.shape[1:]
        out = jnp.zeros((part, nd, cols), BF16)
        for k in range(nd):
            block = take(blocks, dp ^ k)
            if k:
                block = lax.ppermute(block, "dp", [(i, i ^ k) for i in range(nd)])
            out = lax.dynamic_update_slice(out, block[:, None], (0, dp ^ k, 0))
        return out.astype(F32)

    grad_gu = to_rows(g_gu)
    grad_qkv = to_rows(g_qkv)
    grad_qkv = grad_qkv.reshape(-1, nd, 3, width // nd).transpose(0, 2, 1, 3).reshape(-1, 3 * width)
    part_down, part_out = w_down.shape[0] // nc, w_out.shape[0] // nc

    place = dp * nc + ctx
    norms_grad = lax.dynamic_index_in_dim(sums[:4].reshape(4, nd * nc, -1), place, 1, keepdims=False)
    bias = sums[4:, : 3 * width // nd].reshape(nd, 3, -1).transpose(1, 0, 2)

    return (
        result.reshape(tokens.shape),
        tokens_grad.reshape(tokens.shape),
        grad_qkv,
        take(bias.reshape(nd * nc, -1), place),
        g_out[:part_out].astype(F32),
        grad_gu[:, :, :hidden].reshape(-1, nd * hidden),
        grad_gu[:, :, hidden:].reshape(-1, nd * hidden),
        g_down[:part_down].astype(F32),
        norms_grad,
    )


def solution(mesh):
    blocks = P("dp", "ctx", None, None, None)
    owned = P(("dp", "ctx"), None)
    return jax.shard_map(
        shards,
        mesh=mesh,
        in_specs=(
            blocks,
            blocks,
            P("dp", None),
            P("dp"),
            P("dp", None),
            P("dp", None),
            P("dp", None),
            P("dp", None),
            P(None, "dp"),
        ),
        out_specs=(
            blocks,
            blocks,
            owned,
            P(("dp", "ctx")),
            owned,
            owned,
            owned,
            owned,
            P(None, ("dp", "ctx")),
        ),
        check_vma=False,
    )
```

```python
import jax
import jax.numpy as jnp
import numpy as np
from jax import lax
from jax.experimental import pallas as pl
from jax.experimental.pallas import tpu as pltpu
from jax.sharding import PartitionSpec as P

HEADS = 32
HDIM = 64
ROT = 16
MESH = pl.DeviceIdType.MESH
F32 = jnp.float32
BF16 = jnp.bfloat16
VMEM_BYTES = 62 * 1024 * 1024


def normalize_rows(field):
    centre = field - jnp.mean(field, axis=-1, keepdims=True)
    inverse = lax.rsqrt(jnp.mean(centre * centre, axis=-1, keepdims=True) + 1e-05)
    return (centre * inverse, inverse)


def norm_reverse(incoming, gain, scaled, inverse):
    inner = incoming * gain
    return inverse * (
        inner
        - jnp.mean(inner, axis=-1, keepdims=True)
        - scaled * jnp.mean(inner * scaled, axis=-1, keepdims=True)
    )


def last_dims(a, b):
    return lax.dot_general(a, b, (((1,), (1,)), ((), ())), preferred_element_type=F32)


def first_dims(a, b):
    return lax.dot_general(a, b, (((0,), (0,)), ((), ())), preferred_element_type=F32)


def plain(a, b):
    return lax.dot_general(a, b, (((1,), (0,)), ((), ())), preferred_element_type=F32)


def attention_shapes(length):
    block = min(256 if length <= 1024 else 128, length)
    segments = min(4, length // block)
    return block, segments, length // block // segments


def head_columns(heads, what, head):
    at = (what * heads + head) * HDIM
    return slice(at, at + HDIM)


def causal(scores, first_query):
    keys = lax.broadcasted_iota(jnp.int32, scores.shape, 0)
    queries = lax.broadcasted_iota(jnp.int32, scores.shape, 1) + first_query
    return jnp.where(keys <= queries, scores, -1e30)


def flip_one(i):
    return i + 1 - 2 * (i % 2)


def halves(start, size):
    return pl.ds(pl.multiple_of(start, 64), size)


def lanes(start, size):
    return pl.ds(pl.multiple_of(start, 128), size)


class Copies:
    def __init__(self, send, recv, local):
        self.send, self.recv, self.local = send, recv, local
        self.remotes, self.locals, self.left = [], [], []

    def to(self, device, src, dst):
        at = len(self.remotes)
        copy = pltpu.make_async_remote_copy(
            src_ref=src,
            dst_ref=dst,
            send_sem=self.send.at[at],
            recv_sem=self.recv.at[at],
            device_id=device,
            device_id_type=MESH,
        )
        copy.start()
        self.remotes.append(copy)
        self.left.append(copy)
        return copy

    def gone(self, *copies):
        for copy in copies:
            copy.wait_send()
            self.left = [other for other in self.left if other is not copy]

    def here(self, src, dst):
        copy = pltpu.make_async_copy(src, dst, self.local.at[len(self.locals)])
        copy.start()
        self.locals.append(copy)
        return copy


def meet(axis_sizes):
    barrier = pltpu.get_barrier_semaphore()
    met = 0
    for axis, size in axis_sizes:
        me = lax.axis_index(axis)
        for k in range(1, size):
            pl.semaphore_signal(
                barrier, inc=1, device_id={axis: lax.rem(me + k, size)}, device_id_type=MESH
            )
            met += 1
    pl.semaphore_wait(barrier, met)


def attend(x_ref, o_ref, lse_ref, heads, head):
    length = x_ref.shape[0]
    block, segments, inner = attention_shapes(length)
    q_at, k_at, v_at = (head_columns(heads, i, head) for i in range(3))
    for segment in range(segments):
        count = (segment + 1) * inner * block
        keys = x_ref[:count, k_at]
        values = x_ref[:count, v_at]

        def step(i, _):
            start = pl.multiple_of((segment * inner + i) * block, block)
            query = x_ref[pl.ds(start, block), q_at] * 0.125
            scores = causal(last_dims(keys, query), start)
            top = jnp.max(scores, axis=0, keepdims=True)
            expo = jnp.exp(scores - top)
            total = jnp.sum(expo, axis=0, keepdims=True)
            mixed = first_dims(values, expo.astype(BF16)) / total
            o_ref[pl.ds(start, block), head * HDIM : (head + 1) * HDIM] = mixed.T.astype(BF16)
            lse_ref[head : head + 1, pl.ds(start, block)] = top + jnp.log(total)
            return 0

        if inner == 1:
            step(0, 0)
        else:
            lax.fori_loop(0, inner, step, 0)


def rotate_pair(u, keep, sine):
    lane = lax.broadcasted_iota(jnp.int32, u.shape, 1) % HDIM
    other = jnp.where(lane < ROT // 2, pltpu.roll(u, 128 - ROT // 2, 1), pltpu.roll(u, ROT // 2, 1))
    return u * keep + other * sine


def rotary_pair_tables(length):
    pairs = ROT // 2
    inverse = np.power(np.float32(10000.0), -np.arange(pairs, dtype=np.float32) / np.float32(pairs))
    angle = np.arange(length, dtype=np.float32)[:, None] * inverse.astype(np.float32)[None, :]
    cosine, sine = np.cos(angle), np.sin(angle)
    keep = np.concatenate([cosine, cosine, np.ones((length, HDIM - ROT), np.float32)], axis=1)
    signed = np.concatenate([-sine, sine, np.zeros((length, HDIM - ROT), np.float32)], axis=1)
    return np.tile(keep, (1, 2)).astype(np.float32), np.tile(signed, (1, 2)).astype(np.float32)


def tiles(total, size):
    return [(at, min(size, total - at)) for at in range(0, total, size)]


def over_tiles(total, size, step):
    whole = total // size
    if whole:

        def run(i, _):
            step(pl.multiple_of(i * size, size), size)
            return 0

        lax.fori_loop(0, whole, run, 0)
    if total % size:
        step(whole * size, total % size)


def turn_block(block, left, source, nd, nc):
    rows, width = block.shape
    part = width // (nd * nc)
    here = lanes(source * rows, rows)
    for at in range(0, width, 128):
        turned = block[:, at : at + 128].T
        for i in range(0, 128, part):
            d, c = (at + i) // (part * nc), (at + i) // part % nc
            left[c, d * part : (d + 1) * part, here] = turned[i : i + part]


def forward(nd, nc, tokens, cotangent, small, w_qkv, w_gate, w_up, w_out, w_down):
    rows, width = tokens.shape
    half = rows // 2
    many = nd * rows
    length = 2 * nc * half
    depth = w_qkv.shape[0]
    part_depth = depth // 2
    heads_here = HEADS // nd
    groups = nc // nd
    heads = heads_here // groups
    span = heads * HDIM
    cols = heads_here * HDIM
    hidden = w_gate.shape[1] // nd
    down = w_down.shape[0]
    keep, sine = rotary_pair_tables(length)

    def body(
        tok_i, cot_i, small_i, wq_i, wg_i, wu_i, wo_i, wd_i, keep_i, sine_i,
        h1_o, dy_o, wq_o, seq_o, lse_o, mixed_o, r1_o, h2_o, m_o, dgu_o, pout_o, pdh2_o, small_o,
        tok, dy, sm, wq, h1, qkv, seq, lse, o, mixed, wo, part, ra, rb, r1, h2, wg, wu, wd, m, dgu,
        turns, left1, left2, m_t, mixed_t, send, recv, local,
    ):
        dp, ctx = lax.axis_index("dp"), lax.axis_index("ctx")
        odd = ctx % 2
        near, across, far = flip_one(dp), (dp + 2) % nd, nd - 1 - dp
        beside = flip_one(ctx)
        links = Copies(send, recv, local)
        blocks = lambda ref, b: ref.at[halves(b * rows, rows)]

        get_tok = links.here(tok_i, blocks(tok, dp))
        get_turns = [
            links.here(table.at[halves(block * half, half)], turns.at[t, pl.ds(i * half, half)])
            for t, table in enumerate((keep_i, sine_i))
            for i, block in enumerate((ctx, 2 * nc - 1 - ctx))
        ]
        get_small = links.here(small_i, sm.at[dp])
        get_wq = [
            links.here(
                wq_i.at[:, lanes(j * width + dp * cols, cols)],
                wq.at[halves(dp * depth, depth), pl.ds(j * cols, cols)],
            )
            for j in range(3)
        ]
        meet((("dp", nd), ("ctx", nc)))

        send_tok = [links.to({"dp": e}, tok_i, blocks(tok, dp)) for e in (near, across)]
        send_small = [links.to({"dp": e}, small_i, sm.at[dp]) for e in (near, across, far)]

        def columns(w_i, w, e, at, n, to, full):
            start = dp * depth + (0 if full else odd * part_depth)
            size = depth if full else part_depth
            first = 0 if full else odd * part_depth
            return links.to(
                {"dp": e},
                w_i.at[halves(first, size), lanes(at, n)],
                w.at[halves(start, size), pl.ds(to, n)],
            )

        def relay(w, source):
            block = w.at[halves(source * depth + odd * part_depth, part_depth)]
            return links.to({"ctx": beside}, block, block)

        wq_x = [
            [columns(wq_i, wq, e, j * width + e * cols, cols, j * cols, False) for j in range(3)]
            for e in (across, far)
        ]
        wq_near = [
            columns(wq_i, wq, near, j * width + near * cols, cols, j * cols, True) for j in range(3)
        ]
        get_wo = links.here(wo_i, wo)
        get_wd = links.here(wd_i, wd)
        get_dy = links.here(cot_i, blocks(dy, dp))
        get_wgu = [
            links.here(w_i.at[:, lanes(dp * hidden, hidden)], w.at[halves(dp * depth, depth)])
            for w_i, w in ((wg_i, wg), (wu_i, wu))
        ]

        send_tok[1].wait_recv()
        forward_tok = links.to({"dp": near}, blocks(tok, across), blocks(tok, across))
        get_small.wait()
        for copy in send_small:
            copy.wait_recv()

        def gain(row):
            lines = [
                sm[b, row * 4 + q : row * 4 + q + 1, :]
                for b in range(nd)
                for q in range(width // nd // 128)
            ]
            return jnp.concatenate(lines, axis=1)

        def first_norm(b):
            at = halves(b * rows, rows)
            hat, _ = normalize_rows(tok[at, :].astype(F32))
            h1[at, :] = (hat * gain(0) + gain(1)).astype(BF16)

        get_tok.wait()
        first_norm(dp)
        send_tok[0].wait_recv()
        first_norm(near)
        first_norm(across)
        forward_tok.wait_recv()
        first_norm(far)
        for b in range(nd):
            turn_block(h1[b * rows : (b + 1) * rows, :], left1, b, nd, nc)
        put_h1 = links.here(left1, h1_o)
        put_small = links.here(sm, small_o)

        wq_y = []
        for source, copies in ((across, wq_x[0]), (far, wq_x[1])):
            for copy in copies:
                copy.wait_recv()
            wq_y.append(relay(wq, source))
        wgu_x = [
            [columns(w_i, w, e, e * hidden, hidden, 0, False) for e in (across, far)]
            for w_i, w in ((wg_i, wg), (wu_i, wu))
        ]
        wgu_near = [
            columns(w_i, w, near, near * hidden, hidden, 0, True)
            for w_i, w in ((wg_i, wg), (wu_i, wu))
        ]
        for copy in get_wq + get_turns:
            copy.wait()
        for copy in wq_near + wq_y:
            copy.wait_recv()
        put_wq = links.here(wq, wq_o)

        for at, n in tiles(3 * cols, 256):
            j = at // cols
            acc = plain(h1[...], wq[:, at : at + n])
            for q in range(n // 128):
                first = at % cols + q * 128
                line = (j * width + dp * cols + first) // 128
                per = 3 * width // nd // 128
                bias = sm[line // per, pl.ds(4 * (width // nd) // 128 + line % per, 1), :]
                for s in range(nd):
                    u = acc[s * rows : (s + 1) * rows, q * 128 : (q + 1) * 128] + bias
                    if j < 2:
                        u = rotate_pair(u, turns[0], turns[1])
                    u = u.astype(BF16)
                    if heads > 1:
                        g, off = first // span, first % span
                        qkv[g, s * rows : (s + 1) * rows, j * span + off : j * span + off + 128] = u
                    else:
                        for i in range(2):
                            qkv[
                                first // HDIM + i, s * rows : (s + 1) * rows, j * HDIM : (j + 1) * HDIM
                            ] = u[:, i * HDIM : (i + 1) * HDIM]

        mirror = 2 * nc - 1 - ctx
        go = []
        for k in range(1, nc):
            peer = lax.rem(ctx + k, nc)
            s, g = peer // groups, peer % groups
            for i, block in enumerate((ctx, mirror)):
                go.append(
                    links.to(
                        {"ctx": peer},
                        qkv.at[g, halves(s * rows + i * half, half)],
                        seq.at[halves(block * half, half)],
                    )
                )
        s, g = ctx // groups, ctx % groups
        stay = [
            links.here(
                qkv.at[g, halves(s * rows + i * half, half)], seq.at[halves(block * half, half)]
            )
            for i, block in enumerate((ctx, mirror))
        ]
        send_dy = [links.to({"dp": e}, cot_i, blocks(dy, dp)) for e in (near, across)]
        wgu_y = []

        def pass_on(w, source, copy):
            copy.wait_recv()
            wgu_y.append(relay(w, source))

        pass_on(wg, across, wgu_x[0][0])
        pass_on(wg, far, wgu_x[0][1])
        for copy in stay:
            copy.wait()
        for copy in go:
            copy.wait_recv()
        put_seq = links.here(seq, seq_o)
        pass_on(wu, across, wgu_x[1][0])

        for head in range(heads):
            attend(seq, o, lse, heads, head)

        back = []
        for k in range(1, nc):
            peer = lax.rem(ctx + k, nc)
            for i, block in enumerate((peer, 2 * nc - 1 - peer)):
                back.append(
                    links.to(
                        {"ctx": peer},
                        o.at[halves(block * half, half)],
                        mixed.at[g, halves(s * rows + i * half, half)],
                    )
                )
        stay = [
            links.here(
                o.at[halves(block * half, half)], mixed.at[g, halves(s * rows + i * half, half)]
            )
            for i, block in enumerate((ctx, mirror))
        ]
        put_lse = links.here(lse, lse_o)
        pass_on(wu, far, wgu_x[1][1])
        send_dy[1].wait_recv()
        forward_dy = links.to({"dp": near}, blocks(dy, across), blocks(dy, across))
        get_wo.wait()
        for copy in stay:
            copy.wait()
        for copy in back:
            copy.wait_recv()

        def out_tile(at, n):
            acc = plain(mixed[0], wo[0:span, pl.ds(at, n)])
            for i in range(1, groups):
                acc += plain(mixed[i], wo[i * span : (i + 1) * span, pl.ds(at, n)])
            part[:, pl.ds(at, n)] = acc.astype(BF16)

        over_tiles(width, 512, out_tile)

        to_near = [
            links.to({"dp": near}, blocks(part, far), blocks(ra, 0)),
            links.to({"dp": near}, blocks(part, near), blocks(ra, 1)),
        ]
        for i in range(groups):
            mixed_t[i * span : (i + 1) * span, :] = mixed[i].T
        put_mixed = links.here(mixed_t, mixed_o)
        to_near[0].wait_recv()
        across_at = halves(across * rows, rows)
        part[across_at, :] = (part[across_at, :].astype(F32) + ra[:rows, :].astype(F32)).astype(BF16)
        to_across = links.to({"dp": across}, blocks(part, across), rb)
        to_near[1].wait_recv()
        own_at = halves(dp * rows, rows)
        r1[...] = tok[own_at, :].astype(F32) + (
            part[own_at, :].astype(F32) + ra[rows:, :].astype(F32)
        )
        to_across.wait_recv()
        r1[...] += rb[...].astype(F32)
        put_r1 = links.here(r1, r1_o)
        hat, _ = normalize_rows(r1[...])
        h2[own_at, :] = (hat * gain(2) + gain(3)).astype(BF16)
        send_h2 = [links.to({"dp": e}, blocks(h2, dp), blocks(h2, dp)) for e in (near, across)]
        turn_block(h2[own_at, :], left2, dp, nd, nc)
        send_h2[0].wait_recv()
        turn_block(h2[halves(near * rows, rows), :], left2, near, nd, nc)
        send_h2[1].wait_recv()
        forward_h2 = links.to({"dp": near}, blocks(h2, across), blocks(h2, across))
        turn_block(h2[halves(across * rows, rows), :], left2, across, nd, nc)
        get_wd.wait()
        get_dy.wait()
        for copy in get_wgu:
            copy.wait()
        for copy in wgu_near + wgu_y + [send_dy[0], forward_dy, forward_h2]:
            copy.wait_recv()
        turn_block(h2[halves(far * rows, rows), :], left2, far, nd, nc)
        put_h2 = links.here(left2, h2_o)
        put_dy = links.here(dy, dy_o)
        def hidden_tile(at, n):
            here = pl.ds(at, n)
            gate = plain(h2[...], wg[:, here])
            up = plain(h2[...], wu[:, here])
            dm = last_dims(dy[...], wd[here, :])
            sig = jax.nn.sigmoid(gate)
            m[:, here] = (gate * sig * up).astype(BF16)
            dgu[:, here] = (dm * up * sig * (1.0 + gate * (1.0 - sig))).astype(BF16)
            dgu[:, pl.ds(hidden + at, n)] = (dm * gate * sig).astype(BF16)

        over_tiles(hidden, 256, hidden_tile)

        def turn_tile(at, n):
            m_t[pl.ds(at, n), :] = m[:, pl.ds(at, n)].T

        over_tiles(hidden, 128, turn_tile)
        put_m = links.here(m_t, m_o)
        put_dgu = links.here(dgu, dgu_o)

        def dh2_tile(at, n):
            here = pl.ds(at, n)
            acc = last_dims(dgu[:, :hidden], wg[here, :]) + last_dims(dgu[:, hidden:], wu[here, :])
            h1[:, here] = acc.astype(BF16)

        over_tiles(width, 256, dh2_tile)
        put_pdh2 = links.here(h1, pdh2_o)
        links.gone(*send_tok, forward_tok)

        def result_tile(at, n):
            here = pl.ds(at, n)
            tok[:, here] = plain(m[...], wd[:, here]).astype(BF16)

        over_tiles(width, 256, result_tile)
        put_pout = links.here(tok, pout_o)

        links.gone(*links.left)
        for copy in (
            put_small, put_h1, put_wq, put_seq, put_lse, put_mixed, put_r1, put_h2, put_dy, put_m, put_dgu,
            put_pdh2, put_pout,
        ):
            copy.wait()

    anywhere = pl.BlockSpec(memory_space=pl.ANY)
    shape = jax.ShapeDtypeStruct
    remotes = 2 + 3 + 6 + 3 + 1 + 2 + 4 + 2 + 2 * (nc - 1) * 2 + 2 + 4 + 1 + 3 + 2 + 1
    outs = dict(
        h1=((nc, width // nc, many), BF16),
        dy=((many, width), BF16),
        wq=((width, 3 * cols), BF16),
        seq=((length, 3 * span), BF16),
        lse=((heads, length), F32),
        mixed=((cols, many), BF16),
        r1=((rows, width), F32),
        h2=((nc, width // nc, many), BF16),
        m=((hidden, many), BF16),
        dgu=((many, 2 * hidden), BF16),
        pout=((many, width), BF16),
        pdh2=((many, width), BF16),
        small=((nd,) + small.shape, F32),
    )
    scratch = [
        ((many, width), BF16),
        ((many, width), BF16),
        ((nd,) + small.shape, F32),
        ((width, 3 * cols), BF16),
        ((many, width), BF16),
        ((groups, many, 3 * span), BF16),
        ((length, 3 * span), BF16),
        ((heads, length), F32),
        ((length, span), BF16),
        ((groups, many, span), BF16),
        ((cols, width), BF16),
        ((many, width), BF16),
        ((2 * rows, width), BF16),
        ((rows, width), BF16),
        ((rows, width), F32),
        ((many, width), BF16),
        ((width, hidden), BF16),
        ((width, hidden), BF16),
        ((down, width), BF16),
        ((many, hidden), BF16),
        ((many, 2 * hidden), BF16),
        ((2, rows, 128), F32),
        ((nc, width // nc, many), BF16),
        ((nc, width // nc, many), BF16),
        ((hidden, many), BF16),
        ((cols, many), BF16),
    ]
    results = pl.pallas_call(
        body,
        out_shape=[shape(*o) for o in outs.values()],
        in_specs=[anywhere] * 10,
        out_specs=[anywhere] * len(outs),
        scratch_shapes=[pltpu.VMEM(*s) for s in scratch]
        + [
            pltpu.SemaphoreType.DMA((remotes,)),
            pltpu.SemaphoreType.DMA((remotes,)),
            pltpu.SemaphoreType.DMA((40,)),
        ],
        compiler_params=pltpu.CompilerParams(
            collective_id=0, has_side_effects=True, vmem_limit_bytes=VMEM_BYTES
        ),
    )(tokens, cotangent, small, w_qkv, w_gate, w_up, w_out, w_down, keep, sine)
    return dict(zip(outs, results))


def flip_bit(i, bit):
    return i + (1 << bit) - (2 << bit) * ((i // (1 << bit)) % 2)


def attend_back(x_ref, lse_ref, do_ref, d_ref, heads, head):
    length = x_ref.shape[0]
    block, segments, inner = attention_shapes(length)
    q_at, k_at, v_at = (head_columns(heads, i, head) for i in range(3))
    o_at = slice(head * HDIM, (head + 1) * HDIM)
    for segment in range(segments):
        count = (segment + 1) * inner * block
        keys = x_ref[:count, k_at]
        values = x_ref[:count, v_at]

        def step(i, _):
            start = pl.multiple_of((segment * inner + i) * block, block)
            query = x_ref[pl.ds(start, block), q_at] * 0.125
            dout = do_ref[pl.ds(start, block), o_at]
            scores = causal(last_dims(keys, query), start)
            probs = jnp.exp(scores - lse_ref[head : head + 1, pl.ds(start, block)])
            d_probs = last_dims(values, dout)
            centre = jnp.sum(probs * d_probs, axis=0, keepdims=True)
            d_scores = (probs * (d_probs - centre)).astype(BF16)
            d_ref[:count, v_at] += plain(probs.astype(BF16), dout)
            d_ref[:count, k_at] += plain(d_scores, query)
            d_ref[pl.ds(start, block), q_at] = first_dims(keys, d_scores).T * 0.125
            return 0

        if inner == 1:
            step(0, 0)
        else:
            lax.fori_loop(0, inner, step, 0)


class GroupSum:
    def __init__(self, links, dp, nd, rows, part, ra, rb):
        self.links, self.rows = links, rows
        self.part, self.ra, self.rb = part, ra, rb
        self.near, self.across, self.far = flip_one(dp), (dp + 2) % nd, nd - 1 - dp
        self.dp = dp
        block = lambda ref, b: ref.at[halves(b * rows, rows)]
        self.a = [
            links.to({"dp": self.near}, block(part, self.far), block(ra, 0)),
            links.to({"dp": self.near}, block(part, self.near), block(ra, 1)),
        ]

    def middle(self):
        rows, at = self.rows, halves(self.across * self.rows, self.rows)
        self.a[0].wait_recv()
        self.part[at, :] = (
            self.part[at, :].astype(F32) + self.ra[:rows, :].astype(F32)
        ).astype(BF16)
        self.b = self.links.to({"dp": self.across}, self.part.at[at], self.rb)

    def total(self):
        rows, at = self.rows, halves(self.dp * self.rows, self.rows)
        self.a[1].wait_recv()
        self.b.wait_recv()
        return (
            self.part[at, :].astype(F32)
            + self.ra[rows:, :].astype(F32)
            + self.rb[...].astype(F32)
        )


class Gradient:
    def __init__(self, links, ctx, nc, left, right, slots, landing, stage):
        self.links, self.ctx, self.nc = links, ctx, nc
        self.left, self.right, self.slots = left, right, slots
        self.landing = landing
        self.stage = stage.at[pl.ds(0, slots.shape[1]), pl.ds(0, slots.shape[2])]
        self.sent = {}

    def _landing(self, bit, j):
        base = sum(self.nc >> (b + 1) for b in range(bit))
        return self.landing.at[base + (j >> bit)]

    def _owner(self, e):
        owner = self.ctx
        bit = 0
        while e >> bit:
            if (e >> bit) & 1:
                owner = flip_bit(owner, bit)
            bit += 1
        return owner

    def give(self, j):
        left = self.left[self._owner(2 * j + 1)]

        def step(at, n):
            here = pl.ds(at, n)
            self.slots[j, :, here] = plain(left, self.right[:, here]).astype(BF16)

        over_tiles(self.right.shape[1], 512, step)
        self.sent[0, j] = self.links.to(
            {"ctx": flip_bit(self.ctx, 0)}, self.slots.at[j], self._landing(0, j)
        )

    def _load(self, bit, j):
        self.sent[bit, j if bit == 0 else j + (1 << (bit - 1))].wait_recv()
        copy = self.links.here(self._landing(bit, j), self.stage)
        copy.wait()

    def keep(self, j):
        left = self.left[self._owner(2 * j)]
        self._load(0, j)
        self.links.gone(self.sent[0, j])

        def step(at, n):
            here = pl.ds(at, n)
            acc = plain(left, self.right[:, here]) + self.stage[:, here].astype(F32)
            self.slots[j, :, here] = acc.astype(BF16)

        over_tiles(self.right.shape[1], 512, step)
        self._pass(1, j)

    def _pass(self, bit, j):
        low = j & -j
        if j and low == 1 << (bit - 1):
            self.sent[bit, j] = self.links.to(
                {"ctx": flip_bit(self.ctx, bit)}, self.slots.at[j], self._landing(bit, j - low)
            )

    def add(self, bit, j):
        self._load(bit, j)

        def step(at, n):
            here = pl.ds(at, n)
            acc = self.slots[j, :, here].astype(F32) + self.stage[:, here].astype(F32)
            self.slots[j, :, here] = acc.astype(BF16)

        over_tiles(self.right.shape[1], 512, step)
        self._pass(bit + 1, j)

    def order(self):
        return sorted(range(self.nc // 2), key=lambda j: (j & -j) or self.nc)


def backward(nd, nc, f, small, tokens, w_out, lefts):
    rows, width = tokens.shape
    half = rows // 2
    many = nd * rows
    length, wide = f["seq"].shape
    heads = f["lse"].shape[0]
    span = heads * HDIM
    groups = nc // nd
    cols = groups * span
    cot_rows = f["dy"]
    keep_t, sine_t = rotary_pair_tables(length)
    chunk = min(length, 1024)
    names = ("gu", "down", "out", "qkv")
    right_cols = {"gu": f["dgu"].shape[1], "down": width, "out": width, "qkv": 3 * cols}
    left_rows = {k: lefts[k].shape[1] for k in names}
    slots = nc // 2
    share = left_rows["gu"] // nd
    hidden = right_cols["gu"] // 2

    def body(
        h2_l, m_l, mixed_l, h1_l, dy_i, dgu_i, wq_i, seq_i, lse_i, r1_i, pdh2_i, pout_i,
        small_i, tok_i, wo_i, keep_i, sine_i,
        out_o, tg_o, gate_o, up_o, qkv_o, down_o, out_g_o, sums_o, land_gu, land_down, land_out, land_qkv,
        l_gu, l_down, l_out, l_qkv, dgu, dy, da, dq, s_gu, s_down, s_out, s_qkv,
        stage,
        part, ra, rb, ra2, rb2, r1, dr1, x, sm, wq, wo, seq, lse,
        dmix, dseq, dx, keep, sine, dback, sums, sums_in,
        send, recv, local,
    ):
        dp, ctx = lax.axis_index("dp"), lax.axis_index("ctx")
        near, across, far = flip_one(dp), (dp + 2) % nd, nd - 1 - dp
        links = Copies(send, recv, local)
        blocks = lambda ref, b: ref.at[halves(b * rows, rows)]
        own_at = halves(dp * rows, rows)

        get_part = links.here(pdh2_i, part)
        get_gu = [links.here(h2_l, l_gu), links.here(dgu_i, dgu)]
        get_first = [links.here(a, b) for a, b in ((r1_i, r1), (small_i, sm), (dy_i, dy))]
        get_wo = links.here(wo_i, wo)
        get_down = links.here(m_l, l_down)
        get_attn = [
            links.here(a, b)
            for a, b in ((seq_i, seq), (lse_i, lse))
        ]

        def tables(c):
            at = pl.ds(c * chunk, chunk)
            return [links.here(a.at[at], b) for a, b in ((keep_i, keep), (sine_i, sine))]

        get_tables = tables(0)
        get_out = links.here(mixed_l, l_out)
        get_qkv = [links.here(a, b) for a, b in ((wq_i, wq), (h1_l, l_qkv), (tok_i, x))]

        gu = Gradient(links, ctx, nc, l_gu, dgu, s_gu, land_gu, stage)
        down = Gradient(links, ctx, nc, l_down, dy, s_down, land_down, stage)
        out = Gradient(links, ctx, nc, l_out, da, s_out, land_out, stage)
        qkv = Gradient(links, ctx, nc, l_qkv, dq, s_qkv, land_qkv, stage)
        order = gu.order()
        quarter = max(1, len(order) // 4)
        turns = [order[i : i + quarter] for i in range(0, len(order), quarter)]

        def gain(row):
            lines = [
                sm[b, row * 4 + q : row * 4 + q + 1, :]
                for b in range(nd)
                for q in range(width // nd // 128)
            ]
            return jnp.concatenate(lines, axis=1)

        meet((("dp", nd), ("ctx", nc)))
        get_part.wait()
        sum2 = GroupSum(links, dp, nd, rows, part, ra, rb)
        for copy in get_gu:
            copy.wait()
        for j in turns[0]:
            gu.give(j)
        sum2.middle()
        for copy in get_first:
            copy.wait()
        for j in turns[1]:
            gu.give(j)

        dh2 = sum2.total()
        hat, inverse = normalize_rows(r1[...])
        dr1[...] = dy[own_at, :].astype(F32) + norm_reverse(dh2, gain(2), hat, inverse)
        da[own_at, :] = dr1[...].astype(BF16)
        send_da = [links.to({"dp": e}, blocks(da, dp), blocks(da, dp)) for e in (near, across)]
        sums[2:3, :] = jnp.sum(dh2 * hat, axis=0, keepdims=True)
        sums[3:4, :] = jnp.sum(dh2, axis=0, keepdims=True)
        get_down.wait()
        send_da[1].wait_recv()
        forward_da = links.to({"dp": near}, blocks(da, across), blocks(da, across))
        get_wo.wait()
        send_da[0].wait_recv()
        forward_da.wait_recv()

        for g in range(groups):
            dmix[g] = last_dims(da[...], wo[g * span : (g + 1) * span, :]).astype(BF16)
        mirror = 2 * nc - 1 - ctx
        go = []
        for k in range(1, nc):
            peer = lax.rem(ctx + k, nc)
            s, g = peer // groups, peer % groups
            for i, block in enumerate((ctx, mirror)):
                go.append(
                    links.to(
                        {"ctx": peer},
                        dmix.at[g, halves(s * rows + i * half, half)],
                        dseq.at[halves(block * half, half)],
                    )
                )
        s, g = ctx // groups, ctx % groups
        stay = [
            links.here(
                dmix.at[g, halves(s * rows + i * half, half)], dseq.at[halves(block * half, half)]
            )
            for i, block in enumerate((ctx, mirror))
        ]
        dx[...] = jnp.zeros_like(dx)
        for j in turns[0]:
            gu.keep(j)
        for copy in get_attn + stay:
            copy.wait()
        for copy in go:
            copy.wait_recv()
        for j in turns[2]:
            gu.give(j)
        for head in range(heads):
            attend_back(seq, lse, dseq, dx, heads, head)
        for c in range(length // chunk):
            for copy in get_tables if c == 0 else tables(c):
                copy.wait()
            here = slice(c * chunk, (c + 1) * chunk)
            for at in range(0, wide, 128):
                n = min(128, wide - at)
                u = dx[here, at : at + n]
                if at < 2 * span:
                    u = rotate_pair(u, keep[...], -sine[...])
                seq[here, at : at + n] = u.astype(BF16)

        back = []
        for k in range(1, nc):
            peer = lax.rem(ctx + k, nc)
            for i, block in enumerate((peer, 2 * nc - 1 - peer)):
                back.append(
                    links.to(
                        {"ctx": peer},
                        seq.at[halves(block * half, half)],
                        dback.at[g, halves(s * rows + i * half, half)],
                    )
                )
        stay = [
            links.here(
                seq.at[halves(block * half, half)], dback.at[g, halves(s * rows + i * half, half)]
            )
            for i, block in enumerate((ctx, mirror))
        ]
        for j in turns[3]:
            gu.give(j)
        for j in turns[1]:
            gu.keep(j)
        for j in turns[0]:
            down.give(j)
        for copy in get_qkv + stay:
            copy.wait()
        for copy in back:
            copy.wait_recv()
        for g_ in range(groups):
            for j in range(3):
                at = j * cols + g_ * span
                dq[:, at : at + span] = dback[g_, :, j * span : (j + 1) * span]

        def dh1_tile(at, n):
            here = pl.ds(at, n)
            part[:, here] = last_dims(dq[...], wq[here, :]).astype(BF16)

        links.gone(*sum2.a, sum2.b)
        over_tiles(width, 256, dh1_tile)
        sum1 = GroupSum(links, dp, nd, rows, part, ra2, rb2)
        for j in turns[1]:
            down.give(j)
        sums[4:, :] = jnp.zeros((nd, width), F32)
        sums[pl.ds(4 + dp, 1), : 3 * cols] = jnp.sum(dq[...].astype(F32), axis=0, keepdims=True)
        sum1.middle()
        for j in turns[2] + turns[3]:
            down.give(j)
        dh1 = sum1.total()
        hat1, inverse1 = normalize_rows(x[...].astype(F32))
        sums[0:1, :] = jnp.sum(dh1 * hat1, axis=0, keepdims=True)
        sums[1:2, :] = jnp.sum(dh1, axis=0, keepdims=True)
        partners = [("dp", flip_bit(dp, b)) for b in range(nd.bit_length() - 1)]
        partners += [("ctx", flip_bit(ctx, b)) for b in range(nc.bit_length() - 1)]

        def exchange_sums(i):
            copy = links.to({partners[i][0]: partners[i][1]}, sums, sums_in.at[i])
            copy.wait_recv()
            links.gone(copy)
            sums[...] += sums_in[i]

        dr1[...] += norm_reverse(dh1, gain(0), hat1, inverse1)
        put_tg = links.here(dr1, tg_o)
        links.gone(*sum1.a, sum1.b)
        get_pout = links.here(pout_i, part)
        get_pout.wait()
        sum0 = GroupSum(links, dp, nd, rows, part, ra, rb)
        for j in turns[2]:
            gu.keep(j)
        get_out.wait()
        for j in order:
            qkv.give(j)
        sum0.middle()
        for j in order:
            out.give(j)
        exchange_sums(0)
        exchange_sums(1)
        for j in turns[3]:
            gu.keep(j)
        x[...] = (r1[...] + sum0.total()).astype(BF16)
        put_out = links.here(x, out_o)
        arriving, put = [], []

        def to_owner(slots, spans):
            for e in (near, across, far, dp):
                for dst, at, to, n in spans:
                    src = slots.at[0, pl.ds(pl.multiple_of(e * share, 16), share), pl.ds(at, n)]
                    place = dst.at[:, lanes(to + dp * n, n)]
                    if e is dp:
                        put.append(links.here(src, place))
                    else:
                        arriving.append(links.to({"dp": e}, src, place))

        def first_steps(piece):
            for j in order:
                yield lambda j=j: piece.keep(j)

        def later_steps(piece, close):
            bit = 1
            while 1 << bit < nc:
                for j in sorted(range(0, nc // 2, 1 << bit), key=lambda j: (j & -j) or nc):
                    yield lambda bit=bit, j=j: piece.add(bit, j)
                bit += 1
            yield close

        gu_spans = ((gate_o, 0, 0, hidden), (up_o, hidden, 0, hidden))
        qkv_spans = tuple((qkv_o, j * cols, j * width, cols) for j in range(3))
        closes = (
            lambda: to_owner(s_gu, gu_spans),
            lambda: put.append(links.here(s_down.at[0], down_o)),
            lambda: to_owner(s_qkv, qkv_spans),
            lambda: put.append(links.here(s_out.at[0], out_g_o)),
        )
        pieces = (gu, down, qkv, out)
        for i in range(1, len(pieces) + 1):
            later = list(later_steps(pieces[i - 1], closes[i - 1]))
            first = list(first_steps(pieces[i])) if i < len(pieces) else []
            if i == len(pieces):
                exchange_sums(2)
            while later or first:
                if first:
                    first.pop(0)()
                if later and len(first) <= len(later):
                    later.pop(0)()
        for k in range(3, len(partners)):
            exchange_sums(k)
        put_sums = [links.here(sums, sums_o), put_tg, put_out]
        for copy in arriving:
            copy.wait_recv()
        links.gone(*links.left)
        for copy in put + put_sums:
            copy.wait()

    anywhere = pl.BlockSpec(memory_space=pl.ANY)
    shape = jax.ShapeDtypeStruct
    landings = nc - 1
    outs = [
        ((rows, width), BF16),
        ((rows, width), F32),
        ((share, nd * hidden), BF16),
        ((share, nd * hidden), BF16),
        ((share, 3 * width), BF16),
        ((left_rows["down"], width), BF16),
        ((left_rows["out"], width), BF16),
        ((4 + nd, width), F32),
        *[((landings, left_rows[k], right_cols[k]), BF16) for k in names],
    ]
    scratch = [
        *[((nc, left_rows[k], many), BF16) for k in names],
        ((many, right_cols["gu"]), BF16),
        ((many, width), BF16),
        ((many, width), BF16),
        ((many, 3 * cols), BF16),
        *[((slots, left_rows[k], right_cols[k]), BF16) for k in names],
        ((max(left_rows.values()), max(right_cols.values())), BF16),
        ((many, width), BF16),
        *[((2 * rows, width), BF16), ((rows, width), BF16)] * 2,
        ((rows, width), F32),
        ((rows, width), F32),
        ((rows, width), BF16),
        (small.shape, F32),
        ((width, 3 * cols), BF16),
        ((cols, width), BF16),
        ((length, wide), BF16),
        ((heads, length), F32),
        ((groups, many, span), BF16),
        ((length, span), BF16),
        ((length, wide), F32),
        ((chunk, 128), F32),
        ((chunk, 128), F32),
        ((groups, many, wide), BF16),
        ((4 + nd, width), F32),
        ((nc.bit_length() + nd.bit_length() - 2, 4 + nd, width), F32),
    ]
    remotes = 9 + 3 + 4 * (nc - 1) + 4 * (nc - 1) + nc.bit_length() + nd.bit_length() + 3 * 5 + 8
    return pl.pallas_call(
        body,
        out_shape=[shape(*o) for o in outs],
        in_specs=[anywhere] * 17,
        out_specs=[anywhere] * len(outs),
        scratch_shapes=[pltpu.VMEM(*s) for s in scratch]
        + [
            pltpu.SemaphoreType.DMA((remotes,)),
            pltpu.SemaphoreType.DMA((remotes,)),
            pltpu.SemaphoreType.DMA((40 + 4 * nc,)),
        ],
        compiler_params=pltpu.CompilerParams(
            collective_id=1, has_side_effects=True, vmem_limit_bytes=VMEM_BYTES
        ),
    )(
        lefts["gu"], lefts["down"], lefts["out"], lefts["qkv"],
        f["dy"], f["dgu"], f["wq"], f["seq"], f["lse"], f["r1"], f["pdh2"], f["pout"],
        small, tokens, w_out, keep_t, sine_t,
    )


def take(x, index):
    return lax.dynamic_index_in_dim(x, index, 0, keepdims=False)


def shards(tokens, cotangent, w_qkv, b_qkv, w_out, w_gate, w_up, w_down, norms):
    width = tokens.shape[-1]
    rows = 2 * tokens.shape[3]
    nd, nc = lax.axis_size("dp"), lax.axis_size("ctx")
    dp, ctx = lax.axis_index("dp"), lax.axis_index("ctx")
    many = nd * rows
    x = tokens.reshape(rows, width)

    small = jnp.concatenate([norms.reshape(-1), b_qkv]).astype(F32)
    small = jnp.pad(small, (0, -small.shape[0] % 1024)).reshape(-1, 128)
    f = forward(
        nd, nc, x, cotangent.reshape(rows, width), small, w_qkv, w_gate, w_up, w_out, w_down
    )

    def by_owner(left):
        left = left.reshape(nc, -1, many)
        return jnp.pad(left, ((0, 0), (0, -left.shape[1] % 16), (0, 0)))

    lefts = {
        "gu": f["h2"],
        "down": by_owner(f["m"]),
        "out": by_owner(f["mixed"]),
        "qkv": f["h1"],
    }
    result, tokens_grad, g_gate, g_up, g_qkv, g_down, g_out, sums = backward(
        nd, nc, f, f["small"], x, w_out, lefts
    )[:8]
    part_down, part_out = w_down.shape[0] // nc, w_out.shape[0] // nc

    place = dp * nc + ctx
    norms_grad = lax.dynamic_index_in_dim(sums[:4].reshape(4, nd * nc, -1), place, 1, keepdims=False)
    bias = sums[4:, : 3 * width // nd].reshape(nd, 3, -1).transpose(1, 0, 2)

    return (
        result.reshape(tokens.shape),
        tokens_grad.reshape(tokens.shape),
        g_qkv.astype(F32),
        take(bias.reshape(nd * nc, -1), place),
        g_out[:part_out].astype(F32),
        g_gate.astype(F32),
        g_up.astype(F32),
        g_down[:part_down].astype(F32),
        norms_grad,
    )


def solution(mesh):
    blocks = P("dp", "ctx", None, None, None)
    owned = P(("dp", "ctx"), None)
    return jax.shard_map(
        shards,
        mesh=mesh,
        in_specs=(
            blocks,
            blocks,
            P("dp", None),
            P("dp"),
            P("dp", None),
            P("dp", None),
            P("dp", None),
            P("dp", None),
            P(None, "dp"),
        ),
        out_specs=(
            blocks,
            blocks,
            owned,
            P(("dp", "ctx")),
            owned,
            owned,
            owned,
            owned,
            P(None, ("dp", "ctx")),
        ),
        check_vma=False,
    )
```

```python
import jax
import jax.numpy as jnp
import numpy as np
from jax import lax
from jax.experimental import pallas as pl
from jax.experimental.pallas import tpu as pltpu
from jax.sharding import PartitionSpec as P

HEADS = 32
HDIM = 64
ROT = 16
MESH = pl.DeviceIdType.MESH
F32 = jnp.float32
BF16 = jnp.bfloat16
VMEM_BYTES = 62 * 1024 * 1024


def normalize_rows(field):
    centre = field - jnp.mean(field, axis=-1, keepdims=True)
    inverse = lax.rsqrt(jnp.mean(centre * centre, axis=-1, keepdims=True) + 1e-05)
    return (centre * inverse, inverse)


def norm_reverse(incoming, gain, scaled, inverse):
    inner = incoming * gain
    return inverse * (
        inner
        - jnp.mean(inner, axis=-1, keepdims=True)
        - scaled * jnp.mean(inner * scaled, axis=-1, keepdims=True)
    )


def last_dims(a, b):
    return lax.dot_general(a, b, (((1,), (1,)), ((), ())), preferred_element_type=F32)


def first_dims(a, b):
    return lax.dot_general(a, b, (((0,), (0,)), ((), ())), preferred_element_type=F32)


def plain(a, b):
    return lax.dot_general(a, b, (((1,), (0,)), ((), ())), preferred_element_type=F32)


def attention_shapes(length):
    block = min(256 if length <= 1024 else 128, length)
    segments = min(4, length // block)
    return block, segments, length // block // segments


def head_columns(heads, what, head):
    at = (what * heads + head) * HDIM
    return slice(at, at + HDIM)


def causal(scores, first_query):
    keys = lax.broadcasted_iota(jnp.int32, scores.shape, 0)
    queries = lax.broadcasted_iota(jnp.int32, scores.shape, 1) + first_query
    return jnp.where(keys <= queries, scores, -1e30)


def flip_one(i):
    return i + 1 - 2 * (i % 2)


def flip_bit(i, bit):
    return i + (1 << bit) - (2 << bit) * ((i // (1 << bit)) % 2)


def halves(start, size):
    return pl.ds(pl.multiple_of(start, 64), size)


def lanes(start, size):
    return pl.ds(pl.multiple_of(start, 128), size)


class Copies:
    def __init__(self, send, recv, local):
        self.send, self.recv, self.local = send, recv, local
        self.remotes, self.locals, self.left = [], [], []

    def to(self, device, src, dst):
        at = len(self.remotes)
        copy = pltpu.make_async_remote_copy(
            src_ref=src,
            dst_ref=dst,
            send_sem=self.send.at[at],
            recv_sem=self.recv.at[at],
            device_id=device,
            device_id_type=MESH,
        )
        copy.start()
        self.remotes.append(copy)
        self.left.append(copy)
        return copy

    def gone(self, *copies):
        for copy in copies:
            copy.wait_send()
            self.left = [other for other in self.left if other is not copy]

    def here(self, src, dst):
        copy = pltpu.make_async_copy(src, dst, self.local.at[len(self.locals)])
        copy.start()
        self.locals.append(copy)
        return copy


def meet(axis_sizes):
    barrier = pltpu.get_barrier_semaphore()
    met = 0
    for axis, size in axis_sizes:
        me = lax.axis_index(axis)
        for k in range(1, size):
            pl.semaphore_signal(
                barrier, inc=1, device_id={axis: lax.rem(me + k, size)}, device_id_type=MESH
            )
            met += 1
    pl.semaphore_wait(barrier, met)


def attend(x_ref, o_ref, lse_ref, heads, head):
    length = x_ref.shape[0]
    block, segments, inner = attention_shapes(length)
    q_at, k_at, v_at = (head_columns(heads, i, head) for i in range(3))
    for segment in range(segments):
        count = (segment + 1) * inner * block
        keys = x_ref[:count, k_at]
        values = x_ref[:count, v_at]

        def step(i, _):
            start = pl.multiple_of((segment * inner + i) * block, block)
            query = x_ref[pl.ds(start, block), q_at] * 0.125
            scores = causal(last_dims(keys, query), start)
            top = jnp.max(scores, axis=0, keepdims=True)
            expo = jnp.exp(scores - top)
            total = jnp.sum(expo, axis=0, keepdims=True)
            mixed = first_dims(values, expo.astype(BF16)) / total
            o_ref[pl.ds(start, block), head * HDIM : (head + 1) * HDIM] = mixed.T.astype(BF16)
            lse_ref[head : head + 1, pl.ds(start, block)] = top + jnp.log(total)
            return 0

        if inner == 1:
            step(0, 0)
        else:
            lax.fori_loop(0, inner, step, 0)


def rotate_pair(u, keep, sine):
    lane = lax.broadcasted_iota(jnp.int32, u.shape, 1) % HDIM
    other = jnp.where(lane < ROT // 2, pltpu.roll(u, 128 - ROT // 2, 1), pltpu.roll(u, ROT // 2, 1))
    return u * keep + other * sine


def rotary_pair_tables(length):
    pairs = ROT // 2
    inverse = np.power(np.float32(10000.0), -np.arange(pairs, dtype=np.float32) / np.float32(pairs))
    angle = np.arange(length, dtype=np.float32)[:, None] * inverse.astype(np.float32)[None, :]
    cosine, sine = np.cos(angle), np.sin(angle)
    keep = np.concatenate([cosine, cosine, np.ones((length, HDIM - ROT), np.float32)], axis=1)
    signed = np.concatenate([-sine, sine, np.zeros((length, HDIM - ROT), np.float32)], axis=1)
    return np.tile(keep, (1, 2)).astype(np.float32), np.tile(signed, (1, 2)).astype(np.float32)


def tiles(total, size):
    return [(at, min(size, total - at)) for at in range(0, total, size)]


def over_tiles(total, size, step):
    whole = total // size
    if whole:

        def run(i, _):
            step(pl.multiple_of(i * size, size), size)
            return 0

        lax.fori_loop(0, whole, run, 0)
    if total % size:
        step(whole * size, total % size)


def turn_block(block, left, source, nd, nc):
    rows, width = block.shape
    part = width // (nd * nc)
    here = lanes(source * rows, rows)
    for at in range(0, width, 128):
        turned = block[:, at : at + 128].T
        for i in range(0, 128, part):
            d, c = (at + i) // (part * nc), (at + i) // part % nc
            left[c, d * part : (d + 1) * part, here] = turned[i : i + part]


def forward(nd, nc, tokens, cotangent, small, w_qkv, w_gate, w_up, w_out, w_down):
    rows, width = tokens.shape
    half = rows // 2
    many = nd * rows
    length = 2 * nc * half
    depth = w_qkv.shape[0]
    quarter = depth // 4
    heads_here = HEADS // nd
    groups = nc // nd
    heads = heads_here // groups
    span = heads * HDIM
    cols = heads_here * HDIM
    hidden = w_gate.shape[1] // nd
    down = w_down.shape[0]
    keep, sine = rotary_pair_tables(length)

    def body(
        tok_i, cot_i, small_i, wq_i, wg_i, wu_i, wo_i, wd_i, keep_i, sine_i,
        h1_o, dy_o, wq_o, seq_o, lse_o, mixed_o, r1_o, h2_o, m_o, dgu_o, pout_o, pdh2_o, small_o,
        tok, dy, sm, wq, h1, qkv, seq, lse, o, mixed, wo, part, ra, rb, r1, h2, wgu, wd, m, dgu,
        turns, left1, left2, m_t, mixed_t, send, recv, local,
    ):
        dp, ctx = lax.axis_index("dp"), lax.axis_index("ctx")
        near, across, far = flip_one(dp), (dp + 2) % nd, nd - 1 - dp
        spot = ctx % 4
        sides = [{"ctx": flip_bit(ctx, bit)} for bit in range(2)]
        links = Copies(send, recv, local)
        blocks = lambda ref, b: ref.at[halves(b * rows, rows)]

        get_tok = links.here(tok_i, blocks(tok, dp))
        get_turns = [
            links.here(table.at[halves(block * half, half)], turns.at[t, pl.ds(i * half, half)])
            for t, table in enumerate((keep_i, sine_i))
            for i, block in enumerate((ctx, 2 * nc - 1 - ctx))
        ]
        get_small = links.here(small_i, sm.at[dp])
        get_wq = [
            links.here(
                wq_i.at[:, lanes(j * width + dp * cols, cols)],
                wq.at[halves(dp * depth, depth), pl.ds(j * cols, cols)],
            )
            for j in range(3)
        ]
        meet((("dp", nd), ("ctx", nc)))

        send_tok = [links.to({"dp": e}, tok_i, blocks(tok, dp)) for e in (near, across)]
        send_small = [links.to({"dp": e}, small_i, sm.at[dp]) for e in (near, across, far)]

        def columns(w_i, w, e, at, n, to, full):
            first, size = (0, depth) if full else (spot * quarter, quarter)
            return links.to(
                {"dp": e},
                w_i.at[halves(first, size), lanes(at, n)],
                w.at[halves(dp * depth + first, size), pl.ds(to, n)],
            )

        def share(w, copies, source):
            for copy in copies:
                copy.wait_recv()
            block = w.at[halves(source * depth + spot * quarter, quarter)]
            return [links.to(side, block, block) for side in sides]

        def cross(w, shared, source):
            passed = []
            for bit in range(2):
                shared[bit].wait_recv()
                start = source * depth + flip_bit(spot, bit) * quarter + bit * (quarter // 2)
                block = w.at[halves(start, quarter // 2)]
                passed.append(links.to(sides[1 - bit], block, block))
            return passed

        def qkv_columns(e, full):
            return [
                columns(wq_i, wq, e, j * width + e * cols, cols, j * cols, full) for j in range(3)
            ]

        def hidden_columns(e, full):
            return [
                columns(w_i, wgu, e, e * hidden, hidden, i * hidden, full)
                for i, w_i in enumerate((wg_i, wu_i))
            ]

        wq_x = [qkv_columns(e, False) for e in (across, far)]
        wq_near = qkv_columns(near, True)
        get_wo = links.here(wo_i, wo)
        get_wd = links.here(wd_i, wd)
        get_dy = links.here(cot_i, blocks(dy, dp))
        get_wgu = [
            links.here(
                w_i.at[:, lanes(dp * hidden, hidden)],
                wgu.at[halves(dp * depth, depth), pl.ds(i * hidden, hidden)],
            )
            for i, w_i in enumerate((wg_i, wu_i))
        ]

        send_tok[1].wait_recv()
        forward_tok = links.to({"dp": near}, blocks(tok, across), blocks(tok, across))
        get_small.wait()
        for copy in send_small:
            copy.wait_recv()

        def gain(row):
            lines = [
                sm[b, row * 4 + q : row * 4 + q + 1, :]
                for b in range(nd)
                for q in range(width // nd // 128)
            ]
            return jnp.concatenate(lines, axis=1)

        def first_norm(b):
            at = halves(b * rows, rows)
            hat, _ = normalize_rows(tok[at, :].astype(F32))
            h1[at, :] = (hat * gain(0) + gain(1)).astype(BF16)

        get_tok.wait()
        first_norm(dp)
        send_tok[0].wait_recv()
        first_norm(near)
        first_norm(across)
        forward_tok.wait_recv()
        first_norm(far)
        for b in range(nd):
            turn_block(h1[b * rows : (b + 1) * rows, :], left1, b, nd, nc)
        put_h1 = links.here(left1, h1_o)
        put_small = links.here(sm, small_o)

        wq_s = [share(wq, copies, e) for copies, e in zip(wq_x, (across, far))]
        wgu_x = [hidden_columns(e, False) for e in (across, far)]
        wgu_near = hidden_columns(near, True)
        send_dy = [links.to({"dp": e}, cot_i, blocks(dy, dp)) for e in (near, across)]
        wq_c = [c for shared, e in zip(wq_s, (across, far)) for c in cross(wq, shared, e)]
        for copy in get_wq + get_turns:
            copy.wait()
        for copy in wq_near + wq_c:
            copy.wait_recv()
        put_wq = links.here(wq, wq_o)

        for at, n in tiles(3 * cols, 256):
            j = at // cols
            acc = plain(h1[...], wq[:, at : at + n])
            for q in range(n // 128):
                first = at % cols + q * 128
                line = (j * width + dp * cols + first) // 128
                per = 3 * width // nd // 128
                bias = sm[line // per, pl.ds(4 * (width // nd) // 128 + line % per, 1), :]
                for s in range(nd):
                    u = acc[s * rows : (s + 1) * rows, q * 128 : (q + 1) * 128] + bias
                    if j < 2:
                        u = rotate_pair(u, turns[0], turns[1])
                    u = u.astype(BF16)
                    if heads > 1:
                        g, off = first // span, first % span
                        qkv[g, s * rows : (s + 1) * rows, j * span + off : j * span + off + 128] = u
                    else:
                        for i in range(2):
                            qkv[
                                first // HDIM + i, s * rows : (s + 1) * rows, j * HDIM : (j + 1) * HDIM
                            ] = u[:, i * HDIM : (i + 1) * HDIM]

        mirror = 2 * nc - 1 - ctx
        go = []
        for k in range(1, nc):
            peer = lax.rem(ctx + k, nc)
            s, g = peer // groups, peer % groups
            for i, block in enumerate((ctx, mirror)):
                go.append(
                    links.to(
                        {"ctx": peer},
                        qkv.at[g, halves(s * rows + i * half, half)],
                        seq.at[halves(block * half, half)],
                    )
                )
        s, g = ctx // groups, ctx % groups
        stay = [
            links.here(
                qkv.at[g, halves(s * rows + i * half, half)], seq.at[halves(block * half, half)]
            )
            for i, block in enumerate((ctx, mirror))
        ]
        for copy in stay:
            copy.wait()
        for copy in go:
            copy.wait_recv()
        put_seq = links.here(seq, seq_o)
        wgu_s = [share(wgu, copies, e) for copies, e in zip(wgu_x, (across, far))]

        back, stay = [], []
        step = min(heads, 2)
        for head in range(heads):
            attend(seq, o, lse, heads, head)
            if (head + 1) % step:
                continue
            here = pl.ds((head + 1 - step) * HDIM, step * HDIM)
            for k in range(nc):
                peer = lax.rem(ctx + k, nc)
                for i, block in enumerate((peer, 2 * nc - 1 - peer)):
                    src = o.at[halves(block * half, half), here]
                    dst = mixed.at[g, halves(s * rows + i * half, half), here]
                    if k:
                        back.append(links.to({"ctx": peer}, src, dst))
                    else:
                        stay.append(links.here(src, dst))
        put_lse = links.here(lse, lse_o)
        get_wo.wait()
        for copy in stay:
            copy.wait()
        for copy in back:
            copy.wait_recv()

        def out_tile(at, n):
            acc = plain(mixed[0], wo[0:span, pl.ds(at, n)])
            for i in range(1, groups):
                acc += plain(mixed[i], wo[i * span : (i + 1) * span, pl.ds(at, n)])
            part[:, pl.ds(at, n)] = acc.astype(BF16)

        over_tiles(width, 512, out_tile)

        to_near = [
            links.to({"dp": near}, blocks(part, far), blocks(ra, 0)),
            links.to({"dp": near}, blocks(part, near), blocks(ra, 1)),
        ]
        for i in range(groups):
            mixed_t[i * span : (i + 1) * span, :] = mixed[i].T
        put_mixed = links.here(mixed_t, mixed_o)
        to_near[0].wait_recv()
        across_at = halves(across * rows, rows)
        part[across_at, :] = (part[across_at, :].astype(F32) + ra[:rows, :].astype(F32)).astype(BF16)
        to_across = links.to({"dp": across}, blocks(part, across), rb)
        wgu_c = [c for shared, e in zip(wgu_s, (across, far)) for c in cross(wgu, shared, e)]
        send_dy[1].wait_recv()
        forward_dy = links.to({"dp": near}, blocks(dy, across), blocks(dy, across))
        to_near[1].wait_recv()
        own_at = halves(dp * rows, rows)
        r1[...] = tok[own_at, :].astype(F32) + (
            part[own_at, :].astype(F32) + ra[rows:, :].astype(F32)
        )
        to_across.wait_recv()
        r1[...] += rb[...].astype(F32)
        put_r1 = links.here(r1, r1_o)
        hat, _ = normalize_rows(r1[...])
        h2[own_at, :] = (hat * gain(2) + gain(3)).astype(BF16)
        send_h2 = [links.to({"dp": e}, blocks(h2, dp), blocks(h2, dp)) for e in (near, across)]
        turn_block(h2[own_at, :], left2, dp, nd, nc)
        send_h2[0].wait_recv()
        turn_block(h2[halves(near * rows, rows), :], left2, near, nd, nc)
        send_h2[1].wait_recv()
        forward_h2 = links.to({"dp": near}, blocks(h2, across), blocks(h2, across))
        turn_block(h2[halves(across * rows, rows), :], left2, across, nd, nc)
        get_wd.wait()
        get_dy.wait()
        for copy in get_wgu:
            copy.wait()
        for copy in wgu_near + wgu_c + [send_dy[0], forward_dy, forward_h2]:
            copy.wait_recv()
        turn_block(h2[halves(far * rows, rows), :], left2, far, nd, nc)
        put_h2 = links.here(left2, h2_o)
        put_dy = links.here(dy, dy_o)
        def hidden_tile(at, n):
            here = pl.ds(at, n)
            gate = plain(h2[...], wgu[:, here])
            up = plain(h2[...], wgu[:, pl.ds(hidden + at, n)])
            dm = last_dims(dy[...], wd[here, :])
            sig = jax.nn.sigmoid(gate)
            m[:, here] = (gate * sig * up).astype(BF16)
            dgu[:, here] = (dm * up * sig * (1.0 + gate * (1.0 - sig))).astype(BF16)
            dgu[:, pl.ds(hidden + at, n)] = (dm * gate * sig).astype(BF16)

        over_tiles(hidden, 256, hidden_tile)

        def turn_tile(at, n):
            m_t[pl.ds(at, n), :] = m[:, pl.ds(at, n)].T

        over_tiles(hidden, 128, turn_tile)
        put_m = links.here(m_t, m_o)
        put_dgu = links.here(dgu, dgu_o)

        def dh2_tile(at, n):
            here = pl.ds(at, n)
            h1[:, here] = last_dims(dgu[...], wgu[here, :]).astype(BF16)

        over_tiles(width, 256, dh2_tile)
        put_pdh2 = links.here(h1, pdh2_o)
        links.gone(*send_tok, forward_tok)

        def result_tile(at, n):
            here = pl.ds(at, n)
            tok[:, here] = plain(m[...], wd[:, here]).astype(BF16)

        over_tiles(width, 256, result_tile)
        put_pout = links.here(tok, pout_o)

        links.gone(*links.left)
        for copy in (
            put_small, put_h1, put_wq, put_seq, put_lse, put_mixed, put_r1, put_h2, put_dy, put_m, put_dgu,
            put_pdh2, put_pout,
        ):
            copy.wait()

    anywhere = pl.BlockSpec(memory_space=pl.ANY)
    shape = jax.ShapeDtypeStruct
    remotes = 48 + 6 * (nc - 1)
    outs = dict(
        h1=((nc, width // nc, many), BF16),
        dy=((many, width), BF16),
        wq=((width, 3 * cols), BF16),
        seq=((length, 3 * span), BF16),
        lse=((heads, length), F32),
        mixed=((cols, many), BF16),
        r1=((rows, width), F32),
        h2=((nc, width // nc, many), BF16),
        m=((hidden, many), BF16),
        dgu=((many, 2 * hidden), BF16),
        pout=((many, width), BF16),
        pdh2=((many, width), BF16),
        small=((nd,) + small.shape, F32),
    )
    scratch = [
        ((many, width), BF16),
        ((many, width), BF16),
        ((nd,) + small.shape, F32),
        ((width, 3 * cols), BF16),
        ((many, width), BF16),
        ((groups, many, 3 * span), BF16),
        ((length, 3 * span), BF16),
        ((heads, length), F32),
        ((length, span), BF16),
        ((groups, many, span), BF16),
        ((cols, width), BF16),
        ((many, width), BF16),
        ((2 * rows, width), BF16),
        ((rows, width), BF16),
        ((rows, width), F32),
        ((many, width), BF16),
        ((width, 2 * hidden), BF16),
        ((down, width), BF16),
        ((many, hidden), BF16),
        ((many, 2 * hidden), BF16),
        ((2, rows, 128), F32),
        ((nc, width // nc, many), BF16),
        ((nc, width // nc, many), BF16),
        ((hidden, many), BF16),
        ((cols, many), BF16),
    ]
    results = pl.pallas_call(
        body,
        out_shape=[shape(*o) for o in outs.values()],
        in_specs=[anywhere] * 10,
        out_specs=[anywhere] * len(outs),
        scratch_shapes=[pltpu.VMEM(*s) for s in scratch]
        + [
            pltpu.SemaphoreType.DMA((remotes,)),
            pltpu.SemaphoreType.DMA((remotes,)),
            pltpu.SemaphoreType.DMA((40,)),
        ],
        compiler_params=pltpu.CompilerParams(
            collective_id=0, has_side_effects=True, vmem_limit_bytes=VMEM_BYTES
        ),
    )(tokens, cotangent, small, w_qkv, w_gate, w_up, w_out, w_down, keep, sine)
    return dict(zip(outs, results))


def attend_back(x_ref, lse_ref, do_ref, d_ref, heads, head):
    length = x_ref.shape[0]
    block, segments, inner = attention_shapes(length)
    q_at, k_at, v_at = (head_columns(heads, i, head) for i in range(3))
    o_at = slice(head * HDIM, (head + 1) * HDIM)
    for segment in range(segments):
        count = (segment + 1) * inner * block
        keys = x_ref[:count, k_at]
        values = x_ref[:count, v_at]

        def step(i, _):
            start = pl.multiple_of((segment * inner + i) * block, block)
            query = x_ref[pl.ds(start, block), q_at] * 0.125
            dout = do_ref[pl.ds(start, block), o_at]
            scores = causal(last_dims(keys, query), start)
            probs = jnp.exp(scores - lse_ref[head : head + 1, pl.ds(start, block)])
            d_probs = last_dims(values, dout)
            centre = jnp.sum(probs * d_probs, axis=0, keepdims=True)
            d_scores = (probs * (d_probs - centre)).astype(BF16)
            d_ref[:count, v_at] += plain(probs.astype(BF16), dout)
            d_ref[:count, k_at] += plain(d_scores, query)
            d_ref[pl.ds(start, block), q_at] = first_dims(keys, d_scores).T * 0.125
            return 0

        if inner == 1:
            step(0, 0)
        else:
            lax.fori_loop(0, inner, step, 0)


class GroupSum:
    def __init__(self, links, dp, nd, rows, part, ra, rb):
        self.links, self.rows = links, rows
        self.part, self.ra, self.rb = part, ra, rb
        self.near, self.across, self.far = flip_one(dp), (dp + 2) % nd, nd - 1 - dp
        self.dp = dp
        block = lambda ref, b: ref.at[halves(b * rows, rows)]
        self.a = [
            links.to({"dp": self.near}, block(part, self.far), block(ra, 0)),
            links.to({"dp": self.near}, block(part, self.near), block(ra, 1)),
        ]

    def middle(self):
        rows, at = self.rows, halves(self.across * self.rows, self.rows)
        self.a[0].wait_recv()
        self.part[at, :] = (
            self.part[at, :].astype(F32) + self.ra[:rows, :].astype(F32)
        ).astype(BF16)
        self.b = self.links.to({"dp": self.across}, self.part.at[at], self.rb)

    def total(self):
        rows, at = self.rows, halves(self.dp * self.rows, self.rows)
        self.a[1].wait_recv()
        self.b.wait_recv()
        return (
            self.part[at, :].astype(F32)
            + self.ra[rows:, :].astype(F32)
            + self.rb[...].astype(F32)
        )


class Gradient:
    def __init__(self, links, ctx, nc, left, right, slots, landing, stage):
        self.links, self.ctx, self.nc = links, ctx, nc
        self.left, self.right, self.slots = left, right, slots
        self.landing = landing
        self.stage = stage.at[pl.ds(0, slots.shape[1]), pl.ds(0, slots.shape[2])]
        self.sent = {}

    def _landing(self, bit, j):
        base = sum(self.nc >> (b + 1) for b in range(bit))
        return self.landing.at[base + (j >> bit)]

    def _owner(self, e):
        owner = self.ctx
        bit = 0
        while e >> bit:
            if (e >> bit) & 1:
                owner = flip_bit(owner, bit)
            bit += 1
        return owner

    def give(self, j):
        left = self.left[self._owner(2 * j + 1)]

        def step(at, n):
            here = pl.ds(at, n)
            self.slots[j, :, here] = plain(left, self.right[:, here]).astype(BF16)

        over_tiles(self.right.shape[1], 512, step)
        self.sent[0, j] = self.links.to(
            {"ctx": flip_bit(self.ctx, 0)}, self.slots.at[j], self._landing(0, j)
        )

    def _load(self, bit, j):
        self.sent[bit, j if bit == 0 else j + (1 << (bit - 1))].wait_recv()
        copy = self.links.here(self._landing(bit, j), self.stage)
        copy.wait()

    def keep(self, j):
        left = self.left[self._owner(2 * j)]
        self._load(0, j)
        self.links.gone(self.sent[0, j])

        def step(at, n):
            here = pl.ds(at, n)
            acc = plain(left, self.right[:, here]) + self.stage[:, here].astype(F32)
            self.slots[j, :, here] = acc.astype(BF16)

        over_tiles(self.right.shape[1], 512, step)
        self._pass(1, j)

    def _pass(self, bit, j):
        low = j & -j
        if j and low == 1 << (bit - 1):
            self.sent[bit, j] = self.links.to(
                {"ctx": flip_bit(self.ctx, bit)}, self.slots.at[j], self._landing(bit, j - low)
            )

    def add(self, bit, j):
        self._load(bit, j)

        def step(at, n):
            here = pl.ds(at, n)
            acc = self.slots[j, :, here].astype(F32) + self.stage[:, here].astype(F32)
            self.slots[j, :, here] = acc.astype(BF16)

        over_tiles(self.right.shape[1], 512, step)
        self._pass(bit + 1, j)

    def order(self):
        return sorted(range(self.nc // 2), key=lambda j: (j & -j) or self.nc)


def backward(nd, nc, f, small, tokens, w_out, lefts):
    rows, width = tokens.shape
    half = rows // 2
    many = nd * rows
    length, wide = f["seq"].shape
    heads = f["lse"].shape[0]
    span = heads * HDIM
    groups = nc // nd
    cols = groups * span
    cot_rows = f["dy"]
    keep_t, sine_t = rotary_pair_tables(length)
    chunk = min(length, 1024)
    names = ("gu", "down", "out", "qkv")
    right_cols = {"gu": f["dgu"].shape[1], "down": width, "out": width, "qkv": 3 * cols}
    left_rows = {k: lefts[k].shape[1] for k in names}
    slots = nc // 2
    share = left_rows["gu"] // nd
    hidden = right_cols["gu"] // 2

    def body(
        h2_l, m_l, mixed_l, h1_l, dy_i, dgu_i, wq_i, seq_i, lse_i, r1_i, pdh2_i, pout_i,
        small_i, tok_i, wo_i, keep_i, sine_i,
        out_o, tg_o, gate_o, up_o, qkv_o, down_o, out_g_o, sums_o, land_gu, land_down, land_out, land_qkv,
        l_gu, l_down, l_out, l_qkv, dgu, dy, da, dq, s_gu, s_down, s_out, s_qkv,
        stage,
        part, ra, rb, ra2, rb2, r1, dr1, x, sm, wq, wo, seq, lse,
        dmix, dseq, dx, keep, sine, dback, sums, sums_in,
        send, recv, local,
    ):
        dp, ctx = lax.axis_index("dp"), lax.axis_index("ctx")
        near, across, far = flip_one(dp), (dp + 2) % nd, nd - 1 - dp
        links = Copies(send, recv, local)
        blocks = lambda ref, b: ref.at[halves(b * rows, rows)]
        own_at = halves(dp * rows, rows)

        get_part = links.here(pdh2_i, part)
        get_gu = [links.here(h2_l, l_gu), links.here(dgu_i, dgu)]
        get_first = [links.here(a, b) for a, b in ((r1_i, r1), (small_i, sm), (dy_i, dy))]
        get_wo = links.here(wo_i, wo)
        get_down = links.here(m_l, l_down)
        get_attn = [
            links.here(a, b)
            for a, b in ((seq_i, seq), (lse_i, lse))
        ]

        def tables(c):
            at = pl.ds(c * chunk, chunk)
            return [links.here(a.at[at], b) for a, b in ((keep_i, keep), (sine_i, sine))]

        get_tables = tables(0)
        get_out = links.here(mixed_l, l_out)
        get_qkv = [links.here(a, b) for a, b in ((wq_i, wq), (h1_l, l_qkv), (tok_i, x))]

        gu = Gradient(links, ctx, nc, l_gu, dgu, s_gu, land_gu, stage)
        down = Gradient(links, ctx, nc, l_down, dy, s_down, land_down, stage)
        out = Gradient(links, ctx, nc, l_out, da, s_out, land_out, stage)
        qkv = Gradient(links, ctx, nc, l_qkv, dq, s_qkv, land_qkv, stage)
        order = gu.order()
        quarter = max(1, len(order) // 4)
        turns = [order[i : i + quarter] for i in range(0, len(order), quarter)]

        def gain(row):
            lines = [
                sm[b, row * 4 + q : row * 4 + q + 1, :]
                for b in range(nd)
                for q in range(width // nd // 128)
            ]
            return jnp.concatenate(lines, axis=1)

        meet((("dp", nd), ("ctx", nc)))
        get_part.wait()
        sum2 = GroupSum(links, dp, nd, rows, part, ra, rb)
        for copy in get_gu:
            copy.wait()
        for j in turns[0]:
            gu.give(j)
        sum2.middle()
        for copy in get_first:
            copy.wait()
        for j in turns[1]:
            gu.give(j)

        dh2 = sum2.total()
        hat, inverse = normalize_rows(r1[...])
        dr1[...] = dy[own_at, :].astype(F32) + norm_reverse(dh2, gain(2), hat, inverse)
        da[own_at, :] = dr1[...].astype(BF16)
        send_da = [links.to({"dp": e}, blocks(da, dp), blocks(da, dp)) for e in (near, across)]
        sums[2:3, :] = jnp.sum(dh2 * hat, axis=0, keepdims=True)
        sums[3:4, :] = jnp.sum(dh2, axis=0, keepdims=True)
        get_down.wait()
        send_da[1].wait_recv()
        forward_da = links.to({"dp": near}, blocks(da, across), blocks(da, across))
        get_wo.wait()
        send_da[0].wait_recv()
        forward_da.wait_recv()

        for g in range(groups):
            dmix[g] = last_dims(da[...], wo[g * span : (g + 1) * span, :]).astype(BF16)
        mirror = 2 * nc - 1 - ctx
        go = []
        for k in range(1, nc):
            peer = lax.rem(ctx + k, nc)
            s, g = peer // groups, peer % groups
            for i, block in enumerate((ctx, mirror)):
                go.append(
                    links.to(
                        {"ctx": peer},
                        dmix.at[g, halves(s * rows + i * half, half)],
                        dseq.at[halves(block * half, half)],
                    )
                )
        s, g = ctx // groups, ctx % groups
        stay = [
            links.here(
                dmix.at[g, halves(s * rows + i * half, half)], dseq.at[halves(block * half, half)]
            )
            for i, block in enumerate((ctx, mirror))
        ]
        dx[...] = jnp.zeros_like(dx)
        for j in turns[0]:
            gu.keep(j)
        for copy in get_attn + stay:
            copy.wait()
        for copy in go:
            copy.wait_recv()
        for j in turns[2]:
            gu.give(j)
        for head in range(heads):
            attend_back(seq, lse, dseq, dx, heads, head)
        for c in range(length // chunk):
            for copy in get_tables if c == 0 else tables(c):
                copy.wait()
            here = slice(c * chunk, (c + 1) * chunk)
            for at in range(0, wide, 128):
                n = min(128, wide - at)
                u = dx[here, at : at + n]
                if at < 2 * span:
                    u = rotate_pair(u, keep[...], -sine[...])
                seq[here, at : at + n] = u.astype(BF16)

        back = []
        for k in range(1, nc):
            peer = lax.rem(ctx + k, nc)
            for i, block in enumerate((peer, 2 * nc - 1 - peer)):
                back.append(
                    links.to(
                        {"ctx": peer},
                        seq.at[halves(block * half, half)],
                        dback.at[g, halves(s * rows + i * half, half)],
                    )
                )
        stay = [
            links.here(
                seq.at[halves(block * half, half)], dback.at[g, halves(s * rows + i * half, half)]
            )
            for i, block in enumerate((ctx, mirror))
        ]
        for j in turns[3]:
            gu.give(j)
        for j in turns[1]:
            gu.keep(j)
        for j in turns[0]:
            down.give(j)
        for copy in get_qkv + stay:
            copy.wait()
        for copy in back:
            copy.wait_recv()
        for g_ in range(groups):
            for j in range(3):
                at = j * cols + g_ * span
                dq[:, at : at + span] = dback[g_, :, j * span : (j + 1) * span]

        def dh1_tile(at, n):
            here = pl.ds(at, n)
            part[:, here] = last_dims(dq[...], wq[here, :]).astype(BF16)

        links.gone(*sum2.a, sum2.b)
        over_tiles(width, 256, dh1_tile)
        sum1 = GroupSum(links, dp, nd, rows, part, ra2, rb2)
        for j in turns[1]:
            down.give(j)
        sums[4:, :] = jnp.zeros((nd, width), F32)
        sums[pl.ds(4 + dp, 1), : 3 * cols] = jnp.sum(dq[...].astype(F32), axis=0, keepdims=True)
        sum1.middle()
        for j in turns[2] + turns[3]:
            down.give(j)
        dh1 = sum1.total()
        hat1, inverse1 = normalize_rows(x[...].astype(F32))
        sums[0:1, :] = jnp.sum(dh1 * hat1, axis=0, keepdims=True)
        sums[1:2, :] = jnp.sum(dh1, axis=0, keepdims=True)
        partners = [("dp", flip_bit(dp, b)) for b in range(nd.bit_length() - 1)]
        partners += [("ctx", flip_bit(ctx, b)) for b in range(nc.bit_length() - 1)]
        sums_out = []

        def start_sums():
            i = len(sums_out)
            if i < len(partners):
                axis, device = partners[i]
                sums_out.append(links.to({axis: device}, sums, sums_in.at[i]))

        def end_sums():
            i = len(sums_out) - 1
            sums_out[i].wait_recv()
            links.gone(sums_out[i])
            sums[...] += sums_in[i]

        start_sums()
        dr1[...] += norm_reverse(dh1, gain(0), hat1, inverse1)
        put_tg = links.here(dr1, tg_o)
        links.gone(*sum1.a, sum1.b)
        get_pout = links.here(pout_i, part)
        get_pout.wait()
        sum0 = GroupSum(links, dp, nd, rows, part, ra, rb)
        for j in turns[2]:
            gu.keep(j)
        get_out.wait()
        end_sums()
        start_sums()
        for j in order:
            qkv.give(j)
        sum0.middle()
        end_sums()
        start_sums()
        for j in order:
            out.give(j)
        for j in turns[3]:
            gu.keep(j)
        x[...] = (r1[...] + sum0.total()).astype(BF16)
        put_out = links.here(x, out_o)
        arriving, put = [], []

        def to_owner(slots, spans):
            for e in (near, across, far, dp):
                for dst, at, to, n in spans:
                    src = slots.at[0, pl.ds(pl.multiple_of(e * share, 16), share), pl.ds(at, n)]
                    place = dst.at[:, lanes(to + dp * n, n)]
                    if e is dp:
                        put.append(links.here(src, place))
                    else:
                        arriving.append(links.to({"dp": e}, src, place))

        def keep_all(piece):
            for j in order:
                piece.keep(j)

        def add_all(piece, bit):
            for j in sorted(range(0, nc // 2, 1 << bit), key=lambda j: (j & -j) or nc):
                piece.add(bit, j)

        gu_spans = ((gate_o, 0, 0, hidden), (up_o, hidden, 0, hidden))
        qkv_spans = tuple((qkv_o, j * cols, j * width, cols) for j in range(3))
        closes = (
            lambda: to_owner(s_gu, gu_spans),
            lambda: put.append(links.here(s_down.at[0], down_o)),
            lambda: to_owner(s_qkv, qkv_spans),
            lambda: put.append(links.here(s_out.at[0], out_g_o)),
        )
        pieces = (gu, down, qkv, out)
        bits = nc.bit_length() - 1
        for i in range(len(pieces) + bits - 1):
            if 0 < i < len(pieces):
                keep_all(pieces[i])
            if i == len(pieces) - 1:
                end_sums()
                start_sums()
            for bit in range(1, bits):
                if 0 <= i - (bit - 1) < len(pieces):
                    add_all(pieces[i - (bit - 1)], bit)
                    if bit == bits - 1:
                        closes[i - (bit - 1)]()
        while len(sums_out) < len(partners):
            end_sums()
            start_sums()
        end_sums()
        put_sums = [links.here(sums, sums_o), put_tg, put_out]
        for copy in arriving:
            copy.wait_recv()
        links.gone(*links.left)
        for copy in put + put_sums:
            copy.wait()

    anywhere = pl.BlockSpec(memory_space=pl.ANY)
    shape = jax.ShapeDtypeStruct
    landings = nc - 1
    outs = [
        ((rows, width), BF16),
        ((rows, width), F32),
        ((share, nd * hidden), BF16),
        ((share, nd * hidden), BF16),
        ((share, 3 * width), BF16),
        ((left_rows["down"], width), BF16),
        ((left_rows["out"], width), BF16),
        ((4 + nd, width), F32),
        *[((landings, left_rows[k], right_cols[k]), BF16) for k in names],
    ]
    scratch = [
        *[((nc, left_rows[k], many), BF16) for k in names],
        ((many, right_cols["gu"]), BF16),
        ((many, width), BF16),
        ((many, width), BF16),
        ((many, 3 * cols), BF16),
        *[((slots, left_rows[k], right_cols[k]), BF16) for k in names],
        ((max(left_rows.values()), max(right_cols.values())), BF16),
        ((many, width), BF16),
        *[((2 * rows, width), BF16), ((rows, width), BF16)] * 2,
        ((rows, width), F32),
        ((rows, width), F32),
        ((rows, width), BF16),
        (small.shape, F32),
        ((width, 3 * cols), BF16),
        ((cols, width), BF16),
        ((length, wide), BF16),
        ((heads, length), F32),
        ((groups, many, span), BF16),
        ((length, span), BF16),
        ((length, wide), F32),
        ((chunk, 128), F32),
        ((chunk, 128), F32),
        ((groups, many, wide), BF16),
        ((4 + nd, width), F32),
        ((nc.bit_length() + nd.bit_length() - 2, 4 + nd, width), F32),
    ]
    remotes = 9 + 3 + 4 * (nc - 1) + 4 * (nc - 1) + nc.bit_length() + nd.bit_length() + 3 * 5 + 8
    return pl.pallas_call(
        body,
        out_shape=[shape(*o) for o in outs],
        in_specs=[anywhere] * 17,
        out_specs=[anywhere] * len(outs),
        scratch_shapes=[pltpu.VMEM(*s) for s in scratch]
        + [
            pltpu.SemaphoreType.DMA((remotes,)),
            pltpu.SemaphoreType.DMA((remotes,)),
            pltpu.SemaphoreType.DMA((40 + 4 * nc,)),
        ],
        compiler_params=pltpu.CompilerParams(
            collective_id=1, has_side_effects=True, vmem_limit_bytes=VMEM_BYTES
        ),
    )(
        lefts["gu"], lefts["down"], lefts["out"], lefts["qkv"],
        f["dy"], f["dgu"], f["wq"], f["seq"], f["lse"], f["r1"], f["pdh2"], f["pout"],
        small, tokens, w_out, keep_t, sine_t,
    )


def take(x, index):
    return lax.dynamic_index_in_dim(x, index, 0, keepdims=False)


def shards(tokens, cotangent, w_qkv, b_qkv, w_out, w_gate, w_up, w_down, norms):
    width = tokens.shape[-1]
    rows = 2 * tokens.shape[3]
    nd, nc = lax.axis_size("dp"), lax.axis_size("ctx")
    dp, ctx = lax.axis_index("dp"), lax.axis_index("ctx")
    many = nd * rows
    x = tokens.reshape(rows, width)

    small = jnp.concatenate([norms.reshape(-1), b_qkv]).astype(F32)
    small = jnp.pad(small, (0, -small.shape[0] % 1024)).reshape(-1, 128)
    f = forward(
        nd, nc, x, cotangent.reshape(rows, width), small, w_qkv, w_gate, w_up, w_out, w_down
    )

    def by_owner(left):
        left = left.reshape(nc, -1, many)
        return jnp.pad(left, ((0, 0), (0, -left.shape[1] % 16), (0, 0)))

    lefts = {
        "gu": f["h2"],
        "down": by_owner(f["m"]),
        "out": by_owner(f["mixed"]),
        "qkv": f["h1"],
    }
    result, tokens_grad, g_gate, g_up, g_qkv, g_down, g_out, sums = backward(
        nd, nc, f, f["small"], x, w_out, lefts
    )[:8]
    part_down, part_out = w_down.shape[0] // nc, w_out.shape[0] // nc

    place = dp * nc + ctx
    norms_grad = lax.dynamic_index_in_dim(sums[:4].reshape(4, nd * nc, -1), place, 1, keepdims=False)
    bias = sums[4:, : 3 * width // nd].reshape(nd, 3, -1).transpose(1, 0, 2)

    return (
        result.reshape(tokens.shape),
        tokens_grad.reshape(tokens.shape),
        g_qkv.astype(F32),
        take(bias.reshape(nd * nc, -1), place),
        g_out[:part_out].astype(F32),
        g_gate.astype(F32),
        g_up.astype(F32),
        g_down[:part_down].astype(F32),
        norms_grad,
    )


def solution(mesh):
    blocks = P("dp", "ctx", None, None, None)
    owned = P(("dp", "ctx"), None)
    return jax.shard_map(
        shards,
        mesh=mesh,
        in_specs=(
            blocks,
            blocks,
            P("dp", None),
            P("dp"),
            P("dp", None),
            P("dp", None),
            P("dp", None),
            P("dp", None),
            P(None, "dp"),
        ),
        out_specs=(
            blocks,
            blocks,
            owned,
            P(("dp", "ctx")),
            owned,
            owned,
            owned,
            owned,
            P(None, ("dp", "ctx")),
        ),
        check_vma=False,
    )
```

```python
import jax
import jax.numpy as jnp
import numpy as np
from jax import lax
from jax.experimental import pallas as pl
from jax.experimental.pallas import tpu as pltpu
from jax.sharding import PartitionSpec as P

HEADS = 32
HDIM = 64
ROT = 16
MESH = pl.DeviceIdType.MESH
F32 = jnp.float32
BF16 = jnp.bfloat16
VMEM_BYTES = 62 * 1024 * 1024


def normalize_rows(field):
    centre = field - jnp.mean(field, axis=-1, keepdims=True)
    inverse = lax.rsqrt(jnp.mean(centre * centre, axis=-1, keepdims=True) + 1e-05)
    return (centre * inverse, inverse)


def norm_reverse(incoming, gain, scaled, inverse):
    inner = incoming * gain
    return inverse * (
        inner
        - jnp.mean(inner, axis=-1, keepdims=True)
        - scaled * jnp.mean(inner * scaled, axis=-1, keepdims=True)
    )


def last_dims(a, b):
    return lax.dot_general(a, b, (((1,), (1,)), ((), ())), preferred_element_type=F32)


def first_dims(a, b):
    return lax.dot_general(a, b, (((0,), (0,)), ((), ())), preferred_element_type=F32)


def plain(a, b):
    return lax.dot_general(a, b, (((1,), (0,)), ((), ())), preferred_element_type=F32)


def attention_shapes(length):
    block = min(256 if length <= 1024 else 128, length)
    segments = min(4, length // block)
    return block, segments, length // block // segments


def head_columns(heads, what, head):
    at = (what * heads + head) * HDIM
    return slice(at, at + HDIM)


def causal(scores, first_query):
    keys = lax.broadcasted_iota(jnp.int32, scores.shape, 0)
    queries = lax.broadcasted_iota(jnp.int32, scores.shape, 1) + first_query
    return jnp.where(keys <= queries, scores, -1e30)


def flip_one(i):
    return i + 1 - 2 * (i % 2)


def flip_bit(i, bit):
    return i + (1 << bit) - (2 << bit) * ((i // (1 << bit)) % 2)


def flip_bits(i, mask):
    for bit in range(mask.bit_length()):
        if mask >> bit & 1:
            i = flip_bit(i, bit)
    return i


def halves(start, size):
    return pl.ds(pl.multiple_of(start, 64), size)


def lanes(start, size):
    return pl.ds(pl.multiple_of(start, 128), size)


class Copies:
    def __init__(self, send, recv, local):
        self.send, self.recv, self.local = send, recv, local
        self.remotes, self.locals, self.left = [], [], []

    def to(self, device, src, dst):
        at = len(self.remotes)
        copy = pltpu.make_async_remote_copy(
            src_ref=src,
            dst_ref=dst,
            send_sem=self.send.at[at],
            recv_sem=self.recv.at[at],
            device_id=device,
            device_id_type=MESH,
        )
        copy.start()
        self.remotes.append(copy)
        self.left.append(copy)
        return copy

    def gone(self, *copies):
        for copy in copies:
            copy.wait_send()
            self.left = [other for other in self.left if other is not copy]

    def here(self, src, dst):
        copy = pltpu.make_async_copy(src, dst, self.local.at[len(self.locals)])
        copy.start()
        self.locals.append(copy)
        return copy


def meet(axis_sizes):
    barrier = pltpu.get_barrier_semaphore()
    met = 0
    for axis, size in axis_sizes:
        me = lax.axis_index(axis)
        for k in range(1, size):
            pl.semaphore_signal(
                barrier, inc=1, device_id={axis: lax.rem(me + k, size)}, device_id_type=MESH
            )
            met += 1
    pl.semaphore_wait(barrier, met)


def attend(x_ref, o_ref, lse_ref, heads, head):
    length = x_ref.shape[0]
    block, segments, inner = attention_shapes(length)
    q_at, k_at, v_at = (head_columns(heads, i, head) for i in range(3))
    for segment in range(segments):
        count = (segment + 1) * inner * block
        keys = x_ref[:count, k_at]
        values = x_ref[:count, v_at]

        def step(i, _):
            start = pl.multiple_of((segment * inner + i) * block, block)
            query = x_ref[pl.ds(start, block), q_at] * 0.125
            scores = causal(last_dims(keys, query), start)
            top = jnp.max(scores, axis=0, keepdims=True)
            expo = jnp.exp(scores - top)
            total = jnp.sum(expo, axis=0, keepdims=True)
            mixed = first_dims(values, expo.astype(BF16)) / total
            o_ref[pl.ds(start, block), head * HDIM : (head + 1) * HDIM] = mixed.T.astype(BF16)
            lse_ref[head : head + 1, pl.ds(start, block)] = top + jnp.log(total)
            return 0

        if inner == 1:
            step(0, 0)
        else:
            lax.fori_loop(0, inner, step, 0)


def rotate_pair(u, keep, sine):
    lane = lax.broadcasted_iota(jnp.int32, u.shape, 1) % HDIM
    other = jnp.where(lane < ROT // 2, pltpu.roll(u, 128 - ROT // 2, 1), pltpu.roll(u, ROT // 2, 1))
    return u * keep + other * sine


def rotary_pair_tables(length):
    pairs = ROT // 2
    inverse = np.power(np.float32(10000.0), -np.arange(pairs, dtype=np.float32) / np.float32(pairs))
    angle = np.arange(length, dtype=np.float32)[:, None] * inverse.astype(np.float32)[None, :]
    cosine, sine = np.cos(angle), np.sin(angle)
    keep = np.concatenate([cosine, cosine, np.ones((length, HDIM - ROT), np.float32)], axis=1)
    signed = np.concatenate([-sine, sine, np.zeros((length, HDIM - ROT), np.float32)], axis=1)
    return np.tile(keep, (1, 2)).astype(np.float32), np.tile(signed, (1, 2)).astype(np.float32)


def tiles(total, size):
    return [(at, min(size, total - at)) for at in range(0, total, size)]


def over_tiles(total, size, step):
    whole = total // size
    if whole:

        def run(i, _):
            step(pl.multiple_of(i * size, size), size)
            return 0

        lax.fori_loop(0, whole, run, 0)
    if total % size:
        step(whole * size, total % size)


def turn_block(block, left, source, nd, nc):
    rows, width = block.shape
    part = width // (nd * nc)
    here = lanes(source * rows, rows)
    for at in range(0, width, 128):
        turned = block[:, at : at + 128].T
        for i in range(0, 128, part):
            d, c = (at + i) // (part * nc), (at + i) // part % nc
            left[c, d * part : (d + 1) * part, here] = turned[i : i + part]


def forward(nd, nc, tokens, cotangent, small, w_qkv, w_gate, w_up, w_out, w_down):
    rows, width = tokens.shape
    half = rows // 2
    many = nd * rows
    length = 2 * nc * half
    depth = w_qkv.shape[0]
    quarter = depth // 4
    heads_here = HEADS // nd
    groups = nc // nd
    heads = heads_here // groups
    span = heads * HDIM
    cols = heads_here * HDIM
    hidden = w_gate.shape[1] // nd
    down = w_down.shape[0]
    share_down = down // nc
    padded = share_down + -share_down % 16
    keep, sine = rotary_pair_tables(length)

    def body(
        tok_i, cot_i, small_i, wq_i, wg_i, wu_i, wo_i, wd_i, keep_i, sine_i,
        h1_o, dy_o, wq_o, seq_o, lse_o, mixed_o, r1_o, h2_o, m_o, dgu_o, pout_o, pdh2_o, small_o,
        dyp_o, mp_o,
        tok, dy, sm, wq, h1, qkv, seq, lse, o, mixed, wo, part, ra, rb, r1, h2, wgu, wd, m, dgu,
        turns, left1, left2, m_t, mixed_t, send, recv, local,
    ):
        dp, ctx = lax.axis_index("dp"), lax.axis_index("ctx")
        near, across, far = flip_one(dp), (dp + 2) % nd, nd - 1 - dp
        spot = ctx % 4
        sides = [{"ctx": flip_bit(ctx, bit)} for bit in range(2)]
        links = Copies(send, recv, local)
        blocks = lambda ref, b: ref.at[halves(b * rows, rows)]

        get_tok = links.here(tok_i, blocks(tok, dp))
        get_turns = [
            links.here(table.at[halves(block * half, half)], turns.at[t, pl.ds(i * half, half)])
            for t, table in enumerate((keep_i, sine_i))
            for i, block in enumerate((ctx, 2 * nc - 1 - ctx))
        ]
        get_small = links.here(small_i, sm.at[dp])
        get_wq = [
            links.here(
                wq_i.at[:, lanes(j * width + dp * cols, cols)],
                wq.at[halves(dp * depth, depth), pl.ds(j * cols, cols)],
            )
            for j in range(3)
        ]
        meet((("dp", nd), ("ctx", nc)))

        def columns(w_i, w, e, at, n, to, which):
            first, size = (0, depth) if which is None else (which * quarter, quarter)
            return links.to(
                {"dp": e},
                w_i.at[halves(first, size), lanes(at, n)],
                w.at[halves(dp * depth + first, size), pl.ds(to, n)],
            )

        def share(w, copies, source):
            for copy in copies:
                copy.wait_recv()
            block = w.at[halves(source * depth + spot * quarter, quarter)]
            return [links.to(side, block, block) for side in sides]

        def cross(w, shared, source):
            passed = []
            for bit in range(2):
                shared[bit].wait_recv()
                start = source * depth + flip_bit(spot, bit) * quarter + bit * (quarter // 2)
                block = w.at[halves(start, quarter // 2)]
                passed.append(links.to(sides[1 - bit], block, block))
            return passed

        def qkv_columns(e, which):
            return [
                columns(wq_i, wq, e, j * width + e * cols, cols, j * cols, which) for j in range(3)
            ]

        def hidden_columns(e, which):
            return [
                columns(w_i, wgu, e, e * hidden, hidden, i * hidden, which)
                for i, w_i in enumerate((wg_i, wu_i))
            ]

        send_small = [links.to({"dp": e}, small_i, sm.at[dp]) for e in (near, across, far)]
        wq_x = [qkv_columns(e, spot) for e in (across, far)]
        send_tok = [links.to({"dp": e}, tok_i, blocks(tok, dp)) for e in (near, across)]
        wq_near = qkv_columns(near, None)
        wgu_x = [hidden_columns(e, spot) for e in (across, far)]
        send_dyp = [links.to(sides[0], cot_i, blocks(dyp_o, dp))]
        get_wo = links.here(wo_i, wo)
        get_wd = links.here(wd_i, wd)
        get_dy = links.here(cot_i, blocks(dy, dp))
        get_wgu = [
            links.here(
                w_i.at[:, lanes(dp * hidden, hidden)],
                wgu.at[halves(dp * depth, depth), pl.ds(i * hidden, hidden)],
            )
            for i, w_i in enumerate((wg_i, wu_i))
        ]

        get_small.wait()
        for copy in send_small:
            copy.wait_recv()

        def gain(row):
            lines = [
                sm[b, row * 4 + q : row * 4 + q + 1, :]
                for b in range(nd)
                for q in range(width // nd // 128)
            ]
            return jnp.concatenate(lines, axis=1)

        def first_norm(b):
            at = halves(b * rows, rows)
            hat, _ = normalize_rows(tok[at, :].astype(F32))
            h1[at, :] = (hat * gain(0) + gain(1)).astype(BF16)

        def turn_first(b):
            turn_block(h1[halves(b * rows, rows), :], left1, b, nd, nc)

        get_tok.wait()
        wq_s = [share(wq, copies, e) for copies, e in zip(wq_x, (across, far))]
        first_norm(dp)
        send_tok[0].wait_recv()
        first_norm(near)
        wq_c = cross(wq, wq_s[0], across)
        send_tok[1].wait_recv()
        forward_tok = links.to({"dp": near}, blocks(tok, across), blocks(tok, across))
        wq_c += cross(wq, wq_s[1], far)
        first_norm(across)
        forward_tok.wait_recv()
        first_norm(far)
        wgu_d = [hidden_columns(e, 3 - spot) for e in (across, far)]
        wgu_near = hidden_columns(near, None)
        send_dy = [links.to({"dp": e}, cot_i, blocks(dy, dp)) for e in (near, across)]
        put_small = links.here(sm, small_o)
        for copy in get_wq + get_turns:
            copy.wait()
        for copy in wq_near + wq_c:
            copy.wait_recv()
        put_wq = links.here(wq, wq_o)

        for at, n in tiles(3 * cols, 256):
            j = at // cols
            acc = plain(h1[...], wq[:, at : at + n])
            for q in range(n // 128):
                first = at % cols + q * 128
                line = (j * width + dp * cols + first) // 128
                per = 3 * width // nd // 128
                bias = sm[line // per, pl.ds(4 * (width // nd) // 128 + line % per, 1), :]
                for s in range(nd):
                    u = acc[s * rows : (s + 1) * rows, q * 128 : (q + 1) * 128] + bias
                    if j < 2:
                        u = rotate_pair(u, turns[0], turns[1])
                    u = u.astype(BF16)
                    if heads > 1:
                        g, off = first // span, first % span
                        qkv[g, s * rows : (s + 1) * rows, j * span + off : j * span + off + 128] = u
                    else:
                        for i in range(2):
                            qkv[
                                first // HDIM + i, s * rows : (s + 1) * rows, j * HDIM : (j + 1) * HDIM
                            ] = u[:, i * HDIM : (i + 1) * HDIM]

        mirror = 2 * nc - 1 - ctx
        go = []
        for k in range(1, nc):
            peer = lax.rem(ctx + k, nc)
            s, g = peer // groups, peer % groups
            for i, block in enumerate((ctx, mirror)):
                go.append(
                    links.to(
                        {"ctx": peer},
                        qkv.at[g, halves(s * rows + i * half, half)],
                        seq.at[halves(block * half, half)],
                    )
                )
        s, g = ctx // groups, ctx % groups
        stay = [
            links.here(
                qkv.at[g, halves(s * rows + i * half, half)], seq.at[halves(block * half, half)]
            )
            for i, block in enumerate((ctx, mirror))
        ]
        for copy in stay:
            copy.wait()
        for copy in go:
            copy.wait_recv()
        put_seq = links.here(seq, seq_o)
        for b in range(nd):
            turn_first(b)
        put_h1 = links.here(left1, h1_o)

        back, stay = [], []
        step = min(heads, 2)
        for head in range(heads):
            attend(seq, o, lse, heads, head)
            if (head + 1) % step:
                continue
            here = pl.ds((head + 1 - step) * HDIM, step * HDIM)
            for k in range(nc):
                peer = lax.rem(ctx + k, nc)
                for i, block in enumerate((peer, 2 * nc - 1 - peer)):
                    src = o.at[halves(block * half, half), here]
                    dst = mixed.at[g, halves(s * rows + i * half, half), here]
                    if k:
                        back.append(links.to({"ctx": peer}, src, dst))
                    else:
                        stay.append(links.here(src, dst))
        wgu_s = [c for copies, e in zip(wgu_x, (across, far)) for c in share(wgu, copies, e)]
        put_lse = links.here(lse, lse_o)
        get_wo.wait()
        for copy in stay:
            copy.wait()
        for copy in back:
            copy.wait_recv()

        def out_tile(at, n):
            acc = plain(mixed[0], wo[0:span, pl.ds(at, n)])
            for i in range(1, groups):
                acc += plain(mixed[i], wo[i * span : (i + 1) * span, pl.ds(at, n)])
            part[:, pl.ds(at, n)] = acc.astype(BF16)

        over_tiles(width, 512, out_tile)

        to_near = [
            links.to({"dp": near}, blocks(part, far), blocks(ra, 0)),
            links.to({"dp": near}, blocks(part, near), blocks(ra, 1)),
        ]
        for i in range(groups):
            mixed_t[i * span : (i + 1) * span, :] = mixed[i].T
        put_mixed = links.here(mixed_t, mixed_o)
        to_near[0].wait_recv()
        across_at = halves(across * rows, rows)
        part[across_at, :] = (part[across_at, :].astype(F32) + ra[:rows, :].astype(F32)).astype(BF16)
        to_across = links.to({"dp": across}, blocks(part, across), rb)
        send_dy[1].wait_recv()
        forward_dy = links.to({"dp": near}, blocks(dy, across), blocks(dy, across))
        send_dyp.append(links.to(sides[0], blocks(dy, across), blocks(dyp_o, across)))
        to_near[1].wait_recv()
        own_at = halves(dp * rows, rows)
        r1[...] = tok[own_at, :].astype(F32) + (
            part[own_at, :].astype(F32) + ra[rows:, :].astype(F32)
        )
        to_across.wait_recv()
        r1[...] += rb[...].astype(F32)
        put_r1 = links.here(r1, r1_o)
        hat, _ = normalize_rows(r1[...])
        h2[own_at, :] = (hat * gain(2) + gain(3)).astype(BF16)
        send_h2 = [links.to({"dp": e}, blocks(h2, dp), blocks(h2, dp)) for e in (near, across)]
        turn_block(h2[own_at, :], left2, dp, nd, nc)
        send_h2[0].wait_recv()
        turn_block(h2[halves(near * rows, rows), :], left2, near, nd, nc)
        send_h2[1].wait_recv()
        forward_h2 = links.to({"dp": near}, blocks(h2, across), blocks(h2, across))
        turn_block(h2[halves(across * rows, rows), :], left2, across, nd, nc)
        get_wd.wait()
        get_dy.wait()
        for copy in get_wgu:
            copy.wait()
        for copy in wgu_near + wgu_s + wgu_d[0] + wgu_d[1] + [send_dy[0], forward_dy, forward_h2]:
            copy.wait_recv()
        turn_block(h2[halves(far * rows, rows), :], left2, far, nd, nc)
        put_h2 = links.here(left2, h2_o)
        put_dy = links.here(dy, dy_o)
        def hidden_tile(at, n):
            here = pl.ds(at, n)
            gate = plain(h2[...], wgu[:, here])
            up = plain(h2[...], wgu[:, pl.ds(hidden + at, n)])
            dm = last_dims(dy[...], wd[here, :])
            sig = jax.nn.sigmoid(gate)
            m[:, here] = (gate * sig * up).astype(BF16)
            dgu[:, here] = (dm * up * sig * (1.0 + gate * (1.0 - sig))).astype(BF16)
            dgu[:, pl.ds(hidden + at, n)] = (dm * gate * sig).astype(BF16)

        if padded != share_down:
            m[:, hidden:] = jnp.zeros((many, padded - share_down), BF16)
        over_tiles(hidden, 256, hidden_tile)
        for c in range(nc):
            m_t[c] = m[:, c * share_down : c * share_down + padded].T
        put_m = links.here(m_t, m_o)

        send_m, forward_dyp = [], []
        for j in range(nc // 2):
            owner = flip_bits(flip_bit(ctx, 0), 2 * j)
            send_m.append(links.to(sides[0], m_t.at[owner], mp_o.at[j]))
        for copy, b in zip(send_dyp, (dp, across)):
            copy.wait_recv()
            forward_dyp.append(links.to({"dp": near}, blocks(dyp_o, b), blocks(dyp_o, b)))
        put_dgu = links.here(dgu, dgu_o)

        def dh2_tile(at, n):
            here = pl.ds(at, n)
            h1[:, here] = last_dims(dgu[...], wgu[here, :]).astype(BF16)

        over_tiles(width, 256, dh2_tile)
        put_pdh2 = links.here(h1, pdh2_o)
        links.gone(*send_tok, forward_tok)

        def result_tile(at, n):
            here = pl.ds(at, n)
            tok[:, here] = plain(m[:, :hidden], wd[:, here]).astype(BF16)

        over_tiles(width, 256, result_tile)
        put_pout = links.here(tok, pout_o)
        for copy in send_m + forward_dyp:
            copy.wait_recv()

        links.gone(*links.left)
        for copy in (
            put_small, put_h1, put_wq, put_seq, put_lse, put_mixed, put_r1, put_h2, put_dy, put_m, put_dgu,
            put_pdh2, put_pout,
        ):
            copy.wait()

    anywhere = pl.BlockSpec(memory_space=pl.ANY)
    shape = jax.ShapeDtypeStruct
    remotes = 64 + 7 * nc
    outs = dict(
        h1=((nc, width // nc, many), BF16),
        dy=((many, width), BF16),
        wq=((width, 3 * cols), BF16),
        seq=((length, 3 * span), BF16),
        lse=((heads, length), F32),
        mixed=((cols, many), BF16),
        r1=((rows, width), F32),
        h2=((nc, width // nc, many), BF16),
        m=((nc, padded, many), BF16),
        dgu=((many, 2 * hidden), BF16),
        pout=((many, width), BF16),
        pdh2=((many, width), BF16),
        small=((nd,) + small.shape, F32),
        dyp=((many, width), BF16),
        mp=((nc // 2, padded, many), BF16),
    )
    scratch = [
        ((many, width), BF16),
        ((many, width), BF16),
        ((nd,) + small.shape, F32),
        ((width, 3 * cols), BF16),
        ((many, width), BF16),
        ((groups, many, 3 * span), BF16),
        ((length, 3 * span), BF16),
        ((heads, length), F32),
        ((length, span), BF16),
        ((groups, many, span), BF16),
        ((cols, width), BF16),
        ((many, width), BF16),
        ((2 * rows, width), BF16),
        ((rows, width), BF16),
        ((rows, width), F32),
        ((many, width), BF16),
        ((width, 2 * hidden), BF16),
        ((down, width), BF16),
        ((many, hidden + padded - share_down), BF16),
        ((many, 2 * hidden), BF16),
        ((2, rows, 128), F32),
        ((nc, width // nc, many), BF16),
        ((nc, width // nc, many), BF16),
        ((nc, padded, many), BF16),
        ((cols, many), BF16),
    ]
    results = pl.pallas_call(
        body,
        out_shape=[shape(*o) for o in outs.values()],
        in_specs=[anywhere] * 10,
        out_specs=[anywhere] * len(outs),
        scratch_shapes=[pltpu.VMEM(*s) for s in scratch]
        + [
            pltpu.SemaphoreType.DMA((remotes,)),
            pltpu.SemaphoreType.DMA((remotes,)),
            pltpu.SemaphoreType.DMA((40,)),
        ],
        compiler_params=pltpu.CompilerParams(
            collective_id=0, has_side_effects=True, vmem_limit_bytes=VMEM_BYTES
        ),
    )(tokens, cotangent, small, w_qkv, w_gate, w_up, w_out, w_down, keep, sine)
    return dict(zip(outs, results))


def attend_back(x_ref, lse_ref, do_ref, d_ref, heads, head):
    length = x_ref.shape[0]
    block, segments, inner = attention_shapes(length)
    q_at, k_at, v_at = (head_columns(heads, i, head) for i in range(3))
    o_at = slice(head * HDIM, (head + 1) * HDIM)
    for segment in range(segments):
        count = (segment + 1) * inner * block
        keys = x_ref[:count, k_at]
        values = x_ref[:count, v_at]

        def step(i, _):
            start = pl.multiple_of((segment * inner + i) * block, block)
            query = x_ref[pl.ds(start, block), q_at] * 0.125
            dout = do_ref[pl.ds(start, block), o_at]
            scores = causal(last_dims(keys, query), start)
            probs = jnp.exp(scores - lse_ref[head : head + 1, pl.ds(start, block)])
            d_probs = last_dims(values, dout)
            centre = jnp.sum(probs * d_probs, axis=0, keepdims=True)
            d_scores = (probs * (d_probs - centre)).astype(BF16)
            d_ref[:count, v_at] += plain(probs.astype(BF16), dout)
            d_ref[:count, k_at] += plain(d_scores, query)
            d_ref[pl.ds(start, block), q_at] = first_dims(keys, d_scores).T * 0.125
            return 0

        if inner == 1:
            step(0, 0)
        else:
            lax.fori_loop(0, inner, step, 0)


class GroupSum:
    def __init__(self, links, dp, nd, rows, part, ra, rb):
        self.links, self.rows = links, rows
        self.part, self.ra, self.rb = part, ra, rb
        self.near, self.across, self.far = flip_one(dp), (dp + 2) % nd, nd - 1 - dp
        self.dp = dp
        block = lambda ref, b: ref.at[halves(b * rows, rows)]
        self.a = [
            links.to({"dp": self.near}, block(part, self.far), block(ra, 0)),
            links.to({"dp": self.near}, block(part, self.near), block(ra, 1)),
        ]

    def middle(self):
        rows, at = self.rows, halves(self.across * self.rows, self.rows)
        self.a[0].wait_recv()
        self.part[at, :] = (
            self.part[at, :].astype(F32) + self.ra[:rows, :].astype(F32)
        ).astype(BF16)
        self.b = self.links.to({"dp": self.across}, self.part.at[at], self.rb)

    def total(self):
        rows, at = self.rows, halves(self.dp * self.rows, self.rows)
        self.a[1].wait_recv()
        self.b.wait_recv()
        return (
            self.part[at, :].astype(F32)
            + self.ra[rows:, :].astype(F32)
            + self.rb[...].astype(F32)
        )


class Gradient:
    def __init__(self, links, ctx, nc, left, right, slots, landing, stage):
        self.links, self.ctx, self.nc = links, ctx, nc
        self.left, self.right, self.slots = left, right, slots
        self.landing = landing
        self.stage = stage.at[pl.ds(0, slots.shape[1]), pl.ds(0, slots.shape[2])]
        self.sent = {}
        self.order = sorted(range(nc // 2), key=lambda j: (j & -j) or nc)

    def _landing(self, bit, j):
        base = sum(self.nc >> (b + 1) for b in range(1, bit))
        return self.landing.at[base + (j >> bit)]

    def compute(self):
        for j in self.order:
            self.slot(j)

    def slot(self, j):
        mine, other = self.left[0][j], self.left[1][j]

        def step(at, n):
            here = pl.ds(at, n)
            acc = plain(mine, self.right[0][:, here]) + plain(other, self.right[1][:, here])
            self.slots[j, :, here] = acc.astype(BF16)

        over_tiles(self.slots.shape[2], 512, step)
        self._pass(1, j)

    def _pass(self, bit, j):
        low = j & -j
        if j and low == 1 << (bit - 1):
            self.sent[bit, j] = self.links.to(
                {"ctx": flip_bit(self.ctx, bit)}, self.slots.at[j], self._landing(bit, j - low)
            )

    def add(self, bit):
        for j in self.order:
            if j % (1 << bit) == 0:
                self.add_slot(bit, j)

    def add_slot(self, bit, j):
        self.sent[bit, j + (1 << (bit - 1))].wait_recv()
        self.links.here(self._landing(bit, j), self.stage).wait()

        def step(at, n):
            here = pl.ds(at, n)
            acc = self.slots[j, :, here].astype(F32) + self.stage[:, here].astype(F32)
            self.slots[j, :, here] = acc.astype(BF16)

        over_tiles(self.slots.shape[2], 512, step)
        self._pass(bit + 1, j)


def backward(nd, nc, f, tokens, w_out):
    rows, width = tokens.shape
    half = rows // 2
    many = nd * rows
    length, wide = f["seq"].shape
    heads = f["lse"].shape[0]
    span = heads * HDIM
    groups = nc // nd
    cols = groups * span
    hidden = f["dgu"].shape[1] // 2
    slots = nc // 2
    share = width // (nd * nc)
    tall = {"gate": nd * share, "down": f["m"].shape[1], "out": cols // nc, "qkv": nd * share}
    tall["up"] = tall["gate"]
    flat = {"gate": hidden, "up": hidden, "down": width, "out": width, "qkv": 3 * cols}
    names = ("down", "gate", "up", "qkv", "out")
    bits = nc.bit_length() - 1
    keep_t, sine_t = rotary_pair_tables(length)
    chunk = length if length <= 1024 else 256
    strip = 256 if length <= 1024 else 128
    mixed_left = f["mixed"].reshape(nc, cols // nc, many)

    def body(
        h2_l, m_l, mp_l, mixed_l, h1_l, dy_i, dyp_i, dgu_i, wq_i, seq_i, lse_i, r1_i, pdh2_i, pout_i,
        small_i, tok_i, wo_i, keep_i, sine_i,
        out_o, tg_o, gate_o, up_o, qkv_o, down_o, out_g_o, sums_o,
        land_down, land_gate, land_up, land_qkv, land_out,
        l_gu, l_down, l_out, l_qkv, dgu, dgup, dy, dyp, da, dq, dqp,
        s_down, s_gate, s_up, s_qkv, s_out, stage,
        part, ra, rb, r1, dr1, x, sm, wq, wo, seq, lse,
        dmix, dseq, dx, keep, sine, dback, sums, sums_in,
        send, recv, local,
    ):
        dp, ctx = lax.axis_index("dp"), lax.axis_index("ctx")
        near, across, far = flip_one(dp), (dp + 2) % nd, nd - 1 - dp
        core = dp % 2
        links = Copies(send, recv, local)
        blocks = lambda ref, b: ref.at[halves(b * rows, rows)]
        own_at = halves(dp * rows, rows)
        beside = {"ctx": flip_bit(ctx, 0)}

        def get_left(left_i, left):
            return [links.here(left_i.at[flip_bits(ctx, 2 * j)], left.at[0, j]) for j in range(slots)]

        get_part = links.here(pdh2_i, part)
        get_down = get_left(m_l, l_down)
        get_down += [
            links.here(a, b) for a, b in ((mp_l, l_down.at[1]), (dy_i, dy), (dyp_i, dyp))
        ]
        get_first = [links.here(a, b) for a, b in ((r1_i, r1), (small_i, sm))]
        get_wo = links.here(wo_i, wo)
        get_gu = get_left(h2_l, l_gu) + [links.here(dgu_i, dgu)]
        get_attn = [links.here(a, b) for a, b in ((seq_i, seq), (lse_i, lse))]
        get_late = get_left(h1_l, l_qkv) + get_left(mixed_l, l_out) + [links.here(tok_i, x)]

        def tables(c):
            at = pl.ds(c * chunk, chunk)
            return [links.here(a.at[at], b) for a, b in ((keep_i, keep), (sine_i, sine))]

        get_tables = tables(0)

        def strips(i):
            return links.here(wq_i.at[pl.ds(i * strip, strip)], wq.at[i % 2])

        get_wq = [strips(0), strips(1)]

        def gain(row):
            lines = [
                sm[b, row * 4 + q : row * 4 + q + 1, :]
                for b in range(nd)
                for q in range(width // nd // 128)
            ]
            return jnp.concatenate(lines, axis=1)

        def both_lefts(left_i, left):
            n = tall["gate"] // 2
            at = pl.ds(pl.multiple_of(core * n, 16), n)
            return [
                links.to(
                    beside,
                    left_i.at[flip_bits(flip_bit(ctx, 0), 2 * j), at],
                    left.at[1, j, at],
                )
                for j in range(slots)
            ]

        def share_lefts(copies, left):
            n = tall["gate"] // 2
            at = pl.ds(pl.multiple_of(core * n, 16), n)
            for copy in copies:
                copy.wait_recv()
            block = left.at[1, :, at]
            return [links.to({"dp": near}, block, block)]

        down = Gradient(links, ctx, nc, l_down, (dy, dyp), s_down, land_down, stage)
        pieces = [down]
        for i, (slot, land) in enumerate(((s_gate, land_gate), (s_up, land_up))):
            at = pl.ds(i * hidden, hidden)
            right = (dgu.at[:, at], dgup.at[:, at])
            pieces.append(Gradient(links, ctx, nc, l_gu, right, slot, land, stage))
        gate, up = pieces[1:]
        qkv = Gradient(links, ctx, nc, l_qkv, (dq, dqp), s_qkv, land_qkv, stage)
        out = Gradient(links, ctx, nc, l_out, (da, dyp), s_out, land_out, stage)

        meet((("dp", nd), ("ctx", nc)))
        get_part.wait()
        sum2 = GroupSum(links, dp, nd, rows, part, ra, rb)
        left_gu = both_lefts(h2_l, l_gu)
        right_gate = links.to(
            beside, dgu_i.at[:, pl.ds(0, hidden)], dgup.at[:, pl.ds(0, hidden)]
        )
        for copy in get_down:
            copy.wait()
        down.slot(down.order[0])
        sum2.middle()
        for j in down.order[1:]:
            down.slot(j)
        left_gu2 = share_lefts(left_gu, l_gu)
        for copy in get_first:
            copy.wait()

        dh2 = sum2.total()
        hat, inverse = normalize_rows(r1[...])
        dr1[...] = dy[own_at, :].astype(F32) + norm_reverse(dh2, gain(2), hat, inverse)
        da[own_at, :] = dr1[...].astype(BF16)
        send_da = [links.to({"dp": e}, blocks(da, dp), blocks(da, dp)) for e in (near, across)]
        sums[2:3, :] = jnp.sum(dh2 * hat, axis=0, keepdims=True)
        sums[3:4, :] = jnp.sum(dh2, axis=0, keepdims=True)
        dx[...] = jnp.zeros_like(dx)
        send_da[1].wait_recv()
        forward_da = links.to({"dp": near}, blocks(da, across), blocks(da, across))
        get_wo.wait()
        send_da[0].wait_recv()
        forward_da.wait_recv()

        for g in range(groups):
            dmix[g] = last_dims(da[...], wo[g * span : (g + 1) * span, :]).astype(BF16)
        mirror = 2 * nc - 1 - ctx
        go = []
        for k in range(1, nc):
            peer = lax.rem(ctx + k, nc)
            s, g = peer // groups, peer % groups
            for i, block in enumerate((ctx, mirror)):
                go.append(
                    links.to(
                        {"ctx": peer},
                        dmix.at[g, halves(s * rows + i * half, half)],
                        dseq.at[halves(block * half, half)],
                    )
                )
        s, g = ctx // groups, ctx % groups
        stay = [
            links.here(
                dmix.at[g, halves(s * rows + i * half, half)], dseq.at[halves(block * half, half)]
            )
            for i, block in enumerate((ctx, mirror))
        ]
        right_up = links.to(
            beside, dgu_i.at[:, pl.ds(hidden, hidden)], dgup.at[:, pl.ds(hidden, hidden)]
        )
        for copy in get_gu:
            copy.wait()
        right_gate.wait_recv()
        left_gu2[0].wait_recv()
        gate.compute()
        if bits > 1:
            down.add(1)
        for copy in get_attn + stay:
            copy.wait()
        for copy in go:
            copy.wait_recv()
        for head in range(heads):
            attend_back(seq, lse, dseq, dx, heads, head)
        for c in range(length // chunk):
            for copy in get_tables if c == 0 else tables(c):
                copy.wait()
            here = slice(c * chunk, (c + 1) * chunk)
            for at in range(0, wide, 128):
                n = min(128, wide - at)
                u = dx[here, at : at + n]
                if at < 2 * span:
                    u = rotate_pair(u, keep[...], -sine[...])
                seq[here, at : at + n] = u.astype(BF16)

        back = []
        for k in range(1, nc):
            peer = lax.rem(ctx + k, nc)
            for i, block in enumerate((peer, 2 * nc - 1 - peer)):
                back.append(
                    links.to(
                        {"ctx": peer},
                        seq.at[halves(block * half, half)],
                        dback.at[g, halves(s * rows + i * half, half)],
                    )
                )
        stay = [
            links.here(
                seq.at[halves(block * half, half)], dback.at[g, halves(s * rows + i * half, half)]
            )
            for i, block in enumerate((ctx, mirror))
        ]
        for copy in get_late:
            copy.wait()
        left_qkv = both_lefts(h1_l, l_qkv)
        if bits > 1:
            gate.add(1)
        if bits > 2:
            down.add(2)
        right_up.wait_recv()
        up.compute()
        for copy in stay:
            copy.wait()
        for copy in back:
            copy.wait_recv()
        for g_ in range(groups):
            for j in range(3):
                at = j * cols + g_ * span
                dq[:, at : at + span] = dback[g_, :, j * span : (j + 1) * span]
        right_qkv = links.to(beside, dq, dqp)

        n = many // 2
        at = halves(core * n, n)
        right_out = links.to(beside, da.at[at], dyp.at[at])
        left_out = [
            links.to(beside, mixed_l.at[flip_bits(flip_bit(ctx, 0), 2 * j)], l_out.at[1, j])
            for j in range(slots)
        ]

        links.gone(*sum2.a, sum2.b)
        for i in range(width // strip):
            get_wq[i].wait()
            part[:, i * strip : (i + 1) * strip] = last_dims(dq[...], wq[i % 2]).astype(BF16)
            if i + 2 < width // strip:
                get_wq.append(strips(i + 2))
        sum1 = GroupSum(links, dp, nd, rows, part, ra, rb)
        left_qkv2 = share_lefts(left_qkv, l_qkv)
        sums[4:, :] = jnp.zeros((nd, width), F32)
        sums[pl.ds(4 + dp, 1), : 3 * cols] = jnp.sum(dq[...].astype(F32), axis=0, keepdims=True)
        sum1.middle()
        if bits > 1:
            up.add(1)
        dh1 = sum1.total()
        hat1, inverse1 = normalize_rows(x[...].astype(F32))
        sums[0:1, :] = jnp.sum(dh1 * hat1, axis=0, keepdims=True)
        sums[1:2, :] = jnp.sum(dh1, axis=0, keepdims=True)
        partners = [("dp", flip_bit(dp, b)) for b in range(nd.bit_length() - 1)]
        partners += [("ctx", flip_bit(ctx, b)) for b in range(bits)]
        sums_out = []

        def start_sums():
            i = len(sums_out)
            if i < len(partners):
                axis, device = partners[i]
                sums_out.append(links.to({axis: device}, sums, sums_in.at[i]))

        def end_sums():
            i = len(sums_out) - 1
            sums_out[i].wait_recv()
            links.gone(sums_out[i])
            sums[...] += sums_in[i]

        start_sums()
        dr1[...] += norm_reverse(dh1, gain(0), hat1, inverse1)
        put_tg = links.here(dr1, tg_o)
        links.gone(*sum1.a, sum1.b)
        get_pout = links.here(pout_i, part)
        get_pout.wait()
        end_sums()
        start_sums()
        sum0 = GroupSum(links, dp, nd, rows, part, ra, rb)
        end_sums()
        start_sums()
        sum0.middle()

        arriving, put = [], []

        def to_owner(slots_ref, spans):
            for e in (near, across, far, dp):
                for dst, at, to, n in spans:
                    src = slots_ref.at[0, pl.ds(pl.multiple_of(e * share, 16), share), pl.ds(at, n)]
                    place = dst.at[:, lanes(to + dp * n, n)]
                    if e is dp:
                        put.append(links.here(src, place))
                    else:
                        arriving.append(links.to({"dp": e}, src, place))

        qkv_spans = tuple((qkv_o, j * cols, j * width, cols) for j in range(3))

        for bit in range(3, bits):
            down.add(bit)
        put.append(links.here(s_down.at[0], down_o))
        for bit in range(2, bits):
            gate.add(bit)
        to_owner(s_gate, ((gate_o, 0, 0, hidden),))
        right_qkv.wait_recv()
        left_qkv2[0].wait_recv()
        qkv.compute()
        right_out.wait_recv()
        right_out2 = links.to({"dp": near}, dyp.at[at], dyp.at[at])
        for bit in range(2, bits):
            up.add(bit)
        to_owner(s_up, ((up_o, 0, 0, hidden),))
        x[...] = (r1[...] + sum0.total()).astype(BF16)
        put_out = links.here(x, out_o)
        right_out2.wait_recv()
        for copy in left_out:
            copy.wait_recv()
        out.compute()
        end_sums()
        start_sums()
        for bit in range(1, bits):
            qkv.add(bit)
        to_owner(s_qkv, qkv_spans)
        for bit in range(1, bits):
            out.add(bit)
        put.append(links.here(s_out.at[0], out_g_o))
        while len(sums_out) < len(partners):
            end_sums()
            start_sums()
        end_sums()
        put_sums = [links.here(sums, sums_o), put_tg, put_out]
        for copy in arriving:
            copy.wait_recv()
        links.gone(*links.left)
        for copy in put + put_sums:
            copy.wait()

    anywhere = pl.BlockSpec(memory_space=pl.ANY)
    shape = jax.ShapeDtypeStruct
    outs = [
        ((rows, width), BF16),
        ((rows, width), F32),
        ((share, nd * hidden), BF16),
        ((share, nd * hidden), BF16),
        ((share, 3 * width), BF16),
        ((tall["down"], width), BF16),
        ((tall["out"], width), BF16),
        ((4 + nd, width), F32),
        *[((max(1, slots - 1), tall[k], flat[k]), BF16) for k in names],
    ]
    scratch = [
        *[((2, slots, tall[k], many), BF16) for k in ("gate", "down", "out", "qkv")],
        ((many, 2 * hidden), BF16),
        ((many, 2 * hidden), BF16),
        ((many, width), BF16),
        ((many, width), BF16),
        ((many, width), BF16),
        ((many, 3 * cols), BF16),
        ((many, 3 * cols), BF16),
        *[((slots, tall[k], flat[k]), BF16) for k in names],
        ((max(tall.values()), max(flat.values())), BF16),
        ((many, width), BF16),
        ((2 * rows, width), BF16),
        ((rows, width), BF16),
        ((rows, width), F32),
        ((rows, width), F32),
        ((rows, width), BF16),
        (f["small"].shape, F32),
        ((2, strip, 3 * cols), BF16),
        ((cols, width), BF16),
        ((length, wide), BF16),
        ((heads, length), F32),
        ((groups, many, span), BF16),
        ((length, span), BF16),
        ((length, wide), F32),
        ((chunk, 128), F32),
        ((chunk, 128), F32),
        ((groups, many, wide), BF16),
        ((4 + nd, width), F32),
        ((bits + nd.bit_length() - 1, 4 + nd, width), F32),
    ]
    remotes = 64 + 4 * nc + 7 * nc
    return pl.pallas_call(
        body,
        out_shape=[shape(*o) for o in outs],
        in_specs=[anywhere] * 19,
        out_specs=[anywhere] * len(outs),
        scratch_shapes=[pltpu.VMEM(*s) for s in scratch]
        + [
            pltpu.SemaphoreType.DMA((remotes,)),
            pltpu.SemaphoreType.DMA((remotes,)),
            pltpu.SemaphoreType.DMA((64 + 7 * nc,)),
        ],
        compiler_params=pltpu.CompilerParams(
            collective_id=1, has_side_effects=True, vmem_limit_bytes=VMEM_BYTES
        ),
    )(
        f["h2"], f["m"], f["mp"], mixed_left, f["h1"],
        f["dy"], f["dyp"], f["dgu"], f["wq"], f["seq"], f["lse"], f["r1"], f["pdh2"], f["pout"],
        f["small"], tokens, w_out, keep_t, sine_t,
    )


def take(x, index):
    return lax.dynamic_index_in_dim(x, index, 0, keepdims=False)


def shards(tokens, cotangent, w_qkv, b_qkv, w_out, w_gate, w_up, w_down, norms):
    width = tokens.shape[-1]
    rows = 2 * tokens.shape[3]
    nd, nc = lax.axis_size("dp"), lax.axis_size("ctx")
    dp, ctx = lax.axis_index("dp"), lax.axis_index("ctx")
    x = tokens.reshape(rows, width)

    small = jnp.concatenate([norms.reshape(-1), b_qkv]).astype(F32)
    small = jnp.pad(small, (0, -small.shape[0] % 1024)).reshape(-1, 128)
    f = forward(
        nd, nc, x, cotangent.reshape(rows, width), small, w_qkv, w_gate, w_up, w_out, w_down
    )

    result, tokens_grad, g_gate, g_up, g_qkv, g_down, g_out, sums = backward(
        nd, nc, f, x, w_out
    )[:8]
    part_down, part_out = w_down.shape[0] // nc, w_out.shape[0] // nc

    place = dp * nc + ctx
    norms_grad = lax.dynamic_index_in_dim(sums[:4].reshape(4, nd * nc, -1), place, 1, keepdims=False)
    bias = sums[4:, : 3 * width // nd].reshape(nd, 3, -1).transpose(1, 0, 2)

    return (
        result.reshape(tokens.shape),
        tokens_grad.reshape(tokens.shape),
        g_qkv.astype(F32),
        take(bias.reshape(nd * nc, -1), place),
        g_out[:part_out].astype(F32),
        g_gate.astype(F32),
        g_up.astype(F32),
        g_down[:part_down].astype(F32),
        norms_grad,
    )


def solution(mesh):
    blocks = P("dp", "ctx", None, None, None)
    owned = P(("dp", "ctx"), None)
    return jax.shard_map(
        shards,
        mesh=mesh,
        in_specs=(
            blocks,
            blocks,
            P("dp", None),
            P("dp"),
            P("dp", None),
            P("dp", None),
            P("dp", None),
            P("dp", None),
            P(None, "dp"),
        ),
        out_specs=(
            blocks,
            blocks,
            owned,
            P(("dp", "ctx")),
            owned,
            owned,
            owned,
            owned,
            P(None, ("dp", "ctx")),
        ),
        check_vma=False,
    )
```

```python
import jax
import jax.numpy as jnp
import numpy as np
from jax import lax
from jax.experimental import pallas as pl
from jax.experimental.pallas import tpu as pltpu
from jax.sharding import PartitionSpec as P

HEADS = 32
HDIM = 64
ROT = 16
MESH = pl.DeviceIdType.MESH
F32 = jnp.float32
BF16 = jnp.bfloat16
VMEM_BYTES = 63 * 1024 * 1024


def normalize_rows(field):
    centre = field - jnp.mean(field, axis=-1, keepdims=True)
    inverse = lax.rsqrt(jnp.mean(centre * centre, axis=-1, keepdims=True) + 1e-05)
    return (centre * inverse, inverse)


def norm_reverse(incoming, gain, scaled, inverse):
    inner = incoming * gain
    return inverse * (
        inner
        - jnp.mean(inner, axis=-1, keepdims=True)
        - scaled * jnp.mean(inner * scaled, axis=-1, keepdims=True)
    )


def last_dims(a, b):
    return lax.dot_general(a, b, (((1,), (1,)), ((), ())), preferred_element_type=F32)


def first_dims(a, b):
    return lax.dot_general(a, b, (((0,), (0,)), ((), ())), preferred_element_type=F32)


def plain(a, b):
    return lax.dot_general(a, b, (((1,), (0,)), ((), ())), preferred_element_type=F32)


def attention_shapes(length):
    block = min(256 if length <= 1024 else 128, length)
    segments = min(4, length // block)
    return block, segments, length // block // segments


def head_columns(heads, what, head):
    at = (what * heads + head) * HDIM
    return slice(at, at + HDIM)


def causal(scores, first_query):
    keys = lax.broadcasted_iota(jnp.int32, scores.shape, 0)
    queries = lax.broadcasted_iota(jnp.int32, scores.shape, 1) + first_query
    return jnp.where(keys <= queries, scores, -1e30)


def flip_one(i):
    return i + 1 - 2 * (i % 2)


def flip_bit(i, bit):
    return i + (1 << bit) - (2 << bit) * ((i // (1 << bit)) % 2)


def flip_bits(i, mask):
    for bit in range(mask.bit_length()):
        if mask >> bit & 1:
            i = flip_bit(i, bit)
    return i


def first_cut(hidden):
    return min(1024, hidden)


def step_orders(nc):
    usual = list(range(nc.bit_length() - 1))
    return usual, [1, 0] + usual[2:]


def spread(mask, order):
    return sum((mask >> i & 1) << bit for i, bit in enumerate(order))


def halves(start, size):
    return pl.ds(pl.multiple_of(start, 64), size)


def lanes(start, size):
    return pl.ds(pl.multiple_of(start, 128), size)


class Copies:
    def __init__(self, send, recv, local):
        self.send, self.recv, self.local = send, recv, local
        self.remotes, self.locals, self.left = [], [], []

    def to(self, device, src, dst):
        at = len(self.remotes)
        copy = pltpu.make_async_remote_copy(
            src_ref=src,
            dst_ref=dst,
            send_sem=self.send.at[at],
            recv_sem=self.recv.at[at],
            device_id=device,
            device_id_type=MESH,
        )
        copy.start()
        self.remotes.append(copy)
        self.left.append(copy)
        return copy

    def gone(self, *copies):
        for copy in copies:
            copy.wait_send()
            self.left = [other for other in self.left if other is not copy]

    def here(self, src, dst):
        copy = pltpu.make_async_copy(src, dst, self.local.at[len(self.locals)])
        copy.start()
        self.locals.append(copy)
        return copy


def meet(axis_sizes):
    barrier = pltpu.get_barrier_semaphore()
    met = 0
    for axis, size in axis_sizes:
        me = lax.axis_index(axis)
        for k in range(1, size):
            pl.semaphore_signal(
                barrier, inc=1, device_id={axis: lax.rem(me + k, size)}, device_id_type=MESH
            )
            met += 1
    pl.semaphore_wait(barrier, met)


def attend(x_ref, o_ref, lse_ref, heads, head):
    length = x_ref.shape[0]
    block, segments, inner = attention_shapes(length)
    q_at, k_at, v_at = (head_columns(heads, i, head) for i in range(3))
    for segment in range(segments):
        count = (segment + 1) * inner * block
        keys = x_ref[:count, k_at]
        values = x_ref[:count, v_at]

        def step(i, _):
            start = pl.multiple_of((segment * inner + i) * block, block)
            query = x_ref[pl.ds(start, block), q_at] * 0.125
            scores = causal(last_dims(keys, query), start)
            top = jnp.max(scores, axis=0, keepdims=True)
            expo = jnp.exp(scores - top)
            total = jnp.sum(expo, axis=0, keepdims=True)
            mixed = first_dims(values, expo.astype(BF16)) / total
            o_ref[pl.ds(start, block), head * HDIM : (head + 1) * HDIM] = mixed.T.astype(BF16)
            lse_ref[head : head + 1, pl.ds(start, block)] = top + jnp.log(total)
            return 0

        if inner == 1:
            step(0, 0)
        else:
            lax.fori_loop(0, inner, step, 0)


def rotate_pair(u, keep, sine):
    lane = lax.broadcasted_iota(jnp.int32, u.shape, 1) % HDIM
    other = jnp.where(lane < ROT // 2, pltpu.roll(u, 128 - ROT // 2, 1), pltpu.roll(u, ROT // 2, 1))
    return u * keep + other * sine


def rotary_pair_tables(length):
    pairs = ROT // 2
    inverse = np.power(np.float32(10000.0), -np.arange(pairs, dtype=np.float32) / np.float32(pairs))
    angle = np.arange(length, dtype=np.float32)[:, None] * inverse.astype(np.float32)[None, :]
    cosine, sine = np.cos(angle), np.sin(angle)
    keep = np.concatenate([cosine, cosine, np.ones((length, HDIM - ROT), np.float32)], axis=1)
    signed = np.concatenate([-sine, sine, np.zeros((length, HDIM - ROT), np.float32)], axis=1)
    return np.tile(keep, (1, 2)).astype(np.float32), np.tile(signed, (1, 2)).astype(np.float32)


def tiles(total, size):
    return [(at, min(size, total - at)) for at in range(0, total, size)]


def over_tiles(total, size, step):
    whole = total // size
    if whole:

        def run(i, _):
            step(pl.multiple_of(i * size, size), size)
            return 0

        lax.fori_loop(0, whole, run, 0)
    if total % size:
        step(whole * size, total % size)


def turn_block(block, left, source, nd, nc):
    rows, width = block.shape
    part = width // (nd * nc)
    here = lanes(source * rows, rows)
    for at in range(0, width, 128):
        turned = block[:, at : at + 128].T
        for i in range(0, 128, part):
            d, c = (at + i) // (part * nc), (at + i) // part % nc
            left[c, d * part : (d + 1) * part, here] = turned[i : i + part]


def forward(nd, nc, tokens, cotangent, small, w_qkv, w_gate, w_up, w_out, w_down):
    rows, width = tokens.shape
    half = rows // 2
    many = nd * rows
    length = 2 * nc * half
    depth = w_qkv.shape[0]
    quarter = depth // 4
    heads_here = HEADS // nd
    groups = nc // nd
    heads = heads_here // groups
    span = heads * HDIM
    cols = heads_here * HDIM
    hidden = w_gate.shape[1] // nd
    down = w_down.shape[0]
    share_down = down // nc
    padded = share_down + -share_down % 16
    keep, sine = rotary_pair_tables(length)

    def body(
        tok_i, cot_i, small_i, wq_i, wg_i, wu_i, wo_i, wd_i, keep_i, sine_i,
        h1_o, dy_o, wq_o, seq_o, lse_o, mixed_o, r1_o, h2_o, m_o, dgu_o, pout_o, pdh2_o, small_o,
        dyp_o, mp_o, h2p_o, gatep_o,
        tok, dy, sm, wq, h1, qkv, seq, lse, o, mixed, wo, part, ra, rb, r1, h2, wgu, wd, m, dgu,
        turns, left1, left2, m_t, mixed_t, dyp, h2p, send, recv, local,
    ):
        dp, ctx = lax.axis_index("dp"), lax.axis_index("ctx")
        near, across, far = flip_one(dp), (dp + 2) % nd, nd - 1 - dp
        spot = ctx % 4
        sides = [{"ctx": flip_bit(ctx, bit)} for bit in range(2)]
        links = Copies(send, recv, local)
        blocks = lambda ref, b: ref.at[halves(b * rows, rows)]

        get_tok = links.here(tok_i, blocks(tok, dp))
        get_turns = [
            links.here(table.at[halves(block * half, half)], turns.at[t, pl.ds(i * half, half)])
            for t, table in enumerate((keep_i, sine_i))
            for i, block in enumerate((ctx, 2 * nc - 1 - ctx))
        ]
        get_small = links.here(small_i, sm.at[dp])
        get_wq = [
            links.here(
                wq_i.at[:, lanes(j * width + dp * cols, cols)],
                wq.at[halves(dp * depth, depth), pl.ds(j * cols, cols)],
            )
            for j in range(3)
        ]
        meet((("dp", nd), ("ctx", nc)))

        def columns(w_i, w, e, at, n, to, which):
            first, size = (0, depth) if which is None else (which * quarter, quarter)
            return links.to(
                {"dp": e},
                w_i.at[halves(first, size), lanes(at, n)],
                w.at[halves(dp * depth + first, size), pl.ds(to, n)],
            )

        def share(w, copies, source):
            for copy in copies:
                copy.wait_recv()
            block = w.at[halves(source * depth + spot * quarter, quarter)]
            return [links.to(side, block, block) for side in sides]

        def cross(w, shared, source):
            passed = []
            for bit in range(2):
                shared[bit].wait_recv()
                start = source * depth + flip_bit(spot, bit) * quarter + bit * (quarter // 2)
                block = w.at[halves(start, quarter // 2)]
                passed.append(links.to(sides[1 - bit], block, block))
            return passed

        def qkv_columns(e, which):
            return [
                columns(wq_i, wq, e, j * width + e * cols, cols, j * cols, which) for j in range(3)
            ]

        def hidden_columns(e, which):
            return [
                columns(w_i, wgu, e, e * hidden, hidden, i * hidden, which)
                for i, w_i in enumerate((wg_i, wu_i))
            ]

        send_small = [links.to({"dp": e}, small_i, sm.at[dp]) for e in (near, across, far)]
        wq_x = [qkv_columns(e, spot) for e in (across, far)]
        send_tok = [links.to({"dp": e}, tok_i, blocks(tok, dp)) for e in (near, across)]
        wq_near = qkv_columns(near, None)
        send_dyp = [links.to(sides[1], cot_i, blocks(dyp, dp))]
        wgu_x = [hidden_columns(e, spot) for e in (far, across)]
        get_wo = links.here(wo_i, wo)
        get_wd = links.here(wd_i, wd)
        get_dy = links.here(cot_i, blocks(dy, dp))
        get_wgu = [
            links.here(
                w_i.at[:, lanes(dp * hidden, hidden)],
                wgu.at[halves(dp * depth, depth), pl.ds(i * hidden, hidden)],
            )
            for i, w_i in enumerate((wg_i, wu_i))
        ]

        get_small.wait()
        for copy in send_small:
            copy.wait_recv()

        def gain(row):
            lines = [
                sm[b, row * 4 + q : row * 4 + q + 1, :]
                for b in range(nd)
                for q in range(width // nd // 128)
            ]
            return jnp.concatenate(lines, axis=1)

        def first_norm(b):
            at = halves(b * rows, rows)
            hat, _ = normalize_rows(tok[at, :].astype(F32))
            h1[at, :] = (hat * gain(0) + gain(1)).astype(BF16)

        def turn_first(b):
            turn_block(h1[halves(b * rows, rows), :], left1, b, nd, nc)

        get_tok.wait()
        wq_s = [share(wq, copies, e) for copies, e in zip(wq_x, (across, far))]
        first_norm(dp)
        send_tok[0].wait_recv()
        first_norm(near)
        wq_c = cross(wq, wq_s[0], across)
        send_tok[1].wait_recv()
        forward_tok = links.to({"dp": near}, blocks(tok, across), blocks(tok, across))
        wq_c += cross(wq, wq_s[1], far)
        first_norm(across)
        forward_tok.wait_recv()
        first_norm(far)
        wgu_d = [c for e in (across, far) for c in hidden_columns(e, 3 - spot)]
        wgu_near = hidden_columns(near, None)
        send_dy = [links.to({"dp": e}, cot_i, blocks(dy, dp)) for e in (near, across)]
        put_small = links.here(sm, small_o)
        for copy in get_wq + get_turns:
            copy.wait()
        for copy in wq_near + wq_c:
            copy.wait_recv()
        put_wq = links.here(wq, wq_o)

        for at, n in tiles(3 * cols, 256):
            j = at // cols
            acc = plain(h1[...], wq[:, at : at + n])
            for q in range(n // 128):
                first = at % cols + q * 128
                line = (j * width + dp * cols + first) // 128
                per = 3 * width // nd // 128
                bias = sm[line // per, pl.ds(4 * (width // nd) // 128 + line % per, 1), :]
                for s in range(nd):
                    u = acc[s * rows : (s + 1) * rows, q * 128 : (q + 1) * 128] + bias
                    if j < 2:
                        u = rotate_pair(u, turns[0], turns[1])
                    u = u.astype(BF16)
                    if heads > 1:
                        g, off = first // span, first % span
                        qkv[g, s * rows : (s + 1) * rows, j * span + off : j * span + off + 128] = u
                    else:
                        for i in range(2):
                            qkv[
                                first // HDIM + i, s * rows : (s + 1) * rows, j * HDIM : (j + 1) * HDIM
                            ] = u[:, i * HDIM : (i + 1) * HDIM]

        mirror = 2 * nc - 1 - ctx
        go = []
        for k in range(1, nc):
            peer = lax.rem(ctx + k, nc)
            s, g = peer // groups, peer % groups
            for i, block in enumerate((ctx, mirror)):
                go.append(
                    links.to(
                        {"ctx": peer},
                        qkv.at[g, halves(s * rows + i * half, half)],
                        seq.at[halves(block * half, half)],
                    )
                )
        s, g = ctx // groups, ctx % groups
        stay = [
            links.here(
                qkv.at[g, halves(s * rows + i * half, half)], seq.at[halves(block * half, half)]
            )
            for i, block in enumerate((ctx, mirror))
        ]
        for b in range(nd):
            turn_first(b)
        put_h1 = links.here(left1, h1_o)
        for copy in stay:
            copy.wait()
        for copy in go:
            copy.wait_recv()
        put_seq = links.here(seq, seq_o)
        back, stay = [], []
        step = min(heads, 2)
        for head in range(heads):
            attend(seq, o, lse, heads, head)
            if (head + 1) % step:
                continue
            here = pl.ds((head + 1 - step) * HDIM, step * HDIM)
            for k in range(nc):
                peer = lax.rem(ctx + k, nc)
                for i, block in enumerate((peer, 2 * nc - 1 - peer)):
                    src = o.at[halves(block * half, half), here]
                    dst = mixed.at[g, halves(s * rows + i * half, half), here]
                    if k:
                        back.append(links.to({"ctx": peer}, src, dst))
                    else:
                        stay.append(links.here(src, dst))
        wgu_far = share(wgu, wgu_x[0], far)
        wgu_near2 = share(wgu, wgu_x[1], across)
        put_lse = links.here(lse, lse_o)
        get_wo.wait()
        for copy in stay:
            copy.wait()
        for copy in back:
            copy.wait_recv()

        def out_tile(at, n):
            acc = plain(mixed[0], wo[0:span, pl.ds(at, n)])
            for i in range(1, groups):
                acc += plain(mixed[i], wo[i * span : (i + 1) * span, pl.ds(at, n)])
            part[:, pl.ds(at, n)] = acc.astype(BF16)

        over_tiles(width, 512, out_tile)

        to_near = [
            links.to({"dp": near}, blocks(part, far), blocks(ra, 0)),
            links.to({"dp": near}, blocks(part, near), blocks(ra, 1)),
        ]
        for i in range(groups):
            mixed_t[i * span : (i + 1) * span, :] = mixed[i].T
        put_mixed = links.here(mixed_t, mixed_o)
        to_near[0].wait_recv()
        across_at = halves(across * rows, rows)
        part[across_at, :] = (part[across_at, :].astype(F32) + ra[:rows, :].astype(F32)).astype(BF16)
        to_across = links.to({"dp": across}, blocks(part, across), rb)
        send_dy[1].wait_recv()
        forward_dy = links.to({"dp": near}, blocks(dy, across), blocks(dy, across))
        send_dyp.append(links.to(sides[1], blocks(dy, across), blocks(dyp, across)))
        to_near[1].wait_recv()
        own_at = halves(dp * rows, rows)
        r1[...] = tok[own_at, :].astype(F32) + (
            part[own_at, :].astype(F32) + ra[rows:, :].astype(F32)
        )
        to_across.wait_recv()
        r1[...] += rb[...].astype(F32)
        put_r1 = links.here(r1, r1_o)
        hat, _ = normalize_rows(r1[...])
        h2[own_at, :] = (hat * gain(2) + gain(3)).astype(BF16)
        send_h2 = [links.to({"dp": e}, blocks(h2, dp), blocks(h2, dp)) for e in (near, across)]
        turn_block(h2[own_at, :], left2, dp, nd, nc)
        send_h2[0].wait_recv()
        turn_block(h2[halves(near * rows, rows), :], left2, near, nd, nc)
        send_h2[1].wait_recv()
        forward_h2 = links.to({"dp": near}, blocks(h2, across), blocks(h2, across))
        turn_block(h2[halves(across * rows, rows), :], left2, across, nd, nc)
        get_wd.wait()
        get_dy.wait()
        for copy in get_wgu:
            copy.wait()
        for copy in wgu_near + wgu_far + wgu_near2 + wgu_d + [send_dy[0], forward_dy, forward_h2]:
            copy.wait_recv()
        turn_block(h2[halves(far * rows, rows), :], left2, far, nd, nc)
        put_h2 = links.here(left2, h2_o)
        put_dy = links.here(dy, dy_o)

        n = left2.shape[1] // 2
        at = pl.ds(pl.multiple_of(dp % 2 * n, 16), n)
        send_left = [
            links.to(sides[0], left2.at[flip_bits(flip_bit(ctx, 0), 2 * j), at], h2p.at[j, at])
            for j in range(nc // 2)
        ]
        send_gate = []
        def hidden_tile(at, n):
            here = pl.ds(at, n)
            gate = plain(h2[...], wgu[:, here])
            up = plain(h2[...], wgu[:, pl.ds(hidden + at, n)])
            dm = last_dims(dy[...], wd[here, :])
            sig = jax.nn.sigmoid(gate)
            m[:, here] = (gate * sig * up).astype(BF16)
            dgu[:, here] = (dm * up * sig * (1.0 + gate * (1.0 - sig))).astype(BF16)
            dgu[:, pl.ds(hidden + at, n)] = (dm * gate * sig).astype(BF16)

        if padded != share_down:
            m[:, hidden:] = jnp.zeros((many, padded - share_down), BF16)
        for at, n in tiles(hidden, 512):
            over_tiles(n, 256, lambda i, size, at=at: hidden_tile(at + i, size))
            here = pl.ds(at, n)
            if at + n <= first_cut(hidden):
                send_gate.append(links.to(sides[0], dgu.at[:, here], gatep_o.at[:, here]))
        for c in range(nc):
            m_t[c] = m[:, c * share_down : c * share_down + padded].T
        put_m = links.here(m_t, m_o)

        send_m, forward_dyp = [], []
        for j in range(nc // 2):
            owner = flip_bits(flip_bit(ctx, 1), spread(2 * j, step_orders(nc)[1]))
            send_m.append(links.to(sides[1], m_t.at[owner], mp_o.at[j]))
        for copy, b in zip(send_dyp, (dp, across)):
            copy.wait_recv()
            forward_dyp.append(links.to({"dp": near}, blocks(dyp, b), blocks(dyp, b)))
        for copy in send_left:
            copy.wait_recv()
        n = left2.shape[1] // 2
        at = pl.ds(pl.multiple_of(dp % 2 * n, 16), n)
        forward_left = links.to({"dp": near}, h2p.at[:, at], h2p.at[:, at])
        put_dgu = links.here(dgu, dgu_o)

        def dh2_tile(at, n):
            here = pl.ds(at, n)
            h1[:, here] = last_dims(dgu[...], wgu[here, :]).astype(BF16)

        over_tiles(width, 256, dh2_tile)
        put_pdh2 = links.here(h1, pdh2_o)
        links.gone(*send_tok, forward_tok)

        def result_tile(at, n):
            here = pl.ds(at, n)
            tok[:, here] = plain(m[:, :hidden], wd[:, here]).astype(BF16)

        over_tiles(width, 256, result_tile)
        put_pout = links.here(tok, pout_o)
        for copy in forward_dyp + [forward_left]:
            copy.wait_recv()
        put_other = [links.here(dyp, dyp_o), links.here(h2p, h2p_o)]
        for copy in send_m + send_gate:
            copy.wait_recv()

        links.gone(*links.left)
        for copy in (
            *put_other, put_small, put_h1, put_wq, put_seq, put_lse, put_mixed, put_r1, put_h2, put_dy, put_m, put_dgu,
            put_pdh2, put_pout,
        ):
            copy.wait()

    anywhere = pl.BlockSpec(memory_space=pl.ANY)
    shape = jax.ShapeDtypeStruct
    remotes = 64 + 7 * nc
    outs = dict(
        h1=((nc, width // nc, many), BF16),
        dy=((many, width), BF16),
        wq=((width, 3 * cols), BF16),
        seq=((length, 3 * span), BF16),
        lse=((heads, length), F32),
        mixed=((cols, many), BF16),
        r1=((rows, width), F32),
        h2=((nc, width // nc, many), BF16),
        m=((nc, padded, many), BF16),
        dgu=((many, 2 * hidden), BF16),
        pout=((many, width), BF16),
        pdh2=((many, width), BF16),
        small=((nd,) + small.shape, F32),
        dyp=((many, width), BF16),
        mp=((nc // 2, padded, many), BF16),
        h2p=((nc // 2, width // nc, many), BF16),
        gatep=((many, first_cut(hidden)), BF16),
    )
    scratch = [
        ((many, width), BF16),
        ((many, width), BF16),
        ((nd,) + small.shape, F32),
        ((width, 3 * cols), BF16),
        ((many, width), BF16),
        ((groups, many, 3 * span), BF16),
        ((length, 3 * span), BF16),
        ((heads, length), F32),
        ((length, span), BF16),
        ((groups, many, span), BF16),
        ((cols, width), BF16),
        ((many, width), BF16),
        ((2 * rows, width), BF16),
        ((rows, width), BF16),
        ((rows, width), F32),
        ((many, width), BF16),
        ((width, 2 * hidden), BF16),
        ((down, width), BF16),
        ((many, hidden + padded - share_down), BF16),
        ((many, 2 * hidden), BF16),
        ((2, rows, 128), F32),
        ((nc, width // nc, many), BF16),
        ((nc, width // nc, many), BF16),
        ((nc, padded, many), BF16),
        ((cols, many), BF16),
        ((many, width), BF16),
        ((nc // 2, width // nc, many), BF16),
    ]
    results = pl.pallas_call(
        body,
        out_shape=[shape(*o) for o in outs.values()],
        in_specs=[anywhere] * 10,
        out_specs=[anywhere] * len(outs),
        scratch_shapes=[pltpu.VMEM(*s) for s in scratch]
        + [
            pltpu.SemaphoreType.DMA((remotes,)),
            pltpu.SemaphoreType.DMA((remotes,)),
            pltpu.SemaphoreType.DMA((40,)),
        ],
        compiler_params=pltpu.CompilerParams(
            collective_id=0, has_side_effects=True, vmem_limit_bytes=VMEM_BYTES
        ),
    )(tokens, cotangent, small, w_qkv, w_gate, w_up, w_out, w_down, keep, sine)
    return dict(zip(outs, results))


def attend_back(x_ref, lse_ref, do_ref, d_ref, heads, head):
    length = x_ref.shape[0]
    block, segments, inner = attention_shapes(length)
    q_at, k_at, v_at = (head_columns(heads, i, head) for i in range(3))
    o_at = slice(head * HDIM, (head + 1) * HDIM)
    for segment in range(segments):
        count = (segment + 1) * inner * block
        keys = x_ref[:count, k_at]
        values = x_ref[:count, v_at]

        def step(i, _):
            start = pl.multiple_of((segment * inner + i) * block, block)
            query = x_ref[pl.ds(start, block), q_at] * 0.125
            dout = do_ref[pl.ds(start, block), o_at]
            scores = causal(last_dims(keys, query), start)
            probs = jnp.exp(scores - lse_ref[head : head + 1, pl.ds(start, block)])
            d_probs = last_dims(values, dout)
            centre = jnp.sum(probs * d_probs, axis=0, keepdims=True)
            d_scores = (probs * (d_probs - centre)).astype(BF16)
            d_ref[:count, v_at] += plain(probs.astype(BF16), dout)
            d_ref[:count, k_at] += plain(d_scores, query)
            d_ref[pl.ds(start, block), q_at] = first_dims(keys, d_scores).T * 0.125
            return 0

        if inner == 1:
            step(0, 0)
        else:
            lax.fori_loop(0, inner, step, 0)


class GroupSum:
    def __init__(self, links, dp, nd, rows, part, ra, rb):
        self.links, self.rows = links, rows
        self.part, self.ra, self.rb = part, ra, rb
        self.near, self.across, self.far = flip_one(dp), (dp + 2) % nd, nd - 1 - dp
        self.dp = dp
        block = lambda ref, b: ref.at[halves(b * rows, rows)]
        self.a = [
            links.to({"dp": self.near}, block(part, self.far), block(ra, 0)),
            links.to({"dp": self.near}, block(part, self.near), block(ra, 1)),
        ]

    def middle(self):
        rows, at = self.rows, halves(self.across * self.rows, self.rows)
        self.a[0].wait_recv()
        self.part[at, :] = (
            self.part[at, :].astype(F32) + self.ra[:rows, :].astype(F32)
        ).astype(BF16)
        self.b = self.links.to({"dp": self.across}, self.part.at[at], self.rb)

    def total(self):
        rows, at = self.rows, halves(self.dp * self.rows, self.rows)
        self.a[1].wait_recv()
        self.b.wait_recv()
        return (
            self.part[at, :].astype(F32)
            + self.ra[rows:, :].astype(F32)
            + self.rb[...].astype(F32)
        )


class Gradient:
    def __init__(self, links, ctx, bits, left, right, slots, landing, stage):
        self.links, self.ctx, self.bits, self.nc = links, ctx, bits, 1 << len(bits)
        nc = self.nc
        self.left, self.right, self.slots = left, right, slots
        self.landing = landing
        self.stage = stage.at[pl.ds(0, slots.shape[1]), pl.ds(0, slots.shape[2])]
        self.sent = {}
        self.order = sorted(range(nc // 2), key=lambda j: (j & -j) or nc)

    def _landing(self, bit, j):
        base = sum(self.nc >> (b + 1) for b in range(1, bit))
        return self.landing.at[base + (j >> bit)]

    def compute(self, send=True):
        for j in self.order:
            self.slot(j, send)

    def start(self):
        for j in self.order:
            self._pass(1, j)

    def slot(self, j, send=True):
        mine, other = self.left[0][j], self.left[1][j]

        def step(at, n):
            here = pl.ds(at, n)
            acc = plain(mine, self.right[0][:, here]) + plain(other, self.right[1][:, here])
            self.slots[j, :, here] = acc.astype(BF16)

        over_tiles(self.slots.shape[2], 512, step)
        if send:
            self._pass(1, j)

    def _pass(self, bit, j):
        low = j & -j
        if j and low == 1 << (bit - 1):
            self.sent[bit, j] = self.links.to(
                {"ctx": flip_bit(self.ctx, self.bits[bit])},
                self.slots.at[j],
                self._landing(bit, j - low),
            )

    def add(self, bit):
        for j in self.order:
            if j % (1 << bit) == 0:
                self.add_slot(bit, j)

    def add_slot(self, bit, j):
        self.sent[bit, j + (1 << (bit - 1))].wait_recv()
        self.links.here(self._landing(bit, j), self.stage).wait()

        def step(at, n):
            here = pl.ds(at, n)
            acc = self.slots[j, :, here].astype(F32) + self.stage[:, here].astype(F32)
            self.slots[j, :, here] = acc.astype(BF16)

        over_tiles(self.slots.shape[2], 512, step)
        self._pass(bit + 1, j)


def backward(nd, nc, f, tokens, w_out):
    rows, width = tokens.shape
    half = rows // 2
    many = nd * rows
    length, wide = f["seq"].shape
    heads = f["lse"].shape[0]
    span = heads * HDIM
    groups = nc // nd
    cols = groups * span
    hidden = f["dgu"].shape[1] // 2
    slots = nc // 2
    share = width // (nd * nc)
    tall = {"gu": nd * share, "down": f["m"].shape[1], "out": cols // nc, "qkv": nd * share}
    flat = {"gu": 2 * hidden, "down": width, "out": width, "qkv": 3 * cols}
    cut = first_cut(hidden)
    ranges = tiles(2 * hidden, cut)
    names = ("down", "gu", "qkv", "out")
    bits = nc.bit_length() - 1
    keep_t, sine_t = rotary_pair_tables(length)
    chunk = length if length <= 1024 else 256
    strip = 256 if length <= 1024 else 128
    mixed_left = f["mixed"].reshape(nc, cols // nc, many)

    def body(
        h2_l, h2p_l, gatep_i, m_l, mp_l, mixed_l, h1_l, dy_i, dyp_i, dgu_i, wq_i, seq_i, lse_i, r1_i, pdh2_i, pout_i,
        small_i, tok_i, wo_i, keep_i, sine_i,
        out_o, tg_o, gate_o, up_o, qkv_o, down_o, out_g_o, sums_o,
        land_down, land_gu, land_qkv, land_out,
        l_gu, l_down, l_out, l_qkv, dgu, dgup, dy, dyp, da, dq, dqp,
        s_down, s_gu, s_qkv, s_out, stage,
        part, ra, rb, r1, dr1, x, sm, wq, wo, seq, lse,
        dmix, dseq, dx, keep, sine, dback, sums, sums_in,
        send, recv, local, free,
    ):
        dp, ctx = lax.axis_index("dp"), lax.axis_index("ctx")
        near, across, far = flip_one(dp), (dp + 2) % nd, nd - 1 - dp
        core = dp % 2
        links = Copies(send, recv, local)
        blocks = lambda ref, b: ref.at[halves(b * rows, rows)]
        own_at = halves(dp * rows, rows)
        beside = {"ctx": flip_bit(ctx, 0)}

        usual, swapped = step_orders(nc)

        def get_left(left_i, left, order=usual):
            return [
                links.here(left_i.at[flip_bits(ctx, spread(2 * j, order))], left.at[0, j])
                for j in range(slots)
            ]

        get_part = links.here(pdh2_i, part)
        get_gu = get_left(h2_l, l_gu)
        get_gu += [
            links.here(a, b)
            for a, b in ((h2p_l, l_gu.at[1]), (dgu_i, dgu), (gatep_i, dgup.at[:, pl.ds(0, cut)]))
        ]
        get_down = get_left(m_l, l_down, swapped)
        get_down += [
            links.here(a, b) for a, b in ((mp_l, l_down.at[1]), (dy_i, dy), (dyp_i, dyp))
        ]
        get_first = [links.here(a, b) for a, b in ((r1_i, r1), (small_i, sm))]
        get_wo = links.here(wo_i, wo)
        get_attn = [links.here(a, b) for a, b in ((seq_i, seq), (lse_i, lse))]
        get_late = get_left(h1_l, l_qkv) + get_left(mixed_l, l_out) + [links.here(tok_i, x)]

        def tables(c):
            at = pl.ds(c * chunk, chunk)
            return [links.here(a.at[at], b) for a, b in ((keep_i, keep), (sine_i, sine))]

        get_tables = tables(0)

        def strips(i):
            return links.here(wq_i.at[pl.ds(i * strip, strip)], wq.at[i % 2])

        get_wq = [strips(0), strips(1)]

        def gain(row):
            lines = [
                sm[b, row * 4 + q : row * 4 + q + 1, :]
                for b in range(nd)
                for q in range(width // nd // 128)
            ]
            return jnp.concatenate(lines, axis=1)

        def both_lefts(left_i, left):
            n = tall["gu"] // 2
            at = pl.ds(pl.multiple_of(core * n, 16), n)
            return [
                links.to(
                    beside,
                    left_i.at[flip_bits(flip_bit(ctx, 0), 2 * j), at],
                    left.at[1, j, at],
                )
                for j in range(slots)
            ]

        def share_lefts(copies, left):
            n = tall["gu"] // 2
            at = pl.ds(pl.multiple_of(core * n, 16), n)
            for copy in copies:
                copy.wait_recv()
            block = left.at[1, :, at]
            return [links.to({"dp": near}, block, block)]

        down = Gradient(links, ctx, swapped, l_down, (dy, dyp), s_down, land_down, stage)
        gu = []
        for at, n in ranges:
            here = pl.ds(at, n)
            gu.append(
                Gradient(
                    links, ctx, usual, l_gu, (dgu.at[:, here], dgup.at[:, here]),
                    s_gu.at[:, :, here], land_gu.at[:, :, here], stage,
                )
            )
        qkv = []
        for j in range(3):
            at = pl.ds(j * cols, cols)
            qkv.append(
                Gradient(
                    links, ctx, usual, l_qkv, (dq.at[:, at], dqp.at[:, at]),
                    s_qkv.at[:, :, at], land_qkv.at[:, :, at], stage,
                )
            )
        out = Gradient(links, ctx, usual, l_out, (da, dyp), s_out, land_out, stage)

        meet((("dp", nd), ("ctx", nc)))
        get_part.wait()
        sum2 = GroupSum(links, dp, nd, rows, part, ra, rb)

        def send_right(i):
            here = pl.ds(*ranges[i])
            return links.to(beside, dgu_i.at[:, here], dgup.at[:, here])

        right_gu = [None, send_right(1)]
        for copy in get_gu:
            copy.wait()
        gu[0].slot(gu[0].order[0])
        sum2.middle()
        for j in gu[0].order[1:]:
            gu[0].slot(j)
        for copy in get_first + get_down:
            copy.wait()

        dh2 = sum2.total()
        hat, inverse = normalize_rows(r1[...])
        dr1[...] = dy[own_at, :].astype(F32) + norm_reverse(dh2, gain(2), hat, inverse)
        da[own_at, :] = dr1[...].astype(BF16)
        send_da = [links.to({"dp": e}, blocks(da, dp), blocks(da, dp)) for e in (near, across)]
        sums[2:3, :] = jnp.sum(dh2 * hat, axis=0, keepdims=True)
        sums[3:4, :] = jnp.sum(dh2, axis=0, keepdims=True)
        dx[...] = jnp.zeros_like(dx)
        send_da[1].wait_recv()
        forward_da = links.to({"dp": near}, blocks(da, across), blocks(da, across))
        get_wo.wait()
        send_da[0].wait_recv()
        forward_da.wait_recv()

        for g in range(groups):
            dmix[g] = last_dims(da[...], wo[g * span : (g + 1) * span, :]).astype(BF16)
        mirror = 2 * nc - 1 - ctx
        go = []
        for k in range(1, nc):
            peer = lax.rem(ctx + k, nc)
            s, g = peer // groups, peer % groups
            for i, block in enumerate((ctx, mirror)):
                go.append(
                    links.to(
                        {"ctx": peer},
                        dmix.at[g, halves(s * rows + i * half, half)],
                        dseq.at[halves(block * half, half)],
                    )
                )
        s, g = ctx // groups, ctx % groups
        stay = [
            links.here(
                dmix.at[g, halves(s * rows + i * half, half)], dseq.at[halves(block * half, half)]
            )
            for i, block in enumerate((ctx, mirror))
        ]
        right_gu += [send_right(i) for i in range(2, len(ranges))]
        left_qkv = both_lefts(h1_l, l_qkv)
        right_gu[1].wait_recv()
        gu[1].compute()
        if bits > 1:
            gu[0].add(1)
        for copy in get_attn + stay:
            copy.wait()
        for copy in go:
            copy.wait_recv()
        for head in range(heads):
            attend_back(seq, lse, dseq, dx, heads, head)
        for c in range(length // chunk):
            for copy in get_tables if c == 0 else tables(c):
                copy.wait()
            here = slice(c * chunk, (c + 1) * chunk)
            for at in range(0, wide, 128):
                n = min(128, wide - at)
                u = dx[here, at : at + n]
                if at < 2 * span:
                    u = rotate_pair(u, keep[...], -sine[...])
                seq[here, at : at + n] = u.astype(BF16)

        back = []
        for k in range(1, nc):
            peer = lax.rem(ctx + k, nc)
            for i, block in enumerate((peer, 2 * nc - 1 - peer)):
                back.append(
                    links.to(
                        {"ctx": peer},
                        seq.at[halves(block * half, half)],
                        dback.at[g, halves(s * rows + i * half, half)],
                    )
                )
        stay = [
            links.here(
                seq.at[halves(block * half, half)], dback.at[g, halves(s * rows + i * half, half)]
            )
            for i, block in enumerate((ctx, mirror))
        ]
        for copy in get_late:
            copy.wait()
        down.compute()
        for i, device in enumerate((beside, {"dp": near})):
            pl.semaphore_signal(free.at[i], inc=1, device_id=device, device_id_type=MESH)
        for i in range(2, len(ranges)):
            right_gu[i].wait_recv()
            gu[i].compute()
        for copy in stay:
            copy.wait()
        for copy in back:
            copy.wait_recv()
        for g_ in range(groups):
            for j in range(3):
                at = j * cols + g_ * span
                dq[:, at : at + span] = dback[g_, :, j * span : (j + 1) * span]
        right_qkv = [
            links.to(beside, dq.at[:, pl.ds(j * cols, cols)], dqp.at[:, pl.ds(j * cols, cols)])
            for j in range(3)
        ]

        n = many // 2
        at = halves(core * n, n)
        pl.semaphore_wait(free.at[0], 1)
        right_out = links.to(beside, da.at[at], dyp.at[at])
        left_out = [
            links.to(beside, mixed_l.at[flip_bits(flip_bit(ctx, 0), 2 * j)], l_out.at[1, j])
            for j in range(slots)
        ]

        if bits > 1:
            gu[1].add(1)
        links.gone(*sum2.a, sum2.b)
        for i in range(width // strip):
            get_wq[i].wait()
            part[:, i * strip : (i + 1) * strip] = last_dims(dq[...], wq[i % 2]).astype(BF16)
            if i + 2 < width // strip:
                get_wq.append(strips(i + 2))
        sum1 = GroupSum(links, dp, nd, rows, part, ra, rb)
        left_qkv2 = share_lefts(left_qkv, l_qkv)
        sums[4:, :] = jnp.zeros((nd, width), F32)
        sums[pl.ds(4 + dp, 1), : 3 * cols] = jnp.sum(dq[...].astype(F32), axis=0, keepdims=True)
        sum1.middle()

        def compute_qkv(j):
            right_qkv[j].wait_recv()
            qkv[j].compute()

        left_qkv2[0].wait_recv()
        compute_qkv(0)
        if bits > 1:
            for i in range(2, len(ranges)):
                gu[i].add(1)
            down.add(1)
        compute_qkv(1)
        dh1 = sum1.total()
        hat1, inverse1 = normalize_rows(x[...].astype(F32))
        sums[0:1, :] = jnp.sum(dh1 * hat1, axis=0, keepdims=True)
        sums[1:2, :] = jnp.sum(dh1, axis=0, keepdims=True)
        partners = [("dp", flip_bit(dp, b)) for b in range(nd.bit_length() - 1)]
        partners += [("ctx", flip_bit(ctx, b)) for b in range(bits)]
        sums_out = []

        def start_sums():
            i = len(sums_out)
            if i < len(partners):
                axis, device = partners[i]
                sums_out.append(links.to({axis: device}, sums, sums_in.at[i]))

        def end_sums():
            i = len(sums_out) - 1
            sums_out[i].wait_recv()
            links.gone(sums_out[i])
            sums[...] += sums_in[i]

        start_sums()
        dr1[...] += norm_reverse(dh1, gain(0), hat1, inverse1)
        put_tg = links.here(dr1, tg_o)
        arriving, put = [], []

        def to_owner(slots_ref, spans):
            for e in (near, across, far, dp):
                for dst, at, to, n, every in spans:
                    src = slots_ref.at[0, pl.ds(pl.multiple_of(e * share, 16), share), pl.ds(at, n)]
                    place = dst.at[:, lanes(to + dp * every, n)]
                    if e is dp:
                        put.append(links.here(src, place))
                    else:
                        arriving.append(links.to({"dp": e}, src, place))

        qkv_spans = tuple((qkv_o, j * cols, j * width, cols, cols) for j in range(3))

        def close_gu(i):
            for bit in range(2, bits):
                gu[i].add(bit)
            at, n = ranges[i]
            for dst, base in ((gate_o, 0), (up_o, hidden)):
                first, last = max(at, base), min(at + n, base + hidden)
                if first < last:
                    to_owner(s_gu, ((dst, first, first - base, last - first, hidden),))

        def next_sums():
            end_sums()
            start_sums()

        links.gone(*sum1.a, sum1.b)
        get_pout = links.here(pout_i, part)
        compute_qkv(2)
        next_sums()
        get_pout.wait()
        sum0 = GroupSum(links, dp, nd, rows, part, ra, rb)
        close_gu(0)
        next_sums()
        sum0.middle()
        for bit in range(2, bits):
            down.add(bit)
        put.append(links.here(s_down.at[0], down_o))
        right_out.wait_recv()
        pl.semaphore_wait(free.at[1], 1)
        right_out2 = links.to({"dp": near}, dyp.at[at], dyp.at[at])
        if bits > 1:
            qkv[0].add(1)
        next_sums()
        right_out2.wait_recv()
        for copy in left_out:
            copy.wait_recv()
        out.compute(send=False)
        x[...] = (r1[...] + sum0.total()).astype(BF16)
        put_out = links.here(x, out_o)
        close_gu(1)
        if bits > 1:
            qkv[1].add(1)
        out.start()
        next_sums()
        for i in range(2, len(ranges)):
            close_gu(i)
        if bits > 1:
            qkv[2].add(1)

        def close_qkv(j):
            for bit in range(2, bits):
                qkv[j].add(bit)
            to_owner(s_qkv, (qkv_spans[j],))

        close_qkv(0)
        if bits > 1:
            out.add(1)
        close_qkv(1)
        close_qkv(2)
        while len(sums_out) < len(partners):
            next_sums()
        end_sums()
        for bit in range(2, bits):
            out.add(bit)
        put.append(links.here(s_out.at[0], out_g_o))
        put_sums = [links.here(sums, sums_o), put_tg, put_out]
        for copy in arriving:
            copy.wait_recv()
        links.gone(*links.left)
        for copy in put + put_sums:
            copy.wait()

    anywhere = pl.BlockSpec(memory_space=pl.ANY)
    shape = jax.ShapeDtypeStruct
    outs = [
        ((rows, width), BF16),
        ((rows, width), F32),
        ((share, nd * hidden), BF16),
        ((share, nd * hidden), BF16),
        ((share, 3 * width), BF16),
        ((tall["down"], width), BF16),
        ((tall["out"], width), BF16),
        ((4 + nd, width), F32),
        *[((max(1, slots - 1), tall[k], flat[k]), BF16) for k in names],
    ]
    scratch = [
        *[((2, slots, tall[k], many), BF16) for k in ("gu", "down", "out", "qkv")],
        ((many, 2 * hidden), BF16),
        ((many, 2 * hidden), BF16),
        ((many, width), BF16),
        ((many, width), BF16),
        ((many, width), BF16),
        ((many, 3 * cols), BF16),
        ((many, 3 * cols), BF16),
        *[((slots, tall[k], flat[k]), BF16) for k in names],
        ((max(tall.values()), width), BF16),
        ((many, width), BF16),
        ((2 * rows, width), BF16),
        ((rows, width), BF16),
        ((rows, width), F32),
        ((rows, width), F32),
        ((rows, width), BF16),
        (f["small"].shape, F32),
        ((2, strip, 3 * cols), BF16),
        ((cols, width), BF16),
        ((length, wide), BF16),
        ((heads, length), F32),
        ((groups, many, span), BF16),
        ((length, span), BF16),
        ((length, wide), F32),
        ((chunk, 128), F32),
        ((chunk, 128), F32),
        ((groups, many, wide), BF16),
        ((4 + nd, width), F32),
        ((bits + nd.bit_length() - 1, 4 + nd, width), F32),
    ]
    remotes = 64 + 4 * nc + 7 * nc
    return pl.pallas_call(
        body,
        out_shape=[shape(*o) for o in outs],
        in_specs=[anywhere] * 21,
        out_specs=[anywhere] * len(outs),
        scratch_shapes=[pltpu.VMEM(*s) for s in scratch]
        + [
            pltpu.SemaphoreType.DMA((remotes,)),
            pltpu.SemaphoreType.DMA((remotes,)),
            pltpu.SemaphoreType.DMA((64 + 7 * nc,)),
            pltpu.SemaphoreType.REGULAR((2,)),
        ],
        compiler_params=pltpu.CompilerParams(
            collective_id=1, has_side_effects=True, vmem_limit_bytes=VMEM_BYTES
        ),
    )(
        f["h2"], f["h2p"], f["gatep"], f["m"], f["mp"], mixed_left, f["h1"],
        f["dy"], f["dyp"], f["dgu"], f["wq"], f["seq"], f["lse"], f["r1"], f["pdh2"], f["pout"],
        f["small"], tokens, w_out, keep_t, sine_t,
    )


def widen(arrays):
    def body(*refs):
        n = len(arrays)
        ins, outs, held, wide = (refs[i * n : (i + 1) * n] for i in range(4))
        load, store = refs[4 * n :]
        loads = [pltpu.make_async_copy(ins[i], held[i], load.at[i]) for i in range(n)]
        for copy in loads:
            copy.start()
        stores = []
        for i in range(n):
            loads[i].wait()
            wide[i][...] = held[i][: wide[i].shape[0], :].astype(wide[i].dtype)
            stores.append(pltpu.make_async_copy(wide[i], outs[i], store.at[i]))
            stores[-1].start()
        for copy in stores:
            copy.wait()

    anywhere = pl.BlockSpec(memory_space=pl.ANY)
    n = len(arrays)
    shapes = [(rows, x.shape[1]) for x, rows, _ in arrays]
    return pl.pallas_call(
        body,
        out_shape=[jax.ShapeDtypeStruct(k, kind) for k, (_, _, kind) in zip(shapes, arrays)],
        in_specs=[anywhere] * n,
        out_specs=[anywhere] * n,
        scratch_shapes=[pltpu.VMEM(x.shape, x.dtype) for x, _, _ in arrays]
        + [pltpu.VMEM(k, kind) for k, (_, _, kind) in zip(shapes, arrays)]
        + [pltpu.SemaphoreType.DMA((n,)), pltpu.SemaphoreType.DMA((n,))],
        compiler_params=pltpu.CompilerParams(vmem_limit_bytes=VMEM_BYTES),
    )(*[x for x, _, _ in arrays])


def take(x, index):
    return lax.dynamic_index_in_dim(x, index, 0, keepdims=False)


def shards(tokens, cotangent, w_qkv, b_qkv, w_out, w_gate, w_up, w_down, norms):
    width = tokens.shape[-1]
    rows = 2 * tokens.shape[3]
    nd, nc = lax.axis_size("dp"), lax.axis_size("ctx")
    dp, ctx = lax.axis_index("dp"), lax.axis_index("ctx")
    x = tokens.reshape(rows, width)

    small = jnp.concatenate([norms.reshape(-1), b_qkv]).astype(F32)
    small = jnp.pad(small, (0, -small.shape[0] % 1024)).reshape(-1, 128)
    f = forward(
        nd, nc, x, cotangent.reshape(rows, width), small, w_qkv, w_gate, w_up, w_out, w_down
    )

    result, tokens_grad, g_gate, g_up, g_qkv, g_down, g_out, sums = backward(
        nd, nc, f, x, w_out
    )[:8]
    place = dp * nc + ctx
    norms_grad = lax.dynamic_index_in_dim(sums[:4].reshape(4, nd * nc, -1), place, 1, keepdims=False)
    bias = sums[4:, : 3 * width // nd].reshape(nd, 3, -1).transpose(1, 0, 2)

    result, tokens_grad, *grads = widen(
        [
            (result, rows, BF16),
            (tokens_grad, rows, F32),
            *[(g, g.shape[0], F32) for g in (g_qkv, g_gate, g_up)],
            (g_down, w_down.shape[0] // nc, F32),
            (g_out, w_out.shape[0] // nc, F32),
        ]
    )
    grad_qkv, grad_gate, grad_up, grad_down, grad_out = grads
    return (
        result.reshape(tokens.shape),
        tokens_grad.reshape(tokens.shape),
        grad_qkv,
        take(bias.reshape(nd * nc, -1), place),
        grad_out,
        grad_gate,
        grad_up,
        grad_down,
        norms_grad,
    )


def solution(mesh):
    blocks = P("dp", "ctx", None, None, None)
    owned = P(("dp", "ctx"), None)
    return jax.shard_map(
        shards,
        mesh=mesh,
        in_specs=(
            blocks,
            blocks,
            P("dp", None),
            P("dp"),
            P("dp", None),
            P("dp", None),
            P("dp", None),
            P("dp", None),
            P(None, "dp"),
        ),
        out_specs=(
            blocks,
            blocks,
            owned,
            P(("dp", "ctx")),
            owned,
            owned,
            owned,
            owned,
            P(None, ("dp", "ctx")),
        ),
        check_vma=False,
    )
```

```python
import jax
import jax.numpy as jnp
import numpy as np
from jax import lax
from jax.experimental import pallas as pl
from jax.experimental.pallas import tpu as pltpu
from jax.sharding import PartitionSpec as P

HEADS = 32
HDIM = 64
ROT = 16
MESH = pl.DeviceIdType.MESH
F32 = jnp.float32
BF16 = jnp.bfloat16
VMEM_BYTES = 63 * 1024 * 1024


def normalize_rows(field):
    centre = field - jnp.mean(field, axis=-1, keepdims=True)
    inverse = lax.rsqrt(jnp.mean(centre * centre, axis=-1, keepdims=True) + 1e-05)
    return (centre * inverse, inverse)


def norm_reverse(incoming, gain, scaled, inverse):
    inner = incoming * gain
    return inverse * (
        inner
        - jnp.mean(inner, axis=-1, keepdims=True)
        - scaled * jnp.mean(inner * scaled, axis=-1, keepdims=True)
    )


def last_dims(a, b):
    return lax.dot_general(a, b, (((1,), (1,)), ((), ())), preferred_element_type=F32)


def first_dims(a, b):
    return lax.dot_general(a, b, (((0,), (0,)), ((), ())), preferred_element_type=F32)


def plain(a, b):
    return lax.dot_general(a, b, (((1,), (0,)), ((), ())), preferred_element_type=F32)


def attention_shapes(length):
    block = min(256 if length <= 1024 else 128, length)
    segments = min(4, length // block)
    return block, segments, length // block // segments


def head_columns(heads, what, head):
    at = (what * heads + head) * HDIM
    return slice(at, at + HDIM)


def causal(scores, first_query):
    keys = lax.broadcasted_iota(jnp.int32, scores.shape, 0)
    queries = lax.broadcasted_iota(jnp.int32, scores.shape, 1) + first_query
    return jnp.where(keys <= queries, scores, -1e30)


def flip_one(i):
    return i + 1 - 2 * (i % 2)


def flip_bit(i, bit):
    return i + (1 << bit) - (2 << bit) * ((i // (1 << bit)) % 2)


def flip_bits(i, mask):
    for bit in range(mask.bit_length()):
        if mask >> bit & 1:
            i = flip_bit(i, bit)
    return i


def quarter_of(left, device, parts=4):
    n = left.shape[-2] // parts
    return pl.ds(pl.multiple_of(device * n, 16), n)


def first_cut(hidden):
    return min(1024, hidden)


def swapped_cut(hidden):
    return min(512, hidden)


def step_orders(nc):
    usual = list(range(nc.bit_length() - 1))
    return usual, [1, 0] + usual[2:]


def spread(mask, order):
    return sum((mask >> i & 1) << bit for i, bit in enumerate(order))


def halves(start, size):
    return pl.ds(pl.multiple_of(start, 64), size)


def lanes(start, size):
    return pl.ds(pl.multiple_of(start, 128), size)


class Copies:
    def __init__(self, send, recv, local):
        self.send, self.recv, self.local = send, recv, local
        self.remotes, self.locals, self.left = [], [], []

    def to(self, device, src, dst):
        at = len(self.remotes)
        copy = pltpu.make_async_remote_copy(
            src_ref=src,
            dst_ref=dst,
            send_sem=self.send.at[at],
            recv_sem=self.recv.at[at],
            device_id=device,
            device_id_type=MESH,
        )
        copy.start()
        self.remotes.append(copy)
        self.left.append(copy)
        return copy

    def gone(self, *copies):
        for copy in copies:
            copy.wait_send()
            self.left = [other for other in self.left if other is not copy]

    def here(self, src, dst):
        copy = pltpu.make_async_copy(src, dst, self.local.at[len(self.locals)])
        copy.start()
        self.locals.append(copy)
        return copy


def meet(axis_sizes):
    barrier = pltpu.get_barrier_semaphore()
    met = 0
    for axis, size in axis_sizes:
        me = lax.axis_index(axis)
        for k in range(1, size):
            pl.semaphore_signal(
                barrier, inc=1, device_id={axis: lax.rem(me + k, size)}, device_id_type=MESH
            )
            met += 1
    pl.semaphore_wait(barrier, met)


def attend(x_ref, o_ref, lse_ref, heads, head):
    length = x_ref.shape[0]
    block, segments, inner = attention_shapes(length)
    q_at, k_at, v_at = (head_columns(heads, i, head) for i in range(3))
    for segment in range(segments):
        count = (segment + 1) * inner * block
        keys = x_ref[:count, k_at]
        values = x_ref[:count, v_at]

        def step(i, _):
            start = pl.multiple_of((segment * inner + i) * block, block)
            query = x_ref[pl.ds(start, block), q_at] * 0.125
            scores = causal(last_dims(keys, query), start)
            top = jnp.max(scores, axis=0, keepdims=True)
            expo = jnp.exp(scores - top)
            total = jnp.sum(expo, axis=0, keepdims=True)
            mixed = first_dims(values, expo.astype(BF16)) / total
            o_ref[pl.ds(start, block), head * HDIM : (head + 1) * HDIM] = mixed.T.astype(BF16)
            lse_ref[head : head + 1, pl.ds(start, block)] = top + jnp.log(total)
            return 0

        if inner == 1:
            step(0, 0)
        else:
            lax.fori_loop(0, inner, step, 0)


def rotate_pair(u, keep, sine):
    lane = lax.broadcasted_iota(jnp.int32, u.shape, 1) % HDIM
    other = jnp.where(lane < ROT // 2, pltpu.roll(u, 128 - ROT // 2, 1), pltpu.roll(u, ROT // 2, 1))
    return u * keep + other * sine


def rotary_pair_tables(length):
    pairs = ROT // 2
    inverse = np.power(np.float32(10000.0), -np.arange(pairs, dtype=np.float32) / np.float32(pairs))
    angle = np.arange(length, dtype=np.float32)[:, None] * inverse.astype(np.float32)[None, :]
    cosine, sine = np.cos(angle), np.sin(angle)
    keep = np.concatenate([cosine, cosine, np.ones((length, HDIM - ROT), np.float32)], axis=1)
    signed = np.concatenate([-sine, sine, np.zeros((length, HDIM - ROT), np.float32)], axis=1)
    return np.tile(keep, (1, 2)).astype(np.float32), np.tile(signed, (1, 2)).astype(np.float32)


def tiles(total, size):
    return [(at, min(size, total - at)) for at in range(0, total, size)]


def over_tiles(total, size, step):
    whole = total // size
    if whole:

        def run(i, _):
            step(pl.multiple_of(i * size, size), size)
            return 0

        lax.fori_loop(0, whole, run, 0)
    if total % size:
        step(whole * size, total % size)


def turn_block(block, left, source, nd, nc):
    rows, width = block.shape
    part = width // (nd * nc)
    here = lanes(source * rows, rows)
    for at in range(0, width, 128):
        turned = block[:, at : at + 128].T
        for i in range(0, 128, part):
            d, c = (at + i) // (part * nc), (at + i) // part % nc
            left[c, d * part : (d + 1) * part, here] = turned[i : i + part]


def forward(nd, nc, tokens, cotangent, small, w_qkv, w_gate, w_up, w_out, w_down):
    rows, width = tokens.shape
    half = rows // 2
    many = nd * rows
    length = 2 * nc * half
    depth = w_qkv.shape[0]
    quarter = depth // 4
    heads_here = HEADS // nd
    groups = nc // nd
    heads = heads_here // groups
    span = heads * HDIM
    cols = heads_here * HDIM
    hidden = w_gate.shape[1] // nd
    down = w_down.shape[0]
    share_down = down // nc
    padded = share_down + -share_down % 16
    keep, sine = rotary_pair_tables(length)

    def body(
        tok_i, cot_i, small_i, wq_i, wg_i, wu_i, wo_i, wd_i, keep_i, sine_i,
        h1_o, dy_o, wq_o, seq_o, lse_o, mixed_o, r1_o, h2_o, m_o, dgu_o, pout_o, pdh2_o, small_o,
        dyp_o, mp_o, h2p_o, gatep_o, upz_o,
        tok, dy, sm, wq, h1, qkv, seq, lse, o, mixed, wo, part, ra, rb, r1, h2, wgu, wd, m, dgu,
        turns, left1, left2, m_t, mixed_t, dyp, send, recv, local,
    ):
        dp, ctx = lax.axis_index("dp"), lax.axis_index("ctx")
        near, across, far = flip_one(dp), (dp + 2) % nd, nd - 1 - dp
        spot = ctx % 4
        sides = [{"ctx": flip_bit(ctx, bit)} for bit in range(2)]
        links = Copies(send, recv, local)
        blocks = lambda ref, b: ref.at[halves(b * rows, rows)]

        get_tok = links.here(tok_i, blocks(tok, dp))
        get_turns = [
            links.here(table.at[halves(block * half, half)], turns.at[t, pl.ds(i * half, half)])
            for t, table in enumerate((keep_i, sine_i))
            for i, block in enumerate((ctx, 2 * nc - 1 - ctx))
        ]
        get_small = links.here(small_i, sm.at[dp])
        get_wq = [
            links.here(
                wq_i.at[:, lanes(j * width + dp * cols, cols)],
                wq.at[halves(dp * depth, depth), pl.ds(j * cols, cols)],
            )
            for j in range(3)
        ]
        meet((("dp", nd), ("ctx", nc)))

        def columns(w_i, w, e, at, n, to, which):
            first, size = (0, depth) if which is None else (which * quarter, quarter)
            return links.to(
                {"dp": e},
                w_i.at[halves(first, size), lanes(at, n)],
                w.at[halves(dp * depth + first, size), pl.ds(to, n)],
            )

        def share(w, copies, source):
            for copy in copies:
                copy.wait_recv()
            block = w.at[halves(source * depth + spot * quarter, quarter)]
            return [links.to(side, block, block) for side in sides]

        def cross(w, shared, source):
            passed = []
            for bit in range(2):
                shared[bit].wait_recv()
                start = source * depth + flip_bit(spot, bit) * quarter + bit * (quarter // 2)
                block = w.at[halves(start, quarter // 2)]
                passed.append(links.to(sides[1 - bit], block, block))
            return passed

        def qkv_columns(e, which):
            return [
                columns(wq_i, wq, e, j * width + e * cols, cols, j * cols, which) for j in range(3)
            ]

        def hidden_columns(e, which):
            return [
                columns(w_i, wgu, e, e * hidden, hidden, i * hidden, which)
                for i, w_i in enumerate((wg_i, wu_i))
            ]

        send_small = [links.to({"dp": e}, small_i, sm.at[dp]) for e in (near, across, far)]
        wq_x = [qkv_columns(e, spot) for e in (across, far)]
        send_tok = [links.to({"dp": e}, tok_i, blocks(tok, dp)) for e in (near, across)]
        wq_near = qkv_columns(near, None)
        send_dyp = [links.to(sides[1], cot_i, blocks(dyp, dp))]
        wgu_x = [hidden_columns(e, spot) for e in (far, across)]
        get_wo = links.here(wo_i, wo)
        get_wd = links.here(wd_i, wd)
        get_dy = links.here(cot_i, blocks(dy, dp))
        get_wgu = [
            links.here(
                w_i.at[:, lanes(dp * hidden, hidden)],
                wgu.at[halves(dp * depth, depth), pl.ds(i * hidden, hidden)],
            )
            for i, w_i in enumerate((wg_i, wu_i))
        ]

        get_small.wait()
        for copy in send_small:
            copy.wait_recv()

        def gain(row):
            lines = [
                sm[b, row * 4 + q : row * 4 + q + 1, :]
                for b in range(nd)
                for q in range(width // nd // 128)
            ]
            return jnp.concatenate(lines, axis=1)

        def first_norm(b):
            at = halves(b * rows, rows)
            hat, _ = normalize_rows(tok[at, :].astype(F32))
            h1[at, :] = (hat * gain(0) + gain(1)).astype(BF16)

        def turn_first(b):
            turn_block(h1[halves(b * rows, rows), :], left1, b, nd, nc)

        get_tok.wait()
        wq_s = [share(wq, copies, e) for copies, e in zip(wq_x, (across, far))]
        first_norm(dp)
        send_tok[0].wait_recv()
        first_norm(near)
        wq_c = cross(wq, wq_s[0], across)
        send_tok[1].wait_recv()
        forward_tok = links.to({"dp": near}, blocks(tok, across), blocks(tok, across))
        wq_c += cross(wq, wq_s[1], far)
        first_norm(across)
        forward_tok.wait_recv()
        first_norm(far)
        wgu_d = [c for e in (across, far) for c in hidden_columns(e, 3 - spot)]
        wgu_near = hidden_columns(near, None)
        send_dy = [links.to({"dp": e}, cot_i, blocks(dy, dp)) for e in (near, across)]
        put_small = links.here(sm, small_o)
        for copy in get_wq + get_turns:
            copy.wait()
        for copy in wq_near + wq_c:
            copy.wait_recv()
        put_wq = links.here(wq, wq_o)

        for at, n in tiles(3 * cols, 256):
            j = at // cols
            acc = plain(h1[...], wq[:, at : at + n])
            for q in range(n // 128):
                first = at % cols + q * 128
                line = (j * width + dp * cols + first) // 128
                per = 3 * width // nd // 128
                bias = sm[line // per, pl.ds(4 * (width // nd) // 128 + line % per, 1), :]
                for s in range(nd):
                    u = acc[s * rows : (s + 1) * rows, q * 128 : (q + 1) * 128] + bias
                    if j < 2:
                        u = rotate_pair(u, turns[0], turns[1])
                    u = u.astype(BF16)
                    if heads > 1:
                        g, off = first // span, first % span
                        qkv[g, s * rows : (s + 1) * rows, j * span + off : j * span + off + 128] = u
                    else:
                        for i in range(2):
                            qkv[
                                first // HDIM + i, s * rows : (s + 1) * rows, j * HDIM : (j + 1) * HDIM
                            ] = u[:, i * HDIM : (i + 1) * HDIM]

        mirror = 2 * nc - 1 - ctx
        go = []
        for k in range(1, nc):
            peer = lax.rem(ctx + k, nc)
            s, g = peer // groups, peer % groups
            for i, block in enumerate((ctx, mirror)):
                go.append(
                    links.to(
                        {"ctx": peer},
                        qkv.at[g, halves(s * rows + i * half, half)],
                        seq.at[halves(block * half, half)],
                    )
                )
        s, g = ctx // groups, ctx % groups
        stay = [
            links.here(
                qkv.at[g, halves(s * rows + i * half, half)], seq.at[halves(block * half, half)]
            )
            for i, block in enumerate((ctx, mirror))
        ]
        for b in range(nd):
            turn_first(b)
        put_h1 = links.here(left1, h1_o)
        for copy in stay:
            copy.wait()
        for copy in go:
            copy.wait_recv()
        put_seq = links.here(seq, seq_o)
        put_h1.wait()
        back, stay = [], []
        step = min(heads, 2)
        for head in range(heads):
            attend(seq, o, lse, heads, head)
            if (head + 1) % step:
                continue
            here = pl.ds((head + 1 - step) * HDIM, step * HDIM)
            for k in range(nc):
                peer = lax.rem(ctx + k, nc)
                for i, block in enumerate((peer, 2 * nc - 1 - peer)):
                    src = o.at[halves(block * half, half), here]
                    dst = mixed.at[g, halves(s * rows + i * half, half), here]
                    if k:
                        back.append(links.to({"ctx": peer}, src, dst))
                    else:
                        stay.append(links.here(src, dst))
        wgu_far = share(wgu, wgu_x[0], far)
        wgu_near2 = share(wgu, wgu_x[1], across)
        put_lse = links.here(lse, lse_o)
        get_wo.wait()
        for copy in stay:
            copy.wait()
        for copy in back:
            copy.wait_recv()

        def out_tile(at, n):
            acc = plain(mixed[0], wo[0:span, pl.ds(at, n)])
            for i in range(1, groups):
                acc += plain(mixed[i], wo[i * span : (i + 1) * span, pl.ds(at, n)])
            part[:, pl.ds(at, n)] = acc.astype(BF16)

        over_tiles(width, 512, out_tile)

        to_near = [
            links.to({"dp": near}, blocks(part, far), blocks(ra, 0)),
            links.to({"dp": near}, blocks(part, near), blocks(ra, 1)),
        ]
        for i in range(groups):
            mixed_t[i * span : (i + 1) * span, :] = mixed[i].T
        put_mixed = links.here(mixed_t, mixed_o)
        to_near[0].wait_recv()
        across_at = halves(across * rows, rows)
        part[across_at, :] = (part[across_at, :].astype(F32) + ra[:rows, :].astype(F32)).astype(BF16)
        to_across = links.to({"dp": across}, blocks(part, across), rb)
        send_dy[1].wait_recv()
        forward_dy = links.to({"dp": near}, blocks(dy, across), blocks(dy, across))
        to_near[1].wait_recv()
        own_at = halves(dp * rows, rows)
        r1[...] = tok[own_at, :].astype(F32) + (
            part[own_at, :].astype(F32) + ra[rows:, :].astype(F32)
        )
        to_across.wait_recv()
        r1[...] += rb[...].astype(F32)
        put_r1 = links.here(r1, r1_o)
        hat, _ = normalize_rows(r1[...])
        h2[own_at, :] = (hat * gain(2) + gain(3)).astype(BF16)
        send_h2 = [links.to({"dp": e}, blocks(h2, dp), blocks(h2, dp)) for e in (near, across)]
        send_dyp[0].wait_recv()
        share_dyp = [links.to({"dp": e}, blocks(dyp, dp), blocks(dyp, dp)) for e in (near, across)]
        turn_block(h2[own_at, :], left2, dp, nd, nc)
        send_h2[0].wait_recv()
        turn_block(h2[halves(near * rows, rows), :], left2, near, nd, nc)
        send_h2[1].wait_recv()
        forward_h2 = links.to({"dp": near}, blocks(h2, across), blocks(h2, across))
        turn_block(h2[halves(across * rows, rows), :], left2, across, nd, nc)
        get_wd.wait()
        get_dy.wait()
        for copy in get_wgu:
            copy.wait()
        for copy in wgu_near + wgu_far + wgu_near2 + wgu_d + [send_dy[0], forward_dy, forward_h2]:
            copy.wait_recv()
        turn_block(h2[halves(far * rows, rows), :], left2, far, nd, nc)
        put_h2 = links.here(left2, h2_o)
        put_dy = links.here(dy, dy_o)

        spare = nc // 2
        send_left = [
            links.to(
                sides[bit],
                left2.at[
                    flip_bits(flip_bit(ctx, bit), spread(2 * j, step_orders(nc)[bit])),
                    quarter_of(left2, dp),
                ],
                left1.at[bit * spare + j, quarter_of(left2, dp)],
            )
            for bit in range(2)
            for j in range(spare)
        ]
        send_gate = []
        def hidden_tile(at, n):
            here = pl.ds(at, n)
            gate = plain(h2[...], wgu[:, here])
            up = plain(h2[...], wgu[:, pl.ds(hidden + at, n)])
            dm = last_dims(dy[...], wd[here, :])
            sig = jax.nn.sigmoid(gate)
            m[:, here] = (gate * sig * up).astype(BF16)
            dgu[:, here] = (dm * up * sig * (1.0 + gate * (1.0 - sig))).astype(BF16)
            dgu[:, pl.ds(hidden + at, n)] = (dm * gate * sig).astype(BF16)

        if padded != share_down:
            m[:, hidden:] = jnp.zeros((many, padded - share_down), BF16)
        for at, n in tiles(hidden, 512):
            over_tiles(n, 256, lambda i, size, at=at: hidden_tile(at + i, size))
            here = pl.ds(at, n)
            if at + n <= first_cut(hidden):
                send_gate.append(links.to(sides[0], dgu.at[:, here], gatep_o.at[:, here]))
            if at + n <= swapped_cut(hidden):
                there = pl.ds(hidden + at, n)
                send_gate.append(links.to(sides[1], dgu.at[:, there], upz_o.at[:, here]))
        for c in range(nc):
            m_t[c] = m[:, c * share_down : c * share_down + padded].T
        put_m = links.here(m_t, m_o)

        put_dgu = links.here(dgu, dgu_o)
        send_m = []
        for j in range(nc // 2):
            owner = flip_bits(flip_bit(ctx, 1), spread(2 * j, step_orders(nc)[1]))
            send_m.append(links.to(sides[1], m_t.at[owner], mp_o.at[j]))
        share_dyp[1].wait_recv()
        forward_dyp = links.to({"dp": near}, blocks(dyp, across), blocks(dyp, across))
        for copy in send_left:
            copy.wait_recv()
        own_left = left1.at[:, quarter_of(left2, dp)]
        share_left = [links.to({"dp": e}, own_left, own_left) for e in (near, across)]

        def dh2_tile(at, n):
            here = pl.ds(at, n)
            h1[:, here] = last_dims(dgu[...], wgu[here, :]).astype(BF16)

        over_tiles(width, 256, dh2_tile)
        put_pdh2 = links.here(h1, pdh2_o)
        links.gone(*send_tok, forward_tok)

        def result_tile(at, n):
            here = pl.ds(at, n)
            tok[:, here] = plain(m[:, :hidden], wd[:, here]).astype(BF16)

        share_left[1].wait_recv()
        other_left = left1.at[:, quarter_of(left2, across)]
        forward_left = links.to({"dp": near}, other_left, other_left)
        over_tiles(width, 256, result_tile)
        put_pout = links.here(tok, pout_o)
        for copy in (share_dyp[0], forward_dyp, share_left[0], forward_left):
            copy.wait_recv()
        put_other = [links.here(dyp, dyp_o), links.here(left1, h2p_o)]
        for copy in send_m + send_gate:
            copy.wait_recv()

        links.gone(*links.left)
        for copy in (
            *put_other, put_small, put_wq, put_seq, put_lse, put_mixed, put_r1, put_h2, put_dy, put_m, put_dgu,
            put_pdh2, put_pout,
        ):
            copy.wait()

    anywhere = pl.BlockSpec(memory_space=pl.ANY)
    shape = jax.ShapeDtypeStruct
    remotes = 64 + 7 * nc
    outs = dict(
        h1=((nc, width // nc, many), BF16),
        dy=((many, width), BF16),
        wq=((width, 3 * cols), BF16),
        seq=((length, 3 * span), BF16),
        lse=((heads, length), F32),
        mixed=((cols, many), BF16),
        r1=((rows, width), F32),
        h2=((nc, width // nc, many), BF16),
        m=((nc, padded, many), BF16),
        dgu=((many, 2 * hidden), BF16),
        pout=((many, width), BF16),
        pdh2=((many, width), BF16),
        small=((nd,) + small.shape, F32),
        dyp=((many, width), BF16),
        mp=((nc // 2, padded, many), BF16),
        h2p=((nc, width // nc, many), BF16),
        gatep=((many, first_cut(hidden)), BF16),
        upz=((many, swapped_cut(hidden)), BF16),
    )
    scratch = [
        ((many, width), BF16),
        ((many, width), BF16),
        ((nd,) + small.shape, F32),
        ((width, 3 * cols), BF16),
        ((many, width), BF16),
        ((groups, many, 3 * span), BF16),
        ((length, 3 * span), BF16),
        ((heads, length), F32),
        ((length, span), BF16),
        ((groups, many, span), BF16),
        ((cols, width), BF16),
        ((many, width), BF16),
        ((2 * rows, width), BF16),
        ((rows, width), BF16),
        ((rows, width), F32),
        ((many, width), BF16),
        ((width, 2 * hidden), BF16),
        ((down, width), BF16),
        ((many, hidden + padded - share_down), BF16),
        ((many, 2 * hidden), BF16),
        ((2, rows, 128), F32),
        ((nc, width // nc, many), BF16),
        ((nc, width // nc, many), BF16),
        ((nc, padded, many), BF16),
        ((cols, many), BF16),
        ((many, width), BF16),
    ]
    results = pl.pallas_call(
        body,
        out_shape=[shape(*o) for o in outs.values()],
        in_specs=[anywhere] * 10,
        out_specs=[anywhere] * len(outs),
        scratch_shapes=[pltpu.VMEM(*s) for s in scratch]
        + [
            pltpu.SemaphoreType.DMA((remotes,)),
            pltpu.SemaphoreType.DMA((remotes,)),
            pltpu.SemaphoreType.DMA((40,)),
        ],
        compiler_params=pltpu.CompilerParams(
            collective_id=0, has_side_effects=True, vmem_limit_bytes=VMEM_BYTES
        ),
    )(tokens, cotangent, small, w_qkv, w_gate, w_up, w_out, w_down, keep, sine)
    return dict(zip(outs, results))


def attend_back(x_ref, lse_ref, do_ref, d_ref, heads, head):
    length = x_ref.shape[0]
    block, segments, inner = attention_shapes(length)
    q_at, k_at, v_at = (head_columns(heads, i, head) for i in range(3))
    o_at = slice(head * HDIM, (head + 1) * HDIM)
    for segment in range(segments):
        count = (segment + 1) * inner * block
        keys = x_ref[:count, k_at]
        values = x_ref[:count, v_at]

        def step(i, _):
            start = pl.multiple_of((segment * inner + i) * block, block)
            query = x_ref[pl.ds(start, block), q_at] * 0.125
            dout = do_ref[pl.ds(start, block), o_at]
            scores = causal(last_dims(keys, query), start)
            probs = jnp.exp(scores - lse_ref[head : head + 1, pl.ds(start, block)])
            d_probs = last_dims(values, dout)
            centre = jnp.sum(probs * d_probs, axis=0, keepdims=True)
            d_scores = (probs * (d_probs - centre)).astype(BF16)
            d_ref[:count, v_at] += plain(probs.astype(BF16), dout)
            d_ref[:count, k_at] += plain(d_scores, query)
            d_ref[pl.ds(start, block), q_at] = first_dims(keys, d_scores).T * 0.125
            return 0

        if inner == 1:
            step(0, 0)
        else:
            lax.fori_loop(0, inner, step, 0)


class GroupSum:
    def __init__(self, links, dp, nd, rows, part, ra, rb):
        self.links, self.rows = links, rows
        self.part, self.ra, self.rb = part, ra, rb
        self.near, self.across, self.far = flip_one(dp), (dp + 2) % nd, nd - 1 - dp
        self.dp = dp
        block = lambda ref, b: ref.at[halves(b * rows, rows)]
        self.a = [
            links.to({"dp": self.near}, block(part, self.far), block(ra, 0)),
            links.to({"dp": self.near}, block(part, self.near), block(ra, 1)),
        ]

    def middle(self):
        rows, at = self.rows, halves(self.across * self.rows, self.rows)
        self.a[0].wait_recv()
        self.part[at, :] = (
            self.part[at, :].astype(F32) + self.ra[:rows, :].astype(F32)
        ).astype(BF16)
        self.b = self.links.to({"dp": self.across}, self.part.at[at], self.rb)

    def total(self):
        rows, at = self.rows, halves(self.dp * self.rows, self.rows)
        self.a[1].wait_recv()
        self.b.wait_recv()
        return (
            self.part[at, :].astype(F32)
            + self.ra[rows:, :].astype(F32)
            + self.rb[...].astype(F32)
        )


class Gradient:
    def __init__(self, links, ctx, bits, left, right, slots, landing, stage):
        self.links, self.ctx, self.bits, self.nc = links, ctx, bits, 1 << len(bits)
        nc = self.nc
        self.left, self.right, self.slots = left, right, slots
        self.landing = landing
        self.stage = stage.at[pl.ds(0, slots.shape[1]), pl.ds(0, slots.shape[2])]
        self.sent = {}
        self.order = sorted(range(nc // 2), key=lambda j: (j & -j) or nc)

    def _landing(self, bit, j):
        base = sum(self.nc >> (b + 1) for b in range(1, bit))
        return self.landing.at[base + (j >> bit)]

    def compute(self, send=True):
        for j in self.order:
            self.slot(j, send)

    def start(self, part):
        odd = [j for j in self.order if j % 2]
        for j in odd[part * len(odd) // 2 : (part + 1) * len(odd) // 2]:
            self._pass(1, j)

    def slot(self, j, send=True):
        mine, other = self.left[0][j], self.left[1][j]

        def step(at, n):
            here = pl.ds(at, n)
            acc = plain(mine, self.right[0][:, here]) + plain(other, self.right[1][:, here])
            self.slots[j, :, here] = acc.astype(BF16)

        over_tiles(self.slots.shape[2], 512, step)
        if send:
            self._pass(1, j)

    def _pass(self, bit, j):
        low = j & -j
        if j and low == 1 << (bit - 1):
            self.sent[bit, j] = self.links.to(
                {"ctx": flip_bit(self.ctx, self.bits[bit])},
                self.slots.at[j],
                self._landing(bit, j - low),
            )

    def add(self, bit):
        for j in self.order:
            if j % (1 << bit) == 0:
                self.add_slot(bit, j)

    def add_slot(self, bit, j):
        self.sent[bit, j + (1 << (bit - 1))].wait_recv()
        self.links.here(self._landing(bit, j), self.stage).wait()

        def step(at, n):
            here = pl.ds(at, n)
            acc = self.slots[j, :, here].astype(F32) + self.stage[:, here].astype(F32)
            self.slots[j, :, here] = acc.astype(BF16)

        over_tiles(self.slots.shape[2], 512, step)
        self._pass(bit + 1, j)


def backward(nd, nc, f, tokens, w_out):
    rows, width = tokens.shape
    half = rows // 2
    many = nd * rows
    length, wide = f["seq"].shape
    heads = f["lse"].shape[0]
    span = heads * HDIM
    groups = nc // nd
    cols = groups * span
    hidden = f["dgu"].shape[1] // 2
    slots = nc // 2
    share = width // (nd * nc)
    tall = {"gu": nd * share, "down": f["m"].shape[1], "out": cols // nc, "qkv": nd * share}
    flat = {"gu": 2 * hidden, "down": width, "out": width, "qkv": 3 * cols}
    cut = first_cut(hidden)
    cut_z = swapped_cut(hidden)
    ranges = [(0, cut // 2), (cut // 2, cut - cut // 2)]
    ranges += [(hidden + cut_z, hidden - cut_z), (cut, hidden - cut)]
    range_z = (hidden, cut_z)
    names = ("down", "gu", "qkv", "out")
    bits = nc.bit_length() - 1
    keep_t, sine_t = rotary_pair_tables(length)
    chunk = length if length <= 1024 else 256
    strip = 256 if length <= 1024 else 128
    mixed_left = f["mixed"].reshape(nc, cols // nc, many)

    def body(
        h2_l, h2p_l, gatep_i, upz_i, m_l, mp_l, mixed_l, h1_l, dy_i, dyp_i, dgu_i, wq_i, seq_i, lse_i, r1_i, pdh2_i, pout_i,
        small_i, tok_i, wo_i, keep_i, sine_i,
        out_o, tg_o, gate_o, up_o, qkv_o, down_o, out_g_o, sums_o,
        land_down, land_gu, land_qkv, land_out,
        l_gu, l_up, l_down, l_out, l_qkv, dgu, dgup, dy, dyp, da, dq, dqp,
        s_down, s_gu, s_qkv, s_out, stage,
        part, ra, rb, r1, dr1, x, sm, wq, wo, seq, lse,
        dmix, dseq, dx, keep, sine, dback, sums, sums_in,
        send, recv, local, free,
    ):
        dp, ctx = lax.axis_index("dp"), lax.axis_index("ctx")
        near, across, far = flip_one(dp), (dp + 2) % nd, nd - 1 - dp
        links = Copies(send, recv, local)
        blocks = lambda ref, b: ref.at[halves(b * rows, rows)]
        own_at = halves(dp * rows, rows)
        beside = {"ctx": flip_bit(ctx, 0)}

        usual, swapped = step_orders(nc)

        def get_left(left_i, left, order=usual):
            return [
                links.here(left_i.at[flip_bits(ctx, spread(2 * j, order))], left.at[0, j])
                for j in range(slots)
            ]

        get_part = links.here(pdh2_i, part)
        get_gu = get_left(h2_l, l_gu)
        get_gu += [
            links.here(a, b)
            for a, b in (
                (h2p_l.at[pl.ds(0, slots)], l_gu.at[1]),
                (dgu_i, dgu),
                (gatep_i, dgup.at[:, pl.ds(0, cut)]),
            )
        ]
        get_up = get_left(h2_l, l_up, swapped)
        get_up += [
            links.here(a, b)
            for a, b in ((h2p_l.at[pl.ds(slots, slots)], l_up.at[1]), (upz_i, dgup.at[:, pl.ds(*range_z)]))
        ]
        get_down = get_left(m_l, l_down, swapped)
        get_down += [
            links.here(a, b) for a, b in ((mp_l, l_down.at[1]), (dy_i, dy), (dyp_i, dyp))
        ]
        get_first = [links.here(a, b) for a, b in ((r1_i, r1), (small_i, sm))]
        get_wo = links.here(wo_i, wo)
        get_attn = [links.here(a, b) for a, b in ((seq_i, seq), (lse_i, lse))]
        get_late = get_left(h1_l, l_qkv) + get_left(mixed_l, l_out) + [links.here(tok_i, x)]

        def tables(c):
            at = pl.ds(c * chunk, chunk)
            return [links.here(a.at[at], b) for a, b in ((keep_i, keep), (sine_i, sine))]

        get_tables = tables(0)

        def strips(i):
            return links.here(wq_i.at[pl.ds(i * strip, strip)], wq.at[i % 2])

        get_wq = [strips(0), strips(1)]

        def gain(row):
            lines = [
                sm[b, row * 4 + q : row * 4 + q + 1, :]
                for b in range(nd)
                for q in range(width // nd // 128)
            ]
            return jnp.concatenate(lines, axis=1)

        down = Gradient(links, ctx, swapped, l_down, (dy, dyp), s_down, land_down, stage)
        gu = []
        for at, n in ranges + [range_z]:
            here = pl.ds(at, n)
            order, left = (swapped, l_up) if at == hidden else (usual, l_gu)
            gu.append(
                Gradient(
                    links, ctx, order, left, (dgu.at[:, here], dgup.at[:, here]),
                    s_gu.at[:, :, here], land_gu.at[:, :, here], stage,
                )
            )
        up = gu.pop()
        qkv = []
        for j in range(3):
            at = pl.ds(j * cols, cols)
            qkv.append(
                Gradient(
                    links, ctx, usual, l_qkv, (dq.at[:, at], dqp.at[:, at]),
                    s_qkv.at[:, :, at], land_qkv.at[:, :, at], stage,
                )
            )
        out = Gradient(links, ctx, usual, l_out, (da, dyp), s_out, land_out, stage)

        meet((("dp", nd), ("ctx", nc)))
        get_part.wait()
        sum2 = GroupSum(links, dp, nd, rows, part, ra, rb)

        def send_right(i):
            here = pl.ds(*ranges[i])
            return links.to(beside, dgu_i.at[:, here], dgup.at[:, here])

        right_gu = [None, None, send_right(2)]
        for copy in get_gu:
            copy.wait()
        gu[0].slot(gu[0].order[0])
        sum2.middle()
        for j in gu[0].order[1:]:
            gu[0].slot(j)
        for copy in get_first + get_down + get_up:
            copy.wait()
        up.compute()
        gu[1].compute()
        down.compute(send=False)
        for i, device in enumerate((beside, {"dp": near}, {"dp": across})):
            pl.semaphore_signal(free.at[i], inc=1, device_id=device, device_id_type=MESH)

        dh2 = sum2.total()
        hat, inverse = normalize_rows(r1[...])
        dr1[...] = dy[own_at, :].astype(F32) + norm_reverse(dh2, gain(2), hat, inverse)
        da[own_at, :] = dr1[...].astype(BF16)
        send_da = [links.to({"dp": e}, blocks(da, dp), blocks(da, dp)) for e in (near, across)]
        pl.semaphore_wait(free.at[0], 1)
        right_out = links.to(beside, blocks(da, dp), blocks(dyp, dp))
        sums[2:3, :] = jnp.sum(dh2 * hat, axis=0, keepdims=True)
        sums[3:4, :] = jnp.sum(dh2, axis=0, keepdims=True)
        dx[...] = jnp.zeros_like(dx)
        if bits > 1:
            gu[0].add(1)
        send_da[1].wait_recv()
        forward_da = links.to({"dp": near}, blocks(da, across), blocks(da, across))
        get_wo.wait()
        send_da[0].wait_recv()
        forward_da.wait_recv()

        for g in range(groups):
            dmix[g] = last_dims(da[...], wo[g * span : (g + 1) * span, :]).astype(BF16)
        mirror = 2 * nc - 1 - ctx
        go = []
        for k in range(1, nc):
            peer = lax.rem(ctx + k, nc)
            s, g = peer // groups, peer % groups
            for i, block in enumerate((ctx, mirror)):
                go.append(
                    links.to(
                        {"ctx": peer},
                        dmix.at[g, halves(s * rows + i * half, half)],
                        dseq.at[halves(block * half, half)],
                    )
                )
        s, g = ctx // groups, ctx % groups
        stay = [
            links.here(
                dmix.at[g, halves(s * rows + i * half, half)], dseq.at[halves(block * half, half)]
            )
            for i, block in enumerate((ctx, mirror))
        ]
        right_gu.append(send_right(3))

        left_qkv = [
            links.to(
                beside,
                h1_l.at[flip_bits(flip_bit(ctx, 0), 2 * j), quarter_of(l_qkv, dp)],
                l_qkv.at[1, j, quarter_of(l_qkv, dp)],
            )
            for j in range(slots)
        ]
        left_out = [
            links.to(beside, mixed_l.at[flip_bits(flip_bit(ctx, 0), 2 * j)], l_out.at[1, j])
            for j in range(slots)
        ]
        right_gu[2].wait_recv()
        gu[2].compute()
        if bits > 1:
            up.add(1)
            gu[1].add(1)

        def share_right():
            right_out.wait_recv()
            for i in (1, 2):
                pl.semaphore_wait(free.at[i], 1)
            block = blocks(dyp, dp)
            return [links.to({"dp": e}, block, block) for e in (near, across)]

        def share_left():
            for copy in left_qkv:
                copy.wait_recv()
            block = l_qkv.at[1, :, quarter_of(l_qkv, dp)]
            return [links.to({"dp": e}, block, block) for e in (near, across)]

        for copy in get_attn + stay:
            copy.wait()
        for copy in go:
            copy.wait_recv()
        down.start(0)
        shared_right = share_right()
        for head in range(heads):
            attend_back(seq, lse, dseq, dx, heads, head)
        for c in range(length // chunk):
            for copy in get_tables if c == 0 else tables(c):
                copy.wait()
            here = slice(c * chunk, (c + 1) * chunk)
            for at in range(0, wide, 128):
                n = min(128, wide - at)
                u = dx[here, at : at + n]
                if at < 2 * span:
                    u = rotate_pair(u, keep[...], -sine[...])
                seq[here, at : at + n] = u.astype(BF16)

        back = []
        for k in range(1, nc):
            peer = lax.rem(ctx + k, nc)
            for i, block in enumerate((peer, 2 * nc - 1 - peer)):
                back.append(
                    links.to(
                        {"ctx": peer},
                        seq.at[halves(block * half, half)],
                        dback.at[g, halves(s * rows + i * half, half)],
                    )
                )
        stay = [
            links.here(
                seq.at[halves(block * half, half)], dback.at[g, halves(s * rows + i * half, half)]
            )
            for i, block in enumerate((ctx, mirror))
        ]
        shared_left = share_left()
        shared_right[1].wait_recv()
        forward_right = links.to({"dp": near}, blocks(dyp, across), blocks(dyp, across))
        for copy in get_late:
            copy.wait()
        right_gu[3].wait_recv()
        gu[3].compute()
        shared_left[1].wait_recv()
        block = l_qkv.at[1, :, quarter_of(l_qkv, across)]
        forward_left = links.to({"dp": near}, block, block)
        for copy in left_out + [shared_right[0], forward_right]:
            copy.wait_recv()
        out.compute()
        for copy in stay:
            copy.wait()
        for copy in back:
            copy.wait_recv()
        for g_ in range(groups):
            for j in range(3):
                at = j * cols + g_ * span
                dq[:, at : at + span] = dback[g_, :, j * span : (j + 1) * span]
        right_qkv = []

        def send_qkv():
            here = pl.ds(len(right_qkv) * cols, cols)
            right_qkv.append(links.to(beside, dq.at[:, here], dqp.at[:, here]))

        send_qkv()
        if bits > 1:
            gu[2].add(1)
        send_qkv()
        down.start(1)
        links.gone(*sum2.a, sum2.b)
        for i in range(width // strip):
            get_wq[i].wait()
            part[:, i * strip : (i + 1) * strip] = last_dims(dq[...], wq[i % 2]).astype(BF16)
            if i + 2 < width // strip:
                get_wq.append(strips(i + 2))
        sum1 = GroupSum(links, dp, nd, rows, part, ra, rb)
        send_qkv()
        for copy in (shared_left[0], forward_left):
            copy.wait_recv()

        def compute_qkv(j):
            right_qkv[j].wait_recv()
            qkv[j].compute()

        compute_qkv(0)
        sum1.middle()
        if bits > 1:
            gu[3].add(1)
        sums[4:, :] = jnp.zeros((nd, width), F32)
        sums[pl.ds(4 + dp, 1), : 3 * cols] = jnp.sum(dq[...].astype(F32), axis=0, keepdims=True)

        arriving, put = [], []

        def to_owner(slots_ref, spans):
            for e in (near, across, far, dp):
                for dst, at, to, n, every in spans:
                    src = slots_ref.at[0, pl.ds(pl.multiple_of(e * share, 16), share), pl.ds(at, n)]
                    place = dst.at[:, lanes(to + dp * every, n)]
                    if e is dp:
                        put.append(links.here(src, place))
                    else:
                        arriving.append(links.to({"dp": e}, src, place))

        def close_gu(piece, span_of):
            for bit in range(2, bits):
                piece.add(bit)
            at, n = span_of
            for dst, base in ((gate_o, 0), (up_o, hidden)):
                first, last = max(at, base), min(at + n, base + hidden)
                if first < last:
                    to_owner(s_gu, ((dst, first, first - base, last - first, hidden),))

        def close_qkv(j):
            for bit in range(2, bits):
                qkv[j].add(bit)
            to_owner(s_qkv, ((qkv_o, j * cols, j * width, cols, cols),))

        compute_qkv(1)
        close_gu(gu[0], ranges[0])
        close_gu(up, range_z)
        if bits > 1:
            out.add(1)
            down.add(1)

        dh1 = sum1.total()
        hat1, inverse1 = normalize_rows(x[...].astype(F32))
        sums[0:1, :] = jnp.sum(dh1 * hat1, axis=0, keepdims=True)
        sums[1:2, :] = jnp.sum(dh1, axis=0, keepdims=True)
        partners = [("dp", flip_bit(dp, b)) for b in range(nd.bit_length() - 1)]
        partners += [("ctx", flip_bit(ctx, b)) for b in range(bits)]
        sums_out = []

        def start_sums():
            i = len(sums_out)
            if i < len(partners):
                axis, device = partners[i]
                sums_out.append(links.to({axis: device}, sums, sums_in.at[i]))

        def end_sums():
            i = len(sums_out) - 1
            sums_out[i].wait_recv()
            links.gone(sums_out[i])
            sums[...] += sums_in[i]

        def next_sums():
            end_sums()
            start_sums()

        start_sums()
        dr1[...] += norm_reverse(dh1, gain(0), hat1, inverse1)
        put_tg = links.here(dr1, tg_o)
        links.gone(*sum1.a, sum1.b)
        get_pout = links.here(pout_i, part)
        compute_qkv(2)
        next_sums()
        get_pout.wait()
        sum0 = GroupSum(links, dp, nd, rows, part, ra, rb)
        if bits > 1:
            qkv[0].add(1)
        close_gu(gu[1], ranges[1])
        next_sums()
        sum0.middle()
        next_sums()
        if bits > 1:
            qkv[1].add(1)
        x[...] = (r1[...] + sum0.total()).astype(BF16)
        put_out = links.here(x, out_o)
        for i in range(2, len(ranges)):
            close_gu(gu[i], ranges[i])
        if bits > 1:
            qkv[2].add(1)
        next_sums()
        for bit in range(2, bits):
            down.add(bit)
        put.append(links.here(s_down.at[0], down_o))
        for bit in range(2, bits):
            out.add(bit)
        put.append(links.here(s_out.at[0], out_g_o))
        close_qkv(0)
        close_qkv(1)
        while len(sums_out) < len(partners):
            next_sums()
        close_qkv(2)
        end_sums()
        put_sums = [links.here(sums, sums_o), put_tg, put_out]
        for copy in arriving:
            copy.wait_recv()
        links.gone(*links.left)
        for copy in put + put_sums:
            copy.wait()

    anywhere = pl.BlockSpec(memory_space=pl.ANY)
    shape = jax.ShapeDtypeStruct
    outs = [
        ((rows, width), BF16),
        ((rows, width), F32),
        ((share, nd * hidden), BF16),
        ((share, nd * hidden), BF16),
        ((share, 3 * width), BF16),
        ((tall["down"], width), BF16),
        ((tall["out"], width), BF16),
        ((4 + nd, width), F32),
        *[((max(1, slots - 1), tall[k], flat[k]), BF16) for k in names],
    ]
    scratch = [
        *[((2, slots, tall[k], many), BF16) for k in ("gu", "gu", "down", "out", "qkv")],
        ((many, 2 * hidden), BF16),
        ((many, 2 * hidden), BF16),
        ((many, width), BF16),
        ((many, width), BF16),
        ((many, width), BF16),
        ((many, 3 * cols), BF16),
        ((many, 3 * cols), BF16),
        *[((slots, tall[k], flat[k]), BF16) for k in names],
        ((max(tall.values()), width), BF16),
        ((many, width), BF16),
        ((2 * rows, width), BF16),
        ((rows, width), BF16),
        ((rows, width), F32),
        ((rows, width), F32),
        ((rows, width), BF16),
        (f["small"].shape, F32),
        ((2, strip, 3 * cols), BF16),
        ((cols, width), BF16),
        ((length, wide), BF16),
        ((heads, length), F32),
        ((groups, many, span), BF16),
        ((length, span), BF16),
        ((length, wide), F32),
        ((chunk, 128), F32),
        ((chunk, 128), F32),
        ((groups, many, wide), BF16),
        ((4 + nd, width), F32),
        ((bits + nd.bit_length() - 1, 4 + nd, width), F32),
    ]
    remotes = 64 + 4 * nc + 7 * nc
    return pl.pallas_call(
        body,
        out_shape=[shape(*o) for o in outs],
        in_specs=[anywhere] * 22,
        out_specs=[anywhere] * len(outs),
        scratch_shapes=[pltpu.VMEM(*s) for s in scratch]
        + [
            pltpu.SemaphoreType.DMA((remotes,)),
            pltpu.SemaphoreType.DMA((remotes,)),
            pltpu.SemaphoreType.DMA((64 + 7 * nc,)),
            pltpu.SemaphoreType.REGULAR((3,)),
        ],
        compiler_params=pltpu.CompilerParams(
            collective_id=1, has_side_effects=True, vmem_limit_bytes=VMEM_BYTES
        ),
    )(
        f["h2"], f["h2p"], f["gatep"], f["upz"], f["m"], f["mp"], mixed_left, f["h1"],
        f["dy"], f["dyp"], f["dgu"], f["wq"], f["seq"], f["lse"], f["r1"], f["pdh2"], f["pout"],
        f["small"], tokens, w_out, keep_t, sine_t,
    )


def widen(arrays):
    def body(*refs):
        n = len(arrays)
        ins, outs, held, wide = (refs[i * n : (i + 1) * n] for i in range(4))
        load, store = refs[4 * n :]
        loads = [pltpu.make_async_copy(ins[i], held[i], load.at[i]) for i in range(n)]
        for copy in loads:
            copy.start()
        stores = []
        for i in range(n):
            loads[i].wait()
            wide[i][...] = held[i][: wide[i].shape[0], :].astype(wide[i].dtype)
            stores.append(pltpu.make_async_copy(wide[i], outs[i], store.at[i]))
            stores[-1].start()
        for copy in stores:
            copy.wait()

    anywhere = pl.BlockSpec(memory_space=pl.ANY)
    n = len(arrays)
    shapes = [(rows, x.shape[1]) for x, rows, _ in arrays]
    return pl.pallas_call(
        body,
        out_shape=[jax.ShapeDtypeStruct(k, kind) for k, (_, _, kind) in zip(shapes, arrays)],
        in_specs=[anywhere] * n,
        out_specs=[anywhere] * n,
        scratch_shapes=[pltpu.VMEM(x.shape, x.dtype) for x, _, _ in arrays]
        + [pltpu.VMEM(k, kind) for k, (_, _, kind) in zip(shapes, arrays)]
        + [pltpu.SemaphoreType.DMA((n,)), pltpu.SemaphoreType.DMA((n,))],
        compiler_params=pltpu.CompilerParams(vmem_limit_bytes=VMEM_BYTES),
    )(*[x for x, _, _ in arrays])


def take(x, index):
    return lax.dynamic_index_in_dim(x, index, 0, keepdims=False)


def shards(tokens, cotangent, w_qkv, b_qkv, w_out, w_gate, w_up, w_down, norms):
    width = tokens.shape[-1]
    rows = 2 * tokens.shape[3]
    nd, nc = lax.axis_size("dp"), lax.axis_size("ctx")
    dp, ctx = lax.axis_index("dp"), lax.axis_index("ctx")
    x = tokens.reshape(rows, width)

    small = jnp.concatenate([norms.reshape(-1), b_qkv]).astype(F32)
    small = jnp.pad(small, (0, -small.shape[0] % 1024)).reshape(-1, 128)
    f = forward(
        nd, nc, x, cotangent.reshape(rows, width), small, w_qkv, w_gate, w_up, w_out, w_down
    )

    result, tokens_grad, g_gate, g_up, g_qkv, g_down, g_out, sums = backward(
        nd, nc, f, x, w_out
    )[:8]
    place = dp * nc + ctx
    norms_grad = lax.dynamic_index_in_dim(sums[:4].reshape(4, nd * nc, -1), place, 1, keepdims=False)
    bias = sums[4:, : 3 * width // nd].reshape(nd, 3, -1).transpose(1, 0, 2)

    result, tokens_grad, *grads = widen(
        [
            (result, rows, BF16),
            (tokens_grad, rows, F32),
            *[(g, g.shape[0], F32) for g in (g_qkv, g_gate, g_up)],
            (g_down, w_down.shape[0] // nc, F32),
            (g_out, w_out.shape[0] // nc, F32),
        ]
    )
    grad_qkv, grad_gate, grad_up, grad_down, grad_out = grads
    return (
        result.reshape(tokens.shape),
        tokens_grad.reshape(tokens.shape),
        grad_qkv,
        take(bias.reshape(nd * nc, -1), place),
        grad_out,
        grad_gate,
        grad_up,
        grad_down,
        norms_grad,
    )


def solution(mesh):
    blocks = P("dp", "ctx", None, None, None)
    owned = P(("dp", "ctx"), None)
    return jax.shard_map(
        shards,
        mesh=mesh,
        in_specs=(
            blocks,
            blocks,
            P("dp", None),
            P("dp"),
            P("dp", None),
            P("dp", None),
            P("dp", None),
            P("dp", None),
            P(None, "dp"),
        ),
        out_specs=(
            blocks,
            blocks,
            owned,
            P(("dp", "ctx")),
            owned,
            owned,
            owned,
            owned,
            P(None, ("dp", "ctx")),
        ),
        check_vma=False,
    )
```

```python
import jax
import jax.numpy as jnp
import numpy as np
from jax import lax
from jax.experimental import pallas as pl
from jax.experimental.pallas import tpu as pltpu
from jax.sharding import PartitionSpec as P

HEADS = 32
HDIM = 64
ROT = 16
MESH = pl.DeviceIdType.MESH
F32 = jnp.float32
BF16 = jnp.bfloat16
VMEM_BYTES = 63 * 1024 * 1024


def normalize_rows(field):
    centre = field - jnp.mean(field, axis=-1, keepdims=True)
    inverse = lax.rsqrt(jnp.mean(centre * centre, axis=-1, keepdims=True) + 1e-05)
    return (centre * inverse, inverse)


def norm_reverse(incoming, gain, scaled, inverse):
    inner = incoming * gain
    return inverse * (
        inner
        - jnp.mean(inner, axis=-1, keepdims=True)
        - scaled * jnp.mean(inner * scaled, axis=-1, keepdims=True)
    )


def last_dims(a, b):
    return lax.dot_general(a, b, (((1,), (1,)), ((), ())), preferred_element_type=F32)


def first_dims(a, b):
    return lax.dot_general(a, b, (((0,), (0,)), ((), ())), preferred_element_type=F32)


def plain(a, b):
    return lax.dot_general(a, b, (((1,), (0,)), ((), ())), preferred_element_type=F32)


def attention_shapes(length):
    block = min(256 if length <= 1024 else 128, length)
    segments = min(4, length // block)
    return block, segments, length // block // segments


def head_columns(heads, what, head):
    at = (what * heads + head) * HDIM
    return slice(at, at + HDIM)


def causal(scores, first_query):
    keys = lax.broadcasted_iota(jnp.int32, scores.shape, 0)
    queries = lax.broadcasted_iota(jnp.int32, scores.shape, 1) + first_query
    return jnp.where(keys <= queries, scores, -1e30)


def flip_one(i):
    return i + 1 - 2 * (i % 2)


def flip_bit(i, bit):
    return i + (1 << bit) - (2 << bit) * ((i // (1 << bit)) % 2)


def flip_bits(i, mask):
    for bit in range(mask.bit_length()):
        if mask >> bit & 1:
            i = flip_bit(i, bit)
    return i


def quarter_of(left, device, parts=4):
    n = left.shape[-2] // parts
    return pl.ds(pl.multiple_of(device * n, 16), n)


def first_cut(hidden):
    return min(1024, hidden)


def swapped_cut(hidden):
    return min(512, hidden)


def step_orders(nc):
    usual = list(range(nc.bit_length() - 1))
    return usual, [1, 0] + usual[2:]


def spread(mask, order):
    return sum((mask >> i & 1) << bit for i, bit in enumerate(order))


def halves(start, size):
    return pl.ds(pl.multiple_of(start, 64), size)


def lanes(start, size):
    return pl.ds(pl.multiple_of(start, 128), size)


class Copies:
    def __init__(self, send, recv, local):
        self.send, self.recv, self.local = send, recv, local
        self.remotes, self.locals, self.left = [], [], []

    def to(self, device, src, dst):
        at = len(self.remotes)
        copy = pltpu.make_async_remote_copy(
            src_ref=src,
            dst_ref=dst,
            send_sem=self.send.at[at],
            recv_sem=self.recv.at[at],
            device_id=device,
            device_id_type=MESH,
        )
        copy.start()
        self.remotes.append(copy)
        self.left.append(copy)
        return copy

    def gone(self, *copies):
        for copy in copies:
            copy.wait_send()
            self.left = [other for other in self.left if other is not copy]

    def here(self, src, dst):
        copy = pltpu.make_async_copy(src, dst, self.local.at[len(self.locals)])
        copy.start()
        self.locals.append(copy)
        return copy


def meet(axis_sizes):
    barrier = pltpu.get_barrier_semaphore()
    met = 0
    for axis, size in axis_sizes:
        me = lax.axis_index(axis)
        for k in range(1, size):
            pl.semaphore_signal(
                barrier, inc=1, device_id={axis: lax.rem(me + k, size)}, device_id_type=MESH
            )
            met += 1
    pl.semaphore_wait(barrier, met)


def attend(x_ref, o_ref, lse_ref, heads, head):
    length = x_ref.shape[0]
    block, segments, inner = attention_shapes(length)
    q_at, k_at, v_at = (head_columns(heads, i, head) for i in range(3))
    for segment in range(segments):
        count = (segment + 1) * inner * block
        keys = x_ref[:count, k_at]
        values = x_ref[:count, v_at]

        def step(i, _):
            start = pl.multiple_of((segment * inner + i) * block, block)
            query = x_ref[pl.ds(start, block), q_at] * 0.125
            scores = causal(last_dims(keys, query), start)
            top = jnp.max(scores, axis=0, keepdims=True)
            expo = jnp.exp(scores - top)
            total = jnp.sum(expo, axis=0, keepdims=True)
            mixed = first_dims(values, expo.astype(BF16)) / total
            o_ref[pl.ds(start, block), head * HDIM : (head + 1) * HDIM] = mixed.T.astype(BF16)
            lse_ref[head : head + 1, pl.ds(start, block)] = top + jnp.log(total)
            return 0

        if inner == 1:
            step(0, 0)
        else:
            lax.fori_loop(0, inner, step, 0)


def rotate_pair(u, keep, sine):
    lane = lax.broadcasted_iota(jnp.int32, u.shape, 1) % HDIM
    other = jnp.where(lane < ROT // 2, pltpu.roll(u, 128 - ROT // 2, 1), pltpu.roll(u, ROT // 2, 1))
    return u * keep + other * sine


def rotary_pair_tables(length):
    pairs = ROT // 2
    inverse = np.power(np.float32(10000.0), -np.arange(pairs, dtype=np.float32) / np.float32(pairs))
    angle = np.arange(length, dtype=np.float32)[:, None] * inverse.astype(np.float32)[None, :]
    cosine, sine = np.cos(angle), np.sin(angle)
    keep = np.concatenate([cosine, cosine, np.ones((length, HDIM - ROT), np.float32)], axis=1)
    signed = np.concatenate([-sine, sine, np.zeros((length, HDIM - ROT), np.float32)], axis=1)
    return np.tile(keep, (1, 2)).astype(np.float32), np.tile(signed, (1, 2)).astype(np.float32)


def tiles(total, size):
    return [(at, min(size, total - at)) for at in range(0, total, size)]


def over_tiles(total, size, step):
    whole = total // size
    if whole:

        def run(i, _):
            step(pl.multiple_of(i * size, size), size)
            return 0

        lax.fori_loop(0, whole, run, 0)
    if total % size:
        step(whole * size, total % size)


def turn_block(block, left, source, nd, nc):
    rows, width = block.shape
    part = width // (nd * nc)
    here = lanes(source * rows, rows)
    for at in range(0, width, 128):
        turned = block[:, at : at + 128].T
        for i in range(0, 128, part):
            d, c = (at + i) // (part * nc), (at + i) // part % nc
            left[c, d * part : (d + 1) * part, here] = turned[i : i + part]


def forward(nd, nc, tokens, cotangent, small, w_qkv, w_gate, w_up, w_out, w_down):
    rows, width = tokens.shape
    half = rows // 2
    many = nd * rows
    length = 2 * nc * half
    depth = w_qkv.shape[0]
    quarter = depth // 4
    heads_here = HEADS // nd
    groups = nc // nd
    heads = heads_here // groups
    span = heads * HDIM
    cols = heads_here * HDIM
    hidden = w_gate.shape[1] // nd
    down = w_down.shape[0]
    share_down = down // nc
    padded = share_down + -share_down % 16
    keep, sine = rotary_pair_tables(length)

    def body(
        tok_i, cot_i, small_i, wq_i, wg_i, wu_i, wo_i, wd_i, keep_i, sine_i,
        h1_o, dy_o, wq_o, seq_o, lse_o, mixed_o, r1_o, h2_o, m_o, dgu_o, pout_o, pdh2_o, small_o,
        dyp_o, mp_o, h2p_o, gatep_o, upz_o,
        tok, dy, sm, wq, h1, qkv, seq, lse, o, mixed, wo, part, ra, rb, r1, h2, wgu, wd, m, dgu,
        turns, left1, left2, m_t, mixed_t, dyp, send, recv, local,
    ):
        dp, ctx = lax.axis_index("dp"), lax.axis_index("ctx")
        near, across, far = flip_one(dp), (dp + 2) % nd, nd - 1 - dp
        spot = ctx % 4
        sides = [{"ctx": flip_bit(ctx, bit)} for bit in range(2)]
        links = Copies(send, recv, local)
        blocks = lambda ref, b: ref.at[halves(b * rows, rows)]

        get_tok = links.here(tok_i, blocks(tok, dp))
        get_turns = [
            links.here(table.at[halves(block * half, half)], turns.at[t, pl.ds(i * half, half)])
            for t, table in enumerate((keep_i, sine_i))
            for i, block in enumerate((ctx, 2 * nc - 1 - ctx))
        ]
        get_small = links.here(small_i, sm.at[dp])
        get_wq = [
            links.here(
                wq_i.at[:, lanes(j * width + dp * cols, cols)],
                wq.at[halves(dp * depth, depth), pl.ds(j * cols, cols)],
            )
            for j in range(3)
        ]
        meet((("dp", nd), ("ctx", nc)))

        def columns(w_i, w, e, at, n, to, which):
            first, size = (0, depth) if which is None else (which * quarter, quarter)
            return links.to(
                {"dp": e},
                w_i.at[halves(first, size), lanes(at, n)],
                w.at[halves(dp * depth + first, size), pl.ds(to, n)],
            )

        def share(w, copies, source):
            for copy in copies:
                copy.wait_recv()
            block = w.at[halves(source * depth + spot * quarter, quarter)]
            return [links.to(side, block, block) for side in sides]

        def cross(w, shared, source):
            passed = []
            for bit in range(2):
                shared[bit].wait_recv()
                start = source * depth + flip_bit(spot, bit) * quarter + bit * (quarter // 2)
                block = w.at[halves(start, quarter // 2)]
                passed.append(links.to(sides[1 - bit], block, block))
            return passed

        def qkv_columns(e, which):
            return [
                columns(wq_i, wq, e, j * width + e * cols, cols, j * cols, which) for j in range(3)
            ]

        def hidden_columns(e, which):
            return [
                columns(w_i, wgu, e, e * hidden, hidden, i * hidden, which)
                for i, w_i in enumerate((wg_i, wu_i))
            ]

        send_small = [links.to({"dp": e}, small_i, sm.at[dp]) for e in (near, across, far)]
        wq_x = [qkv_columns(e, spot) for e in (across, far)]
        send_tok = [links.to({"dp": e}, tok_i, blocks(tok, dp)) for e in (near, across)]
        wq_near = qkv_columns(near, None)
        send_dyp = [links.to(sides[1], cot_i, blocks(dyp, dp))]
        wgu_x = [hidden_columns(e, spot) for e in (far, across)]
        get_wo = links.here(wo_i, wo)
        get_wd = links.here(wd_i, wd)
        get_dy = links.here(cot_i, blocks(dy, dp))
        get_wgu = [
            links.here(
                w_i.at[:, lanes(dp * hidden, hidden)],
                wgu.at[halves(dp * depth, depth), pl.ds(i * hidden, hidden)],
            )
            for i, w_i in enumerate((wg_i, wu_i))
        ]

        get_small.wait()
        for copy in send_small:
            copy.wait_recv()

        def gain(row):
            lines = [
                sm[b, row * 4 + q : row * 4 + q + 1, :]
                for b in range(nd)
                for q in range(width // nd // 128)
            ]
            return jnp.concatenate(lines, axis=1)

        def first_norm(b):
            at = halves(b * rows, rows)
            hat, _ = normalize_rows(tok[at, :].astype(F32))
            h1[at, :] = (hat * gain(0) + gain(1)).astype(BF16)

        def turn_first(b):
            turn_block(h1[halves(b * rows, rows), :], left1, b, nd, nc)

        get_tok.wait()
        wq_s = [share(wq, copies, e) for copies, e in zip(wq_x, (across, far))]
        first_norm(dp)
        send_tok[0].wait_recv()
        first_norm(near)
        wq_c = cross(wq, wq_s[0], across)
        send_tok[1].wait_recv()
        forward_tok = links.to({"dp": near}, blocks(tok, across), blocks(tok, across))
        wq_c += cross(wq, wq_s[1], far)
        first_norm(across)
        forward_tok.wait_recv()
        first_norm(far)
        wgu_d = [c for e in (across, far) for c in hidden_columns(e, 3 - spot)]
        wgu_near = hidden_columns(near, None)
        send_dy = [links.to({"dp": e}, cot_i, blocks(dy, dp)) for e in (near, across)]
        put_small = links.here(sm, small_o)
        for copy in get_wq + get_turns:
            copy.wait()
        for copy in wq_near + wq_c:
            copy.wait_recv()
        put_wq = links.here(wq, wq_o)

        for at, n in tiles(3 * cols, 256):
            j = at // cols
            acc = plain(h1[...], wq[:, at : at + n])
            for q in range(n // 128):
                first = at % cols + q * 128
                line = (j * width + dp * cols + first) // 128
                per = 3 * width // nd // 128
                bias = sm[line // per, pl.ds(4 * (width // nd) // 128 + line % per, 1), :]
                for s in range(nd):
                    u = acc[s * rows : (s + 1) * rows, q * 128 : (q + 1) * 128] + bias
                    if j < 2:
                        u = rotate_pair(u, turns[0], turns[1])
                    u = u.astype(BF16)
                    if heads > 1:
                        g, off = first // span, first % span
                        qkv[g, s * rows : (s + 1) * rows, j * span + off : j * span + off + 128] = u
                    else:
                        for i in range(2):
                            qkv[
                                first // HDIM + i, s * rows : (s + 1) * rows, j * HDIM : (j + 1) * HDIM
                            ] = u[:, i * HDIM : (i + 1) * HDIM]

        mirror = 2 * nc - 1 - ctx
        go = []
        for k in range(1, nc):
            peer = lax.rem(ctx + k, nc)
            s, g = peer // groups, peer % groups
            for i, block in enumerate((ctx, mirror)):
                go.append(
                    links.to(
                        {"ctx": peer},
                        qkv.at[g, halves(s * rows + i * half, half)],
                        seq.at[halves(block * half, half)],
                    )
                )
        s, g = ctx // groups, ctx % groups
        stay = [
            links.here(
                qkv.at[g, halves(s * rows + i * half, half)], seq.at[halves(block * half, half)]
            )
            for i, block in enumerate((ctx, mirror))
        ]
        for b in range(nd):
            turn_first(b)
        put_h1 = links.here(left1, h1_o)
        for copy in stay:
            copy.wait()
        for copy in go:
            copy.wait_recv()
        put_seq = links.here(seq, seq_o)
        put_h1.wait()
        back, stay = [], []
        step = min(heads, 2)
        for head in range(heads):
            attend(seq, o, lse, heads, head)
            if (head + 1) % step:
                continue
            here = pl.ds((head + 1 - step) * HDIM, step * HDIM)
            for k in range(nc):
                peer = lax.rem(ctx + k, nc)
                for i, block in enumerate((peer, 2 * nc - 1 - peer)):
                    src = o.at[halves(block * half, half), here]
                    dst = mixed.at[g, halves(s * rows + i * half, half), here]
                    if k:
                        back.append(links.to({"ctx": peer}, src, dst))
                    else:
                        stay.append(links.here(src, dst))
        wgu_far = share(wgu, wgu_x[0], far)
        wgu_near2 = share(wgu, wgu_x[1], across)
        put_lse = links.here(lse, lse_o)
        get_wo.wait()
        for copy in stay:
            copy.wait()
        for copy in back:
            copy.wait_recv()

        def out_tile(at, n):
            acc = plain(mixed[0], wo[0:span, pl.ds(at, n)])
            for i in range(1, groups):
                acc += plain(mixed[i], wo[i * span : (i + 1) * span, pl.ds(at, n)])
            part[:, pl.ds(at, n)] = acc.astype(BF16)

        over_tiles(width, 512, out_tile)

        to_near = [
            links.to({"dp": near}, blocks(part, far), blocks(ra, 0)),
            links.to({"dp": near}, blocks(part, near), blocks(ra, 1)),
        ]
        for i in range(groups):
            mixed_t[i * span : (i + 1) * span, :] = mixed[i].T
        put_mixed = links.here(mixed_t, mixed_o)
        to_near[0].wait_recv()
        across_at = halves(across * rows, rows)
        part[across_at, :] = (part[across_at, :].astype(F32) + ra[:rows, :].astype(F32)).astype(BF16)
        to_across = links.to({"dp": across}, blocks(part, across), rb)
        send_dy[1].wait_recv()
        forward_dy = links.to({"dp": near}, blocks(dy, across), blocks(dy, across))
        to_near[1].wait_recv()
        own_at = halves(dp * rows, rows)
        r1[...] = tok[own_at, :].astype(F32) + (
            part[own_at, :].astype(F32) + ra[rows:, :].astype(F32)
        )
        to_across.wait_recv()
        r1[...] += rb[...].astype(F32)
        put_r1 = links.here(r1, r1_o)
        hat, _ = normalize_rows(r1[...])
        h2[own_at, :] = (hat * gain(2) + gain(3)).astype(BF16)
        send_h2 = [links.to({"dp": e}, blocks(h2, dp), blocks(h2, dp)) for e in (near, across)]
        send_dyp[0].wait_recv()
        share_dyp = [links.to({"dp": e}, blocks(dyp, dp), blocks(dyp, dp)) for e in (near, across)]
        turn_block(h2[own_at, :], left2, dp, nd, nc)
        send_h2[0].wait_recv()
        turn_block(h2[halves(near * rows, rows), :], left2, near, nd, nc)
        send_h2[1].wait_recv()
        forward_h2 = links.to({"dp": near}, blocks(h2, across), blocks(h2, across))
        turn_block(h2[halves(across * rows, rows), :], left2, across, nd, nc)
        get_wd.wait()
        get_dy.wait()
        for copy in get_wgu:
            copy.wait()
        for copy in wgu_near + wgu_far + wgu_near2 + wgu_d + [send_dy[0], forward_dy, forward_h2]:
            copy.wait_recv()
        turn_block(h2[halves(far * rows, rows), :], left2, far, nd, nc)
        put_h2 = links.here(left2, h2_o)
        put_dy = links.here(dy, dy_o)

        spare = nc // 2
        send_left = [
            links.to(
                sides[bit],
                left2.at[
                    flip_bits(flip_bit(ctx, bit), spread(2 * j, step_orders(nc)[bit])),
                    quarter_of(left2, dp),
                ],
                left1.at[bit * spare + j, quarter_of(left2, dp)],
            )
            for bit in range(2)
            for j in range(spare)
        ]
        send_gate = []
        def hidden_tile(at, n):
            here = pl.ds(at, n)
            gate = plain(h2[...], wgu[:, here])
            up = plain(h2[...], wgu[:, pl.ds(hidden + at, n)])
            dm = last_dims(dy[...], wd[here, :])
            sig = jax.nn.sigmoid(gate)
            m[:, here] = (gate * sig * up).astype(BF16)
            dgu[:, here] = (dm * up * sig * (1.0 + gate * (1.0 - sig))).astype(BF16)
            dgu[:, pl.ds(hidden + at, n)] = (dm * gate * sig).astype(BF16)

        if padded != share_down:
            m[:, hidden:] = jnp.zeros((many, padded - share_down), BF16)
        for at, n in tiles(hidden, 512):
            over_tiles(n, 256, lambda i, size, at=at: hidden_tile(at + i, size))
            here = pl.ds(at, n)
            if at + n <= first_cut(hidden):
                send_gate.append(links.to(sides[0], dgu.at[:, here], gatep_o.at[:, here]))
            if at + n <= swapped_cut(hidden):
                there = pl.ds(hidden + at, n)
                send_gate.append(links.to(sides[1], dgu.at[:, there], upz_o.at[:, here]))
        for c in range(nc):
            m_t[c] = m[:, c * share_down : c * share_down + padded].T
        put_m = links.here(m_t, m_o)

        put_dgu = links.here(dgu, dgu_o)
        send_m = []
        for j in range(nc // 2):
            owner = flip_bits(flip_bit(ctx, 1), spread(2 * j, step_orders(nc)[1]))
            send_m.append(links.to(sides[1], m_t.at[owner], mp_o.at[j]))
        share_dyp[1].wait_recv()
        forward_dyp = links.to({"dp": near}, blocks(dyp, across), blocks(dyp, across))
        for copy in send_left:
            copy.wait_recv()
        own_left = left1.at[:, quarter_of(left2, dp)]
        share_left = [links.to({"dp": e}, own_left, own_left) for e in (near, across)]

        def dh2_tile(at, n):
            here = pl.ds(at, n)
            h1[:, here] = last_dims(dgu[...], wgu[here, :]).astype(BF16)

        over_tiles(width, 256, dh2_tile)
        put_pdh2 = links.here(h1, pdh2_o)
        links.gone(*send_tok, forward_tok)

        def result_tile(at, n):
            here = pl.ds(at, n)
            tok[:, here] = plain(m[:, :hidden], wd[:, here]).astype(BF16)

        share_left[1].wait_recv()
        other_left = left1.at[:, quarter_of(left2, across)]
        forward_left = links.to({"dp": near}, other_left, other_left)
        over_tiles(width, 256, result_tile)
        put_pout = links.here(tok, pout_o)
        for copy in (share_dyp[0], forward_dyp, share_left[0], forward_left):
            copy.wait_recv()
        put_other = [links.here(dyp, dyp_o), links.here(left1, h2p_o)]
        for copy in send_m + send_gate:
            copy.wait_recv()

        links.gone(*links.left)
        for copy in (
            *put_other, put_small, put_wq, put_seq, put_lse, put_mixed, put_r1, put_h2, put_dy, put_m, put_dgu,
            put_pdh2, put_pout,
        ):
            copy.wait()

    anywhere = pl.BlockSpec(memory_space=pl.ANY)
    shape = jax.ShapeDtypeStruct
    remotes = 64 + 7 * nc
    outs = dict(
        h1=((nc, width // nc, many), BF16),
        dy=((many, width), BF16),
        wq=((width, 3 * cols), BF16),
        seq=((length, 3 * span), BF16),
        lse=((heads, length), F32),
        mixed=((cols, many), BF16),
        r1=((rows, width), F32),
        h2=((nc, width // nc, many), BF16),
        m=((nc, padded, many), BF16),
        dgu=((many, 2 * hidden), BF16),
        pout=((many, width), BF16),
        pdh2=((many, width), BF16),
        small=((nd,) + small.shape, F32),
        dyp=((many, width), BF16),
        mp=((nc // 2, padded, many), BF16),
        h2p=((nc, width // nc, many), BF16),
        gatep=((many, first_cut(hidden)), BF16),
        upz=((many, swapped_cut(hidden)), BF16),
    )
    scratch = [
        ((many, width), BF16),
        ((many, width), BF16),
        ((nd,) + small.shape, F32),
        ((width, 3 * cols), BF16),
        ((many, width), BF16),
        ((groups, many, 3 * span), BF16),
        ((length, 3 * span), BF16),
        ((heads, length), F32),
        ((length, span), BF16),
        ((groups, many, span), BF16),
        ((cols, width), BF16),
        ((many, width), BF16),
        ((2 * rows, width), BF16),
        ((rows, width), BF16),
        ((rows, width), F32),
        ((many, width), BF16),
        ((width, 2 * hidden), BF16),
        ((down, width), BF16),
        ((many, hidden + padded - share_down), BF16),
        ((many, 2 * hidden), BF16),
        ((2, rows, 128), F32),
        ((nc, width // nc, many), BF16),
        ((nc, width // nc, many), BF16),
        ((nc, padded, many), BF16),
        ((cols, many), BF16),
        ((many, width), BF16),
    ]
    results = pl.pallas_call(
        body,
        out_shape=[shape(*o) for o in outs.values()],
        in_specs=[anywhere] * 10,
        out_specs=[anywhere] * len(outs),
        scratch_shapes=[pltpu.VMEM(*s) for s in scratch]
        + [
            pltpu.SemaphoreType.DMA((remotes,)),
            pltpu.SemaphoreType.DMA((remotes,)),
            pltpu.SemaphoreType.DMA((40,)),
        ],
        compiler_params=pltpu.CompilerParams(
            collective_id=0, has_side_effects=True, vmem_limit_bytes=VMEM_BYTES
        ),
    )(tokens, cotangent, small, w_qkv, w_gate, w_up, w_out, w_down, keep, sine)
    return dict(zip(outs, results))


def attend_back(x_ref, lse_ref, do_ref, d_ref, heads, head):
    length = x_ref.shape[0]
    block, segments, inner = attention_shapes(length)
    q_at, k_at, v_at = (head_columns(heads, i, head) for i in range(3))
    o_at = slice(head * HDIM, (head + 1) * HDIM)
    for segment in range(segments):
        count = (segment + 1) * inner * block
        keys = x_ref[:count, k_at]
        values = x_ref[:count, v_at]

        def step(i, _):
            start = pl.multiple_of((segment * inner + i) * block, block)
            query = x_ref[pl.ds(start, block), q_at] * 0.125
            dout = do_ref[pl.ds(start, block), o_at]
            scores = causal(last_dims(keys, query), start)
            probs = jnp.exp(scores - lse_ref[head : head + 1, pl.ds(start, block)])
            d_probs = last_dims(values, dout)
            centre = jnp.sum(probs * d_probs, axis=0, keepdims=True)
            d_scores = (probs * (d_probs - centre)).astype(BF16)
            d_ref[:count, v_at] += plain(probs.astype(BF16), dout)
            d_ref[:count, k_at] += plain(d_scores, query)
            d_ref[pl.ds(start, block), q_at] = first_dims(keys, d_scores).T * 0.125
            return 0

        if inner == 1:
            step(0, 0)
        else:
            lax.fori_loop(0, inner, step, 0)


class GroupSum:
    def __init__(self, links, dp, nd, rows, part, ra, rb):
        self.links, self.rows = links, rows
        self.part, self.ra, self.rb = part, ra, rb
        self.near, self.across, self.far = flip_one(dp), (dp + 2) % nd, nd - 1 - dp
        self.dp = dp
        block = lambda ref, b: ref.at[halves(b * rows, rows)]
        self.a = [
            links.to({"dp": self.near}, block(part, self.far), block(ra, 0)),
            links.to({"dp": self.near}, block(part, self.near), block(ra, 1)),
        ]

    def middle(self):
        rows, at = self.rows, halves(self.across * self.rows, self.rows)
        self.a[0].wait_recv()
        self.part[at, :] = (
            self.part[at, :].astype(F32) + self.ra[:rows, :].astype(F32)
        ).astype(BF16)
        self.b = self.links.to({"dp": self.across}, self.part.at[at], self.rb)

    def total(self):
        rows, at = self.rows, halves(self.dp * self.rows, self.rows)
        self.a[1].wait_recv()
        self.b.wait_recv()
        return (
            self.part[at, :].astype(F32)
            + self.ra[rows:, :].astype(F32)
            + self.rb[...].astype(F32)
        )


class Gradient:
    def __init__(self, links, ctx, bits, left, right, slots, landing, stage):
        self.links, self.ctx, self.bits, self.nc = links, ctx, bits, 1 << len(bits)
        nc = self.nc
        self.left, self.right, self.slots = left, right, slots
        self.landing = landing
        self.stage = stage.at[pl.ds(0, slots.shape[1]), pl.ds(0, slots.shape[2])]
        self.sent = {}
        low = lambda j: (j & -j) or nc
        self.order = sorted(range(nc // 2), key=lambda j: (low(j), low(j & (j - 1))))

    def _landing(self, bit, j):
        base = sum(self.nc >> (b + 1) for b in range(1, bit))
        return self.landing.at[base + (j >> bit)]

    def compute(self, send=True):
        for j in self.order:
            self.slot(j, send)

    def start(self, part):
        for j in self.half(part):
            self._pass(1, j)

    def half(self, part):
        odd = [j for j in self.order if j % 2]
        return odd[part * len(odd) // 2 : (part + 1) * len(odd) // 2]

    def add_half(self, part):
        for j in self.half(part):
            self.add_slot(1, j - 1)

    def slot(self, j, send=True):
        mine, other = self.left[0][j], self.left[1][j]

        def step(at, n):
            here = pl.ds(at, n)
            acc = plain(mine, self.right[0][:, here]) + plain(other, self.right[1][:, here])
            self.slots[j, :, here] = acc.astype(BF16)

        over_tiles(self.slots.shape[2], 512, step)
        if send:
            self._pass(1, j)

    def _pass(self, bit, j):
        low = j & -j
        if j and low == 1 << (bit - 1):
            self.sent[bit, j] = self.links.to(
                {"ctx": flip_bit(self.ctx, self.bits[bit])},
                self.slots.at[j],
                self._landing(bit, j - low),
            )

    def add(self, bit):
        for j in self.order:
            if j % (1 << bit) == 0:
                self.add_slot(bit, j)

    def add_slot(self, bit, j):
        self.sent[bit, j + (1 << (bit - 1))].wait_recv()
        self.links.here(self._landing(bit, j), self.stage).wait()

        def step(at, n):
            here = pl.ds(at, n)
            acc = self.slots[j, :, here].astype(F32) + self.stage[:, here].astype(F32)
            self.slots[j, :, here] = acc.astype(BF16)

        over_tiles(self.slots.shape[2], 512, step)
        self._pass(bit + 1, j)


def backward(nd, nc, f, tokens, w_out):
    rows, width = tokens.shape
    half = rows // 2
    many = nd * rows
    length, wide = f["seq"].shape
    heads = f["lse"].shape[0]
    span = heads * HDIM
    groups = nc // nd
    cols = groups * span
    hidden = f["dgu"].shape[1] // 2
    slots = nc // 2
    share = width // (nd * nc)
    tall = {"gu": nd * share, "down": f["m"].shape[1], "out": cols // nc, "qkv": nd * share}
    flat = {"gu": 2 * hidden, "down": width, "out": width, "qkv": 3 * cols}
    cut = first_cut(hidden)
    cut_z = swapped_cut(hidden)
    ranges = [(0, cut // 2), (cut // 2, cut - cut // 2)]
    ranges += [(hidden + cut_z, hidden - cut_z), (cut, hidden - cut)]
    range_z = (hidden, cut_z)
    names = ("down", "gu", "qkv", "out")
    bits = nc.bit_length() - 1
    keep_t, sine_t = rotary_pair_tables(length)
    chunk = length if length <= 1024 else 256
    strip = 256 if length <= 1024 else 128
    mixed_left = f["mixed"].reshape(nc, cols // nc, many)

    def body(
        h2_l, h2p_l, gatep_i, upz_i, m_l, mp_l, mixed_l, h1_l, dy_i, dyp_i, dgu_i, wq_i, seq_i, lse_i, r1_i, pdh2_i, pout_i,
        small_i, tok_i, wo_i, keep_i, sine_i,
        out_o, tg_o, gate_o, up_o, qkv_o, down_o, out_g_o, sums_o,
        land_down, land_gu, land_qkv, land_out,
        l_gu, l_up, l_down, l_out, l_qkv, dgu, dgup, dy, dyp, da, dq, dqp,
        s_down, s_gu, s_qkv, s_out, stage,
        part, ra, rb, r1, dr1, x, sm, wq, wo, seq, lse,
        dmix, dseq, dx, keep, sine, dback, sums, sums_in,
        send, recv, local, free,
    ):
        dp, ctx = lax.axis_index("dp"), lax.axis_index("ctx")
        near, across, far = flip_one(dp), (dp + 2) % nd, nd - 1 - dp
        links = Copies(send, recv, local)
        blocks = lambda ref, b: ref.at[halves(b * rows, rows)]
        own_at = halves(dp * rows, rows)
        beside = {"ctx": flip_bit(ctx, 0)}

        usual, swapped = step_orders(nc)

        def get_left(left_i, left, order=usual):
            return [
                links.here(left_i.at[flip_bits(ctx, spread(2 * j, order))], left.at[0, j])
                for j in range(slots)
            ]

        get_part = links.here(pdh2_i, part)
        get_gu = get_left(h2_l, l_gu)
        get_gu += [
            links.here(a, b)
            for a, b in (
                (h2p_l.at[pl.ds(0, slots)], l_gu.at[1]),
                (dgu_i, dgu),
                (gatep_i, dgup.at[:, pl.ds(0, cut)]),
            )
        ]
        get_up = get_left(h2_l, l_up, swapped)
        get_up += [
            links.here(a, b)
            for a, b in ((h2p_l.at[pl.ds(slots, slots)], l_up.at[1]), (upz_i, dgup.at[:, pl.ds(*range_z)]))
        ]
        get_down = get_left(m_l, l_down, swapped)
        get_down += [
            links.here(a, b) for a, b in ((mp_l, l_down.at[1]), (dy_i, dy), (dyp_i, dyp))
        ]
        get_first = [links.here(a, b) for a, b in ((r1_i, r1), (small_i, sm))]
        get_wo = links.here(wo_i, wo)
        get_attn = [links.here(a, b) for a, b in ((seq_i, seq), (lse_i, lse))]
        get_late = get_left(h1_l, l_qkv) + get_left(mixed_l, l_out) + [links.here(tok_i, x)]

        def tables(c):
            at = pl.ds(c * chunk, chunk)
            return [links.here(a.at[at], b) for a, b in ((keep_i, keep), (sine_i, sine))]

        get_tables = tables(0)

        def strips(i):
            return links.here(wq_i.at[pl.ds(i * strip, strip)], wq.at[i % 2])

        get_wq = [strips(0), strips(1)]

        def gain(row):
            lines = [
                sm[b, row * 4 + q : row * 4 + q + 1, :]
                for b in range(nd)
                for q in range(width // nd // 128)
            ]
            return jnp.concatenate(lines, axis=1)

        down = Gradient(links, ctx, swapped, l_down, (dy, dyp), s_down, land_down, stage)
        gu = []
        for at, n in ranges + [range_z]:
            here = pl.ds(at, n)
            order, left = (swapped, l_up) if at == hidden else (usual, l_gu)
            gu.append(
                Gradient(
                    links, ctx, order, left, (dgu.at[:, here], dgup.at[:, here]),
                    s_gu.at[:, :, here], land_gu.at[:, :, here], stage,
                )
            )
        up = gu.pop()
        qkv = []
        for j in range(3):
            at = pl.ds(j * cols, cols)
            qkv.append(
                Gradient(
                    links, ctx, usual, l_qkv, (dq.at[:, at], dqp.at[:, at]),
                    s_qkv.at[:, :, at], land_qkv.at[:, :, at], stage,
                )
            )
        out = Gradient(links, ctx, usual, l_out, (da, dyp), s_out, land_out, stage)

        meet((("dp", nd), ("ctx", nc)))
        get_part.wait()
        sum2 = GroupSum(links, dp, nd, rows, part, ra, rb)

        def send_right(i):
            here = pl.ds(*ranges[i])
            return links.to(beside, dgu_i.at[:, here], dgup.at[:, here])

        right_gu = [None, None, send_right(2)]
        for copy in get_gu:
            copy.wait()
        gu[0].slot(gu[0].order[0])
        sum2.middle()
        for j in gu[0].order[1:]:
            gu[0].slot(j)
        for copy in get_first + get_down + get_up:
            copy.wait()
        up.compute()
        gu[1].compute()
        down.compute(send=False)
        for i, device in enumerate((beside, {"dp": near}, {"dp": across})):
            pl.semaphore_signal(free.at[i], inc=1, device_id=device, device_id_type=MESH)

        dh2 = sum2.total()
        hat, inverse = normalize_rows(r1[...])
        dr1[...] = dy[own_at, :].astype(F32) + norm_reverse(dh2, gain(2), hat, inverse)
        da[own_at, :] = dr1[...].astype(BF16)
        send_da = [links.to({"dp": e}, blocks(da, dp), blocks(da, dp)) for e in (near, across)]
        pl.semaphore_wait(free.at[0], 1)
        right_out = links.to(beside, blocks(da, dp), blocks(dyp, dp))
        sums[2:3, :] = jnp.sum(dh2 * hat, axis=0, keepdims=True)
        sums[3:4, :] = jnp.sum(dh2, axis=0, keepdims=True)
        dx[...] = jnp.zeros_like(dx)
        if bits > 1:
            gu[0].add(1)
        send_da[1].wait_recv()
        forward_da = links.to({"dp": near}, blocks(da, across), blocks(da, across))
        get_wo.wait()
        send_da[0].wait_recv()
        forward_da.wait_recv()

        for g in range(groups):
            dmix[g] = last_dims(da[...], wo[g * span : (g + 1) * span, :]).astype(BF16)
        mirror = 2 * nc - 1 - ctx
        go = []
        for k in range(1, nc):
            peer = lax.rem(ctx + k, nc)
            s, g = peer // groups, peer % groups
            for i, block in enumerate((ctx, mirror)):
                go.append(
                    links.to(
                        {"ctx": peer},
                        dmix.at[g, halves(s * rows + i * half, half)],
                        dseq.at[halves(block * half, half)],
                    )
                )
        s, g = ctx // groups, ctx % groups
        stay = [
            links.here(
                dmix.at[g, halves(s * rows + i * half, half)], dseq.at[halves(block * half, half)]
            )
            for i, block in enumerate((ctx, mirror))
        ]
        right_gu.append(send_right(3))

        left_qkv = [
            links.to(
                beside,
                h1_l.at[flip_bits(flip_bit(ctx, 0), 2 * j), quarter_of(l_qkv, dp)],
                l_qkv.at[1, j, quarter_of(l_qkv, dp)],
            )
            for j in range(slots)
        ]
        left_out = [
            links.to(beside, mixed_l.at[flip_bits(flip_bit(ctx, 0), 2 * j)], l_out.at[1, j])
            for j in range(slots)
        ]
        right_gu[2].wait_recv()
        gu[2].compute()
        if bits > 1:
            up.add(1)
            gu[1].add(1)

        def share_right():
            right_out.wait_recv()
            for i in (1, 2):
                pl.semaphore_wait(free.at[i], 1)
            block = blocks(dyp, dp)
            return [links.to({"dp": e}, block, block) for e in (near, across)]

        def share_left():
            for copy in left_qkv:
                copy.wait_recv()
            block = l_qkv.at[1, :, quarter_of(l_qkv, dp)]
            return [links.to({"dp": e}, block, block) for e in (near, across)]

        for copy in get_attn + stay:
            copy.wait()
        for copy in go:
            copy.wait_recv()
        down.start(0)
        shared_right = share_right()
        for head in range(heads):
            attend_back(seq, lse, dseq, dx, heads, head)
        for c in range(length // chunk):
            for copy in get_tables if c == 0 else tables(c):
                copy.wait()
            here = slice(c * chunk, (c + 1) * chunk)
            for at in range(0, wide, 128):
                n = min(128, wide - at)
                u = dx[here, at : at + n]
                if at < 2 * span:
                    u = rotate_pair(u, keep[...], -sine[...])
                seq[here, at : at + n] = u.astype(BF16)

        back = []
        for k in range(1, nc):
            peer = lax.rem(ctx + k, nc)
            for i, block in enumerate((peer, 2 * nc - 1 - peer)):
                back.append(
                    links.to(
                        {"ctx": peer},
                        seq.at[halves(block * half, half)],
                        dback.at[g, halves(s * rows + i * half, half)],
                    )
                )
        stay = [
            links.here(
                seq.at[halves(block * half, half)], dback.at[g, halves(s * rows + i * half, half)]
            )
            for i, block in enumerate((ctx, mirror))
        ]
        shared_left = share_left()
        shared_right[1].wait_recv()
        forward_right = links.to({"dp": near}, blocks(dyp, across), blocks(dyp, across))
        for copy in get_late:
            copy.wait()
        right_gu[3].wait_recv()
        gu[3].compute()
        shared_left[1].wait_recv()
        block = l_qkv.at[1, :, quarter_of(l_qkv, across)]
        forward_left = links.to({"dp": near}, block, block)
        for copy in left_out + [shared_right[0], forward_right]:
            copy.wait_recv()
        out.compute()
        for copy in stay:
            copy.wait()
        for copy in back:
            copy.wait_recv()
        for g_ in range(groups):
            for j in range(3):
                at = j * cols + g_ * span
                dq[:, at : at + span] = dback[g_, :, j * span : (j + 1) * span]
        right_qkv = []

        def send_qkv():
            here = pl.ds(len(right_qkv) * cols, cols)
            right_qkv.append(links.to(beside, dq.at[:, here], dqp.at[:, here]))

        send_qkv()
        if bits > 1:
            gu[2].add(1)
        send_qkv()
        down.add_half(0)
        links.gone(*sum2.a, sum2.b)
        for i in range(width // strip):
            get_wq[i].wait()
            part[:, i * strip : (i + 1) * strip] = last_dims(dq[...], wq[i % 2]).astype(BF16)
            if i + 2 < width // strip:
                get_wq.append(strips(i + 2))
        sum1 = GroupSum(links, dp, nd, rows, part, ra, rb)
        send_qkv()
        down.start(1)
        for copy in (shared_left[0], forward_left):
            copy.wait_recv()

        def compute_qkv(j):
            right_qkv[j].wait_recv()
            qkv[j].compute()

        compute_qkv(0)
        sum1.middle()
        if bits > 1:
            gu[3].add(1)
        sums[4:, :] = jnp.zeros((nd, width), F32)
        sums[pl.ds(4 + dp, 1), : 3 * cols] = jnp.sum(dq[...].astype(F32), axis=0, keepdims=True)

        arriving, put = [], []

        def to_owner(slots_ref, spans):
            for e in (near, across, far, dp):
                for dst, at, to, n, every in spans:
                    src = slots_ref.at[0, pl.ds(pl.multiple_of(e * share, 16), share), pl.ds(at, n)]
                    place = dst.at[:, lanes(to + dp * every, n)]
                    if e is dp:
                        put.append(links.here(src, place))
                    else:
                        arriving.append(links.to({"dp": e}, src, place))

        def close_gu(piece, span_of):
            for bit in range(2, bits):
                piece.add(bit)
            at, n = span_of
            for dst, base in ((gate_o, 0), (up_o, hidden)):
                first, last = max(at, base), min(at + n, base + hidden)
                if first < last:
                    to_owner(s_gu, ((dst, first, first - base, last - first, hidden),))

        def close_qkv(j):
            for bit in range(2, bits):
                qkv[j].add(bit)
            to_owner(s_qkv, ((qkv_o, j * cols, j * width, cols, cols),))

        compute_qkv(1)
        close_gu(gu[0], ranges[0])
        close_gu(up, range_z)
        if bits > 1:
            out.add(1)
        compute_qkv(2)

        dh1 = sum1.total()
        hat1, inverse1 = normalize_rows(x[...].astype(F32))
        sums[0:1, :] = jnp.sum(dh1 * hat1, axis=0, keepdims=True)
        sums[1:2, :] = jnp.sum(dh1, axis=0, keepdims=True)
        partners = [("dp", flip_bit(dp, b)) for b in range(nd.bit_length() - 1)]
        partners += [("ctx", flip_bit(ctx, b)) for b in range(bits)]
        sums_out = []

        def start_sums():
            i = len(sums_out)
            if i < len(partners):
                axis, device = partners[i]
                sums_out.append(links.to({axis: device}, sums, sums_in.at[i]))

        def end_sums():
            i = len(sums_out) - 1
            sums_out[i].wait_recv()
            links.gone(sums_out[i])
            sums[...] += sums_in[i]

        def next_sums():
            end_sums()
            start_sums()

        start_sums()
        dr1[...] += norm_reverse(dh1, gain(0), hat1, inverse1)
        put_tg = links.here(dr1, tg_o)
        links.gone(*sum1.a, sum1.b)
        get_pout = links.here(pout_i, part)
        next_sums()
        get_pout.wait()
        sum0 = GroupSum(links, dp, nd, rows, part, ra, rb)
        if bits > 1:
            qkv[0].add(1)
        close_gu(gu[1], ranges[1])
        next_sums()
        sum0.middle()
        next_sums()
        if bits > 1:
            qkv[1].add(1)
        x[...] = (r1[...] + sum0.total()).astype(BF16)
        put_out = links.here(x, out_o)
        for i in range(2, len(ranges)):
            close_gu(gu[i], ranges[i])
        if bits > 1:
            qkv[2].add(1)
        next_sums()
        down.add_half(1)
        for bit in range(2, bits):
            down.add(bit)
        put.append(links.here(s_down.at[0], down_o))
        for bit in range(2, bits):
            out.add(bit)
        put.append(links.here(s_out.at[0], out_g_o))
        close_qkv(0)
        close_qkv(1)
        while len(sums_out) < len(partners):
            next_sums()
        close_qkv(2)
        end_sums()
        put_sums = [links.here(sums, sums_o), put_tg, put_out]
        for copy in arriving:
            copy.wait_recv()
        links.gone(*links.left)
        for copy in put + put_sums:
            copy.wait()

    anywhere = pl.BlockSpec(memory_space=pl.ANY)
    shape = jax.ShapeDtypeStruct
    outs = [
        ((rows, width), BF16),
        ((rows, width), F32),
        ((share, nd * hidden), BF16),
        ((share, nd * hidden), BF16),
        ((share, 3 * width), BF16),
        ((tall["down"], width), BF16),
        ((tall["out"], width), BF16),
        ((4 + nd, width), F32),
        *[((max(1, slots - 1), tall[k], flat[k]), BF16) for k in names],
    ]
    scratch = [
        *[((2, slots, tall[k], many), BF16) for k in ("gu", "gu", "down", "out", "qkv")],
        ((many, 2 * hidden), BF16),
        ((many, 2 * hidden), BF16),
        ((many, width), BF16),
        ((many, width), BF16),
        ((many, width), BF16),
        ((many, 3 * cols), BF16),
        ((many, 3 * cols), BF16),
        *[((slots, tall[k], flat[k]), BF16) for k in names],
        ((max(tall.values()), width), BF16),
        ((many, width), BF16),
        ((2 * rows, width), BF16),
        ((rows, width), BF16),
        ((rows, width), F32),
        ((rows, width), F32),
        ((rows, width), BF16),
        (f["small"].shape, F32),
        ((2, strip, 3 * cols), BF16),
        ((cols, width), BF16),
        ((length, wide), BF16),
        ((heads, length), F32),
        ((groups, many, span), BF16),
        ((length, span), BF16),
        ((length, wide), F32),
        ((chunk, 128), F32),
        ((chunk, 128), F32),
        ((groups, many, wide), BF16),
        ((4 + nd, width), F32),
        ((bits + nd.bit_length() - 1, 4 + nd, width), F32),
    ]
    remotes = 64 + 4 * nc + 7 * nc
    return pl.pallas_call(
        body,
        out_shape=[shape(*o) for o in outs],
        in_specs=[anywhere] * 22,
        out_specs=[anywhere] * len(outs),
        scratch_shapes=[pltpu.VMEM(*s) for s in scratch]
        + [
            pltpu.SemaphoreType.DMA((remotes,)),
            pltpu.SemaphoreType.DMA((remotes,)),
            pltpu.SemaphoreType.DMA((64 + 10 * nc,)),
            pltpu.SemaphoreType.REGULAR((3,)),
        ],
        compiler_params=pltpu.CompilerParams(
            collective_id=1, has_side_effects=True, vmem_limit_bytes=VMEM_BYTES
        ),
    )(
        f["h2"], f["h2p"], f["gatep"], f["upz"], f["m"], f["mp"], mixed_left, f["h1"],
        f["dy"], f["dyp"], f["dgu"], f["wq"], f["seq"], f["lse"], f["r1"], f["pdh2"], f["pout"],
        f["small"], tokens, w_out, keep_t, sine_t,
    )


def widen(arrays):
    def body(*refs):
        n = len(arrays)
        ins, outs, held, wide = (refs[i * n : (i + 1) * n] for i in range(4))
        load, store = refs[4 * n :]
        loads = [pltpu.make_async_copy(ins[i], held[i], load.at[i]) for i in range(n)]
        for copy in loads:
            copy.start()
        stores = []
        for i in range(n):
            loads[i].wait()
            wide[i][...] = held[i][: wide[i].shape[0], :].astype(wide[i].dtype)
            stores.append(pltpu.make_async_copy(wide[i], outs[i], store.at[i]))
            stores[-1].start()
        for copy in stores:
            copy.wait()

    anywhere = pl.BlockSpec(memory_space=pl.ANY)
    n = len(arrays)
    shapes = [(rows, x.shape[1]) for x, rows, _ in arrays]
    return pl.pallas_call(
        body,
        out_shape=[jax.ShapeDtypeStruct(k, kind) for k, (_, _, kind) in zip(shapes, arrays)],
        in_specs=[anywhere] * n,
        out_specs=[anywhere] * n,
        scratch_shapes=[pltpu.VMEM(x.shape, x.dtype) for x, _, _ in arrays]
        + [pltpu.VMEM(k, kind) for k, (_, _, kind) in zip(shapes, arrays)]
        + [pltpu.SemaphoreType.DMA((n,)), pltpu.SemaphoreType.DMA((n,))],
        compiler_params=pltpu.CompilerParams(vmem_limit_bytes=VMEM_BYTES),
    )(*[x for x, _, _ in arrays])


def take(x, index):
    return lax.dynamic_index_in_dim(x, index, 0, keepdims=False)


def shards(tokens, cotangent, w_qkv, b_qkv, w_out, w_gate, w_up, w_down, norms):
    width = tokens.shape[-1]
    rows = 2 * tokens.shape[3]
    nd, nc = lax.axis_size("dp"), lax.axis_size("ctx")
    dp, ctx = lax.axis_index("dp"), lax.axis_index("ctx")
    x = tokens.reshape(rows, width)

    small = jnp.concatenate([norms.reshape(-1), b_qkv]).astype(F32)
    small = jnp.pad(small, (0, -small.shape[0] % 1024)).reshape(-1, 128)
    f = forward(
        nd, nc, x, cotangent.reshape(rows, width), small, w_qkv, w_gate, w_up, w_out, w_down
    )

    result, tokens_grad, g_gate, g_up, g_qkv, g_down, g_out, sums = backward(
        nd, nc, f, x, w_out
    )[:8]
    place = dp * nc + ctx
    norms_grad = lax.dynamic_index_in_dim(sums[:4].reshape(4, nd * nc, -1), place, 1, keepdims=False)
    bias = sums[4:, : 3 * width // nd].reshape(nd, 3, -1).transpose(1, 0, 2)

    result, tokens_grad, *grads = widen(
        [
            (result, rows, BF16),
            (tokens_grad, rows, F32),
            *[(g, g.shape[0], F32) for g in (g_qkv, g_gate, g_up)],
            (g_down, w_down.shape[0] // nc, F32),
            (g_out, w_out.shape[0] // nc, F32),
        ]
    )
    grad_qkv, grad_gate, grad_up, grad_down, grad_out = grads
    return (
        result.reshape(tokens.shape),
        tokens_grad.reshape(tokens.shape),
        grad_qkv,
        take(bias.reshape(nd * nc, -1), place),
        grad_out,
        grad_gate,
        grad_up,
        grad_down,
        norms_grad,
    )


def solution(mesh):
    blocks = P("dp", "ctx", None, None, None)
    owned = P(("dp", "ctx"), None)
    return jax.shard_map(
        shards,
        mesh=mesh,
        in_specs=(
            blocks,
            blocks,
            P("dp", None),
            P("dp"),
            P("dp", None),
            P("dp", None),
            P("dp", None),
            P("dp", None),
            P(None, "dp"),
        ),
        out_specs=(
            blocks,
            blocks,
            owned,
            P(("dp", "ctx")),
            owned,
            owned,
            owned,
            owned,
            P(None, ("dp", "ctx")),
        ),
        check_vma=False,
    )
```

```python
import jax
import jax.numpy as jnp
import numpy as np
from jax import lax
from jax.experimental import pallas as pl
from jax.experimental.pallas import tpu as pltpu
from jax.sharding import PartitionSpec as P

HEADS = 32
HDIM = 64
ROT = 16
MESH = pl.DeviceIdType.MESH
F32 = jnp.float32
BF16 = jnp.bfloat16
VMEM_BYTES = 63 * 1024 * 1024


def normalize_rows(field):
    centre = field - jnp.mean(field, axis=-1, keepdims=True)
    inverse = lax.rsqrt(jnp.mean(centre * centre, axis=-1, keepdims=True) + 1e-05)
    return (centre * inverse, inverse)


def norm_reverse(incoming, gain, scaled, inverse):
    inner = incoming * gain
    return inverse * (
        inner
        - jnp.mean(inner, axis=-1, keepdims=True)
        - scaled * jnp.mean(inner * scaled, axis=-1, keepdims=True)
    )


def last_dims(a, b):
    return lax.dot_general(a, b, (((1,), (1,)), ((), ())), preferred_element_type=F32)


def first_dims(a, b):
    return lax.dot_general(a, b, (((0,), (0,)), ((), ())), preferred_element_type=F32)


def plain(a, b):
    return lax.dot_general(a, b, (((1,), (0,)), ((), ())), preferred_element_type=F32)


def attention_shapes(length):
    block = min(256 if length <= 1024 else 128, length)
    segments = min(4, length // block)
    return block, segments, length // block // segments


def head_columns(heads, what, head):
    at = (what * heads + head) * HDIM
    return slice(at, at + HDIM)


def causal(scores, first_query):
    keys = lax.broadcasted_iota(jnp.int32, scores.shape, 0)
    queries = lax.broadcasted_iota(jnp.int32, scores.shape, 1) + first_query
    return jnp.where(keys <= queries, scores, -1e30)


def flip_one(i):
    return i + 1 - 2 * (i % 2)


def flip_bit(i, bit):
    return i + (1 << bit) - (2 << bit) * ((i // (1 << bit)) % 2)


def flip_bits(i, mask):
    for bit in range(mask.bit_length()):
        if mask >> bit & 1:
            i = flip_bit(i, bit)
    return i


def quarter_of(left, device, parts=4):
    n = left.shape[-2] // parts
    return pl.ds(pl.multiple_of(device * n, 16), n)


def first_cut(hidden):
    return min(1024, hidden)


def swapped_cut(hidden):
    return min(512, hidden)


def step_orders(nc):
    usual = list(range(nc.bit_length() - 1))
    return usual, [1, 0] + usual[2:]


def spread(mask, order):
    return sum((mask >> i & 1) << bit for i, bit in enumerate(order))


def halves(start, size):
    return pl.ds(pl.multiple_of(start, 64), size)


def lanes(start, size):
    return pl.ds(pl.multiple_of(start, 128), size)


class Copies:
    def __init__(self, send, recv, local):
        self.send, self.recv, self.local = send, recv, local
        self.remotes, self.locals, self.left = [], [], []

    def to(self, device, src, dst):
        at = len(self.remotes)
        copy = pltpu.make_async_remote_copy(
            src_ref=src,
            dst_ref=dst,
            send_sem=self.send.at[at],
            recv_sem=self.recv.at[at],
            device_id=device,
            device_id_type=MESH,
        )
        copy.start()
        self.remotes.append(copy)
        self.left.append(copy)
        return copy

    def gone(self, *copies):
        for copy in copies:
            copy.wait_send()
            self.left = [other for other in self.left if other is not copy]

    def here(self, src, dst):
        copy = pltpu.make_async_copy(src, dst, self.local.at[len(self.locals)])
        copy.start()
        self.locals.append(copy)
        return copy


def meet(axis_sizes):
    barrier = pltpu.get_barrier_semaphore()
    met = 0
    for axis, size in axis_sizes:
        me = lax.axis_index(axis)
        for k in range(1, size):
            pl.semaphore_signal(
                barrier, inc=1, device_id={axis: lax.rem(me + k, size)}, device_id_type=MESH
            )
            met += 1
    pl.semaphore_wait(barrier, met)


def attend(x_ref, o_ref, lse_ref, heads, head):
    length = x_ref.shape[0]
    block, segments, inner = attention_shapes(length)
    q_at, k_at, v_at = (head_columns(heads, i, head) for i in range(3))
    for segment in range(segments):
        count = (segment + 1) * inner * block
        keys = x_ref[:count, k_at]
        values = x_ref[:count, v_at]

        def step(i, _):
            start = pl.multiple_of((segment * inner + i) * block, block)
            query = x_ref[pl.ds(start, block), q_at] * 0.125
            scores = causal(last_dims(keys, query), start)
            top = jnp.max(scores, axis=0, keepdims=True)
            expo = jnp.exp(scores - top)
            total = jnp.sum(expo, axis=0, keepdims=True)
            mixed = first_dims(values, expo.astype(BF16)) / total
            o_ref[pl.ds(start, block), head * HDIM : (head + 1) * HDIM] = mixed.T.astype(BF16)
            lse_ref[head : head + 1, pl.ds(start, block)] = top + jnp.log(total)
            return 0

        if inner == 1:
            step(0, 0)
        else:
            lax.fori_loop(0, inner, step, 0)


def rotate_pair(u, keep, sine):
    lane = lax.broadcasted_iota(jnp.int32, u.shape, 1) % HDIM
    other = jnp.where(lane < ROT // 2, pltpu.roll(u, 128 - ROT // 2, 1), pltpu.roll(u, ROT // 2, 1))
    return u * keep + other * sine


def rotary_pair_tables(length):
    pairs = ROT // 2
    inverse = np.power(np.float32(10000.0), -np.arange(pairs, dtype=np.float32) / np.float32(pairs))
    angle = np.arange(length, dtype=np.float32)[:, None] * inverse.astype(np.float32)[None, :]
    cosine, sine = np.cos(angle), np.sin(angle)
    keep = np.concatenate([cosine, cosine, np.ones((length, HDIM - ROT), np.float32)], axis=1)
    signed = np.concatenate([-sine, sine, np.zeros((length, HDIM - ROT), np.float32)], axis=1)
    return np.tile(keep, (1, 2)).astype(np.float32), np.tile(signed, (1, 2)).astype(np.float32)


def tiles(total, size):
    return [(at, min(size, total - at)) for at in range(0, total, size)]


def over_tiles(total, size, step):
    whole = total // size
    if whole:

        def run(i, _):
            step(pl.multiple_of(i * size, size), size)
            return 0

        lax.fori_loop(0, whole, run, 0)
    if total % size:
        step(whole * size, total % size)


def turn_block(block, left, source, nd, nc):
    rows, width = block.shape
    part = width // (nd * nc)
    here = lanes(source * rows, rows)
    for at in range(0, width, 128):
        turned = block[:, at : at + 128].T
        for i in range(0, 128, part):
            d, c = (at + i) // (part * nc), (at + i) // part % nc
            left[c, d * part : (d + 1) * part, here] = turned[i : i + part]


def forward(nd, nc, tokens, cotangent, small, w_qkv, w_gate, w_up, w_out, w_down):
    rows, width = tokens.shape
    half = rows // 2
    many = nd * rows
    length = 2 * nc * half
    depth = w_qkv.shape[0]
    quarter = depth // 4
    heads_here = HEADS // nd
    groups = nc // nd
    heads = heads_here // groups
    span = heads * HDIM
    cols = heads_here * HDIM
    hidden = w_gate.shape[1] // nd
    down = w_down.shape[0]
    share_down = down // nc
    padded = share_down + -share_down % 16
    keep, sine = rotary_pair_tables(length)

    def body(
        tok_i, cot_i, small_i, wq_i, wg_i, wu_i, wo_i, wd_i, keep_i, sine_i,
        h1_o, dy_o, wq_o, seq_o, lse_o, mixed_o, r1_o, h2_o, m_o, dgu_o, pout_o, pdh2_o, small_o,
        dyp_o, mp_o, h2p_o, gatep_o, upz_o,
        tok, dy, sm, wq, h1, qkv, seq, lse, o, mixed, wo, part, ra, rb, r1, h2, wgu, wd, m, dgu,
        turns, left1, left2, m_t, mixed_t, dyp, send, recv, local,
    ):
        dp, ctx = lax.axis_index("dp"), lax.axis_index("ctx")
        near, across, far = flip_one(dp), (dp + 2) % nd, nd - 1 - dp
        spot = ctx % 4
        sides = [{"ctx": flip_bit(ctx, bit)} for bit in range(2)]
        links = Copies(send, recv, local)
        blocks = lambda ref, b: ref.at[halves(b * rows, rows)]

        get_tok = links.here(tok_i, blocks(tok, dp))
        get_turns = [
            links.here(table.at[halves(block * half, half)], turns.at[t, pl.ds(i * half, half)])
            for t, table in enumerate((keep_i, sine_i))
            for i, block in enumerate((ctx, 2 * nc - 1 - ctx))
        ]
        get_small = links.here(small_i, sm.at[dp])
        get_wq = [
            links.here(
                wq_i.at[:, lanes(j * width + dp * cols, cols)],
                wq.at[halves(dp * depth, depth), pl.ds(j * cols, cols)],
            )
            for j in range(3)
        ]
        meet((("dp", nd), ("ctx", nc)))

        def columns(w_i, w, e, at, n, to, which):
            first, size = (0, depth) if which is None else (which * quarter, quarter)
            return links.to(
                {"dp": e},
                w_i.at[halves(first, size), lanes(at, n)],
                w.at[halves(dp * depth + first, size), pl.ds(to, n)],
            )

        def share(w, copies, source):
            for copy in copies:
                copy.wait_recv()
            block = w.at[halves(source * depth + spot * quarter, quarter)]
            return [links.to(side, block, block) for side in sides]

        def cross(w, shared, source):
            passed = []
            for bit in range(2):
                shared[bit].wait_recv()
                start = source * depth + flip_bit(spot, bit) * quarter + bit * (quarter // 2)
                block = w.at[halves(start, quarter // 2)]
                passed.append(links.to(sides[1 - bit], block, block))
            return passed

        def qkv_columns(e, which):
            return [
                columns(wq_i, wq, e, j * width + e * cols, cols, j * cols, which) for j in range(3)
            ]

        def hidden_columns(e, which):
            return [
                columns(w_i, wgu, e, e * hidden, hidden, i * hidden, which)
                for i, w_i in enumerate((wg_i, wu_i))
            ]

        send_small = [links.to({"dp": e}, small_i, sm.at[dp]) for e in (near, across, far)]
        wq_x = [qkv_columns(e, spot) for e in (across, far)]
        send_tok = [links.to({"dp": e}, tok_i, blocks(tok, dp)) for e in (near, across)]
        wq_near = qkv_columns(near, None)
        send_dyp = [links.to(sides[1], cot_i, blocks(dyp, dp))]
        wgu_x = [hidden_columns(e, spot) for e in (far, across)]
        get_wo = links.here(wo_i, wo)
        get_wd = links.here(wd_i, wd)
        get_dy = links.here(cot_i, blocks(dy, dp))
        get_wgu = [
            links.here(
                w_i.at[:, lanes(dp * hidden, hidden)],
                wgu.at[halves(dp * depth, depth), pl.ds(i * hidden, hidden)],
            )
            for i, w_i in enumerate((wg_i, wu_i))
        ]

        get_small.wait()
        for copy in send_small:
            copy.wait_recv()

        def gain(row):
            lines = [
                sm[b, row * 4 + q : row * 4 + q + 1, :]
                for b in range(nd)
                for q in range(width // nd // 128)
            ]
            return jnp.concatenate(lines, axis=1)

        def first_norm(b):
            at = halves(b * rows, rows)
            hat, _ = normalize_rows(tok[at, :].astype(F32))
            h1[at, :] = (hat * gain(0) + gain(1)).astype(BF16)

        def turn_first(b):
            turn_block(h1[halves(b * rows, rows), :], left1, b, nd, nc)

        get_tok.wait()
        wq_s = [share(wq, copies, e) for copies, e in zip(wq_x, (across, far))]
        first_norm(dp)
        send_tok[0].wait_recv()
        first_norm(near)
        wq_c = cross(wq, wq_s[0], across)
        send_tok[1].wait_recv()
        forward_tok = links.to({"dp": near}, blocks(tok, across), blocks(tok, across))
        wq_c += cross(wq, wq_s[1], far)
        first_norm(across)
        forward_tok.wait_recv()
        first_norm(far)
        wgu_d = [c for e in (across, far) for c in hidden_columns(e, 3 - spot)]
        wgu_near = hidden_columns(near, None)
        send_dy = [links.to({"dp": e}, cot_i, blocks(dy, dp)) for e in (near, across)]
        put_small = links.here(sm, small_o)
        for copy in get_wq + get_turns:
            copy.wait()
        for copy in wq_near + wq_c:
            copy.wait_recv()
        put_wq = links.here(wq, wq_o)

        for at, n in tiles(3 * cols, 256):
            j = at // cols
            acc = plain(h1[...], wq[:, at : at + n])
            for q in range(n // 128):
                first = at % cols + q * 128
                line = (j * width + dp * cols + first) // 128
                per = 3 * width // nd // 128
                bias = sm[line // per, pl.ds(4 * (width // nd) // 128 + line % per, 1), :]
                for s in range(nd):
                    u = acc[s * rows : (s + 1) * rows, q * 128 : (q + 1) * 128] + bias
                    if j < 2:
                        u = rotate_pair(u, turns[0], turns[1])
                    u = u.astype(BF16)
                    if heads > 1:
                        g, off = first // span, first % span
                        qkv[g, s * rows : (s + 1) * rows, j * span + off : j * span + off + 128] = u
                    else:
                        for i in range(2):
                            qkv[
                                first // HDIM + i, s * rows : (s + 1) * rows, j * HDIM : (j + 1) * HDIM
                            ] = u[:, i * HDIM : (i + 1) * HDIM]

        mirror = 2 * nc - 1 - ctx
        go = []
        for k in range(1, nc):
            peer = lax.rem(ctx + k, nc)
            s, g = peer // groups, peer % groups
            for i, block in enumerate((ctx, mirror)):
                go.append(
                    links.to(
                        {"ctx": peer},
                        qkv.at[g, halves(s * rows + i * half, half)],
                        seq.at[halves(block * half, half)],
                    )
                )
        s, g = ctx // groups, ctx % groups
        stay = [
            links.here(
                qkv.at[g, halves(s * rows + i * half, half)], seq.at[halves(block * half, half)]
            )
            for i, block in enumerate((ctx, mirror))
        ]
        for b in range(nd):
            turn_first(b)
        put_h1 = links.here(left1, h1_o)
        for copy in stay:
            copy.wait()
        for copy in go:
            copy.wait_recv()
        put_seq = links.here(seq, seq_o)
        put_h1.wait()
        back, stay = [], []
        step = min(heads, 2)
        for head in range(heads):
            attend(seq, o, lse, heads, head)
            if (head + 1) % step:
                continue
            here = pl.ds((head + 1 - step) * HDIM, step * HDIM)
            for k in range(nc):
                peer = lax.rem(ctx + k, nc)
                for i, block in enumerate((peer, 2 * nc - 1 - peer)):
                    src = o.at[halves(block * half, half), here]
                    dst = mixed.at[g, halves(s * rows + i * half, half), here]
                    if k:
                        back.append(links.to({"ctx": peer}, src, dst))
                    else:
                        stay.append(links.here(src, dst))
        wgu_far = share(wgu, wgu_x[0], far)
        wgu_near2 = share(wgu, wgu_x[1], across)
        put_lse = links.here(lse, lse_o)
        get_wo.wait()
        for copy in stay:
            copy.wait()
        for copy in back:
            copy.wait_recv()

        def out_tile(at, n):
            acc = plain(mixed[0], wo[0:span, pl.ds(at, n)])
            for i in range(1, groups):
                acc += plain(mixed[i], wo[i * span : (i + 1) * span, pl.ds(at, n)])
            part[:, pl.ds(at, n)] = acc.astype(BF16)

        over_tiles(width, 512, out_tile)

        to_near = [
            links.to({"dp": near}, blocks(part, far), blocks(ra, 0)),
            links.to({"dp": near}, blocks(part, near), blocks(ra, 1)),
        ]
        for i in range(groups):
            mixed_t[i * span : (i + 1) * span, :] = mixed[i].T
        put_mixed = links.here(mixed_t, mixed_o)
        to_near[0].wait_recv()
        across_at = halves(across * rows, rows)
        part[across_at, :] = (part[across_at, :].astype(F32) + ra[:rows, :].astype(F32)).astype(BF16)
        to_across = links.to({"dp": across}, blocks(part, across), rb)
        send_dy[1].wait_recv()
        forward_dy = links.to({"dp": near}, blocks(dy, across), blocks(dy, across))
        to_near[1].wait_recv()
        own_at = halves(dp * rows, rows)
        r1[...] = tok[own_at, :].astype(F32) + (
            part[own_at, :].astype(F32) + ra[rows:, :].astype(F32)
        )
        to_across.wait_recv()
        r1[...] += rb[...].astype(F32)
        put_r1 = links.here(r1, r1_o)
        hat, _ = normalize_rows(r1[...])
        h2[own_at, :] = (hat * gain(2) + gain(3)).astype(BF16)
        send_h2 = [links.to({"dp": e}, blocks(h2, dp), blocks(h2, dp)) for e in (near, across)]
        send_dyp[0].wait_recv()
        share_dyp = [links.to({"dp": e}, blocks(dyp, dp), blocks(dyp, dp)) for e in (near, across)]
        turn_block(h2[own_at, :], left2, dp, nd, nc)
        send_h2[0].wait_recv()
        turn_block(h2[halves(near * rows, rows), :], left2, near, nd, nc)
        send_h2[1].wait_recv()
        forward_h2 = links.to({"dp": near}, blocks(h2, across), blocks(h2, across))
        turn_block(h2[halves(across * rows, rows), :], left2, across, nd, nc)
        get_wd.wait()
        get_dy.wait()
        for copy in get_wgu:
            copy.wait()
        for copy in wgu_near + wgu_far + wgu_near2 + wgu_d + [send_dy[0], forward_dy, forward_h2]:
            copy.wait_recv()
        turn_block(h2[halves(far * rows, rows), :], left2, far, nd, nc)
        put_h2 = links.here(left2, h2_o)
        put_dy = links.here(dy, dy_o)

        spare = nc // 2
        send_left = [
            links.to(
                sides[bit],
                left2.at[
                    flip_bits(flip_bit(ctx, bit), spread(2 * j, step_orders(nc)[bit])),
                    quarter_of(left2, dp),
                ],
                left1.at[bit * spare + j, quarter_of(left2, dp)],
            )
            for bit in range(2)
            for j in range(spare)
        ]
        send_gate = []
        def hidden_tile(at, n):
            here = pl.ds(at, n)
            gate = plain(h2[...], wgu[:, here])
            up = plain(h2[...], wgu[:, pl.ds(hidden + at, n)])
            dm = last_dims(dy[...], wd[here, :])
            sig = jax.nn.sigmoid(gate)
            m[:, here] = (gate * sig * up).astype(BF16)
            dgu[:, here] = (dm * up * sig * (1.0 + gate * (1.0 - sig))).astype(BF16)
            dgu[:, pl.ds(hidden + at, n)] = (dm * gate * sig).astype(BF16)

        if padded != share_down:
            m[:, hidden:] = jnp.zeros((many, padded - share_down), BF16)
        for at, n in tiles(hidden, 512):
            over_tiles(n, 256, lambda i, size, at=at: hidden_tile(at + i, size))
            here = pl.ds(at, n)
            if at + n <= first_cut(hidden):
                send_gate.append(links.to(sides[0], dgu.at[:, here], gatep_o.at[:, here]))
            if at + n <= swapped_cut(hidden):
                there = pl.ds(hidden + at, n)
                send_gate.append(links.to(sides[1], dgu.at[:, there], upz_o.at[:, here]))
        for c in range(nc):
            m_t[c] = m[:, c * share_down : c * share_down + padded].T
        put_m = links.here(m_t, m_o)

        put_dgu = links.here(dgu, dgu_o)
        send_m = []
        for j in range(nc // 2):
            owner = flip_bits(flip_bit(ctx, 1), spread(2 * j, step_orders(nc)[1]))
            send_m.append(links.to(sides[1], m_t.at[owner], mp_o.at[j]))
        share_dyp[1].wait_recv()
        forward_dyp = links.to({"dp": near}, blocks(dyp, across), blocks(dyp, across))
        for copy in send_left:
            copy.wait_recv()
        own_left = left1.at[:, quarter_of(left2, dp)]
        share_left = [links.to({"dp": e}, own_left, own_left) for e in (near, across)]

        def dh2_tile(at, n):
            here = pl.ds(at, n)
            h1[:, here] = last_dims(dgu[...], wgu[here, :]).astype(BF16)

        over_tiles(width, 256, dh2_tile)
        put_pdh2 = links.here(h1, pdh2_o)
        links.gone(*send_tok, forward_tok)

        def result_tile(at, n):
            here = pl.ds(at, n)
            tok[:, here] = plain(m[:, :hidden], wd[:, here]).astype(BF16)

        over_tiles(width, 256, result_tile)
        share_left[1].wait_recv()
        other_left = left1.at[:, quarter_of(left2, across)]
        forward_left = links.to({"dp": near}, other_left, other_left)
        put_pout = links.here(tok, pout_o)
        for copy in (share_dyp[0], forward_dyp, share_left[0], forward_left):
            copy.wait_recv()
        put_other = [links.here(dyp, dyp_o), links.here(left1, h2p_o)]
        for copy in send_m + send_gate:
            copy.wait_recv()

        links.gone(*links.left)
        for copy in (
            *put_other, put_small, put_wq, put_seq, put_lse, put_mixed, put_r1, put_h2, put_dy, put_m, put_dgu,
            put_pdh2, put_pout,
        ):
            copy.wait()

    anywhere = pl.BlockSpec(memory_space=pl.ANY)
    shape = jax.ShapeDtypeStruct
    remotes = 64 + 7 * nc
    outs = dict(
        h1=((nc, width // nc, many), BF16),
        dy=((many, width), BF16),
        wq=((width, 3 * cols), BF16),
        seq=((length, 3 * span), BF16),
        lse=((heads, length), F32),
        mixed=((cols, many), BF16),
        r1=((rows, width), F32),
        h2=((nc, width // nc, many), BF16),
        m=((nc, padded, many), BF16),
        dgu=((many, 2 * hidden), BF16),
        pout=((many, width), BF16),
        pdh2=((many, width), BF16),
        small=((nd,) + small.shape, F32),
        dyp=((many, width), BF16),
        mp=((nc // 2, padded, many), BF16),
        h2p=((nc, width // nc, many), BF16),
        gatep=((many, first_cut(hidden)), BF16),
        upz=((many, swapped_cut(hidden)), BF16),
    )
    scratch = [
        ((many, width), BF16),
        ((many, width), BF16),
        ((nd,) + small.shape, F32),
        ((width, 3 * cols), BF16),
        ((many, width), BF16),
        ((groups, many, 3 * span), BF16),
        ((length, 3 * span), BF16),
        ((heads, length), F32),
        ((length, span), BF16),
        ((groups, many, span), BF16),
        ((cols, width), BF16),
        ((many, width), BF16),
        ((2 * rows, width), BF16),
        ((rows, width), BF16),
        ((rows, width), F32),
        ((many, width), BF16),
        ((width, 2 * hidden), BF16),
        ((down, width), BF16),
        ((many, hidden + padded - share_down), BF16),
        ((many, 2 * hidden), BF16),
        ((2, rows, 128), F32),
        ((nc, width // nc, many), BF16),
        ((nc, width // nc, many), BF16),
        ((nc, padded, many), BF16),
        ((cols, many), BF16),
        ((many, width), BF16),
    ]
    results = pl.pallas_call(
        body,
        out_shape=[shape(*o) for o in outs.values()],
        in_specs=[anywhere] * 10,
        out_specs=[anywhere] * len(outs),
        scratch_shapes=[pltpu.VMEM(*s) for s in scratch]
        + [
            pltpu.SemaphoreType.DMA((remotes,)),
            pltpu.SemaphoreType.DMA((remotes,)),
            pltpu.SemaphoreType.DMA((40,)),
        ],
        compiler_params=pltpu.CompilerParams(
            collective_id=0, has_side_effects=True, vmem_limit_bytes=VMEM_BYTES
        ),
    )(tokens, cotangent, small, w_qkv, w_gate, w_up, w_out, w_down, keep, sine)
    return dict(zip(outs, results))


def attend_back(x_ref, lse_ref, do_ref, d_ref, heads, head):
    length = x_ref.shape[0]
    block, segments, inner = attention_shapes(length)
    q_at, k_at, v_at = (head_columns(heads, i, head) for i in range(3))
    o_at = slice(head * HDIM, (head + 1) * HDIM)
    for segment in range(segments):
        count = (segment + 1) * inner * block
        keys = x_ref[:count, k_at]
        values = x_ref[:count, v_at]

        def step(i, _):
            start = pl.multiple_of((segment * inner + i) * block, block)
            query = x_ref[pl.ds(start, block), q_at] * 0.125
            dout = do_ref[pl.ds(start, block), o_at]
            scores = causal(last_dims(keys, query), start)
            probs = jnp.exp(scores - lse_ref[head : head + 1, pl.ds(start, block)])
            d_probs = last_dims(values, dout)
            centre = jnp.sum(probs * d_probs, axis=0, keepdims=True)
            d_scores = (probs * (d_probs - centre)).astype(BF16)
            d_ref[:count, v_at] += plain(probs.astype(BF16), dout)
            d_ref[:count, k_at] += plain(d_scores, query)
            d_ref[pl.ds(start, block), q_at] = first_dims(keys, d_scores).T * 0.125
            return 0

        if inner == 1:
            step(0, 0)
        else:
            lax.fori_loop(0, inner, step, 0)


class GroupSum:
    def __init__(self, links, dp, nd, rows, part, ra, rb):
        self.links, self.rows = links, rows
        self.part, self.ra, self.rb = part, ra, rb
        self.near, self.across, self.far = flip_one(dp), (dp + 2) % nd, nd - 1 - dp
        self.dp = dp
        block = lambda ref, b: ref.at[halves(b * rows, rows)]
        self.a = [
            links.to({"dp": self.near}, block(part, self.far), block(ra, 0)),
            links.to({"dp": self.near}, block(part, self.near), block(ra, 1)),
        ]

    def middle(self):
        rows, at = self.rows, halves(self.across * self.rows, self.rows)
        self.a[0].wait_recv()
        self.part[at, :] = (
            self.part[at, :].astype(F32) + self.ra[:rows, :].astype(F32)
        ).astype(BF16)
        self.b = self.links.to({"dp": self.across}, self.part.at[at], self.rb)

    def total(self):
        rows, at = self.rows, halves(self.dp * self.rows, self.rows)
        self.a[1].wait_recv()
        self.b.wait_recv()
        return (
            self.part[at, :].astype(F32)
            + self.ra[rows:, :].astype(F32)
            + self.rb[...].astype(F32)
        )


class Gradient:
    def __init__(self, links, ctx, bits, left, right, slots, landing, stage):
        self.links, self.ctx, self.bits, self.nc = links, ctx, bits, 1 << len(bits)
        nc = self.nc
        self.left, self.right, self.slots = left, right, slots
        self.landing = landing
        self.stage = stage.at[pl.ds(0, slots.shape[1]), pl.ds(0, slots.shape[2])]
        self.sent = {}
        low = lambda j: (j & -j) or nc
        self.order = sorted(range(nc // 2), key=lambda j: (low(j), low(j & (j - 1))))

    def _landing(self, bit, j):
        base = sum(self.nc >> (b + 1) for b in range(1, bit))
        return self.landing.at[base + (j >> bit)]

    def compute(self, send=True):
        for j in self.order:
            self.slot(j, send)

    def start(self, part):
        for j in self.half(part):
            self._pass(1, j)

    def half(self, part):
        odd = [j for j in self.order if j % 2]
        return odd[part * len(odd) // 2 : (part + 1) * len(odd) // 2]

    def add_half(self, part):
        for j in self.half(part):
            self.add_slot(1, j - 1)

    def slot(self, j, send=True):
        mine, other = self.left[0][j], self.left[1][j]

        def step(at, n):
            here = pl.ds(at, n)
            acc = plain(mine, self.right[0][:, here]) + plain(other, self.right[1][:, here])
            self.slots[j, :, here] = acc.astype(BF16)

        over_tiles(self.slots.shape[2], 512, step)
        if send:
            self._pass(1, j)

    def _pass(self, bit, j):
        low = j & -j
        if j and low == 1 << (bit - 1):
            self.sent[bit, j] = self.links.to(
                {"ctx": flip_bit(self.ctx, self.bits[bit])},
                self.slots.at[j],
                self._landing(bit, j - low),
            )

    def add(self, bit):
        for j in self.order:
            if j % (1 << bit) == 0:
                self.add_slot(bit, j)

    def add_slot(self, bit, j):
        self.sent[bit, j + (1 << (bit - 1))].wait_recv()
        self.links.here(self._landing(bit, j), self.stage).wait()

        def step(at, n):
            here = pl.ds(at, n)
            acc = self.slots[j, :, here].astype(F32) + self.stage[:, here].astype(F32)
            self.slots[j, :, here] = acc.astype(BF16)

        over_tiles(self.slots.shape[2], 512, step)
        self._pass(bit + 1, j)


def backward(nd, nc, f, tokens, w_out):
    rows, width = tokens.shape
    half = rows // 2
    many = nd * rows
    length, wide = f["seq"].shape
    heads = f["lse"].shape[0]
    span = heads * HDIM
    groups = nc // nd
    cols = groups * span
    hidden = f["dgu"].shape[1] // 2
    slots = nc // 2
    share = width // (nd * nc)
    tall = {"gu": nd * share, "down": f["m"].shape[1], "out": cols // nc, "qkv": nd * share}
    flat = {"gu": 2 * hidden, "down": width, "out": width, "qkv": 3 * cols}
    cut = first_cut(hidden)
    cut_z = swapped_cut(hidden)
    ranges = [(0, cut // 2), (cut // 2, cut - cut // 2)]
    ranges += [(hidden + cut_z, hidden - cut_z), (cut, hidden - cut)]
    range_z = (hidden, cut_z)
    names = ("down", "gu", "qkv", "out")
    bits = nc.bit_length() - 1
    keep_t, sine_t = rotary_pair_tables(length)
    chunk = length if length <= 1024 else 256
    strip = 256 if length <= 1024 else 128
    mixed_left = f["mixed"].reshape(nc, cols // nc, many)

    def body(
        h2_l, h2p_l, gatep_i, upz_i, m_l, mp_l, mixed_l, h1_l, dy_i, dyp_i, dgu_i, wq_i, seq_i, lse_i, r1_i, pdh2_i, pout_i,
        small_i, tok_i, wo_i, keep_i, sine_i,
        out_o, tg_o, gate_o, up_o, qkv_o, down_o, out_g_o, sums_o,
        land_down, land_gu, land_qkv, land_out,
        l_gu, l_up, l_down, l_out, l_qkv, dgu, dgup, dy, dyp, da, dq, dqp,
        s_down, s_gu, s_qkv, s_out, stage,
        part, ra, rb, r1, dr1, x, sm, wq, wo, seq, lse,
        dmix, dseq, dx, keep, sine, dback, sums, sums_in,
        send, recv, local, free,
    ):
        dp, ctx = lax.axis_index("dp"), lax.axis_index("ctx")
        near, across, far = flip_one(dp), (dp + 2) % nd, nd - 1 - dp
        links = Copies(send, recv, local)
        blocks = lambda ref, b: ref.at[halves(b * rows, rows)]
        own_at = halves(dp * rows, rows)
        beside = {"ctx": flip_bit(ctx, 0)}

        usual, swapped = step_orders(nc)

        def get_left(left_i, left, order=usual):
            return [
                links.here(left_i.at[flip_bits(ctx, spread(2 * j, order))], left.at[0, j])
                for j in range(slots)
            ]

        get_part = links.here(pdh2_i, part)
        get_gu = get_left(h2_l, l_gu)
        get_gu += [
            links.here(a, b)
            for a, b in (
                (h2p_l.at[pl.ds(0, slots)], l_gu.at[1]),
                (dgu_i, dgu),
                (gatep_i, dgup.at[:, pl.ds(0, cut)]),
            )
        ]
        get_up = get_left(h2_l, l_up, swapped)
        get_up += [
            links.here(a, b)
            for a, b in ((h2p_l.at[pl.ds(slots, slots)], l_up.at[1]), (upz_i, dgup.at[:, pl.ds(*range_z)]))
        ]
        get_down = get_left(m_l, l_down, swapped)
        get_down += [
            links.here(a, b) for a, b in ((mp_l, l_down.at[1]), (dy_i, dy), (dyp_i, dyp))
        ]
        get_first = [links.here(a, b) for a, b in ((r1_i, r1), (small_i, sm))]
        get_wo = links.here(wo_i, wo)
        get_attn = [links.here(a, b) for a, b in ((seq_i, seq), (lse_i, lse))]
        get_late = get_left(h1_l, l_qkv) + get_left(mixed_l, l_out) + [links.here(tok_i, x)]

        def tables(c):
            at = pl.ds(c * chunk, chunk)
            return [links.here(a.at[at], b) for a, b in ((keep_i, keep), (sine_i, sine))]

        get_tables = tables(0)

        def strips(i):
            return links.here(wq_i.at[pl.ds(i * strip, strip)], wq.at[i % 2])

        get_wq = [strips(0), strips(1)]

        def gain(row):
            lines = [
                sm[b, row * 4 + q : row * 4 + q + 1, :]
                for b in range(nd)
                for q in range(width // nd // 128)
            ]
            return jnp.concatenate(lines, axis=1)

        down = Gradient(links, ctx, swapped, l_down, (dy, dyp), s_down, land_down, stage)
        gu = []
        for at, n in ranges + [range_z]:
            here = pl.ds(at, n)
            order, left = (swapped, l_up) if at == hidden else (usual, l_gu)
            gu.append(
                Gradient(
                    links, ctx, order, left, (dgu.at[:, here], dgup.at[:, here]),
                    s_gu.at[:, :, here], land_gu.at[:, :, here], stage,
                )
            )
        up = gu.pop()
        qkv = []
        for j in range(3):
            at = pl.ds(j * cols, cols)
            qkv.append(
                Gradient(
                    links, ctx, usual, l_qkv, (dq.at[:, at], dqp.at[:, at]),
                    s_qkv.at[:, :, at], land_qkv.at[:, :, at], stage,
                )
            )
        out = Gradient(links, ctx, usual, l_out, (da, dyp), s_out, land_out, stage)

        meet((("dp", nd), ("ctx", nc)))
        get_part.wait()
        sum2 = GroupSum(links, dp, nd, rows, part, ra, rb)

        def send_right(i):
            here = pl.ds(*ranges[i])
            return links.to(beside, dgu_i.at[:, here], dgup.at[:, here])

        right_gu = [None, None, send_right(2)]
        for copy in get_gu:
            copy.wait()
        gu[0].slot(gu[0].order[0])
        sum2.middle()
        for j in gu[0].order[1:]:
            gu[0].slot(j)
        for copy in get_first + get_down + get_up:
            copy.wait()
        up.compute()
        gu[1].compute()
        down.compute(send=False)
        for i, device in enumerate((beside, {"dp": near}, {"dp": across})):
            pl.semaphore_signal(free.at[i], inc=1, device_id=device, device_id_type=MESH)

        dh2 = sum2.total()
        hat, inverse = normalize_rows(r1[...])
        dr1[...] = dy[own_at, :].astype(F32) + norm_reverse(dh2, gain(2), hat, inverse)
        da[own_at, :] = dr1[...].astype(BF16)
        send_da = [links.to({"dp": e}, blocks(da, dp), blocks(da, dp)) for e in (near, across)]
        pl.semaphore_wait(free.at[0], 1)
        right_out = links.to(beside, blocks(da, dp), blocks(dyp, dp))
        sums[2:3, :] = jnp.sum(dh2 * hat, axis=0, keepdims=True)
        sums[3:4, :] = jnp.sum(dh2, axis=0, keepdims=True)
        dx[...] = jnp.zeros_like(dx)
        if bits > 1:
            gu[0].add(1)
        send_da[1].wait_recv()
        forward_da = links.to({"dp": near}, blocks(da, across), blocks(da, across))
        get_wo.wait()
        send_da[0].wait_recv()
        forward_da.wait_recv()

        for g in range(groups):
            dmix[g] = last_dims(da[...], wo[g * span : (g + 1) * span, :]).astype(BF16)
        mirror = 2 * nc - 1 - ctx
        go = []
        for k in range(1, nc):
            peer = lax.rem(ctx + k, nc)
            s, g = peer // groups, peer % groups
            for i, block in enumerate((ctx, mirror)):
                go.append(
                    links.to(
                        {"ctx": peer},
                        dmix.at[g, halves(s * rows + i * half, half)],
                        dseq.at[halves(block * half, half)],
                    )
                )
        s, g = ctx // groups, ctx % groups
        stay = [
            links.here(
                dmix.at[g, halves(s * rows + i * half, half)], dseq.at[halves(block * half, half)]
            )
            for i, block in enumerate((ctx, mirror))
        ]
        right_gu.append(send_right(3))

        left_qkv = [
            links.to(
                beside,
                h1_l.at[flip_bits(flip_bit(ctx, 0), 2 * j), quarter_of(l_qkv, dp)],
                l_qkv.at[1, j, quarter_of(l_qkv, dp)],
            )
            for j in range(slots)
        ]
        left_out = [
            links.to(beside, mixed_l.at[flip_bits(flip_bit(ctx, 0), 2 * j)], l_out.at[1, j])
            for j in range(slots)
        ]
        right_gu[2].wait_recv()
        gu[2].compute()
        if bits > 1:
            up.add(1)
            gu[1].add(1)

        def share_right():
            right_out.wait_recv()
            for i in (1, 2):
                pl.semaphore_wait(free.at[i], 1)
            block = blocks(dyp, dp)
            return [links.to({"dp": e}, block, block) for e in (near, across)]

        def share_left():
            for copy in left_qkv:
                copy.wait_recv()
            block = l_qkv.at[1, :, quarter_of(l_qkv, dp)]
            return [links.to({"dp": e}, block, block) for e in (near, across)]

        for copy in get_attn + stay:
            copy.wait()
        for copy in go:
            copy.wait_recv()
        down.start(0)
        shared_right = share_right()
        for head in range(heads):
            attend_back(seq, lse, dseq, dx, heads, head)
        for c in range(length // chunk):
            for copy in get_tables if c == 0 else tables(c):
                copy.wait()
            here = slice(c * chunk, (c + 1) * chunk)
            for at in range(0, wide, 128):
                n = min(128, wide - at)
                u = dx[here, at : at + n]
                if at < 2 * span:
                    u = rotate_pair(u, keep[...], -sine[...])
                seq[here, at : at + n] = u.astype(BF16)

        back = []
        for k in range(1, nc):
            peer = lax.rem(ctx + k, nc)
            for i, block in enumerate((peer, 2 * nc - 1 - peer)):
                back.append(
                    links.to(
                        {"ctx": peer},
                        seq.at[halves(block * half, half)],
                        dback.at[g, halves(s * rows + i * half, half)],
                    )
                )
        stay = [
            links.here(
                seq.at[halves(block * half, half)], dback.at[g, halves(s * rows + i * half, half)]
            )
            for i, block in enumerate((ctx, mirror))
        ]
        shared_left = share_left()
        shared_right[1].wait_recv()
        forward_right = links.to({"dp": near}, blocks(dyp, across), blocks(dyp, across))
        for copy in get_late:
            copy.wait()
        right_gu[3].wait_recv()
        gu[3].compute()
        shared_left[1].wait_recv()
        block = l_qkv.at[1, :, quarter_of(l_qkv, across)]
        forward_left = links.to({"dp": near}, block, block)
        for copy in left_out + [shared_right[0], forward_right]:
            copy.wait_recv()
        out.compute()
        for copy in stay:
            copy.wait()
        for copy in back:
            copy.wait_recv()
        for g_ in range(groups):
            for j in range(3):
                at = j * cols + g_ * span
                dq[:, at : at + span] = dback[g_, :, j * span : (j + 1) * span]
        right_qkv = []

        def send_qkv():
            here = pl.ds(len(right_qkv) * cols, cols)
            right_qkv.append(links.to(beside, dq.at[:, here], dqp.at[:, here]))

        send_qkv()
        if bits > 1:
            gu[2].add(1)
        send_qkv()
        down.add_half(0)
        links.gone(*sum2.a, sum2.b)
        for i in range(width // strip):
            get_wq[i].wait()
            part[:, i * strip : (i + 1) * strip] = last_dims(dq[...], wq[i % 2]).astype(BF16)
            if i + 2 < width // strip:
                get_wq.append(strips(i + 2))
        sum1 = GroupSum(links, dp, nd, rows, part, ra, rb)
        send_qkv()
        for copy in (shared_left[0], forward_left):
            copy.wait_recv()

        def compute_qkv(j):
            right_qkv[j].wait_recv()
            qkv[j].compute()

        compute_qkv(0)
        sum1.middle()
        if bits > 1:
            gu[3].add(1)
        sums[4:, :] = jnp.zeros((nd, width), F32)
        sums[pl.ds(4 + dp, 1), : 3 * cols] = jnp.sum(dq[...].astype(F32), axis=0, keepdims=True)

        arriving, put = [], []

        def to_owner(slots_ref, spans):
            for e in (near, across, far, dp):
                for dst, at, to, n, every in spans:
                    src = slots_ref.at[0, pl.ds(pl.multiple_of(e * share, 16), share), pl.ds(at, n)]
                    place = dst.at[:, lanes(to + dp * every, n)]
                    if e is dp:
                        put.append(links.here(src, place))
                    else:
                        arriving.append(links.to({"dp": e}, src, place))

        def close_gu(piece, span_of):
            for bit in range(2, bits):
                piece.add(bit)
            at, n = span_of
            for dst, base in ((gate_o, 0), (up_o, hidden)):
                first, last = max(at, base), min(at + n, base + hidden)
                if first < last:
                    to_owner(s_gu, ((dst, first, first - base, last - first, hidden),))

        def close_qkv(j):
            for bit in range(2, bits):
                qkv[j].add(bit)
            to_owner(s_qkv, ((qkv_o, j * cols, j * width, cols, cols),))

        compute_qkv(1)
        down.start(1)
        close_gu(gu[0], ranges[0])
        close_gu(up, range_z)
        if bits > 1:
            out.add(1)
        compute_qkv(2)

        dh1 = sum1.total()
        hat1, inverse1 = normalize_rows(x[...].astype(F32))
        sums[0:1, :] = jnp.sum(dh1 * hat1, axis=0, keepdims=True)
        sums[1:2, :] = jnp.sum(dh1, axis=0, keepdims=True)
        partners = [("dp", flip_bit(dp, b)) for b in range(nd.bit_length() - 1)]
        partners += [("ctx", flip_bit(ctx, b)) for b in range(bits)]
        sums_out = []

        def start_sums():
            i = len(sums_out)
            if i < len(partners):
                axis, device = partners[i]
                sums_out.append(links.to({axis: device}, sums, sums_in.at[i]))

        def end_sums():
            i = len(sums_out) - 1
            sums_out[i].wait_recv()
            links.gone(sums_out[i])
            sums[...] += sums_in[i]

        def next_sums():
            end_sums()
            start_sums()

        start_sums()
        dr1[...] += norm_reverse(dh1, gain(0), hat1, inverse1)
        put_tg = links.here(dr1, tg_o)
        links.gone(*sum1.a, sum1.b)
        get_pout = links.here(pout_i, part)
        next_sums()
        get_pout.wait()
        sum0 = GroupSum(links, dp, nd, rows, part, ra, rb)
        if bits > 1:
            qkv[0].add(1)
        close_gu(gu[1], ranges[1])
        next_sums()
        sum0.middle()
        next_sums()
        if bits > 1:
            qkv[1].add(1)
        x[...] = (r1[...] + sum0.total()).astype(BF16)
        put_out = links.here(x, out_o)
        for i in range(2, len(ranges)):
            close_gu(gu[i], ranges[i])
        if bits > 1:
            qkv[2].add(1)
        next_sums()
        down.add_half(1)
        for bit in range(2, bits):
            down.add(bit)
        put.append(links.here(s_down.at[0], down_o))
        for bit in range(2, bits):
            out.add(bit)
        put.append(links.here(s_out.at[0], out_g_o))
        close_qkv(0)
        close_qkv(1)
        while len(sums_out) < len(partners):
            next_sums()
        close_qkv(2)
        end_sums()
        put_sums = [links.here(sums, sums_o), put_tg, put_out]
        for copy in arriving:
            copy.wait_recv()
        links.gone(*links.left)
        for copy in put + put_sums:
            copy.wait()

    anywhere = pl.BlockSpec(memory_space=pl.ANY)
    shape = jax.ShapeDtypeStruct
    outs = [
        ((rows, width), BF16),
        ((rows, width), F32),
        ((share, nd * hidden), BF16),
        ((share, nd * hidden), BF16),
        ((share, 3 * width), BF16),
        ((tall["down"], width), BF16),
        ((tall["out"], width), BF16),
        ((4 + nd, width), F32),
        *[((max(1, slots - 1), tall[k], flat[k]), BF16) for k in names],
    ]
    scratch = [
        *[((2, slots, tall[k], many), BF16) for k in ("gu", "gu", "down", "out", "qkv")],
        ((many, 2 * hidden), BF16),
        ((many, 2 * hidden), BF16),
        ((many, width), BF16),
        ((many, width), BF16),
        ((many, width), BF16),
        ((many, 3 * cols), BF16),
        ((many, 3 * cols), BF16),
        *[((slots, tall[k], flat[k]), BF16) for k in names],
        ((max(tall.values()), width), BF16),
        ((many, width), BF16),
        ((2 * rows, width), BF16),
        ((rows, width), BF16),
        ((rows, width), F32),
        ((rows, width), F32),
        ((rows, width), BF16),
        (f["small"].shape, F32),
        ((2, strip, 3 * cols), BF16),
        ((cols, width), BF16),
        ((length, wide), BF16),
        ((heads, length), F32),
        ((groups, many, span), BF16),
        ((length, span), BF16),
        ((length, wide), F32),
        ((chunk, 128), F32),
        ((chunk, 128), F32),
        ((groups, many, wide), BF16),
        ((4 + nd, width), F32),
        ((bits + nd.bit_length() - 1, 4 + nd, width), F32),
    ]
    remotes = 64 + 4 * nc + 7 * nc
    return pl.pallas_call(
        body,
        out_shape=[shape(*o) for o in outs],
        in_specs=[anywhere] * 22,
        out_specs=[anywhere] * len(outs),
        scratch_shapes=[pltpu.VMEM(*s) for s in scratch]
        + [
            pltpu.SemaphoreType.DMA((remotes,)),
            pltpu.SemaphoreType.DMA((remotes,)),
            pltpu.SemaphoreType.DMA((64 + 10 * nc,)),
            pltpu.SemaphoreType.REGULAR((3,)),
        ],
        compiler_params=pltpu.CompilerParams(
            collective_id=1, has_side_effects=True, vmem_limit_bytes=VMEM_BYTES
        ),
    )(
        f["h2"], f["h2p"], f["gatep"], f["upz"], f["m"], f["mp"], mixed_left, f["h1"],
        f["dy"], f["dyp"], f["dgu"], f["wq"], f["seq"], f["lse"], f["r1"], f["pdh2"], f["pout"],
        f["small"], tokens, w_out, keep_t, sine_t,
    )


def widen(arrays):
    def body(*refs):
        n = len(arrays)
        ins, outs, held, wide = (refs[i * n : (i + 1) * n] for i in range(4))
        load, store = refs[4 * n :]
        loads = [pltpu.make_async_copy(ins[i], held[i], load.at[i]) for i in range(n)]
        for copy in loads:
            copy.start()
        stores = []
        for i in range(n):
            loads[i].wait()
            wide[i][...] = held[i][: wide[i].shape[0], :].astype(wide[i].dtype)
            stores.append(pltpu.make_async_copy(wide[i], outs[i], store.at[i]))
            stores[-1].start()
        for copy in stores:
            copy.wait()

    anywhere = pl.BlockSpec(memory_space=pl.ANY)
    n = len(arrays)
    shapes = [(rows, x.shape[1]) for x, rows, _ in arrays]
    return pl.pallas_call(
        body,
        out_shape=[jax.ShapeDtypeStruct(k, kind) for k, (_, _, kind) in zip(shapes, arrays)],
        in_specs=[anywhere] * n,
        out_specs=[anywhere] * n,
        scratch_shapes=[pltpu.VMEM(x.shape, x.dtype) for x, _, _ in arrays]
        + [pltpu.VMEM(k, kind) for k, (_, _, kind) in zip(shapes, arrays)]
        + [pltpu.SemaphoreType.DMA((n,)), pltpu.SemaphoreType.DMA((n,))],
        compiler_params=pltpu.CompilerParams(vmem_limit_bytes=VMEM_BYTES),
    )(*[x for x, _, _ in arrays])


def take(x, index):
    return lax.dynamic_index_in_dim(x, index, 0, keepdims=False)


def shards(tokens, cotangent, w_qkv, b_qkv, w_out, w_gate, w_up, w_down, norms):
    width = tokens.shape[-1]
    rows = 2 * tokens.shape[3]
    nd, nc = lax.axis_size("dp"), lax.axis_size("ctx")
    dp, ctx = lax.axis_index("dp"), lax.axis_index("ctx")
    x = tokens.reshape(rows, width)

    small = jnp.concatenate([norms.reshape(-1), b_qkv]).astype(F32)
    small = jnp.pad(small, (0, -small.shape[0] % 1024)).reshape(-1, 128)
    f = forward(
        nd, nc, x, cotangent.reshape(rows, width), small, w_qkv, w_gate, w_up, w_out, w_down
    )

    result, tokens_grad, g_gate, g_up, g_qkv, g_down, g_out, sums = backward(
        nd, nc, f, x, w_out
    )[:8]
    place = dp * nc + ctx
    norms_grad = lax.dynamic_index_in_dim(sums[:4].reshape(4, nd * nc, -1), place, 1, keepdims=False)
    bias = sums[4:, : 3 * width // nd].reshape(nd, 3, -1).transpose(1, 0, 2)

    result, tokens_grad, *grads = widen(
        [
            (result, rows, BF16),
            (tokens_grad, rows, F32),
            *[(g, g.shape[0], F32) for g in (g_qkv, g_gate, g_up)],
            (g_down, w_down.shape[0] // nc, F32),
            (g_out, w_out.shape[0] // nc, F32),
        ]
    )
    grad_qkv, grad_gate, grad_up, grad_down, grad_out = grads
    return (
        result.reshape(tokens.shape),
        tokens_grad.reshape(tokens.shape),
        grad_qkv,
        take(bias.reshape(nd * nc, -1), place),
        grad_out,
        grad_gate,
        grad_up,
        grad_down,
        norms_grad,
    )


def solution(mesh):
    blocks = P("dp", "ctx", None, None, None)
    owned = P(("dp", "ctx"), None)
    return jax.shard_map(
        shards,
        mesh=mesh,
        in_specs=(
            blocks,
            blocks,
            P("dp", None),
            P("dp"),
            P("dp", None),
            P("dp", None),
            P("dp", None),
            P("dp", None),
            P(None, "dp"),
        ),
        out_specs=(
            blocks,
            blocks,
            owned,
            P(("dp", "ctx")),
            owned,
            owned,
            owned,
            owned,
            P(None, ("dp", "ctx")),
        ),
        check_vma=False,
    )
```
